32 devices in a mesh: table: 16 (over z, y, x), group: 2 (over core).
Axes of the slice: x: 2, y: 2, z: 4, core: 2. Of those that a mesh axis runs over, the one named last changes fastest.
Arguments:
- item_owner: int32 [16384, 1], P(('table', 'group')), may hold values from 0 to 15; in each aligned block of 512 rows (0 to 511, 512 to 1023, ...) at most 48 rows name the same one
- item_row: int32 [16384], P(('table', 'group')), may hold values from 0 to 2047
- lengths: int32 [32, 8], P(('table', 'group')), may hold values from 1 to 256, 512 in all within a row
- table: bfloat16 [32768, 512], P('table'), may hold values from -6 to 6
- w_in: bfloat16 [512, 2048], replicated, may hold values from -0.25 to 0.25
- w_out: bfloat16 [512, 512], replicated, may hold values from -0.25 to 0.25
- gain: float32 [512], replicated, may hold values from 0.1 to 1.9
- cotangent: bfloat16 [16384, 512], P(('table', 'group')), may hold values from -6 to 6
Outputs:
- result: bfloat16 [16384, 512], P(('table', 'group'))
- table_grad: float32 [32768, 512], P(('table', 'group'))
- w_in_grad: float32 [512, 2048], P('table', 'group')
- w_out_grad: float32 [512, 512], P('table')
- gain_grad: float32 [512], P('table')
The draws below stay inside these ranges and needn't reach their ends.
Inputs may be any that keep to these rules, and one draw needn't show every extreme that they name: `item_owner`: among the 512 items of one device, no index of table owns more than 48 items' rows, a bound that some block reaches.
All inputs are finite; a program needn't handle non-finite values.
Results may differ from the reference program's by a relative error of at most 0.008.
Values may be sent and summed in bfloat16 or wider, within the bound.
No kernel may reach another device: no remote copies, remote signals or barrier semaphores. Data moves between devices by JAX's collectives and lax.ppermute only.
A program may use at most 128 MiB of HBM per device.

```python
import math
import jax
import jax.numpy as jnp
import numpy as np
from jax import lax

D = 512
HEADS = 8
HEAD_DIM = 64
TOK_DEV = 512
SEGS = 8
LMAX = 256
ITEM_DEV = 2048
CAP = 48
OWNERS = 16
TOKENS = 16384
ITEMS = 32768
N_TABLE = 16
N_GROUP = 2


def touch_ends(drawn, own_key, low, largest):
    place = [jax.random.randint(jax.random.fold_in(own_key, axis), (), 0, length) for axis, length in enumerate(drawn.shape)]
    widest = drawn.shape.index(max(drawn.shape))
    next_to = place[:widest] + [(place[widest] + 1) % drawn.shape[widest]] + place[widest + 1:]
    return drawn.at[tuple(place)].set(low).at[tuple(next_to)].set(largest)


def block_scale(key, shape, pieces, low, largest):
    def one(dim, shards_of):
        steps = jax.random.uniform(jax.random.fold_in(jax.random.fold_in(key, 6), dim), (shards_of,), jnp.float32, low / len(pieces), largest / len(pieces))
        return jnp.repeat(jnp.exp(steps), shape[dim] // shards_of).reshape((-1,) + (1,) * (len(shape) - dim - 1))

    factor_of = one(*pieces[0])
    for cut in pieces[1:]:
        factor_of = factor_of * one(*cut)
    return factor_of


def profile(amount, total, bound, lean):
    portions = [(1 << 20) // math.isqrt(standing ** lean) + 1 for standing in range(2, amount + 1)]
    rest, given = total - bound - (amount - 1), [1] * (amount - 1)
    while rest > 0:
        candidates = [i for i in range(amount - 1) if given[i] < bound]
        mass, remaining = sum([portions[i] for i in candidates]), rest
        for i in candidates:
            extra = min(bound - given[i], max(1, remaining * portions[i] // mass), rest)
            given[i] = given[i] + extra
            rest = rest - extra
    return np.array([bound] + given)


def uneven(stream_key, number_of, total, bound, lean):
    if number_of == 2:
        one = jax.random.randint(stream_key, (), max(1, total - bound), min(bound, total - 1) + 1)
        return jnp.stack([one, total - one])
    sizes = jnp.asarray(profile(number_of, total, bound, lean), jnp.int32)
    couples = (number_of - 1) // 2
    giver, receiver = sizes[1:1 + 2 * couples:2], sizes[2:2 + 2 * couples:2]
    room = jnp.minimum(giver - 1, bound - receiver)
    shifted = jax.random.randint(jax.random.fold_in(stream_key, 1), (couples,), 0, 1 << 20) % (room + 1)
    sizes = sizes.at[1:1 + 2 * couples:2].set(giver - shifted).at[2:2 + 2 * couples:2].set(receiver + shifted)
    return sizes[jax.random.permutation(jax.random.fold_in(stream_key, 2), number_of)]


def assign_block(own_key, own, number, rows, count, top, most, skew):
    ranking = jax.random.permutation(own_key, count)
    crowded, ordinary = shares(count, rows * top, most, skew, True), shares(count, rows * top, most, skew, False)
    places = jnp.arange(count)

    def named(sizes, turn):
        used = int((sizes > 0).sum())
        fixed = max(1, used // 4)
        passed = fixed + (places - fixed + turn * (used - fixed)) % max(1, count - fixed)
        return jnp.zeros((count,), jnp.int32).at[ranking[jnp.where(places < fixed, places, passed)]].set(jnp.asarray(sizes, jnp.int32))

    sizes = jnp.where(number % 4 == 0, named(crowded, number // 4), named(ordinary, number - number // 4 - 1))
    mixed = jax.random.permutation(jax.random.fold_in(own, 3), count)
    donor, taker = mixed[0:count // 2 * 2:2], mixed[1:count // 2 * 2:2]
    room = jnp.minimum(sizes[donor] - 1, most - sizes[taker]) // 2
    room = jnp.where((donor == ranking[0]) | (taker == ranking[0]) | (sizes[taker] == 0), 0, jnp.maximum(room, 0))
    passed = jax.random.randint(jax.random.fold_in(own, 4), (count // 2,), 0, 1 << 20) % (room + 1)
    sizes = sizes.at[donor].add(-passed).at[taker].add(passed)
    labels = jnp.searchsorted(jnp.cumsum(sizes), jnp.arange(rows * top), side="right").astype(jnp.int32)
    table = labels.reshape(top, rows).T
    table = table[jax.random.permutation(jax.random.fold_in(own, 1), rows)]
    turn = jax.random.randint(jax.random.fold_in(own, 2), (rows, 1), 0, top)
    return jnp.take_along_axis(table, (jnp.arange(top)[None, :] + turn) % top, axis=1)


def shares(amount, total, limit, skew, full):
    loads = [(1 << 20) // math.isqrt(rank ** skew) + 1 for rank in range(1, amount + 1)]
    largest = limit if full else min(limit, max(-(-total // amount), total * loads[0] // sum(loads)))
    least = 1 if total - largest >= amount - 1 else 0
    holding, surplus = [largest] + [least] * (amount - 1), total - largest - least * (amount - 1)
    while surplus > 0:
        candidates = [i for i in range(1, amount) if holding[i] < largest] or [i for i in range(1, amount) if holding[i] < limit]
        whole, budget = sum([loads[i] for i in candidates]), surplus
        for i in candidates:
            extra = min(limit - holding[i], max(1, budget * loads[i] // whole), surplus)
            holding[i] = holding[i] + extra
            surplus = surplus - extra
    return np.array(holding)


def scatter_about(own_key, extent, width, limit, split=(), kind=jnp.bfloat16):
    values = jax.random.normal(own_key, extent, jnp.float32) * width
    if len(split) > 0:
        values = block_scale(own_key, extent, split, -0.22, 0.18) * values
    return jnp.clip(values, min=-limit, max=limit).astype(kind)


def setup_inputs(seed: int = 0) -> dict:
    splits = jax.random.split(jax.random.key(seed), 9)
    item_owner_keys = jax.random.split(jax.random.fold_in(splits[0], 1), TOKENS // TOK_DEV)
    item_owner_turns = jax.random.permutation(jax.random.fold_in(splits[0], 3), TOKENS // TOK_DEV)
    item_owner = jax.vmap(lambda own, number: assign_block(jax.random.fold_in(splits[0], 2), own, number, TOK_DEV, OWNERS, 1, CAP, 2))(item_owner_keys, item_owner_turns).reshape((TOKENS, 1))
    item_row = touch_ends(jax.random.randint(splits[1], (TOKENS,), 0, ITEM_DEV), jax.random.fold_in(splits[1], 1), 0, ITEM_DEV - 1).astype(jnp.int32)
    lengths = jax.vmap(lambda own: uneven(own, SEGS, TOK_DEV, LMAX, 2))(jax.random.split(splits[2], (N_TABLE * N_GROUP))).reshape((N_TABLE * N_GROUP, SEGS)).astype(jnp.int32)
    table = scatter_about(splits[3], (ITEMS, D), 1.0, 6.0, ((0, 16),))
    w_in = scatter_about(splits[4], (D, 4 * D), D ** -0.5, 0.25)
    w_out = scatter_about(splits[5], (D, D), D ** -0.5, 0.25)
    gain = jnp.clip(1.0 + 0.18 * jax.random.normal(splits[6], (D,), jnp.float32), 0.1, 1.9)
    cotangent = scatter_about(splits[7], (TOKENS, D), 1.0, 6.0, ((0, 32),))
    return {"item_owner": item_owner, "item_row": item_row, "lengths": lengths, "table": table, "w_in": w_in, "w_out": w_out, "gain": gain, "cotangent": cotangent}


def rounded(value):
    return lax.optimization_barrier(value.astype(jnp.bfloat16))

def silu_slope(value):
    sig_val = jax.nn.sigmoid(value)
    return sig_val * (1.0 + value * (1.0 - sig_val))

def layer_block(embedded, lengths_row, w_in, w_out, gain, grad_out):
    count = embedded.shape[0]
    scale = 1.0 / math.sqrt(HEAD_DIM)
    position = jnp.arange(count, dtype=jnp.int32)
    ends = jnp.cumsum(lengths_row)
    segment = lax.optimization_barrier(jnp.sum((position[:, None] >= ends[None, :]).astype(jnp.int32), 1))
    allowed = (segment[:, None] == segment[None, :]) & (position[None, :] <= position[:, None])
    pre_act = jnp.dot(embedded, w_in, preferred_element_type=jnp.float32)
    projected = rounded(jax.nn.silu(pre_act))
    upd_part = projected[:, :D].astype(jnp.float32)
    val_heads = projected[:, D:2 * D].astype(jnp.float32).reshape(count, HEADS, HEAD_DIM)
    qry_heads = projected[:, 2 * D:3 * D].astype(jnp.float32).reshape(count, HEADS, HEAD_DIM)
    key_heads = projected[:, 3 * D:].astype(jnp.float32).reshape(count, HEADS, HEAD_DIM)
    scores = jnp.einsum('thd,shd->hts', qry_heads, key_heads) * scale
    weights = rounded(jnp.where(allowed[None], jax.nn.silu(scores), 0.0))
    weights_f = weights.astype(jnp.float32)
    attended = jnp.einsum('hts,shd->thd', weights_f, val_heads).reshape(count, D)
    centered = attended - lax.optimization_barrier(jnp.mean(attended, 1, keepdims=True))
    inv_std = lax.rsqrt(lax.optimization_barrier(jnp.mean(centered * centered, 1, keepdims=True)) + 1e-05)
    normed = centered * inv_std
    mixed = (normed * gain * upd_part).astype(jnp.bfloat16)
    result = (embedded.astype(jnp.float32) + jnp.dot(mixed, w_out, preferred_element_type=jnp.float32)).astype(jnp.bfloat16)
    grad_w_out = jnp.dot(mixed.T, grad_out, preferred_element_type=jnp.float32)
    grad_mixed = rounded(jnp.dot(grad_out, w_out.T, preferred_element_type=jnp.float32)).astype(jnp.float32)
    grad_upd = grad_mixed * normed * gain
    grad_normed = grad_mixed * gain * upd_part
    grad_gain = lax.optimization_barrier(jnp.sum(grad_mixed * normed * upd_part, 0))
    grad_att = rounded((grad_normed - lax.optimization_barrier(jnp.mean(grad_normed, 1, keepdims=True)) - normed * lax.optimization_barrier(jnp.mean(grad_normed * normed, 1, keepdims=True))) * inv_std)
    att_heads = grad_att.astype(jnp.float32).reshape(count, HEADS, HEAD_DIM)
    grad_weights = jnp.einsum('thd,shd->hts', att_heads, val_heads)
    grad_val = jnp.einsum('hts,thd->shd', weights_f, att_heads).reshape(count, D)
    grad_score = rounded(jnp.where(allowed[None], grad_weights * silu_slope(scores), 0.0) * scale).astype(jnp.float32)
    grad_qry = jnp.einsum('hts,shd->thd', grad_score, key_heads).reshape(count, D)
    grad_key = jnp.einsum('hts,thd->shd', grad_score, qry_heads).reshape(count, D)
    grad_proj = jnp.concatenate([grad_upd, grad_val, grad_qry, grad_key], 1)
    grad_pre = (grad_proj * silu_slope(pre_act)).astype(jnp.bfloat16)
    grad_w_in = jnp.dot(embedded.T, grad_pre, preferred_element_type=jnp.float32)
    grad_emb = (grad_out.astype(jnp.float32) + jnp.dot(grad_pre, w_in.T, preferred_element_type=jnp.float32)).astype(jnp.bfloat16)
    return (result, grad_emb, grad_w_in, grad_w_out, grad_gain)

def reference(item_owner, item_row, lengths, table, w_in, w_out, gain, cotangent):
    blocks = N_TABLE * N_GROUP
    item_ids = (item_owner[:, 0] * ITEM_DEV + item_row).astype(jnp.int32)
    embedded = table[item_ids]
    emb_blocks = embedded.reshape(blocks, TOK_DEV, D)
    grad_blocks = cotangent.reshape(blocks, TOK_DEV, D)

    def step(carry, piece):
        emb_piece, lens_piece, grad_piece = piece
        result, grad_emb, grad_w_in, grad_w_out, grad_gain = layer_block(emb_piece, lens_piece, w_in, w_out, gain, grad_piece)
        return ((carry[0] + grad_w_in, carry[1] + grad_w_out, carry[2] + grad_gain), (result, grad_emb))
    start = (jnp.zeros((D, 4 * D), jnp.float32), jnp.zeros((D, D), jnp.float32), jnp.zeros((D,), jnp.float32))
    sums, outputs = lax.scan(step, start, (emb_blocks, lengths, grad_blocks))
    result = outputs[0].reshape(blocks * TOK_DEV, D)
    grad_emb = outputs[1].reshape(blocks * TOK_DEV, D)
    table_grad = jax.ops.segment_sum(grad_emb.astype(jnp.float32), item_ids, num_segments=N_TABLE * ITEM_DEV)
    return (result, table_grad, sums[0], sums[1], sums[2])
```

```python
import functools
import math

import jax
import jax.numpy as jnp
from jax import lax
from jax.experimental import pallas as pl
from jax.experimental.pallas import tpu as pltpu
from jax.sharding import PartitionSpec as P

HEADS = 8
HEAD_DIM = 64
LANES = 128
QUERY_ROWS = 256
VMEM_LIMIT = 56 * 1024 * 1024

F32 = jnp.float32
BF16 = jnp.bfloat16


def iota(shape, dim):
    return lax.broadcasted_iota(jnp.int32, shape, dim)


def hot(cond):
    return jnp.where(cond, 1.0, 0.0).astype(BF16)


def dot_nn(a, b):
    return lax.dot_general(a, b, (((1,), (0,)), ((), ())), preferred_element_type=F32)


def dot_nt(a, b):
    return lax.dot_general(a, b, (((1,), (1,)), ((), ())), preferred_element_type=F32)


def dot_tn(a, b):
    return lax.dot_general(a, b, (((0,), (0,)), ((), ())), preferred_element_type=F32)


def call(kernel, out_shape, flops, nbytes, operands, smem=(), scratch=()):
    specs = [
        pl.BlockSpec(memory_space=pltpu.SMEM if i in smem else pltpu.VMEM)
        for i in range(len(operands))
    ]
    return pl.pallas_call(
        kernel,
        out_shape=out_shape,
        in_specs=specs,
        out_specs=jax.tree.map(lambda _: pl.BlockSpec(memory_space=pltpu.VMEM), out_shape),
        scratch_shapes=scratch,
        compiler_params=pltpu.CompilerParams(vmem_limit_bytes=VMEM_LIMIT),
        cost_estimate=pl.CostEstimate(flops=flops, bytes_accessed=nbytes, transcendentals=0),
    )(*operands)


def request_kernel(cap, owner_ref, row_ref, req_ref, slot_ref):
    owners, width = req_ref.shape
    count = owner_ref.shape[1]
    owner = owner_ref[...]
    row = row_ref[...]
    mine = iota((owners, count), 0) == owner
    mine_b = hot(mine)
    before = hot(iota((count, count), 0) < iota((count, count), 1))
    earlier = dot_nn(mine_b, before)
    place = jnp.sum(jnp.where(mine, earlier, 0.0), axis=0, keepdims=True)
    slot_ref[...] = owner.astype(F32) * float(cap) + place
    at_place = hot(iota((width, count), 0).astype(F32) == place)
    high = jnp.where(mine, (row >> 8).astype(F32), 0.0).astype(BF16)
    low = jnp.where(mine, (row & 255).astype(F32), 0.0).astype(BF16)
    found = dot_nt(high, at_place) * 256.0 + dot_nt(low, at_place)
    req_ref[...] = found.astype(jnp.int32)


def lookup_kernel(cap, wanted_ref, table_ref, found_ref, ids_ref):
    owners, width = wanted_ref.shape
    slots = found_ref.shape[0]
    rows = table_ref.shape[0]
    wanted = wanted_ref[...]
    high = (wanted >> 8).astype(F32).astype(BF16)
    low = (wanted & 255).astype(F32).astype(BF16)
    slot = iota((slots, owners), 0).astype(F32)
    holder = jnp.floor((slot + 0.5) * (1.0 / cap))
    spread = hot(holder == iota((slots, owners), 1).astype(F32))
    ids = dot_nn(spread, high) * 256.0 + dot_nn(spread, low)
    slot = iota((slots, width), 0).astype(F32)
    place = slot - jnp.floor((slot + 0.5) * (1.0 / cap)) * float(cap)
    ids = jnp.sum(
        jnp.where(iota((slots, width), 1).astype(F32) == place, ids, 0.0), axis=1, keepdims=True
    )
    wide = jnp.broadcast_to(ids, (slots, LANES))
    ids_ref[...] = wide.T[0:1, :]
    step = 256 if slots % 256 == 0 else slots
    for start in range(0, slots, step):
        part = ids[start : start + step]
        pick = hot(iota((step, rows), 1).astype(F32) == part)
        found_ref[start : start + step, :] = dot_nn(pick, table_ref[...]).astype(BF16)


def collect_kernel(groups, *refs):
    ids_refs, in_refs, out_ref = refs[:groups], refs[groups : 2 * groups], refs[-1]
    rows = out_ref.shape[0]
    slots = in_refs[0].shape[0]
    base = lax.axis_index("group") * rows
    step = 256 if rows % 256 == 0 else rows

    def chunk(i, _):
        start = pl.multiple_of(i * step, step)
        own = (iota((step, slots), 0) + (base + start)).astype(F32)
        total = None
        for ids_ref, in_ref in zip(ids_refs, in_refs):
            part = dot_nn(hot(own == ids_ref[...]), in_ref[...])
            total = part if total is None else total + part
        out_ref[pl.ds(start, step), :] = total
        return 0

    lax.fori_loop(0, rows // step, chunk, 0)


def layer_kernel(
    groups,
    wparts,
    len_ref,
    slot_ref,
    ret_ref,
    w_in_ref,
    w_out_ref,
    gain_ref,
    cot_ref,
    result_ref,
    outgoing_ref,
    grads_ref,
    emb_ref,
    proj_ref,
    slope_ref,
    bias_ref,
    weight_ref,
    wslope_ref,
    att_ref,
    mixed_ref,
    gatt_ref,
    gpre_ref,
    gval_ref,
    gkey_ref,
    gwo_ref,
):
    count, width = cot_ref.shape
    slots = ret_ref.shape[0]
    per = LANES // HEAD_DIM
    slabs = width // LANES
    qrows = QUERY_ROWS if count % QUERY_ROWS == 0 else count
    half_scale = 0.5 / math.sqrt(HEAD_DIM)

    slot = jnp.broadcast_to(slot_ref[...], (LANES, count)).T
    emb = None
    for start in range(0, slots, LANES):
        pick = hot(slot == (iota((count, LANES), 1) + start).astype(F32))
        part = dot_nn(pick, ret_ref[start : start + LANES, :])
        emb = part if emb is None else emb + part
    emb_ref[...] = emb.astype(BF16)

    def project(i, _):
        cols = pl.ds(pl.multiple_of(i * width, width), width)
        pre = dot_nn(emb_ref[...], w_in_ref[:, cols])
        sig = 0.5 * jnp.tanh(0.5 * pre) + 0.5
        act = pre * sig
        proj_ref[i] = act.astype(BF16)
        slope_ref[i] = sig + act * (1.0 - sig)
        return 0

    lax.fori_loop(0, 4, project, 0)

    pos = iota((count, 1), 0)
    begin = jnp.zeros((count, 1), jnp.int32)
    end = jnp.int32(0)
    for s in range(len_ref.shape[1]):
        end = end + len_ref[0, s]
        begin = jnp.where(pos >= end, end, begin)
    key = iota((count, count), 1)
    allowed = (key >= begin) & (key <= iota((count, count), 0))
    bias_ref[...] = jnp.where(allowed, 3.0e38, -30.0)

    lane = iota((count, LANES), 1)

    def only(value, head, factor=1.0):
        inside = (lane >= head * HEAD_DIM) & (lane < (head + 1) * HEAD_DIM)
        return jnp.where(inside, value.astype(F32) * factor, 0.0).astype(BF16)

    def forward(p, _):
        cols = pl.ds(pl.multiple_of(p * LANES, LANES), LANES)
        val, qry, key_all = proj_ref[1, :, cols], proj_ref[2, :, cols], proj_ref[3, :, cols]
        qrys = [only(qry, a, half_scale) for a in range(per)]
        vals = [only(val, a) for a in range(per)]
        for r0 in range(0, count, qrows):
            r1 = r0 + qrows
            total = None
            for a in range(per):
                half = dot_nt(qrys[a][r0:r1], key_all[:r1])
                half = jnp.minimum(half, bias_ref[r0:r1, :r1])
                th = jnp.tanh(half)
                weight = half + half * th
                weight_b = weight.astype(BF16)
                weight_ref[p * per + a, r0:r1, :r1] = weight_b
                wslope_ref[p * per + a, r0:r1, :r1] = (1.0 + th) + weight * (1.0 - th)
                part = dot_nn(weight_b, vals[a][:r1])
                total = part if total is None else total + part
            att_ref[r0:r1, cols] = total
        return 0

    lax.fori_loop(0, slabs, forward, 0)

    gain = gain_ref[...]
    gain_sum = jnp.zeros((1, width), F32)
    for r0 in range(0, count, qrows):
        rows = slice(r0, r0 + qrows)
        att = att_ref[rows, :]
        centered = att - jnp.mean(att, 1, keepdims=True)
        inv = lax.rsqrt(jnp.mean(centered * centered, 1, keepdims=True) + 1e-05)
        normed = centered * inv
        upd = proj_ref[0, rows, :].astype(F32)
        scaled = normed * gain
        mixed = (scaled * upd).astype(BF16)
        mixed_ref[rows, :] = mixed
        result_ref[rows, :] = (
            emb_ref[rows, :].astype(F32) + dot_nn(mixed, w_out_ref[...])
        ).astype(BF16)
        gmix = dot_nt(cot_ref[rows, :], w_out_ref[...]).astype(BF16).astype(F32)
        gpre_ref[rows, 0:width] = (gmix * scaled * slope_ref[0, rows, :]).astype(BF16)
        gnorm = gmix * gain * upd
        gain_sum = gain_sum + jnp.sum(gmix * normed * upd, 0, keepdims=True)
        mean1 = jnp.mean(gnorm, 1, keepdims=True)
        mean2 = jnp.mean(gnorm * normed, 1, keepdims=True)
        gatt_ref[rows, :] = ((gnorm - mean1 - normed * mean2) * inv).astype(BF16)
    gwo_ref[...] = dot_tn(mixed_ref[...], cot_ref[...]).astype(BF16)

    def backward(p, _):
        start = pl.multiple_of(p * LANES, LANES)
        cols = pl.ds(start, LANES)
        val, qry, key_all = proj_ref[1, :, cols], proj_ref[2, :, cols], proj_ref[3, :, cols]
        gatt = gatt_ref[:, cols]
        qrys = [only(qry, a, half_scale) for a in range(per)]
        keys = [only(key_all, a) for a in range(per)]
        gatts = [only(gatt, a) for a in range(per)]
        gval_ref[...] = jnp.zeros_like(gval_ref)
        gkey_ref[...] = jnp.zeros_like(gkey_ref)
        for r0 in range(0, count, qrows):
            r1 = r0 + qrows
            gqry = None
            for a in range(per):
                gweight = dot_nt(gatts[a][r0:r1], val[:r1])
                gscore = (gweight * wslope_ref[p * per + a, r0:r1, :r1]).astype(BF16)
                part = dot_nn(gscore, keys[a][:r1])
                gqry = part if gqry is None else gqry + part
                gval_ref[:r1, :] += dot_tn(weight_ref[p * per + a, r0:r1, :r1], gatts[a][r0:r1])
                gkey_ref[:r1, :] += dot_tn(gscore, qrys[a][r0:r1])
            gpre_ref[r0:r1, pl.ds(2 * width + start, LANES)] = (
                gqry * half_scale * slope_ref[2, r0:r1, cols]
            ).astype(BF16)
        gpre_ref[:, pl.ds(width + start, LANES)] = (gval_ref[...] * slope_ref[1, :, cols]).astype(BF16)
        gpre_ref[:, pl.ds(3 * width + start, LANES)] = (gkey_ref[...] * slope_ref[3, :, cols]).astype(BF16)
        return 0

    lax.fori_loop(0, slabs, backward, 0)

    gemb = (cot_ref[...].astype(F32) + dot_nt(gpre_ref[...], w_in_ref[...])).astype(BF16)
    for start in range(0, slots, 256):
        stop = min(start + 256, slots)
        put = hot((iota((stop - start, count), 0) + start).astype(F32) == slot_ref[...])
        outgoing_ref[start:stop, :] = dot_nn(put, gemb).astype(BF16)

    me = lax.axis_index("group")
    emb_t = emb_ref[...].T
    cols_in = 4 * width // groups
    cols_out = width // wparts
    chunk = min(cols_in, 512)
    gain_col = jnp.broadcast_to(gain_sum, (LANES, width)).T.astype(BF16)
    for k in range(groups):
        part = lax.rem(me + k, groups)
        for c in range(0, cols_in, chunk):
            cols = pl.ds(pl.multiple_of(part * cols_in + c, LANES), chunk)
            grads_ref[k, :, c : c + chunk] = dot_nn(emb_t, gpre_ref[:, cols]).astype(BF16)
        cols = pl.ds(pl.multiple_of(lax.rem(part, wparts) * cols_out, LANES), cols_out)
        grads_ref[k, :, cols_in : cols_in + cols_out] = gwo_ref[:, cols]
        grads_ref[k, :, cols_in + cols_out :] = gain_col


def shift(value, axis, size, amount):
    return lax.ppermute(value, axis, [(i, (i + amount) % size) for i in range(size)])


def sum_scatter(value, owners):
    inner = 4 if owners % 4 == 0 else 1
    outer = owners // inner
    me = lax.axis_index("table")
    high, low = me // inner, me % inner
    rows, cols = value.shape[1:]
    value = value.reshape(outer, inner, rows, cols)

    def pick_low(k):
        return lax.dynamic_index_in_dim(value, low ^ k, 1, keepdims=False)

    total = pick_low(0).astype(F32)
    for k in range(1, inner):
        perm = [(i, i // inner * inner + ((i % inner) ^ k)) for i in range(owners)]
        total = total + lax.ppermute(pick_low(k), "table", perm).astype(F32)
    part = total.astype(BF16)
    final = lax.dynamic_index_in_dim(total, high, 0, keepdims=False)
    for k in range(1, outer):
        perm = [(i, ((i // inner + k) % outer) * inner + i % inner) for i in range(owners)]
        sent = lax.dynamic_index_in_dim(part, (high + k) % outer, 0, keepdims=False)
        final = final + lax.ppermute(sent, "table", perm).astype(F32)
    return final


def on_device(item_owner, item_row, lengths, table, w_in, w_out, gain, cotangent):
    owners = lax.axis_size("table")
    groups = lax.axis_size("group")
    count = item_row.shape[0]
    width = table.shape[1]
    capacity = max(2, 3 * count // (2 * owners))
    slots = owners * capacity
    padded = -(-capacity // LANES) * LANES
    me = lax.axis_index("group")

    requested, slot = call(
        functools.partial(request_kernel, capacity),
        (
            jax.ShapeDtypeStruct((owners, padded), jnp.int32),
            jax.ShapeDtypeStruct((1, count), F32),
        ),
        4 * count * count * owners,
        8 * count,
        (item_owner.reshape(1, count), item_row.reshape(1, count)),
    )
    wanted = lax.all_to_all(requested, "table", split_axis=0, concat_axis=0, tiled=True)
    found, ids = call(
        functools.partial(lookup_kernel, capacity),
        (
            jax.ShapeDtypeStruct((slots, width), BF16),
            jax.ShapeDtypeStruct((1, slots), F32),
        ),
        2 * slots * table.shape[0] * width,
        2 * (slots + table.shape[0]) * width,
        (wanted, table),
    )
    returned = lax.all_to_all(found, "table", split_axis=0, concat_axis=0, tiled=True)
    all_ids = [ids] + [shift(ids, "group", groups, k) for k in range(1, groups)]

    wparts = min(groups, width // LANES)
    cols_in = 4 * width // groups
    cols_out = width // wparts
    cols_all = cols_in + cols_out + LANES
    square = pltpu.VMEM((count, width), BF16)
    result, outgoing, grads = call(
        functools.partial(layer_kernel, groups, wparts),
        (
            jax.ShapeDtypeStruct((count, width), BF16),
            jax.ShapeDtypeStruct((slots, width), BF16),
            jax.ShapeDtypeStruct((groups, width, cols_all), BF16),
        ),
        32 * count * width * width + 14 * count * count * width,
        24 * count * width,
        (lengths, slot, returned, w_in, w_out, gain.reshape(1, width), cotangent),
        smem=(0,),
        scratch=[
            square,
            pltpu.VMEM((4, count, width), BF16),
            pltpu.VMEM((4, count, width), F32),
            pltpu.VMEM((count, count), F32),
            pltpu.VMEM((HEADS, count, count), BF16),
            pltpu.VMEM((HEADS, count, count), F32),
            pltpu.VMEM((count, width), F32),
            square,
            square,
            pltpu.VMEM((count, 4 * width), BF16),
            pltpu.VMEM((count, LANES), F32),
            pltpu.VMEM((count, LANES), F32),
            pltpu.VMEM((width, width), BF16),
        ],
    )

    incoming = lax.all_to_all(outgoing, "table", split_axis=0, concat_axis=0, tiled=True)
    all_incoming = [incoming] + [shift(incoming, "group", groups, k) for k in range(1, groups)]
    table_grad = call(
        functools.partial(collect_kernel, groups),
        jax.ShapeDtypeStruct((table.shape[0] // groups, width), F32),
        2 * slots * table.shape[0] * width,
        2 * groups * slots * width + 4 * table.shape[0] // groups * width,
        (*all_ids, *all_incoming),
    )

    chip = grads[0].astype(F32)
    for k in range(1, groups):
        chip = chip + shift(grads[k], "group", groups, k).astype(F32)
    rows = width // owners
    summed = sum_scatter(chip.astype(BF16).reshape(owners, rows, cols_all), owners)
    w_in_grad = summed[:, :cols_in]
    mine = summed[:, cols_in : cols_in + cols_out]
    pieces = jnp.stack([mine] + [shift(mine, "group", groups, k) for k in range(1, groups)])
    w_out_grad = jnp.concatenate(
        [
            lax.dynamic_index_in_dim(pieces, (me - p) % groups, 0, keepdims=False)
            for p in range(wparts)
        ],
        1,
    )
    gain_grad = summed[:, cols_in + cols_out]
    return (result, table_grad, w_in_grad, w_out_grad, gain_grad)


def solution(mesh):
    return jax.shard_map(
        on_device,
        mesh=mesh,
        in_specs=(
            P(("table", "group"), None),
            P(("table", "group")),
            P(("table", "group"), None),
            P("table", None),
            P(),
            P(),
            P(),
            P(("table", "group"), None),
        ),
        out_specs=(
            P(("table", "group"), None),
            P(("table", "group"), None),
            P("table", "group"),
            P("table", None),
            P("table"),
        ),
        check_vma=False,
    )
```

```python
import functools
import math

import jax
import jax.numpy as jnp
from jax import lax
from jax.experimental import pallas as pl
from jax.experimental.pallas import tpu as pltpu
from jax.sharding import PartitionSpec as P

HEADS = 8
HEAD_DIM = 64
LANES = 128
QUERY_ROWS = 256

F32 = jnp.float32
BF16 = jnp.bfloat16


def iota(shape, dim):
    return lax.broadcasted_iota(jnp.int32, shape, dim)


def hot(cond):
    return jnp.where(cond, 1.0, 0.0).astype(BF16)


def dot_nn(a, b):
    return lax.dot_general(a, b, (((1,), (0,)), ((), ())), preferred_element_type=F32)


def dot_nt(a, b):
    return lax.dot_general(a, b, (((1,), (1,)), ((), ())), preferred_element_type=F32)


def dot_tn(a, b):
    return lax.dot_general(a, b, (((0,), (0,)), ((), ())), preferred_element_type=F32)


def row_step(rows):
    return 256 if rows % 256 == 0 else rows


def call(kernel, out_shape, flops, nbytes, operands, smem=(), far=(), far_out=(), limit=20, scratch=()):
    spaces = [
        pltpu.SMEM if i in smem else pl.ANY if i in far else pltpu.VMEM
        for i in range(len(operands))
    ]
    out_spaces = [pl.ANY if i in far_out else pltpu.VMEM for i in range(len(out_shape))]
    return pl.pallas_call(
        kernel,
        out_shape=out_shape,
        in_specs=[pl.BlockSpec(memory_space=space) for space in spaces],
        out_specs=[pl.BlockSpec(memory_space=space) for space in out_spaces],
        scratch_shapes=scratch,
        compiler_params=pltpu.CompilerParams(vmem_limit_bytes=limit * 1024 * 1024),
        cost_estimate=pl.CostEstimate(flops=flops, bytes_accessed=nbytes, transcendentals=0),
    )(*operands)


def request_kernel(cap, owner_ref, row_ref, req_ref, slot_ref):
    owners, width = req_ref.shape
    count = owner_ref.shape[1]
    owner = owner_ref[...]
    row = row_ref[...]
    mine = iota((owners, count), 0) == owner
    mine_b = hot(mine)
    before = hot(iota((count, count), 0) < iota((count, count), 1))
    earlier = dot_nn(mine_b, before)
    place = jnp.sum(jnp.where(mine, earlier, 0.0), axis=0, keepdims=True)
    slot_ref[...] = owner.astype(F32) * float(cap) + place
    at_place = hot(iota((width, count), 0).astype(F32) == place)
    high = jnp.where(mine, (row >> 8).astype(F32), 0.0).astype(BF16)
    low = jnp.where(mine, (row & 255).astype(F32), 0.0).astype(BF16)
    found = dot_nt(high, at_place) * 256.0 + dot_nt(low, at_place)
    req_ref[...] = found.astype(jnp.int32)


def lookup_kernel(cap, wanted_ref, table_hbm, found_hbm, ids_ref, table_ref, found_ref, sems):
    owners, width = wanted_ref.shape
    slots = found_ref.shape[0]
    rows = table_ref.shape[0]
    fetch = pltpu.make_async_copy(table_hbm, table_ref, sems.at[0])
    fetch.start()
    wanted = wanted_ref[...]
    high = (wanted >> 8).astype(F32).astype(BF16)
    low = (wanted & 255).astype(F32).astype(BF16)
    slot = iota((slots, owners), 0).astype(F32)
    holder = jnp.floor((slot + 0.5) * (1.0 / cap))
    spread = hot(holder == iota((slots, owners), 1).astype(F32))
    ids = dot_nn(spread, high) * 256.0 + dot_nn(spread, low)
    slot = iota((slots, width), 0).astype(F32)
    place = slot - jnp.floor((slot + 0.5) * (1.0 / cap)) * float(cap)
    ids = jnp.sum(
        jnp.where(iota((slots, width), 1).astype(F32) == place, ids, 0.0), axis=1, keepdims=True
    )
    wide = jnp.broadcast_to(ids, (slots, LANES))
    ids_ref[...] = wide.T[0:1, :]
    step = row_step(slots)
    fetch.wait()
    stores = []
    for n, start in enumerate(range(0, slots, step)):
        part = ids[start : start + step]
        pick = hot(iota((step, rows), 1).astype(F32) == part)
        found_ref[start : start + step, :] = dot_nn(pick, table_ref[...]).astype(BF16)
        here = pl.ds(start, step)
        stores.append(
            pltpu.make_async_copy(found_ref.at[here], found_hbm.at[here], sems.at[1 + n])
        )
        stores[-1].start()
    for store in stores:
        store.wait()


def collect_kernel(groups, *refs):
    ids_refs, in_hbms, out_hbm = refs[:groups], refs[groups : 2 * groups], refs[2 * groups]
    in_refs, out_ref, sems = refs[2 * groups + 1 : 3 * groups + 1], refs[-2], refs[-1]
    rows = out_ref.shape[0]
    slots = in_refs[0].shape[0]
    fetches = [
        pltpu.make_async_copy(hbm, ref, sems.at[n])
        for n, (hbm, ref) in enumerate(zip(in_hbms, in_refs))
    ]
    for fetch in fetches:
        fetch.start()
    base = lax.axis_index("group") * rows
    step = row_step(rows)
    for fetch in fetches:
        fetch.wait()
    stores = []
    for n, start in enumerate(range(0, rows, step)):
        own = (iota((step, slots), 0) + (base + start)).astype(F32)
        total = None
        for ids_ref, in_ref in zip(ids_refs, in_refs):
            part = dot_nn(hot(own == ids_ref[...]), in_ref[...])
            total = part if total is None else total + part
        out_ref[start : start + step, :] = total
        here = pl.ds(start, step)
        stores.append(
            pltpu.make_async_copy(out_ref.at[here], out_hbm.at[here], sems.at[groups + n])
        )
        stores[-1].start()
    for store in stores:
        store.wait()


def layer_kernel(
    groups,
    wparts,
    len_ref,
    slot_ref,
    ret_ref,
    w_in_hbm,
    w_out_hbm,
    gain_ref,
    cot_hbm,
    *rest,
):
    result_hbm, gpre_hbm = rest[:2]
    grads_hbms = rest[2 : 2 + groups]
    (
    w_in_ref,
    w_out_ref,
    cot_ref,
    result_ref,
    grads_ref,
    pick_ref,
    emb_ref,
    proj_ref,
    slope_ref,
    bias_ref,
    weight_ref,
    wslope_ref,
    att_ref,
    mixed_ref,
    gatt_ref,
    gpre_ref,
    gval_ref,
    gkey_ref,
    gwo_ref,
    sems,
    ) = rest[2 + groups :]
    count, width = cot_ref.shape
    slots = ret_ref.shape[0]
    per = LANES // HEAD_DIM
    slabs = width // LANES
    qrows = QUERY_ROWS if count % QUERY_ROWS == 0 else count
    half_scale = 0.5 / math.sqrt(HEAD_DIM)

    get_in = pltpu.make_async_copy(w_in_hbm, w_in_ref, sems.at[0])
    get_cot = pltpu.make_async_copy(cot_hbm, cot_ref, sems.at[1])
    get_out = pltpu.make_async_copy(w_out_hbm, w_out_ref, sems.at[2])
    for fetch in (get_in, get_cot, get_out):
        fetch.start()

    slot = jnp.broadcast_to(slot_ref[...], (LANES, count)).T
    for start in range(0, slots, LANES):
        pick_ref[:, start : start + LANES] = hot(
            slot == (iota((count, LANES), 1) + start).astype(F32)
        )
    emb_ref[...] = dot_nn(pick_ref[...], ret_ref[...]).astype(BF16)
    get_in.wait()

    def project(i, _):
        cols = pl.ds(pl.multiple_of(i * width, width), width)
        pre = dot_nn(emb_ref[...], w_in_ref[:, cols])
        sig = 0.5 * jnp.tanh(0.5 * pre) + 0.5
        act = pre * sig
        proj_ref[i] = act.astype(BF16)
        slope_ref[i] = sig + act * (1.0 - sig)
        return 0

    lax.fori_loop(0, 4, project, 0)

    pos = iota((count, 1), 0)
    begin = jnp.zeros((count, 1), jnp.int32)
    end = jnp.int32(0)
    for s in range(len_ref.shape[1]):
        end = end + len_ref[0, s]
        begin = jnp.where(pos >= end, end, begin)
    key = iota((count, count), 1)
    allowed = (key >= begin) & (key <= iota((count, count), 0))
    bias_ref[...] = jnp.where(allowed, 3.0e38, -30.0)

    lane = iota((count, LANES), 1)

    def only(value, head, factor=1.0):
        inside = (lane >= head * HEAD_DIM) & (lane < (head + 1) * HEAD_DIM)
        return jnp.where(inside, value.astype(F32) * factor, 0.0).astype(BF16)

    def forward(p, _):
        cols = pl.ds(pl.multiple_of(p * LANES, LANES), LANES)
        val, qry, key_all = proj_ref[1, :, cols], proj_ref[2, :, cols], proj_ref[3, :, cols]
        qrys = [only(qry, a, half_scale) for a in range(per)]
        vals = [only(val, a) for a in range(per)]
        for r0 in range(0, count, qrows):
            r1 = r0 + qrows
            total = None
            for a in range(per):
                half = dot_nt(qrys[a][r0:r1], key_all[:r1])
                half = jnp.minimum(half, bias_ref[r0:r1, :r1])
                th = jnp.tanh(half)
                weight = half + half * th
                weight_b = weight.astype(BF16)
                weight_ref[p * per + a, r0:r1, :r1] = weight_b
                wslope_ref[p * per + a, r0:r1, :r1] = (1.0 + th) + weight * (1.0 - th)
                part = dot_nn(weight_b, vals[a][:r1])
                total = part if total is None else total + part
            att_ref[r0:r1, cols] = total
        return 0

    lax.fori_loop(0, slabs, forward, 0)

    get_cot.wait()
    get_out.wait()
    gain = gain_ref[...]
    gain_sum = jnp.zeros((1, width), F32)
    for r0 in range(0, count, qrows):
        rows = slice(r0, r0 + qrows)
        att = att_ref[rows, :]
        centered = att - jnp.mean(att, 1, keepdims=True)
        inv = lax.rsqrt(jnp.mean(centered * centered, 1, keepdims=True) + 1e-05)
        normed = centered * inv
        upd = proj_ref[0, rows, :].astype(F32)
        scaled = normed * gain
        mixed = (scaled * upd).astype(BF16)
        mixed_ref[rows, :] = mixed
        result_ref[rows, :] = (
            emb_ref[rows, :].astype(F32) + dot_nn(mixed, w_out_ref[...])
        ).astype(BF16)
        gmix = dot_nt(cot_ref[rows, :], w_out_ref[...]).astype(BF16).astype(F32)
        gpre_ref[rows, 0:width] = (gmix * scaled * slope_ref[0, rows, :]).astype(BF16)
        gnorm = gmix * gain * upd
        gain_sum = gain_sum + jnp.sum(gmix * normed * upd, 0, keepdims=True)
        mean1 = jnp.mean(gnorm, 1, keepdims=True)
        mean2 = jnp.mean(gnorm * normed, 1, keepdims=True)
        gatt_ref[rows, :] = ((gnorm - mean1 - normed * mean2) * inv).astype(BF16)
    put_result = pltpu.make_async_copy(result_ref, result_hbm, sems.at[3])
    put_result.start()
    gwo_ref[...] = dot_tn(mixed_ref[...], cot_ref[...]).astype(BF16)

    def backward(p, _):
        start = pl.multiple_of(p * LANES, LANES)
        cols = pl.ds(start, LANES)
        val, qry, key_all = proj_ref[1, :, cols], proj_ref[2, :, cols], proj_ref[3, :, cols]
        gatt = gatt_ref[:, cols]
        qrys = [only(qry, a, half_scale) for a in range(per)]
        keys = [only(key_all, a) for a in range(per)]
        gatts = [only(gatt, a) for a in range(per)]
        gval_ref[...] = jnp.zeros_like(gval_ref)
        gkey_ref[...] = jnp.zeros_like(gkey_ref)
        for r0 in range(0, count, qrows):
            r1 = r0 + qrows
            gqry = None
            for a in range(per):
                gweight = dot_nt(gatts[a][r0:r1], val[:r1])
                gscore = (gweight * wslope_ref[p * per + a, r0:r1, :r1]).astype(BF16)
                part = dot_nn(gscore, keys[a][:r1])
                gqry = part if gqry is None else gqry + part
                gval_ref[:r1, :] += dot_tn(weight_ref[p * per + a, r0:r1, :r1], gatts[a][r0:r1])
                gkey_ref[:r1, :] += dot_tn(gscore, qrys[a][r0:r1])
            gpre_ref[r0:r1, pl.ds(2 * width + start, LANES)] = (
                gqry * half_scale * slope_ref[2, r0:r1, cols]
            ).astype(BF16)
        gpre_ref[:, pl.ds(width + start, LANES)] = (gval_ref[...] * slope_ref[1, :, cols]).astype(BF16)
        gpre_ref[:, pl.ds(3 * width + start, LANES)] = (gkey_ref[...] * slope_ref[3, :, cols]).astype(BF16)
        return 0

    lax.fori_loop(0, slabs, backward, 0)

    put_gpre = pltpu.make_async_copy(gpre_ref, gpre_hbm, sems.at[4])
    put_gpre.start()

    me = lax.axis_index("group")
    emb_t = emb_ref[...].T
    cols_in = 4 * width // groups
    cols_out = width // wparts
    chunk = min(cols_in, 512)
    gain_col = jnp.broadcast_to(gain_sum, (LANES, width)).T.astype(BF16)
    puts = [put_result, put_gpre]
    for k in [*range(1, groups), 0]:
        part = lax.rem(me + k, groups)
        for c in range(0, cols_in, chunk):
            cols = pl.ds(pl.multiple_of(part * cols_in + c, LANES), chunk)
            grads_ref[k, :, c : c + chunk] = dot_nn(emb_t, gpre_ref[:, cols]).astype(BF16)
        cols = pl.ds(pl.multiple_of(lax.rem(part, wparts) * cols_out, LANES), cols_out)
        grads_ref[k, :, cols_in : cols_in + cols_out] = gwo_ref[:, cols]
        grads_ref[k, :, cols_in + cols_out :] = gain_col
        put = pltpu.make_async_copy(grads_ref.at[k], grads_hbms[k], sems.at[5 + k])
        put.start()
        puts.append(put)
    for put in puts:
        put.wait()


def rows_kernel(slot_ref, gpre_hbm, w_in_hbm, cot_ref, out_hbm, gpre_ref, w_in_ref, out_ref, sems):
    count, width = cot_ref.shape
    slots = out_ref.shape[0]
    fetches = []
    for i in range(4):
        cols = pl.ds(i * width, width)
        pair = (
            pltpu.make_async_copy(gpre_hbm.at[:, cols], gpre_ref.at[:, cols], sems.at[2 * i]),
            pltpu.make_async_copy(w_in_hbm.at[:, cols], w_in_ref.at[:, cols], sems.at[2 * i + 1]),
        )
        for fetch in pair:
            fetch.start()
        fetches.append(pair)
    total = cot_ref[...].astype(F32)
    for i in range(4):
        for fetch in fetches[i]:
            fetch.wait()
        cols = slice(i * width, (i + 1) * width)
        total = total + dot_nt(gpre_ref[:, cols], w_in_ref[:, cols])
    gemb = total.astype(BF16)
    step = row_step(slots)
    stores = []
    for n, start in enumerate(range(0, slots, step)):
        put = hot((iota((step, count), 0) + start).astype(F32) == slot_ref[...])
        out_ref[start : start + step, :] = dot_nn(put, gemb).astype(BF16)
        here = pl.ds(start, step)
        stores.append(pltpu.make_async_copy(out_ref.at[here], out_hbm.at[here], sems.at[8 + n]))
        stores[-1].start()
    for store in stores:
        store.wait()


def shift(value, axis, size, amount):
    return lax.ppermute(value, axis, [(i, (i + amount) % size) for i in range(size)])


def on_device(item_owner, item_row, lengths, table, w_in, w_out, gain, cotangent):
    owners = lax.axis_size("table")
    groups = lax.axis_size("group")
    count = item_row.shape[0]
    width = table.shape[1]
    capacity = max(2, 3 * count // (2 * owners))
    slots = owners * capacity
    padded = -(-capacity // LANES) * LANES
    me = lax.axis_index("group")

    requested, slot = call(
        functools.partial(request_kernel, capacity),
        [
            jax.ShapeDtypeStruct((owners, padded), jnp.int32),
            jax.ShapeDtypeStruct((1, count), F32),
        ],
        4 * count * count * owners,
        8 * count,
        (item_owner.reshape(1, count), item_row.reshape(1, count)),
    )
    wanted = lax.all_to_all(requested, "table", split_axis=0, concat_axis=0, tiled=True)
    found, ids = call(
        functools.partial(lookup_kernel, capacity),
        [
            jax.ShapeDtypeStruct((slots, width), BF16),
            jax.ShapeDtypeStruct((1, slots), F32),
        ],
        2 * slots * table.shape[0] * width,
        2 * (slots + table.shape[0]) * width,
        (wanted, table),
        far=(1,),
        far_out=(0,),
        scratch=[
            pltpu.VMEM(table.shape, BF16),
            pltpu.VMEM((slots, width), BF16),
            pltpu.SemaphoreType.DMA((1 + slots // row_step(slots),)),
        ],
    )
    returned = lax.all_to_all(found, "table", split_axis=0, concat_axis=0, tiled=True)
    all_ids = [ids] + [shift(ids, "group", groups, k) for k in range(1, groups)]
    returned, *all_ids = lax.optimization_barrier((returned, *all_ids))

    wparts = min(groups, width // LANES)
    cols_in = 4 * width // groups
    cols_out = width // wparts
    cols_all = cols_in + cols_out + LANES
    square = pltpu.VMEM((count, width), BF16)
    result, gpre, *grads = call(
        functools.partial(layer_kernel, groups, wparts),
        [
            jax.ShapeDtypeStruct((count, width), BF16),
            jax.ShapeDtypeStruct((count, 4 * width), BF16),
            *[jax.ShapeDtypeStruct((width, cols_all), BF16) for _ in range(groups)],
        ],
        24 * count * width * width + 14 * count * count * width,
        24 * count * width,
        (lengths, slot, returned, w_in, w_out, gain.reshape(1, width), cotangent),
        smem=(0,),
        far=(3, 4, 6),
        far_out=range(2 + groups),
        limit=44,
        scratch=[
            pltpu.VMEM(w_in.shape, BF16),
            pltpu.VMEM(w_out.shape, BF16),
            square,
            square,
            pltpu.VMEM((groups, width, cols_all), BF16),
            pltpu.VMEM((count, slots), BF16),
            square,
            pltpu.VMEM((4, count, width), BF16),
            pltpu.VMEM((4, count, width), F32),
            pltpu.VMEM((count, count), F32),
            pltpu.VMEM((HEADS, count, count), BF16),
            pltpu.VMEM((HEADS, count, count), F32),
            pltpu.VMEM((count, width), F32),
            square,
            square,
            pltpu.VMEM((count, 4 * width), BF16),
            pltpu.VMEM((count, LANES), F32),
            pltpu.VMEM((count, LANES), F32),
            pltpu.VMEM((width, width), BF16),
            pltpu.SemaphoreType.DMA((5 + groups,)),
        ],
    )
    (outgoing,) = call(
        rows_kernel,
        [jax.ShapeDtypeStruct((slots, width), BF16)],
        8 * count * width * width + 2 * slots * count * width,
        20 * count * width,
        (slot, gpre, w_in, cotangent),
        far=(1, 2),
        far_out=(0,),
        scratch=[
            pltpu.VMEM((count, 4 * width), BF16),
            pltpu.VMEM(w_in.shape, BF16),
            pltpu.VMEM((slots, width), BF16),
            pltpu.SemaphoreType.DMA((8 + slots // row_step(slots),)),
        ],
    )

    rows = width // owners
    inner = 4 if owners % 4 == 0 else 1
    outer = owners // inner
    here = lax.axis_index("table")
    high, low = here // inner, here % inner
    chip = grads[0].astype(F32)
    for k in range(1, groups):
        chip = chip + shift(grads[k], "group", groups, k).astype(F32)
    chip = chip.astype(BF16).reshape(outer, inner, rows, cols_all)
    planes = [
        lax.dynamic_index_in_dim(chip, low ^ k, 1, keepdims=False) for k in range(inner)
    ]
    outgoing, *planes = lax.optimization_barrier((outgoing, *planes))
    total = planes[0].astype(F32)
    for k in range(1, inner):
        perm = [(i, i // inner * inner + ((i % inner) ^ k)) for i in range(owners)]
        total = total + lax.ppermute(planes[k], "table", perm).astype(F32)
    part = total.astype(BF16)
    summed = lax.dynamic_index_in_dim(part, high, 0, keepdims=False).astype(F32)
    for k in range(1, outer):
        perm = [(i, ((i // inner + k) % outer) * inner + i % inner) for i in range(owners)]
        sent = lax.dynamic_index_in_dim(part, (high + k) % outer, 0, keepdims=False)
        summed = summed + lax.ppermute(sent, "table", perm).astype(F32)

    incoming = lax.all_to_all(outgoing, "table", split_axis=0, concat_axis=0, tiled=True)
    all_incoming = [incoming] + [shift(incoming, "group", groups, k) for k in range(1, groups)]
    grad_rows = table.shape[0] // groups
    (table_grad,) = call(
        functools.partial(collect_kernel, groups),
        [jax.ShapeDtypeStruct((grad_rows, width), F32)],
        2 * slots * table.shape[0] * width,
        2 * groups * slots * width + 4 * grad_rows * width,
        (*all_ids, *all_incoming),
        far=range(groups, 2 * groups),
        far_out=(0,),
        scratch=[
            *[pltpu.VMEM((slots, width), BF16) for _ in range(groups)],
            pltpu.VMEM((grad_rows, width), F32),
            pltpu.SemaphoreType.DMA((groups + grad_rows // row_step(grad_rows),)),
        ],
    )

    w_in_grad = summed[:, :cols_in]
    mine = summed[:, cols_in : cols_in + cols_out]
    pieces = jnp.stack([mine] + [shift(mine, "group", groups, k) for k in range(1, groups)])
    w_out_grad = jnp.concatenate(
        [
            lax.dynamic_index_in_dim(pieces, (me - p) % groups, 0, keepdims=False)
            for p in range(wparts)
        ],
        1,
    )
    gain_grad = summed[:, cols_in + cols_out]
    return (result, table_grad, w_in_grad, w_out_grad, gain_grad)


def solution(mesh):
    return jax.shard_map(
        on_device,
        mesh=mesh,
        in_specs=(
            P(("table", "group"), None),
            P(("table", "group")),
            P(("table", "group"), None),
            P("table", None),
            P(),
            P(),
            P(),
            P(("table", "group"), None),
        ),
        out_specs=(
            P(("table", "group"), None),
            P(("table", "group"), None),
            P("table", "group"),
            P("table", None),
            P("table"),
        ),
        check_vma=False,
    )
```

```python
import functools
import math

import jax
import jax.numpy as jnp
from jax import lax
from jax.experimental import pallas as pl
from jax.experimental.pallas import tpu as pltpu
from jax.sharding import PartitionSpec as P

HEADS = 8
HEAD_DIM = 64
LANES = 128
QUERY_ROWS = 256

F32 = jnp.float32
BF16 = jnp.bfloat16


def iota(shape, dim):
    return lax.broadcasted_iota(jnp.int32, shape, dim)


def hot(cond):
    return jnp.where(cond, 1.0, 0.0).astype(BF16)


def dot_nn(a, b):
    return lax.dot_general(a, b, (((1,), (0,)), ((), ())), preferred_element_type=F32)


def dot_nt(a, b):
    return lax.dot_general(a, b, (((1,), (1,)), ((), ())), preferred_element_type=F32)


def dot_tn(a, b):
    return lax.dot_general(a, b, (((0,), (0,)), ((), ())), preferred_element_type=F32)


def row_step(rows):
    return 256 if rows % 256 == 0 else rows


def call(kernel, out_shape, flops, nbytes, operands, smem=(), far=(), far_out=(), limit=56, scratch=()):
    spaces = [
        pltpu.SMEM if i in smem else pl.ANY if i in far else pltpu.VMEM
        for i in range(len(operands))
    ]
    out_spaces = [pl.ANY if i in far_out else pltpu.VMEM for i in range(len(out_shape))]
    return pl.pallas_call(
        kernel,
        out_shape=out_shape,
        in_specs=[pl.BlockSpec(memory_space=space) for space in spaces],
        out_specs=[pl.BlockSpec(memory_space=space) for space in out_spaces],
        scratch_shapes=scratch,
        compiler_params=pltpu.CompilerParams(vmem_limit_bytes=limit * 1024 * 1024),
        cost_estimate=pl.CostEstimate(flops=flops, bytes_accessed=nbytes, transcendentals=0),
    )(*operands)


def request_kernel(cap, owner_ref, row_ref, req_ref, slot_ref):
    owners, width = req_ref.shape
    count = owner_ref.shape[1]
    owner = owner_ref[...]
    row = row_ref[...]
    mine = iota((owners, count), 0) == owner
    mine_b = hot(mine)
    before = hot(iota((count, count), 0) < iota((count, count), 1))
    earlier = dot_nn(mine_b, before)
    place = jnp.sum(jnp.where(mine, earlier, 0.0), axis=0, keepdims=True)
    slot_ref[...] = owner.astype(F32) * float(cap) + place
    at_place = hot(iota((width, count), 0).astype(F32) == place)
    high = jnp.where(mine, (row >> 8).astype(F32), 0.0).astype(BF16)
    low = jnp.where(mine, (row & 255).astype(F32), 0.0).astype(BF16)
    found = dot_nt(high, at_place) * 256.0 + dot_nt(low, at_place)
    req_ref[...] = found.astype(jnp.int32)


def lookup_kernel(cap, wanted_ref, table_hbm, found_hbm, ids_ref, table_ref, found_ref, sems):
    owners, width = wanted_ref.shape
    slots = found_ref.shape[0]
    rows = table_ref.shape[0]
    fetch = pltpu.make_async_copy(table_hbm, table_ref, sems.at[0])
    fetch.start()
    wanted = wanted_ref[...]
    high = (wanted >> 8).astype(F32).astype(BF16)
    low = (wanted & 255).astype(F32).astype(BF16)
    slot = iota((slots, owners), 0).astype(F32)
    holder = jnp.floor((slot + 0.5) * (1.0 / cap))
    spread = hot(holder == iota((slots, owners), 1).astype(F32))
    ids = dot_nn(spread, high) * 256.0 + dot_nn(spread, low)
    slot = iota((slots, width), 0).astype(F32)
    place = slot - jnp.floor((slot + 0.5) * (1.0 / cap)) * float(cap)
    ids = jnp.sum(
        jnp.where(iota((slots, width), 1).astype(F32) == place, ids, 0.0), axis=1, keepdims=True
    )
    wide = jnp.broadcast_to(ids, (slots, LANES))
    ids_ref[...] = wide.T[0:1, :]
    step = row_step(slots)
    fetch.wait()
    stores = []
    for n, start in enumerate(range(0, slots, step)):
        part = ids[start : start + step]
        pick = hot(iota((step, rows), 1).astype(F32) == part)
        found_ref[start : start + step, :] = dot_nn(pick, table_ref[...]).astype(BF16)
        here = pl.ds(start, step)
        stores.append(
            pltpu.make_async_copy(found_ref.at[here], found_hbm.at[here], sems.at[1 + n])
        )
        stores[-1].start()
    for store in stores:
        store.wait()


def collect_kernel(groups, *refs):
    ids_refs, in_hbms, out_hbm = refs[:groups], refs[groups : 2 * groups], refs[2 * groups]
    in_refs, out_ref, sems = refs[2 * groups + 1 : 3 * groups + 1], refs[-2], refs[-1]
    rows = out_ref.shape[0]
    slots = in_refs[0].shape[0]
    fetches = [
        pltpu.make_async_copy(hbm, ref, sems.at[n])
        for n, (hbm, ref) in enumerate(zip(in_hbms, in_refs))
    ]
    for fetch in fetches:
        fetch.start()
    base = lax.axis_index("group") * rows
    step = row_step(rows)
    for fetch in fetches:
        fetch.wait()
    stores = []
    for n, start in enumerate(range(0, rows, step)):
        own = (iota((step, slots), 0) + (base + start)).astype(F32)
        total = None
        for ids_ref, in_ref in zip(ids_refs, in_refs):
            part = dot_nn(hot(own == ids_ref[...]), in_ref[...])
            total = part if total is None else total + part
        out_ref[start : start + step, :] = total
        here = pl.ds(start, step)
        stores.append(
            pltpu.make_async_copy(out_ref.at[here], out_hbm.at[here], sems.at[groups + n])
        )
        stores[-1].start()
    for store in stores:
        store.wait()


def layer_kernel(
    owners,
    groups,
    wparts,
    len_ref,
    slot_ref,
    ret_ref,
    w_in_hbm,
    w_out_hbm,
    gain_ref,
    cot_hbm,
    *rest,
):
    result_hbm, gpre_hbm, gin_hbm, gout_hbm = rest[:4]
    (
    w_in_ref,
    w_out_ref,
    cot_ref,
    result_ref,
    gin_ref,
    gout_ref,
    pick_ref,
    emb_ref,
    proj_ref,
    slope_ref,
    bias_ref,
    weight_ref,
    wslope_ref,
    att_ref,
    mixed_ref,
    gatt_ref,
    gpre_ref,
    gval_ref,
    gkey_ref,
    sems,
    ) = rest[4:]
    count, width = cot_ref.shape
    slots = ret_ref.shape[0]
    per = LANES // HEAD_DIM
    slabs = width // LANES
    qrows = QUERY_ROWS if count % QUERY_ROWS == 0 else count
    half_scale = 0.5 / math.sqrt(HEAD_DIM)

    get_in = pltpu.make_async_copy(w_in_hbm, w_in_ref, sems.at[0])
    get_cot = pltpu.make_async_copy(cot_hbm, cot_ref, sems.at[1])
    get_out = pltpu.make_async_copy(w_out_hbm, w_out_ref, sems.at[2])
    for fetch in (get_in, get_cot, get_out):
        fetch.start()

    slot = jnp.broadcast_to(slot_ref[...], (LANES, count)).T
    for start in range(0, slots, LANES):
        pick_ref[:, start : start + LANES] = hot(
            slot == (iota((count, LANES), 1) + start).astype(F32)
        )
    emb_ref[...] = dot_nn(pick_ref[...], ret_ref[...]).astype(BF16)
    get_in.wait()

    def project(i, _):
        cols = pl.ds(pl.multiple_of(i * width, width), width)
        pre = dot_nn(emb_ref[...], w_in_ref[:, cols])
        sig = 0.5 * jnp.tanh(0.5 * pre) + 0.5
        act = pre * sig
        proj_ref[i] = act.astype(BF16)
        slope_ref[i] = sig + act * (1.0 - sig)
        return 0

    lax.fori_loop(0, 4, project, 0)

    pos = iota((count, 1), 0)
    begin = jnp.zeros((count, 1), jnp.int32)
    end = jnp.int32(0)
    for s in range(len_ref.shape[1]):
        end = end + len_ref[0, s]
        begin = jnp.where(pos >= end, end, begin)
    key = iota((count, count), 1)
    allowed = (key >= begin) & (key <= iota((count, count), 0))
    bias_ref[...] = jnp.where(allowed, 3.0e38, -30.0)

    lane = iota((count, LANES), 1)

    def only(value, head, factor=1.0):
        inside = (lane >= head * HEAD_DIM) & (lane < (head + 1) * HEAD_DIM)
        return jnp.where(inside, value.astype(F32) * factor, 0.0).astype(BF16)

    def forward(p, _):
        cols = pl.ds(pl.multiple_of(p * LANES, LANES), LANES)
        val, qry, key_all = proj_ref[1, :, cols], proj_ref[2, :, cols], proj_ref[3, :, cols]
        qrys = [only(qry, a, half_scale) for a in range(per)]
        vals = [only(val, a) for a in range(per)]
        for r0 in range(0, count, qrows):
            r1 = r0 + qrows
            total = None
            for a in range(per):
                half = dot_nt(qrys[a][r0:r1], key_all[:r1])
                half = jnp.minimum(half, bias_ref[r0:r1, :r1])
                th = jnp.tanh(half)
                weight = half + half * th
                weight_b = weight.astype(BF16)
                weight_ref[p * per + a, r0:r1, :r1] = weight_b
                wslope_ref[p * per + a, r0:r1, :r1] = (1.0 + th) + weight * (1.0 - th)
                part = dot_nn(weight_b, vals[a][:r1])
                total = part if total is None else total + part
            att_ref[r0:r1, cols] = total
        return 0

    lax.fori_loop(0, slabs, forward, 0)

    get_cot.wait()
    get_out.wait()
    gain = gain_ref[...]
    gain_sum = jnp.zeros((1, width), F32)
    for r0 in range(0, count, qrows):
        rows = slice(r0, r0 + qrows)
        att = att_ref[rows, :]
        centered = att - jnp.mean(att, 1, keepdims=True)
        inv = lax.rsqrt(jnp.mean(centered * centered, 1, keepdims=True) + 1e-05)
        normed = centered * inv
        upd = proj_ref[0, rows, :].astype(F32)
        scaled = normed * gain
        mixed = (scaled * upd).astype(BF16)
        mixed_ref[rows, :] = mixed
        result_ref[rows, :] = (
            emb_ref[rows, :].astype(F32) + dot_nn(mixed, w_out_ref[...])
        ).astype(BF16)
        gmix = dot_nt(cot_ref[rows, :], w_out_ref[...]).astype(BF16).astype(F32)
        gpre_ref[rows, 0:width] = (gmix * scaled * slope_ref[0, rows, :]).astype(BF16)
        gnorm = gmix * gain * upd
        gain_sum = gain_sum + jnp.sum(gmix * normed * upd, 0, keepdims=True)
        mean1 = jnp.mean(gnorm, 1, keepdims=True)
        mean2 = jnp.mean(gnorm * normed, 1, keepdims=True)
        gatt_ref[rows, :] = ((gnorm - mean1 - normed * mean2) * inv).astype(BF16)
    put_result = pltpu.make_async_copy(result_ref, result_hbm, sems.at[3])
    put_result.start()

    def backward(p, _):
        start = pl.multiple_of(p * LANES, LANES)
        cols = pl.ds(start, LANES)
        val, qry, key_all = proj_ref[1, :, cols], proj_ref[2, :, cols], proj_ref[3, :, cols]
        gatt = gatt_ref[:, cols]
        qrys = [only(qry, a, half_scale) for a in range(per)]
        keys = [only(key_all, a) for a in range(per)]
        gatts = [only(gatt, a) for a in range(per)]
        gval_ref[...] = jnp.zeros_like(gval_ref)
        gkey_ref[...] = jnp.zeros_like(gkey_ref)
        for r0 in range(0, count, qrows):
            r1 = r0 + qrows
            gqry = None
            for a in range(per):
                gweight = dot_nt(gatts[a][r0:r1], val[:r1])
                gscore = (gweight * wslope_ref[p * per + a, r0:r1, :r1]).astype(BF16)
                part = dot_nn(gscore, keys[a][:r1])
                gqry = part if gqry is None else gqry + part
                gval_ref[:r1, :] += dot_tn(weight_ref[p * per + a, r0:r1, :r1], gatts[a][r0:r1])
                gkey_ref[:r1, :] += dot_tn(gscore, qrys[a][r0:r1])
            gpre_ref[r0:r1, pl.ds(2 * width + start, LANES)] = (
                gqry * half_scale * slope_ref[2, r0:r1, cols]
            ).astype(BF16)
        gpre_ref[:, pl.ds(width + start, LANES)] = (gval_ref[...] * slope_ref[1, :, cols]).astype(BF16)
        gpre_ref[:, pl.ds(3 * width + start, LANES)] = (gkey_ref[...] * slope_ref[3, :, cols]).astype(BF16)
        return 0

    lax.fori_loop(0, slabs, backward, 0)

    put_gpre = pltpu.make_async_copy(gpre_ref, gpre_hbm, sems.at[4])
    put_gpre.start()

    emb_t = emb_ref[...].T
    rows = width // owners
    cols_in = 4 * width // groups
    cols_out = width // wparts
    puts = [put_result, put_gpre]
    for g in range(groups):
        part = dot_nn(emb_t, gpre_ref[:, g * cols_in : (g + 1) * cols_in]).astype(BF16)
        gin_ref[:, g] = part.reshape(owners, rows, cols_in)
    puts.append(pltpu.make_async_copy(gin_ref, gin_hbm, sems.at[5]))
    puts[-1].start()
    gwo = dot_tn(mixed_ref[...], cot_ref[...]).astype(BF16)
    gain_col = jnp.broadcast_to(gain_sum, (LANES, width)).T.astype(BF16)
    for g in range(groups):
        p = g % wparts
        part = gwo[:, p * cols_out : (p + 1) * cols_out]
        gout_ref[:, g, :, 0:cols_out] = part.reshape(owners, rows, cols_out)
        gout_ref[:, g, :, cols_out:] = gain_col.reshape(owners, rows, LANES)
    puts.append(pltpu.make_async_copy(gout_ref, gout_hbm, sems.at[6]))
    puts[-1].start()
    for put in puts:
        put.wait()


def rows_kernel(slot_ref, gpre_hbm, w_in_hbm, cot_ref, out_hbm, gpre_ref, w_in_ref, out_ref, sems):
    count, width = cot_ref.shape
    slots = out_ref.shape[0]
    fetches = []
    for i in range(4):
        cols = pl.ds(i * width, width)
        pair = (
            pltpu.make_async_copy(gpre_hbm.at[:, cols], gpre_ref.at[:, cols], sems.at[2 * i]),
            pltpu.make_async_copy(w_in_hbm.at[:, cols], w_in_ref.at[:, cols], sems.at[2 * i + 1]),
        )
        for fetch in pair:
            fetch.start()
        fetches.append(pair)
    total = cot_ref[...].astype(F32)
    for i in range(4):
        for fetch in fetches[i]:
            fetch.wait()
        cols = slice(i * width, (i + 1) * width)
        total = total + dot_nt(gpre_ref[:, cols], w_in_ref[:, cols])
    gemb = total.astype(BF16)
    step = row_step(slots)
    stores = []
    for n, start in enumerate(range(0, slots, step)):
        put = hot((iota((step, count), 0) + start).astype(F32) == slot_ref[...])
        out_ref[start : start + step, :] = dot_nn(put, gemb).astype(BF16)
        here = pl.ds(start, step)
        stores.append(pltpu.make_async_copy(out_ref.at[here], out_hbm.at[here], sems.at[8 + n]))
        stores[-1].start()
    for store in stores:
        store.wait()


def shift(value, axis, size, amount):
    return lax.ppermute(value, axis, [(i, (i + amount) % size) for i in range(size)])


def on_device(item_owner, item_row, lengths, table, w_in, w_out, gain, cotangent):
    owners = lax.axis_size("table")
    groups = lax.axis_size("group")
    count = item_row.shape[0]
    width = table.shape[1]
    capacity = max(2, 3 * count // (2 * owners))
    slots = owners * capacity
    padded = -(-capacity // LANES) * LANES
    me = lax.axis_index("group")

    requested, slot = call(
        functools.partial(request_kernel, capacity),
        [
            jax.ShapeDtypeStruct((owners, padded), jnp.int32),
            jax.ShapeDtypeStruct((1, count), F32),
        ],
        4 * count * count * owners,
        8 * count,
        (item_owner.reshape(1, count), item_row.reshape(1, count)),
    )
    wanted = lax.all_to_all(requested, "table", split_axis=0, concat_axis=0, tiled=True)
    found, ids = call(
        functools.partial(lookup_kernel, capacity),
        [
            jax.ShapeDtypeStruct((slots, width), BF16),
            jax.ShapeDtypeStruct((1, slots), F32),
        ],
        2 * slots * table.shape[0] * width,
        2 * (slots + table.shape[0]) * width,
        (wanted, table),
        far=(1,),
        far_out=(0,),
        scratch=[
            pltpu.VMEM(table.shape, BF16),
            pltpu.VMEM((slots, width), BF16),
            pltpu.SemaphoreType.DMA((1 + slots // row_step(slots),)),
        ],
    )
    returned = lax.all_to_all(found, "table", split_axis=0, concat_axis=0, tiled=True)
    all_ids = [ids] + [shift(ids, "group", groups, k) for k in range(1, groups)]
    returned, *all_ids = lax.optimization_barrier((returned, *all_ids))

    wparts = min(groups, width // LANES)
    cols_in = 4 * width // groups
    cols_out = width // wparts
    rows = width // owners
    square = pltpu.VMEM((count, width), BF16)
    result, gpre, grad_in, grad_out = call(
        functools.partial(layer_kernel, owners, groups, wparts),
        [
            jax.ShapeDtypeStruct((count, width), BF16),
            jax.ShapeDtypeStruct((count, 4 * width), BF16),
            jax.ShapeDtypeStruct((owners, groups, rows, cols_in), BF16),
            jax.ShapeDtypeStruct((owners, groups, rows, cols_out + LANES), BF16),
        ],
        24 * count * width * width + 14 * count * count * width,
        24 * count * width,
        (lengths, slot, returned, w_in, w_out, gain.reshape(1, width), cotangent),
        smem=(0,),
        far=(3, 4, 6),
        far_out=range(4),
        scratch=[
            pltpu.VMEM(w_in.shape, BF16),
            pltpu.VMEM(w_out.shape, BF16),
            square,
            square,
            pltpu.VMEM((owners, groups, rows, cols_in), BF16),
            pltpu.VMEM((owners, groups, rows, cols_out + LANES), BF16),
            pltpu.VMEM((count, slots), BF16),
            square,
            pltpu.VMEM((4, count, width), BF16),
            pltpu.VMEM((4, count, width), F32),
            pltpu.VMEM((count, count), F32),
            pltpu.VMEM((HEADS, count, count), BF16),
            pltpu.VMEM((HEADS, count, count), F32),
            pltpu.VMEM((count, width), F32),
            square,
            square,
            pltpu.VMEM((count, 4 * width), BF16),
            pltpu.VMEM((count, LANES), F32),
            pltpu.VMEM((count, LANES), F32),
            pltpu.SemaphoreType.DMA((7,)),
        ],
    )
    (outgoing,) = call(
        rows_kernel,
        [jax.ShapeDtypeStruct((slots, width), BF16)],
        8 * count * width * width + 2 * slots * count * width,
        20 * count * width,
        (slot, gpre, w_in, cotangent),
        far=(1, 2),
        far_out=(0,),
        scratch=[
            pltpu.VMEM((count, 4 * width), BF16),
            pltpu.VMEM(w_in.shape, BF16),
            pltpu.VMEM((slots, width), BF16),
            pltpu.SemaphoreType.DMA((8 + slots // row_step(slots),)),
        ],
    )

    everyone = ("table", "group")
    sum_in = lax.psum_scatter(
        grad_in.reshape(owners * groups * rows, cols_in), everyone, scatter_dimension=0, tiled=True
    )
    sum_out = lax.psum_scatter(
        grad_out.reshape(owners * groups * rows, cols_out + LANES),
        everyone,
        scatter_dimension=0,
        tiled=True,
    )

    incoming = lax.all_to_all(outgoing, "table", split_axis=0, concat_axis=0, tiled=True)
    all_incoming = [incoming] + [shift(incoming, "group", groups, k) for k in range(1, groups)]
    grad_rows = table.shape[0] // groups
    (table_grad,) = call(
        functools.partial(collect_kernel, groups),
        [jax.ShapeDtypeStruct((grad_rows, width), F32)],
        2 * slots * table.shape[0] * width,
        2 * groups * slots * width + 4 * grad_rows * width,
        (*all_ids, *all_incoming),
        far=range(groups, 2 * groups),
        far_out=(0,),
        limit=24,
        scratch=[
            *[pltpu.VMEM((slots, width), BF16) for _ in range(groups)],
            pltpu.VMEM((grad_rows, width), F32),
            pltpu.SemaphoreType.DMA((groups + grad_rows // row_step(grad_rows),)),
        ],
    )

    w_in_grad = sum_in.astype(F32)
    mine = sum_out[:, :cols_out].astype(F32)
    pieces = jnp.stack([mine] + [shift(mine, "group", groups, k) for k in range(1, groups)])
    w_out_grad = jnp.concatenate(
        [
            lax.dynamic_index_in_dim(pieces, (me - p) % groups, 0, keepdims=False)
            for p in range(wparts)
        ],
        1,
    )
    gain_grad = sum_out[:, cols_out].astype(F32)
    return (result, table_grad, w_in_grad, w_out_grad, gain_grad)


def solution(mesh):
    return jax.shard_map(
        on_device,
        mesh=mesh,
        in_specs=(
            P(("table", "group"), None),
            P(("table", "group")),
            P(("table", "group"), None),
            P("table", None),
            P(),
            P(),
            P(),
            P(("table", "group"), None),
        ),
        out_specs=(
            P(("table", "group"), None),
            P(("table", "group"), None),
            P("table", "group"),
            P("table", None),
            P("table"),
        ),
        check_vma=False,
    )
```

```python
import functools
import math

import jax
import jax.numpy as jnp
from jax import lax
from jax.experimental import pallas as pl
from jax.experimental.pallas import tpu as pltpu
from jax.sharding import PartitionSpec as P

HEADS = 8
HEAD_DIM = 64
LANES = 128
QUERY_ROWS = 256

F32 = jnp.float32
BF16 = jnp.bfloat16


def iota(shape, dim):
    return lax.broadcasted_iota(jnp.int32, shape, dim)


def hot(cond):
    return jnp.where(cond, 1.0, 0.0).astype(BF16)


def dot_nn(a, b):
    return lax.dot_general(a, b, (((1,), (0,)), ((), ())), preferred_element_type=F32)


def dot_nt(a, b):
    return lax.dot_general(a, b, (((1,), (1,)), ((), ())), preferred_element_type=F32)


def dot_tn(a, b):
    return lax.dot_general(a, b, (((0,), (0,)), ((), ())), preferred_element_type=F32)


def row_step(rows):
    return 256 if rows % 256 == 0 else rows


def call(kernel, out_shape, flops, nbytes, operands, smem=(), far=(), far_out=(), limit=56, scratch=()):
    spaces = [
        pltpu.SMEM if i in smem else pl.ANY if i in far else pltpu.VMEM
        for i in range(len(operands))
    ]
    out_spaces = [pl.ANY if i in far_out else pltpu.VMEM for i in range(len(out_shape))]
    return pl.pallas_call(
        kernel,
        out_shape=out_shape,
        in_specs=[pl.BlockSpec(memory_space=space) for space in spaces],
        out_specs=[pl.BlockSpec(memory_space=space) for space in out_spaces],
        scratch_shapes=scratch,
        compiler_params=pltpu.CompilerParams(vmem_limit_bytes=limit * 1024 * 1024),
        cost_estimate=pl.CostEstimate(flops=flops, bytes_accessed=nbytes, transcendentals=0),
    )(*operands)


def request_kernel(cap, owner_ref, row_ref, req_ref, slot_ref):
    owners, width = req_ref.shape
    count = owner_ref.shape[1]
    owner = owner_ref[...]
    row = row_ref[...]
    mine = iota((owners, count), 0) == owner
    mine_b = hot(mine)
    before = hot(iota((count, count), 0) < iota((count, count), 1))
    earlier = dot_nn(mine_b, before)
    place = jnp.sum(jnp.where(mine, earlier, 0.0), axis=0, keepdims=True)
    slot_ref[...] = owner.astype(F32) * float(cap) + place
    at_place = hot(iota((width, count), 0).astype(F32) == place)
    high = jnp.where(mine, (row >> 8).astype(F32), 0.0).astype(BF16)
    low = jnp.where(mine, (row & 255).astype(F32), 0.0).astype(BF16)
    found = dot_nt(high, at_place) * 256.0 + dot_nt(low, at_place)
    req_ref[...] = found.astype(jnp.int32)


def lookup_kernel(cap, wanted_ref, table_hbm, found_hbm, ids_ref, table_ref, found_ref, pick_ref, sems):
    owners, width = wanted_ref.shape
    slots = found_ref.shape[0]
    rows = table_ref.shape[0]
    half_width = table_ref.shape[1] // 2
    halves = [pl.ds(i * half_width, half_width) for i in range(2)]
    fetches = []
    for i, half in enumerate(halves):
        for j in range(2):
            at = (pl.ds(j * (rows // 2), rows // 2), half)
            fetches.append(
                pltpu.make_async_copy(table_hbm.at[at], table_ref.at[at], sems.at[2 * i + j])
            )
            fetches[-1].start()
    wanted = wanted_ref[...]
    high = (wanted >> 8).astype(F32).astype(BF16)
    low = (wanted & 255).astype(F32).astype(BF16)
    slot = iota((slots, owners), 0).astype(F32)
    holder = jnp.floor((slot + 0.5) * (1.0 / cap))
    spread = hot(holder == iota((slots, owners), 1).astype(F32))
    ids = dot_nn(spread, high) * 256.0 + dot_nn(spread, low)
    slot = iota((slots, width), 0).astype(F32)
    place = slot - jnp.floor((slot + 0.5) * (1.0 / cap)) * float(cap)
    ids = jnp.sum(
        jnp.where(iota((slots, width), 1).astype(F32) == place, ids, 0.0), axis=1, keepdims=True
    )
    wide = jnp.broadcast_to(ids, (slots, LANES))
    ids_ref[...] = wide.T[0:1, :]
    step = row_step(slots)
    for start in range(0, slots, step):
        part = ids[start : start + step]
        pick_ref[start : start + step, :] = hot(iota((step, rows), 1).astype(F32) == part)
    stores = []
    for i, half in enumerate(halves):
        for fetch in fetches[2 * i : 2 * i + 2]:
            fetch.wait()
        found_ref[:, half] = dot_nn(pick_ref[...], table_ref[:, half]).astype(BF16)
        stores.append(
            pltpu.make_async_copy(found_ref.at[:, half], found_hbm.at[:, half], sems.at[4 + i])
        )
        stores[-1].start()
    for store in stores:
        store.wait()


def collect_kernel(groups, *refs):
    ids_refs, in_hbms, out_hbm = refs[:groups], refs[groups : 2 * groups], refs[2 * groups]
    in_refs, out_ref, sems = refs[2 * groups + 1 : 3 * groups + 1], refs[-2], refs[-1]
    rows = out_ref.shape[0]
    slots = in_refs[0].shape[0]
    fetches = [
        pltpu.make_async_copy(hbm, ref, sems.at[n])
        for n, (hbm, ref) in enumerate(zip(in_hbms, in_refs))
    ]
    for fetch in fetches:
        fetch.start()
    base = lax.axis_index("group") * rows
    step = row_step(rows)
    for fetch in fetches:
        fetch.wait()
    stores = []
    for n, start in enumerate(range(0, rows, step)):
        own = (iota((step, slots), 0) + (base + start)).astype(F32)
        total = None
        for ids_ref, in_ref in zip(ids_refs, in_refs):
            part = dot_nn(hot(own == ids_ref[...]), in_ref[...])
            total = part if total is None else total + part
        out_ref[start : start + step, :] = total
        here = pl.ds(start, step)
        stores.append(
            pltpu.make_async_copy(out_ref.at[here], out_hbm.at[here], sems.at[groups + n])
        )
        stores[-1].start()
    for store in stores:
        store.wait()


def layer_kernel(
    groups,
    wparts,
    len_ref,
    slot_ref,
    ret_ref,
    w_in_hbm,
    w_out_hbm,
    gain_ref,
    cot_hbm,
    *rest,
):
    result_hbm, gpre_hbm = rest[:2]
    grads_hbms = rest[2 : 2 + 2 * groups]
    (
    w_in_ref,
    w_out_ref,
    cot_ref,
    result_ref,
    grads_ref,
    pick_ref,
    emb_ref,
    proj_ref,
    slope_ref,
    bias_ref,
    weight_ref,
    wslope_ref,
    att_ref,
    mixed_ref,
    gatt_ref,
    gpre_ref,
    gval_ref,
    gkey_ref,
    gwo_ref,
    sems,
    ) = rest[2 + 2 * groups :]
    count, width = cot_ref.shape
    slots = ret_ref.shape[0]
    per = LANES // HEAD_DIM
    slabs = width // LANES
    qrows = QUERY_ROWS if count % QUERY_ROWS == 0 else count
    half_scale = 0.5 / math.sqrt(HEAD_DIM)

    parts = [pl.ds(i * width, width) for i in range(4)]
    get_ins = [
        pltpu.make_async_copy(w_in_hbm.at[:, part], w_in_ref.at[:, part], sems.at[i])
        for i, part in enumerate(parts)
    ]
    get_cot = pltpu.make_async_copy(cot_hbm, cot_ref, sems.at[4])
    get_out = pltpu.make_async_copy(w_out_hbm, w_out_ref, sems.at[5])
    for fetch in (*get_ins, get_cot, get_out):
        fetch.start()

    slot = jnp.broadcast_to(slot_ref[...], (LANES, count)).T
    for start in range(0, slots, LANES):
        pick_ref[:, start : start + LANES] = hot(
            slot == (iota((count, LANES), 1) + start).astype(F32)
        )
    emb_ref[...] = dot_nn(pick_ref[...], ret_ref[...]).astype(BF16)

    for i in range(4):
        get_ins[i].wait()
        pre = dot_nn(emb_ref[...], w_in_ref[:, parts[i]])
        sig = 0.5 * jnp.tanh(0.5 * pre) + 0.5
        act = pre * sig
        proj_ref[i] = act.astype(BF16)
        slope_ref[i] = sig + act * (1.0 - sig)

    pos = iota((count, 1), 0)
    begin = jnp.zeros((count, 1), jnp.int32)
    end = jnp.int32(0)
    for s in range(len_ref.shape[1]):
        end = end + len_ref[0, s]
        begin = jnp.where(pos >= end, end, begin)
    key = iota((count, count), 1)
    allowed = (key >= begin) & (key <= iota((count, count), 0))
    bias_ref[...] = jnp.where(allowed, 3.0e38, -30.0)

    lane = iota((count, LANES), 1)

    def only(value, head, factor=1.0):
        inside = (lane >= head * HEAD_DIM) & (lane < (head + 1) * HEAD_DIM)
        return jnp.where(inside, value.astype(F32) * factor, 0.0).astype(BF16)

    def forward(p, _):
        cols = pl.ds(pl.multiple_of(p * LANES, LANES), LANES)
        val, qry, key_all = proj_ref[1, :, cols], proj_ref[2, :, cols], proj_ref[3, :, cols]
        qrys = [only(qry, a, half_scale) for a in range(per)]
        vals = [only(val, a) for a in range(per)]
        for r0 in range(0, count, qrows):
            r1 = r0 + qrows
            total = None
            for a in range(per):
                half = dot_nt(qrys[a][r0:r1], key_all[:r1])
                half = jnp.minimum(half, bias_ref[r0:r1, :r1])
                th = jnp.tanh(half)
                weight = half + half * th
                weight_b = weight.astype(BF16)
                weight_ref[p * per + a, r0:r1, :r1] = weight_b
                wslope_ref[p * per + a, r0:r1, :r1] = (1.0 + th) + weight * (1.0 - th)
                part = dot_nn(weight_b, vals[a][:r1])
                total = part if total is None else total + part
            att_ref[r0:r1, cols] = total
        return 0

    lax.fori_loop(0, slabs, forward, 0)

    get_cot.wait()
    get_out.wait()
    gain = gain_ref[...]
    gain_sum = jnp.zeros((1, width), F32)
    for r0 in range(0, count, qrows):
        rows = slice(r0, r0 + qrows)
        att = att_ref[rows, :]
        centered = att - jnp.mean(att, 1, keepdims=True)
        inv = lax.rsqrt(jnp.mean(centered * centered, 1, keepdims=True) + 1e-05)
        normed = centered * inv
        upd = proj_ref[0, rows, :].astype(F32)
        scaled = normed * gain
        mixed = (scaled * upd).astype(BF16)
        mixed_ref[rows, :] = mixed
        result_ref[rows, :] = (
            emb_ref[rows, :].astype(F32) + dot_nn(mixed, w_out_ref[...])
        ).astype(BF16)
        gmix = dot_nt(cot_ref[rows, :], w_out_ref[...]).astype(BF16).astype(F32)
        gpre_ref[rows, 0:width] = (gmix * scaled * slope_ref[0, rows, :]).astype(BF16)
        gnorm = gmix * gain * upd
        gain_sum = gain_sum + jnp.sum(gmix * normed * upd, 0, keepdims=True)
        mean1 = jnp.mean(gnorm, 1, keepdims=True)
        mean2 = jnp.mean(gnorm * normed, 1, keepdims=True)
        gatt_ref[rows, :] = ((gnorm - mean1 - normed * mean2) * inv).astype(BF16)
    put_result = pltpu.make_async_copy(result_ref, result_hbm, sems.at[6])
    put_result.start()
    gwo_ref[...] = dot_tn(mixed_ref[...], cot_ref[...]).astype(BF16)

    def backward(p, _):
        start = pl.multiple_of(p * LANES, LANES)
        cols = pl.ds(start, LANES)
        val, qry, key_all = proj_ref[1, :, cols], proj_ref[2, :, cols], proj_ref[3, :, cols]
        gatt = gatt_ref[:, cols]
        qrys = [only(qry, a, half_scale) for a in range(per)]
        keys = [only(key_all, a) for a in range(per)]
        gatts = [only(gatt, a) for a in range(per)]
        gval_ref[...] = jnp.zeros_like(gval_ref)
        gkey_ref[...] = jnp.zeros_like(gkey_ref)
        for r0 in range(0, count, qrows):
            r1 = r0 + qrows
            gqry = None
            for a in range(per):
                gweight = dot_nt(gatts[a][r0:r1], val[:r1])
                gscore = (gweight * wslope_ref[p * per + a, r0:r1, :r1]).astype(BF16)
                part = dot_nn(gscore, keys[a][:r1])
                gqry = part if gqry is None else gqry + part
                gval_ref[:r1, :] += dot_tn(weight_ref[p * per + a, r0:r1, :r1], gatts[a][r0:r1])
                gkey_ref[:r1, :] += dot_tn(gscore, qrys[a][r0:r1])
            gpre_ref[r0:r1, pl.ds(2 * width + start, LANES)] = (
                gqry * half_scale * slope_ref[2, r0:r1, cols]
            ).astype(BF16)
        gpre_ref[:, pl.ds(width + start, LANES)] = (gval_ref[...] * slope_ref[1, :, cols]).astype(BF16)
        gpre_ref[:, pl.ds(3 * width + start, LANES)] = (gkey_ref[...] * slope_ref[3, :, cols]).astype(BF16)
        return 0

    lax.fori_loop(0, slabs, backward, 0)

    puts = [put_result]
    for i, part in enumerate(parts):
        puts.append(
            pltpu.make_async_copy(gpre_ref.at[:, part], gpre_hbm.at[:, part], sems.at[7 + i])
        )
        puts[-1].start()

    me = lax.axis_index("group")
    emb_t = emb_ref[...].T
    cols_in = 4 * width // groups
    cols_out = width // wparts
    chunk = min(cols_in, 512)
    gain_col = jnp.broadcast_to(gain_sum, (LANES, width)).T.astype(BF16)
    for k in [*range(1, groups), 0]:
        part = lax.rem(me + k, groups)
        for c in range(0, cols_in, chunk):
            cols = pl.ds(pl.multiple_of(part * cols_in + c, LANES), chunk)
            grads_ref[k, :, c : c + chunk] = dot_nn(emb_t, gpre_ref[:, cols]).astype(BF16)
        cols = pl.ds(pl.multiple_of(lax.rem(part, wparts) * cols_out, LANES), cols_out)
        grads_ref[k, :, cols_in : cols_in + cols_out] = gwo_ref[:, cols]
        grads_ref[k, :, cols_in + cols_out :] = gain_col
        cut = grads_hbms[2 * k].shape[1]
        for i, cols in enumerate((pl.ds(0, cut), pl.ds(cut, grads_ref.shape[2] - cut))):
            put = pltpu.make_async_copy(
                grads_ref.at[k, :, cols], grads_hbms[2 * k + i], sems.at[11 + 2 * k + i]
            )
            put.start()
            puts.append(put)
    for put in puts:
        put.wait()


def row_grad_kernel(gpre_hbm, w_in_hbm, cot_ref, out_ref, gpre_ref, w_in_ref, sems):
    width = cot_ref.shape[1]
    fetches = []
    for i in range(4):
        cols = pl.ds(i * width, width)
        pair = (
            pltpu.make_async_copy(gpre_hbm.at[:, cols], gpre_ref.at[:, cols], sems.at[2 * i]),
            pltpu.make_async_copy(w_in_hbm.at[:, cols], w_in_ref.at[:, cols], sems.at[2 * i + 1]),
        )
        for fetch in pair:
            fetch.start()
        fetches.append(pair)
    total = cot_ref[...].astype(F32)
    for i in range(4):
        for fetch in fetches[i]:
            fetch.wait()
        cols = slice(i * width, (i + 1) * width)
        total = total + dot_nt(gpre_ref[:, cols], w_in_ref[:, cols])
    out_ref[...] = total.astype(BF16)


def slots_kernel(slot_ref, grad_ref, out_hbm, out_ref, sems):
    count = grad_ref.shape[0]
    slots = out_ref.shape[0]
    step = row_step(slots)
    stores = []
    for n, start in enumerate(range(0, slots, step)):
        put = hot((iota((step, count), 0) + start).astype(F32) == slot_ref[...])
        out_ref[start : start + step, :] = dot_nn(put, grad_ref[...]).astype(BF16)
        here = pl.ds(start, step)
        stores.append(pltpu.make_async_copy(out_ref.at[here], out_hbm.at[here], sems.at[n]))
        stores[-1].start()
    for store in stores:
        store.wait()


def shift(value, axis, size, amount):
    return lax.ppermute(value, axis, [(i, (i + amount) % size) for i in range(size)])


def on_device(item_owner, item_row, lengths, table, w_in, w_out, gain, cotangent):
    owners = lax.axis_size("table")
    groups = lax.axis_size("group")
    count = item_row.shape[0]
    width = table.shape[1]
    capacity = max(2, 3 * count // (2 * owners))
    slots = owners * capacity
    padded = -(-capacity // LANES) * LANES
    me = lax.axis_index("group")

    requested, slot = call(
        functools.partial(request_kernel, capacity),
        [
            jax.ShapeDtypeStruct((owners, padded), jnp.int32),
            jax.ShapeDtypeStruct((1, count), F32),
        ],
        4 * count * count * owners,
        8 * count,
        (item_owner.reshape(1, count), item_row.reshape(1, count)),
    )
    wanted = lax.all_to_all(requested, "table", split_axis=0, concat_axis=0, tiled=True)
    found, ids = call(
        functools.partial(lookup_kernel, capacity),
        [
            jax.ShapeDtypeStruct((slots, width), BF16),
            jax.ShapeDtypeStruct((1, slots), F32),
        ],
        2 * slots * table.shape[0] * width,
        2 * (slots + table.shape[0]) * width,
        (wanted, table),
        far=(1,),
        far_out=(0,),
        scratch=[
            pltpu.VMEM(table.shape, BF16),
            pltpu.VMEM((slots, width), BF16),
            pltpu.VMEM((slots, table.shape[0]), BF16),
            pltpu.SemaphoreType.DMA((6,)),
        ],
    )
    returned = lax.all_to_all(found, "table", split_axis=0, concat_axis=0, tiled=True)
    all_ids = [ids] + [shift(ids, "group", groups, k) for k in range(1, groups)]
    returned, *all_ids = lax.optimization_barrier((returned, *all_ids))

    wparts = min(groups, width // LANES)
    cols_in = 4 * width // groups
    cols_out = width // wparts
    cols_all = cols_in + cols_out + LANES
    cut = cols_all // LANES // 2 * LANES
    square = pltpu.VMEM((count, width), BF16)
    result, gpre, *grads = call(
        functools.partial(layer_kernel, groups, wparts),
        [
            jax.ShapeDtypeStruct((count, width), BF16),
            jax.ShapeDtypeStruct((count, 4 * width), BF16),
            *[
                jax.ShapeDtypeStruct((width, cols), BF16)
                for _ in range(groups)
                for cols in (cut, cols_all - cut)
            ],
        ],
        24 * count * width * width + 14 * count * count * width,
        24 * count * width,
        (lengths, slot, returned, w_in, w_out, gain.reshape(1, width), cotangent),
        smem=(0,),
        far=(3, 4, 6),
        far_out=range(2 + 2 * groups),
        scratch=[
            pltpu.VMEM(w_in.shape, BF16),
            pltpu.VMEM(w_out.shape, BF16),
            square,
            square,
            pltpu.VMEM((groups, width, cols_all), BF16),
            pltpu.VMEM((count, slots), BF16),
            square,
            pltpu.VMEM((4, count, width), BF16),
            pltpu.VMEM((4, count, width), F32),
            pltpu.VMEM((count, count), F32),
            pltpu.VMEM((HEADS, count, count), BF16),
            pltpu.VMEM((HEADS, count, count), F32),
            pltpu.VMEM((count, width), F32),
            square,
            square,
            pltpu.VMEM((count, 4 * width), BF16),
            pltpu.VMEM((count, LANES), F32),
            pltpu.VMEM((count, LANES), F32),
            pltpu.VMEM((width, width), BF16),
            pltpu.SemaphoreType.DMA((11 + 2 * groups,)),
        ],
    )
    (row_grad,) = call(
        row_grad_kernel,
        [jax.ShapeDtypeStruct((count, width), BF16)],
        8 * count * width * width,
        20 * count * width,
        (gpre, w_in, cotangent),
        far=(0, 1),
        scratch=[
            pltpu.VMEM((count, 4 * width), BF16),
            pltpu.VMEM(w_in.shape, BF16),
            pltpu.SemaphoreType.DMA((8,)),
        ],
    )

    rows = width // owners
    side = 2 if owners % 4 == 0 else 1
    plane = side * side
    outer = owners // plane
    here = lax.axis_index("table")
    high, middle, low = here // plane, here // side % side, here % side
    sides = []
    for i in range(2):
        terms = [grads[i]] + [shift(grads[2 * k + i], "group", groups, k) for k in range(1, groups)]
        sides.append([term.reshape(outer, side, side, rows, term.shape[1]) for term in terms])

    def entry(value, index, axis):
        return lax.dynamic_index_in_dim(value, index, axis, keepdims=False)

    def add(terms):
        return sum(term.astype(F32) for term in terms)

    def halve(terms, index, axis, bit, tie=None):
        send = add([entry(term, 1 - index, axis) for term in terms]).astype(BF16)
        if tie is not None:
            tie, send = lax.optimization_barrier((tie, send))
        got = lax.ppermute(send, "table", [(i, i ^ bit) for i in range(owners)])
        return [entry(term, index, axis) for term in terms] + [got], tie

    if side == 2:
        left, row_grad = halve(sides[0], low, 2, 1, row_grad)
        right, row_grad = halve(sides[1], middle, 1, 2, row_grad)
        left, _ = halve(left, middle, 1, 2)
        right, _ = halve(right, low, 1, 1)
    else:
        left, right = [[term[:, 0, 0] for term in terms] for terms in sides]
    sums = [[add([entry(term, high, 0) for term in terms])] for terms in (left, right)]
    for k in range(1, outer):
        perm = [(i, ((i // plane + k) % outer) * plane + i % plane) for i in range(owners)]
        send = [add([entry(term, (high + k) % outer, 0) for term in terms]) for terms in (left, right)]
        got = lax.ppermute(jnp.concatenate(send, 1).astype(BF16), "table", perm)
        sums[0].append(got[:, :cut])
        sums[1].append(got[:, cut:])
    summed = jnp.concatenate([add(terms) for terms in sums], 1)

    (outgoing,) = call(
        slots_kernel,
        [jax.ShapeDtypeStruct((slots, width), BF16)],
        2 * slots * count * width,
        4 * count * width,
        (slot, row_grad),
        far_out=(0,),
        scratch=[
            pltpu.VMEM((slots, width), BF16),
            pltpu.SemaphoreType.DMA((slots // row_step(slots),)),
        ],
    )
    incoming = lax.all_to_all(outgoing, "table", split_axis=0, concat_axis=0, tiled=True)
    all_incoming = [incoming] + [shift(incoming, "group", groups, k) for k in range(1, groups)]
    grad_rows = table.shape[0] // groups
    (table_grad,) = call(
        functools.partial(collect_kernel, groups),
        [jax.ShapeDtypeStruct((grad_rows, width), F32)],
        2 * slots * table.shape[0] * width,
        2 * groups * slots * width + 4 * grad_rows * width,
        (*all_ids, *all_incoming),
        far=range(groups, 2 * groups),
        far_out=(0,),
        limit=24,
        scratch=[
            *[pltpu.VMEM((slots, width), BF16) for _ in range(groups)],
            pltpu.VMEM((grad_rows, width), F32),
            pltpu.SemaphoreType.DMA((groups + grad_rows // row_step(grad_rows),)),
        ],
    )

    w_in_grad = summed[:, :cols_in]
    mine = summed[:, cols_in : cols_in + cols_out]
    pieces = jnp.stack([mine] + [shift(mine, "group", groups, k) for k in range(1, groups)])
    w_out_grad = jnp.concatenate(
        [
            lax.dynamic_index_in_dim(pieces, (me - p) % groups, 0, keepdims=False)
            for p in range(wparts)
        ],
        1,
    )
    gain_grad = summed[:, cols_in + cols_out]
    return (result, table_grad, w_in_grad, w_out_grad, gain_grad)


def solution(mesh):
    return jax.shard_map(
        on_device,
        mesh=mesh,
        in_specs=(
            P(("table", "group"), None),
            P(("table", "group")),
            P(("table", "group"), None),
            P("table", None),
            P(),
            P(),
            P(),
            P(("table", "group"), None),
        ),
        out_specs=(
            P(("table", "group"), None),
            P(("table", "group"), None),
            P("table", "group"),
            P("table", None),
            P("table"),
        ),
        check_vma=False,
    )
```

```python
import functools
import math

import jax
import jax.numpy as jnp
from jax import lax
from jax.experimental import pallas as pl
from jax.experimental.pallas import tpu as pltpu
from jax.sharding import PartitionSpec as P

HEADS = 8
HEAD_DIM = 64
LANES = 128
QUERY_ROWS = 256

F32 = jnp.float32
BF16 = jnp.bfloat16


def iota(shape, dim):
    return lax.broadcasted_iota(jnp.int32, shape, dim)


def hot(cond):
    return jnp.where(cond, 1.0, 0.0).astype(BF16)


def dot_nn(a, b):
    return lax.dot_general(a, b, (((1,), (0,)), ((), ())), preferred_element_type=F32)


def dot_nt(a, b):
    return lax.dot_general(a, b, (((1,), (1,)), ((), ())), preferred_element_type=F32)


def dot_tn(a, b):
    return lax.dot_general(a, b, (((0,), (0,)), ((), ())), preferred_element_type=F32)


def row_step(rows):
    return 256 if rows % 256 == 0 else rows


def call(kernel, out_shape, flops, nbytes, operands, smem=(), far=(), far_out=(), limit=56, scratch=()):
    spaces = [
        pltpu.SMEM if i in smem else pl.ANY if i in far else pltpu.VMEM
        for i in range(len(operands))
    ]
    out_spaces = [pl.ANY if i in far_out else pltpu.VMEM for i in range(len(out_shape))]
    return pl.pallas_call(
        kernel,
        out_shape=out_shape,
        in_specs=[pl.BlockSpec(memory_space=space) for space in spaces],
        out_specs=[pl.BlockSpec(memory_space=space) for space in out_spaces],
        scratch_shapes=scratch,
        compiler_params=pltpu.CompilerParams(vmem_limit_bytes=limit * 1024 * 1024),
        cost_estimate=pl.CostEstimate(flops=flops, bytes_accessed=nbytes, transcendentals=0),
    )(*operands)


def request_kernel(cap, owner_ref, row_ref, req_ref, slot_ref):
    owners, width = req_ref.shape
    count = owner_ref.shape[1]
    owner = owner_ref[...]
    row = row_ref[...]
    mine = iota((owners, count), 0) == owner
    mine_b = hot(mine)
    before = hot(iota((count, count), 0) < iota((count, count), 1))
    earlier = dot_nn(mine_b, before)
    place = jnp.sum(jnp.where(mine, earlier, 0.0), axis=0, keepdims=True)
    slot_ref[...] = owner.astype(F32) * float(cap) + place
    at_place = hot(iota((width, count), 0).astype(F32) == place)
    high = jnp.where(mine, (row >> 8).astype(F32), 0.0).astype(BF16)
    low = jnp.where(mine, (row & 255).astype(F32), 0.0).astype(BF16)
    found = dot_nt(high, at_place) * 256.0 + dot_nt(low, at_place)
    req_ref[...] = found.astype(jnp.int32)


def lookup_kernel(cap, wanted_ref, table_ref, found_ref, ids_ref):
    owners, width = wanted_ref.shape
    slots = found_ref.shape[0]
    rows = table_ref.shape[0]
    wanted = wanted_ref[...]
    high = (wanted >> 8).astype(F32).astype(BF16)
    low = (wanted & 255).astype(F32).astype(BF16)
    slot = iota((slots, owners), 0).astype(F32)
    holder = jnp.floor((slot + 0.5) * (1.0 / cap))
    spread = hot(holder == iota((slots, owners), 1).astype(F32))
    ids = dot_nn(spread, high) * 256.0 + dot_nn(spread, low)
    slot = iota((slots, width), 0).astype(F32)
    place = slot - jnp.floor((slot + 0.5) * (1.0 / cap)) * float(cap)
    ids = jnp.sum(
        jnp.where(iota((slots, width), 1).astype(F32) == place, ids, 0.0), axis=1, keepdims=True
    )
    wide = jnp.broadcast_to(ids, (slots, LANES))
    ids_ref[...] = wide.T[0:1, :]
    step = 256 if slots % 256 == 0 else slots
    for start in range(0, slots, step):
        part = ids[start : start + step]
        pick = hot(iota((step, rows), 1).astype(F32) == part)
        found_ref[start : start + step, :] = dot_nn(pick, table_ref[...]).astype(BF16)


def collect_kernel(groups, *refs):
    ids_refs, in_hbms, out_hbm = refs[:groups], refs[groups : 2 * groups], refs[2 * groups]
    in_refs, out_ref, sems = refs[2 * groups + 1 : 3 * groups + 1], refs[-2], refs[-1]
    rows = out_ref.shape[0]
    slots = in_refs[0].shape[0]
    fetches = [
        pltpu.make_async_copy(hbm, ref, sems.at[n])
        for n, (hbm, ref) in enumerate(zip(in_hbms, in_refs))
    ]
    for fetch in fetches:
        fetch.start()
    base = lax.axis_index("group") * rows
    step = row_step(rows)
    for fetch in fetches:
        fetch.wait()
    stores = []
    for n, start in enumerate(range(0, rows, step)):
        own = (iota((step, slots), 0) + (base + start)).astype(F32)
        total = None
        for ids_ref, in_ref in zip(ids_refs, in_refs):
            part = dot_nn(hot(own == ids_ref[...]), in_ref[...])
            total = part if total is None else total + part
        out_ref[start : start + step, :] = total
        here = pl.ds(start, step)
        stores.append(
            pltpu.make_async_copy(out_ref.at[here], out_hbm.at[here], sems.at[groups + n])
        )
        stores[-1].start()
    for store in stores:
        store.wait()


def layer_kernel(
    groups,
    wparts,
    len_ref,
    slot_ref,
    ret_ref,
    w_in_hbm,
    w_out_hbm,
    gain_ref,
    cot_hbm,
    *rest,
):
    result_hbm, row_hbm = rest[:2]
    grads_hbms = rest[2 : 2 + 2 * groups]
    (
    w_in_ref,
    w_out_ref,
    cot_ref,
    result_ref,
    row_ref,
    grads_ref,
    pick_ref,
    emb_ref,
    proj_ref,
    slope_ref,
    bias_ref,
    weight_ref,
    wslope_ref,
    att_ref,
    mixed_ref,
    gatt_ref,
    gpre_ref,
    gval_ref,
    gkey_ref,
    gwo_ref,
    sems,
    ) = rest[2 + 2 * groups :]
    count, width = cot_ref.shape
    slots = ret_ref.shape[0]
    per = LANES // HEAD_DIM
    slabs = width // LANES
    qrows = QUERY_ROWS if count % QUERY_ROWS == 0 else count
    half_scale = 0.5 / math.sqrt(HEAD_DIM)

    parts = [pl.ds(i * width, width) for i in range(4)]
    get_ins = [
        pltpu.make_async_copy(w_in_hbm.at[:, part], w_in_ref.at[:, part], sems.at[i])
        for i, part in enumerate(parts)
    ]
    get_cot = pltpu.make_async_copy(cot_hbm, cot_ref, sems.at[4])
    get_out = pltpu.make_async_copy(w_out_hbm, w_out_ref, sems.at[5])
    for fetch in (*get_ins, get_cot, get_out):
        fetch.start()

    slot = jnp.broadcast_to(slot_ref[...], (LANES, count)).T
    for start in range(0, slots, LANES):
        pick_ref[:, start : start + LANES] = hot(
            slot == (iota((count, LANES), 1) + start).astype(F32)
        )
    emb_ref[...] = dot_nn(pick_ref[...], ret_ref[...]).astype(BF16)

    for i in range(4):
        get_ins[i].wait()
        pre = dot_nn(emb_ref[...], w_in_ref[:, parts[i]])
        sig = 0.5 * jnp.tanh(0.5 * pre) + 0.5
        act = pre * sig
        proj_ref[i] = act.astype(BF16)
        slope_ref[i] = sig + act * (1.0 - sig)

    pos = iota((count, 1), 0)
    begin = jnp.zeros((count, 1), jnp.int32)
    end = jnp.int32(0)
    for s in range(len_ref.shape[1]):
        end = end + len_ref[0, s]
        begin = jnp.where(pos >= end, end, begin)
    key = iota((count, count), 1)
    allowed = (key >= begin) & (key <= iota((count, count), 0))
    bias_ref[...] = jnp.where(allowed, 3.0e38, -30.0)

    lane = iota((count, LANES), 1)

    def only(value, head, factor=1.0):
        inside = (lane >= head * HEAD_DIM) & (lane < (head + 1) * HEAD_DIM)
        return jnp.where(inside, value.astype(F32) * factor, 0.0).astype(BF16)

    def forward(p, _):
        cols = pl.ds(pl.multiple_of(p * LANES, LANES), LANES)
        val, qry, key_all = proj_ref[1, :, cols], proj_ref[2, :, cols], proj_ref[3, :, cols]
        qrys = [only(qry, a, half_scale) for a in range(per)]
        vals = [only(val, a) for a in range(per)]
        for r0 in range(0, count, qrows):
            r1 = r0 + qrows
            total = None
            for a in range(per):
                half = dot_nt(qrys[a][r0:r1], key_all[:r1])
                half = jnp.minimum(half, bias_ref[r0:r1, :r1])
                th = jnp.tanh(half)
                weight = half + half * th
                weight_b = weight.astype(BF16)
                weight_ref[p * per + a, r0:r1, :r1] = weight_b
                wslope_ref[p * per + a, r0:r1, :r1] = (1.0 + th) + weight * (1.0 - th)
                part = dot_nn(weight_b, vals[a][:r1])
                total = part if total is None else total + part
            att_ref[r0:r1, cols] = total
        return 0

    lax.fori_loop(0, slabs, forward, 0)

    get_cot.wait()
    get_out.wait()
    gain = gain_ref[...]
    gain_sum = jnp.zeros((1, width), F32)
    for r0 in range(0, count, qrows):
        rows = slice(r0, r0 + qrows)
        att = att_ref[rows, :]
        centered = att - jnp.mean(att, 1, keepdims=True)
        inv = lax.rsqrt(jnp.mean(centered * centered, 1, keepdims=True) + 1e-05)
        normed = centered * inv
        upd = proj_ref[0, rows, :].astype(F32)
        scaled = normed * gain
        mixed = (scaled * upd).astype(BF16)
        mixed_ref[rows, :] = mixed
        result_ref[rows, :] = (
            emb_ref[rows, :].astype(F32) + dot_nn(mixed, w_out_ref[...])
        ).astype(BF16)
        gmix = dot_nt(cot_ref[rows, :], w_out_ref[...]).astype(BF16).astype(F32)
        gpre_ref[rows, 0:width] = (gmix * scaled * slope_ref[0, rows, :]).astype(BF16)
        gnorm = gmix * gain * upd
        gain_sum = gain_sum + jnp.sum(gmix * normed * upd, 0, keepdims=True)
        mean1 = jnp.mean(gnorm, 1, keepdims=True)
        mean2 = jnp.mean(gnorm * normed, 1, keepdims=True)
        gatt_ref[rows, :] = ((gnorm - mean1 - normed * mean2) * inv).astype(BF16)
    put_result = pltpu.make_async_copy(result_ref, result_hbm, sems.at[6])
    put_result.start()
    gwo_ref[...] = dot_tn(mixed_ref[...], cot_ref[...]).astype(BF16)

    def backward(p, _):
        start = pl.multiple_of(p * LANES, LANES)
        cols = pl.ds(start, LANES)
        val, qry, key_all = proj_ref[1, :, cols], proj_ref[2, :, cols], proj_ref[3, :, cols]
        gatt = gatt_ref[:, cols]
        qrys = [only(qry, a, half_scale) for a in range(per)]
        keys = [only(key_all, a) for a in range(per)]
        gatts = [only(gatt, a) for a in range(per)]
        gval_ref[...] = jnp.zeros_like(gval_ref)
        gkey_ref[...] = jnp.zeros_like(gkey_ref)
        for r0 in range(0, count, qrows):
            r1 = r0 + qrows
            gqry = None
            for a in range(per):
                gweight = dot_nt(gatts[a][r0:r1], val[:r1])
                gscore = (gweight * wslope_ref[p * per + a, r0:r1, :r1]).astype(BF16)
                part = dot_nn(gscore, keys[a][:r1])
                gqry = part if gqry is None else gqry + part
                gval_ref[:r1, :] += dot_tn(weight_ref[p * per + a, r0:r1, :r1], gatts[a][r0:r1])
                gkey_ref[:r1, :] += dot_tn(gscore, qrys[a][r0:r1])
            gpre_ref[r0:r1, pl.ds(2 * width + start, LANES)] = (
                gqry * half_scale * slope_ref[2, r0:r1, cols]
            ).astype(BF16)
        gpre_ref[:, pl.ds(width + start, LANES)] = (gval_ref[...] * slope_ref[1, :, cols]).astype(BF16)
        gpre_ref[:, pl.ds(3 * width + start, LANES)] = (gkey_ref[...] * slope_ref[3, :, cols]).astype(BF16)
        return 0

    lax.fori_loop(0, slabs, backward, 0)

    puts = [put_result]
    me = lax.axis_index("group")
    emb_t = emb_ref[...].T
    cols_in = 4 * width // groups
    cols_out = width // wparts
    chunk = min(cols_in, 512)
    gain_col = jnp.broadcast_to(gain_sum, (LANES, width)).T.astype(BF16)
    for k in [*range(1, groups), 0]:
        part = lax.rem(me + k, groups)
        for c in range(0, cols_in, chunk):
            cols = pl.ds(pl.multiple_of(part * cols_in + c, LANES), chunk)
            grads_ref[k, :, c : c + chunk] = dot_nn(emb_t, gpre_ref[:, cols]).astype(BF16)
        cols = pl.ds(pl.multiple_of(lax.rem(part, wparts) * cols_out, LANES), cols_out)
        grads_ref[k, :, cols_in : cols_in + cols_out] = gwo_ref[:, cols]
        grads_ref[k, :, cols_in + cols_out :] = gain_col
        cut = grads_hbms[2 * k].shape[1]
        for i, cols in enumerate((pl.ds(0, cut), pl.ds(cut, grads_ref.shape[2] - cut))):
            put = pltpu.make_async_copy(
                grads_ref.at[k, :, cols], grads_hbms[2 * k + i], sems.at[8 + 2 * k + i]
            )
            put.start()
            puts.append(put)
    row_ref[...] = (
        cot_ref[...].astype(F32) + dot_nt(gpre_ref[...], w_in_ref[...])
    ).astype(BF16)
    puts.append(pltpu.make_async_copy(row_ref, row_hbm, sems.at[7]))
    puts[-1].start()
    for put in puts:
        put.wait()


def slots_kernel(slot_ref, grad_ref, out_hbm, out_ref, sems):
    count = grad_ref.shape[0]
    slots = out_ref.shape[0]
    step = row_step(slots)
    stores = []
    for n, start in enumerate(range(0, slots, step)):
        put = hot((iota((step, count), 0) + start).astype(F32) == slot_ref[...])
        out_ref[start : start + step, :] = dot_nn(put, grad_ref[...]).astype(BF16)
        here = pl.ds(start, step)
        stores.append(pltpu.make_async_copy(out_ref.at[here], out_hbm.at[here], sems.at[n]))
        stores[-1].start()
    for store in stores:
        store.wait()


def plane_kernel(outer, terms, *refs):
    left, right, outs = refs[:terms], refs[terms : 2 * terms], refs[2 * terms :]
    cut = left[0].shape[2]
    high = lax.div(lax.axis_index("table"), lax.axis_size("table") // outer)
    for k in range(outer):
        at = lax.rem(high + k, outer)
        for parts, cols in ((left, slice(0, cut)), (right, slice(cut, None))):
            total = parts[0][at].astype(F32)
            for part in parts[1:]:
                total = total + part[at].astype(F32)
            outs[k][:, cols] = total.astype(outs[k].dtype)


def finish_kernel(kept_ref, *refs):
    got_refs, (in_ref, out_ref, gain_ref) = refs[:-3], refs[-3:]
    total = kept_ref[...]
    for got_ref in got_refs:
        total = total + got_ref[...].astype(F32)
    cols_in, cols_out = in_ref.shape[1], out_ref.shape[1]
    in_ref[...] = total[:, :cols_in]
    out_ref[...] = total[:, cols_in : cols_in + cols_out]
    gain_ref[...] = total[:, cols_in + cols_out :].T[0:1, :]


def shift(value, axis, size, amount):
    return lax.ppermute(value, axis, [(i, (i + amount) % size) for i in range(size)])


def on_device(item_owner, item_row, lengths, table, w_in, w_out, gain, cotangent):
    owners = lax.axis_size("table")
    groups = lax.axis_size("group")
    count = item_row.shape[0]
    width = table.shape[1]
    capacity = max(2, 3 * count // (2 * owners))
    slots = owners * capacity
    padded = -(-capacity // LANES) * LANES
    me = lax.axis_index("group")

    requested, slot = call(
        functools.partial(request_kernel, capacity),
        [
            jax.ShapeDtypeStruct((owners, padded), jnp.int32),
            jax.ShapeDtypeStruct((1, count), F32),
        ],
        4 * count * count * owners,
        8 * count,
        (item_owner.reshape(1, count), item_row.reshape(1, count)),
    )
    wanted = lax.all_to_all(requested, "table", split_axis=0, concat_axis=0, tiled=True)
    found, ids = call(
        functools.partial(lookup_kernel, capacity),
        [
            jax.ShapeDtypeStruct((slots, width), BF16),
            jax.ShapeDtypeStruct((1, slots), F32),
        ],
        2 * slots * table.shape[0] * width,
        2 * (slots + table.shape[0]) * width,
        (wanted, table),
    )
    returned = lax.all_to_all(found, "table", split_axis=0, concat_axis=0, tiled=True)
    all_ids = [ids] + [shift(ids, "group", groups, k) for k in range(1, groups)]
    returned, *all_ids = lax.optimization_barrier((returned, *all_ids))

    wparts = min(groups, width // LANES)
    cols_in = 4 * width // groups
    cols_out = width // wparts
    cols_all = cols_in + cols_out + LANES
    cut = cols_all // LANES // 2 * LANES
    square = pltpu.VMEM((count, width), BF16)
    result, row_grad, *grads = call(
        functools.partial(layer_kernel, groups, wparts),
        [
            jax.ShapeDtypeStruct((count, width), BF16),
            jax.ShapeDtypeStruct((count, width), BF16),
            *[
                jax.ShapeDtypeStruct((width, cols), BF16)
                for _ in range(groups)
                for cols in (cut, cols_all - cut)
            ],
        ],
        32 * count * width * width + 14 * count * count * width,
        24 * count * width,
        (lengths, slot, returned, w_in, w_out, gain.reshape(1, width), cotangent),
        smem=(0,),
        far=(3, 4, 6),
        far_out=range(2 + 2 * groups),
        scratch=[
            pltpu.VMEM(w_in.shape, BF16),
            pltpu.VMEM(w_out.shape, BF16),
            square,
            square,
            square,
            pltpu.VMEM((groups, width, cols_all), BF16),
            pltpu.VMEM((count, slots), BF16),
            square,
            pltpu.VMEM((4, count, width), BF16),
            pltpu.VMEM((4, count, width), F32),
            pltpu.VMEM((count, count), F32),
            pltpu.VMEM((HEADS, count, count), BF16),
            pltpu.VMEM((HEADS, count, count), F32),
            pltpu.VMEM((count, width), F32),
            square,
            square,
            pltpu.VMEM((count, 4 * width), BF16),
            pltpu.VMEM((count, LANES), F32),
            pltpu.VMEM((count, LANES), F32),
            pltpu.VMEM((width, width), BF16),
            pltpu.SemaphoreType.DMA((8 + 2 * groups,)),
        ],
    )
    rows = width // owners
    side = 2 if owners % 4 == 0 else 1
    plane = side * side
    outer = owners // plane
    here = lax.axis_index("table")
    high, middle, low = here // plane, here // side % side, here % side
    sides = []
    for i in range(2):
        terms = [grads[i]] + [shift(grads[2 * k + i], "group", groups, k) for k in range(1, groups)]
        sides.append([term.reshape(outer, side, side, rows, term.shape[1]) for term in terms])

    def entry(value, index, axis):
        return lax.dynamic_index_in_dim(value, index, axis, keepdims=False)

    def add(terms):
        return sum(term.astype(F32) for term in terms)

    def halve(terms, index, axis, bit, tie=None):
        send = add([entry(term, 1 - index, axis) for term in terms]).astype(BF16)
        if tie is not None:
            tie, send = lax.optimization_barrier((tie, send))
        got = lax.ppermute(send, "table", [(i, i ^ bit) for i in range(owners)])
        return [add([entry(term, index, axis) for term in terms]), got], tie

    if side == 2:
        left, row_grad = halve(sides[0], low, 2, 1, row_grad)
        right, row_grad = halve(sides[1], middle, 1, 2, row_grad)
        left, _ = halve(left, middle, 1, 2)
        right, _ = halve(right, low, 1, 1)
    else:
        left, right = [[term[:, 0, 0] for term in terms] for terms in sides]
    cols = cols_all
    kept, *sends = call(
        functools.partial(plane_kernel, outer, len(left)),
        [
            jax.ShapeDtypeStruct((rows, cols), F32),
            *[jax.ShapeDtypeStruct((rows, cols), BF16) for _ in range(1, outer)],
        ],
        12 * outer * rows * cols,
        8 * outer * rows * cols,
        (*left, *right),
        limit=24,
    )
    got = [
        lax.ppermute(
            sends[k - 1],
            "table",
            [(i, ((i // plane + k) % outer) * plane + i % plane) for i in range(owners)],
        )
        for k in range(1, outer)
    ]

    (outgoing,) = call(
        slots_kernel,
        [jax.ShapeDtypeStruct((slots, width), BF16)],
        2 * slots * count * width,
        4 * count * width,
        (slot, row_grad),
        far_out=(0,),
        scratch=[
            pltpu.VMEM((slots, width), BF16),
            pltpu.SemaphoreType.DMA((slots // row_step(slots),)),
        ],
    )
    incoming = lax.all_to_all(outgoing, "table", split_axis=0, concat_axis=0, tiled=True)
    all_incoming = [incoming] + [shift(incoming, "group", groups, k) for k in range(1, groups)]
    grad_rows = table.shape[0] // groups
    (table_grad,) = call(
        functools.partial(collect_kernel, groups),
        [jax.ShapeDtypeStruct((grad_rows, width), F32)],
        2 * slots * table.shape[0] * width,
        2 * groups * slots * width + 4 * grad_rows * width,
        (*all_ids, *all_incoming),
        far=range(groups, 2 * groups),
        far_out=(0,),
        limit=24,
        scratch=[
            *[pltpu.VMEM((slots, width), BF16) for _ in range(groups)],
            pltpu.VMEM((grad_rows, width), F32),
            pltpu.SemaphoreType.DMA((groups + grad_rows // row_step(grad_rows),)),
        ],
    )

    kept, table_grad = lax.optimization_barrier((kept, table_grad))
    w_in_grad, mine, gain_grad = call(
        finish_kernel,
        [
            jax.ShapeDtypeStruct((rows, cols_in), F32),
            jax.ShapeDtypeStruct((rows, cols_out), F32),
            jax.ShapeDtypeStruct((1, rows), F32),
        ],
        4 * rows * cols_all,
        14 * rows * cols_all,
        (kept, *got),
        limit=24,
    )
    pieces = jnp.stack([mine] + [shift(mine, "group", groups, k) for k in range(1, groups)])
    w_out_grad = jnp.concatenate(
        [
            lax.dynamic_index_in_dim(pieces, (me - p) % groups, 0, keepdims=False)
            for p in range(wparts)
        ],
        1,
    )
    return (result, table_grad, w_in_grad, w_out_grad, gain_grad.reshape(rows))


def solution(mesh):
    return jax.shard_map(
        on_device,
        mesh=mesh,
        in_specs=(
            P(("table", "group"), None),
            P(("table", "group")),
            P(("table", "group"), None),
            P("table", None),
            P(),
            P(),
            P(),
            P(("table", "group"), None),
        ),
        out_specs=(
            P(("table", "group"), None),
            P(("table", "group"), None),
            P("table", "group"),
            P("table", None),
            P("table"),
        ),
        check_vma=False,
    )
```

```python
import functools
import math

import jax
import jax.numpy as jnp
from jax import lax
from jax.experimental import pallas as pl
from jax.experimental.pallas import tpu as pltpu
from jax.sharding import PartitionSpec as P

HEAD_DIM = 64
LANES = 128
QUERY_ROWS = 256

F32 = jnp.float32
BF16 = jnp.bfloat16


def iota(shape, dim):
    return lax.broadcasted_iota(jnp.int32, shape, dim)


def hot(cond):
    return jnp.where(cond, 1.0, 0.0).astype(BF16)


def dot_nn(a, b):
    return lax.dot_general(a, b, (((1,), (0,)), ((), ())), preferred_element_type=F32)


def dot_nt(a, b):
    return lax.dot_general(a, b, (((1,), (1,)), ((), ())), preferred_element_type=F32)


def dot_tn(a, b):
    return lax.dot_general(a, b, (((0,), (0,)), ((), ())), preferred_element_type=F32)


def row_step(rows):
    return 256 if rows % 256 == 0 else rows


def call(kernel, out_shape, flops, nbytes, operands, smem=(), far=(), far_out=(), limit=56, scratch=()):
    spaces = [
        pltpu.SMEM if i in smem else pl.ANY if i in far else pltpu.VMEM
        for i in range(len(operands))
    ]
    out_spaces = [pl.ANY if i in far_out else pltpu.VMEM for i in range(len(out_shape))]
    return pl.pallas_call(
        kernel,
        out_shape=out_shape,
        in_specs=[pl.BlockSpec(memory_space=space) for space in spaces],
        out_specs=[pl.BlockSpec(memory_space=space) for space in out_spaces],
        scratch_shapes=scratch,
        compiler_params=pltpu.CompilerParams(vmem_limit_bytes=limit * 1024 * 1024),
        cost_estimate=pl.CostEstimate(flops=flops, bytes_accessed=nbytes, transcendentals=0),
    )(*operands)


def request_kernel(cap, owner_ref, row_ref, req_ref, slot_ref):
    owners, width = req_ref.shape
    count = owner_ref.shape[1]
    owner = owner_ref[...]
    row = row_ref[...]
    mine = iota((owners, count), 0) == owner
    mine_b = hot(mine)
    before = hot(iota((count, count), 0) < iota((count, count), 1))
    earlier = dot_nn(mine_b, before)
    place = jnp.sum(jnp.where(mine, earlier, 0.0), axis=0, keepdims=True)
    slot_ref[...] = owner.astype(F32) * float(cap) + place
    at_place = hot(iota((width, count), 0).astype(F32) == place)
    high = jnp.where(mine, (row >> 8).astype(F32), 0.0).astype(BF16)
    low = jnp.where(mine, (row & 255).astype(F32), 0.0).astype(BF16)
    found = dot_nt(high, at_place) * 256.0 + dot_nt(low, at_place)
    req_ref[...] = found.astype(jnp.int32)


def lookup_kernel(cap, wanted_ref, table_ref, found_ref, ids_ref):
    owners, width = wanted_ref.shape
    slots = found_ref.shape[0]
    rows = table_ref.shape[0]
    wanted = wanted_ref[...]
    high = (wanted >> 8).astype(F32).astype(BF16)
    low = (wanted & 255).astype(F32).astype(BF16)
    slot = iota((slots, owners), 0).astype(F32)
    holder = jnp.floor((slot + 0.5) * (1.0 / cap))
    spread = hot(holder == iota((slots, owners), 1).astype(F32))
    ids = dot_nn(spread, high) * 256.0 + dot_nn(spread, low)
    slot = iota((slots, width), 0).astype(F32)
    place = slot - jnp.floor((slot + 0.5) * (1.0 / cap)) * float(cap)
    ids = jnp.sum(
        jnp.where(iota((slots, width), 1).astype(F32) == place, ids, 0.0), axis=1, keepdims=True
    )
    wide = jnp.broadcast_to(ids, (slots, LANES))
    ids_ref[...] = wide.T[0:1, :]
    step = 256 if slots % 256 == 0 else slots
    for start in range(0, slots, step):
        part = ids[start : start + step]
        pick = hot(iota((step, rows), 1).astype(F32) == part)
        found_ref[start : start + step, :] = dot_nn(pick, table_ref[...]).astype(BF16)


def collect_kernel(groups, *refs):
    ids_refs, in_hbms, out_hbm = refs[:groups], refs[groups : 2 * groups], refs[2 * groups]
    in_refs, out_ref, sems = refs[2 * groups + 1 : 3 * groups + 1], refs[-2], refs[-1]
    rows = out_ref.shape[0]
    slots = in_refs[0].shape[0]
    fetches = [
        pltpu.make_async_copy(hbm, ref, sems.at[n])
        for n, (hbm, ref) in enumerate(zip(in_hbms, in_refs))
    ]
    for fetch in fetches:
        fetch.start()
    base = lax.axis_index("group") * rows
    step = row_step(rows)
    for fetch in fetches:
        fetch.wait()
    stores = []
    for n, start in enumerate(range(0, rows, step)):
        own = (iota((step, slots), 0) + (base + start)).astype(F32)
        total = None
        for ids_ref, in_ref in zip(ids_refs, in_refs):
            part = dot_nn(hot(own == ids_ref[...]), in_ref[...])
            total = part if total is None else total + part
        out_ref[start : start + step, :] = total
        here = pl.ds(start, step)
        stores.append(
            pltpu.make_async_copy(out_ref.at[here], out_hbm.at[here], sems.at[groups + n])
        )
        stores[-1].start()
    for store in stores:
        store.wait()


def layer_kernel(
    groups,
    wparts,
    len_ref,
    slot_ref,
    ret_hbm,
    w_in_hbm,
    w_out_hbm,
    gain_ref,
    cot_hbm,
    *rest,
):
    result_hbm, row_hbm = rest[:2]
    grads_hbms = rest[2 : 2 + 2 * groups]
    (
    ret_ref,
    w_in_ref,
    w_out_ref,
    cot_ref,
    result_ref,
    row_ref,
    grads_ref,
    pick_ref,
    emb_ref,
    proj_ref,
    slope_ref,
    bias_ref,
    weight_ref,
    wslope_ref,
    att_ref,
    mixed_ref,
    gatt_ref,
    gpre_ref,
    gval_ref,
    gkey_ref,
    gwo_ref,
    sems,
    ) = rest[2 + 2 * groups :]
    count, width = cot_ref.shape
    slots = ret_hbm.shape[0]
    per = LANES // HEAD_DIM
    slabs = width // LANES
    qrows = QUERY_ROWS if count % QUERY_ROWS == 0 else count
    half_scale = 0.5 / math.sqrt(HEAD_DIM)

    get_ret = pltpu.make_async_copy(ret_hbm, ret_ref, sems.at[8 + 2 * groups])
    get_ret.start()
    parts = [pl.ds(i * width, width) for i in range(4)]
    get_ins = [
        pltpu.make_async_copy(w_in_hbm.at[:, part], w_in_ref.at[:, part], sems.at[i])
        for i, part in enumerate(parts)
    ]
    get_cot = pltpu.make_async_copy(cot_hbm, cot_ref, sems.at[4])
    get_out = pltpu.make_async_copy(w_out_hbm, w_out_ref, sems.at[5])
    for fetch in (*get_ins, get_cot, get_out):
        fetch.start()

    slot = jnp.broadcast_to(slot_ref[...], (LANES, count)).T
    for start in range(0, slots, LANES):
        pick_ref[:, start : start + LANES] = hot(
            slot == (iota((count, LANES), 1) + start).astype(F32)
        )
    get_ret.wait()
    emb_ref[...] = dot_nn(pick_ref[...], ret_ref[...]).astype(BF16)

    for i in range(4):
        get_ins[i].wait()
        pre = dot_nn(emb_ref[...], w_in_ref[:, parts[i]])
        half = 0.5 * pre
        th = jnp.tanh(half)
        act = half + half * th
        proj_ref[i] = act.astype(BF16)
        slope_ref[i] = 0.5 * ((1.0 + th) + act * (1.0 - th))

    pos = iota((count, 1), 0)
    begin = jnp.zeros((count, 1), jnp.int32)
    end = jnp.int32(0)
    for s in range(len_ref.shape[1]):
        end = end + len_ref[0, s]
        begin = jnp.where(pos >= end, end, begin)
    key = iota((count, count), 1)
    allowed = (key >= begin) & (key <= iota((count, count), 0))
    bias_ref[...] = jnp.where(allowed, 3.0e38, -30.0)

    lane = iota((qrows, LANES), 1)
    inside = [(lane >= a * HEAD_DIM) & (lane < (a + 1) * HEAD_DIM) for a in range(per)]
    lane = iota((count, LANES), 1)
    inside_all = [(lane >= a * HEAD_DIM) & (lane < (a + 1) * HEAD_DIM) for a in range(per)]

    def stacked(value, factor=1.0):
        value = value.astype(F32) * factor
        return jnp.concatenate([jnp.where(m, value, 0.0) for m in inside], 0).astype(BF16)

    def apart(value):
        value = value.astype(F32)
        return [jnp.where(m, value, 0.0).astype(BF16) for m in inside_all]

    def forward(p, _):
        cols = pl.ds(pl.multiple_of(p * LANES, LANES), LANES)
        key_all = proj_ref[3, :, cols]
        vals = apart(proj_ref[1, :, cols])
        for r0 in range(0, count, qrows):
            r1 = r0 + qrows
            half = dot_nt(stacked(proj_ref[2, r0:r1, cols], half_scale), key_all[:r1])
            half = jnp.minimum(half.reshape(per, qrows, r1), bias_ref[r0:r1, :r1][None])
            th = jnp.tanh(half)
            weight = half + half * th
            weight_b = weight.astype(BF16)
            base = per * r0
            weight_ref[p, base : base + per * qrows, :r1] = weight_b.reshape(per * qrows, r1)
            wslope_ref[p, base : base + per * qrows, :r1] = (
                (1.0 + th) + weight * (1.0 - th)
            ).reshape(per * qrows, r1)
            total = dot_nn(weight_b[0], vals[0][:r1])
            for a in range(1, per):
                total = total + dot_nn(weight_b[a], vals[a][:r1])
            att_ref[r0:r1, cols] = total
        return 0

    lax.fori_loop(0, slabs, forward, 0)

    get_cot.wait()
    get_out.wait()
    gain = gain_ref[...]
    gain_sum = jnp.zeros((1, width), F32)
    for r0 in range(0, count, qrows):
        rows = slice(r0, r0 + qrows)
        att = att_ref[rows, :]
        centered = att - jnp.mean(att, 1, keepdims=True)
        inv = lax.rsqrt(jnp.mean(centered * centered, 1, keepdims=True) + 1e-05)
        normed = centered * inv
        upd = proj_ref[0, rows, :].astype(F32)
        scaled = normed * gain
        mixed = (scaled * upd).astype(BF16)
        mixed_ref[rows, :] = mixed
        result_ref[rows, :] = (
            emb_ref[rows, :].astype(F32) + dot_nn(mixed, w_out_ref[...])
        ).astype(BF16)
        gmix = dot_nt(cot_ref[rows, :], w_out_ref[...]).astype(BF16).astype(F32)
        gpre_ref[rows, 0:width] = (gmix * scaled * slope_ref[0, rows, :]).astype(BF16)
        gnorm = gmix * gain * upd
        gain_sum = gain_sum + jnp.sum(gmix * normed * upd, 0, keepdims=True)
        mean1 = jnp.mean(gnorm, 1, keepdims=True)
        mean2 = jnp.mean(gnorm * normed, 1, keepdims=True)
        gatt_ref[rows, :] = ((gnorm - mean1 - normed * mean2) * inv).astype(BF16)
    put_result = pltpu.make_async_copy(result_ref, result_hbm, sems.at[6])
    put_result.start()
    gwo_ref[...] = dot_tn(mixed_ref[...], cot_ref[...]).astype(BF16)

    def backward(p, _):
        start = pl.multiple_of(p * LANES, LANES)
        cols = pl.ds(start, LANES)
        val = proj_ref[1, :, cols]
        keys = apart(proj_ref[3, :, cols])
        for r0 in reversed(range(0, count, qrows)):
            r1 = r0 + qrows
            base = per * r0
            rows = slice(base, base + per * qrows)
            gatt = stacked(gatt_ref[r0:r1, cols])
            gweight = dot_nt(gatt, val[:r1])
            gscore = (gweight * wslope_ref[p, rows, :r1]).astype(BF16)
            gqry = dot_nn(gscore[:qrows], keys[0][:r1])
            for a in range(1, per):
                gqry = gqry + dot_nn(gscore[a * qrows : (a + 1) * qrows], keys[a][:r1])
            gval = dot_tn(weight_ref[p, rows, :r1], gatt)
            gkey = dot_tn(gscore, stacked(proj_ref[2, r0:r1, cols], half_scale))
            if r1 == count:
                gval_ref[...] = gval
                gkey_ref[...] = gkey
            else:
                gval_ref[:r1, :] += gval
                gkey_ref[:r1, :] += gkey
            gpre_ref[r0:r1, pl.ds(2 * width + start, LANES)] = (
                gqry * half_scale * slope_ref[2, r0:r1, cols]
            ).astype(BF16)
        gpre_ref[:, pl.ds(width + start, LANES)] = (gval_ref[...] * slope_ref[1, :, cols]).astype(BF16)
        gpre_ref[:, pl.ds(3 * width + start, LANES)] = (gkey_ref[...] * slope_ref[3, :, cols]).astype(BF16)
        return 0

    lax.fori_loop(0, slabs, backward, 0)

    puts = [put_result]
    me = lax.axis_index("group")
    emb_t = emb_ref[...].T
    cols_in = 4 * width // groups
    cols_out = width // wparts
    chunk = min(cols_in, 512)
    gain_col = jnp.broadcast_to(gain_sum, (LANES, width)).T.astype(BF16)
    for k in [*range(1, groups), 0]:
        part = lax.rem(me + k, groups)
        for c in range(0, cols_in, chunk):
            cols = pl.ds(pl.multiple_of(part * cols_in + c, LANES), chunk)
            grads_ref[k, :, c : c + chunk] = dot_nn(emb_t, gpre_ref[:, cols]).astype(BF16)
        cols = pl.ds(pl.multiple_of(lax.rem(part, wparts) * cols_out, LANES), cols_out)
        grads_ref[k, :, cols_in : cols_in + cols_out] = gwo_ref[:, cols]
        grads_ref[k, :, cols_in + cols_out :] = gain_col
        cut = grads_hbms[2 * k].shape[1]
        for i, cols in enumerate((pl.ds(0, cut), pl.ds(cut, grads_ref.shape[2] - cut))):
            put = pltpu.make_async_copy(
                grads_ref.at[k, :, cols], grads_hbms[2 * k + i], sems.at[8 + 2 * k + i]
            )
            put.start()
            puts.append(put)
    for i, r0 in enumerate((0, count // 2)):
        rows = pl.ds(r0, count // 2)
        row_ref[rows, :] = (
            cot_ref[rows, :].astype(F32) + dot_nt(gpre_ref[rows, :], w_in_ref[...])
        ).astype(BF16)
        sem = sems.at[7 + i * (2 + 2 * groups)]
        puts.append(pltpu.make_async_copy(row_ref.at[rows], row_hbm.at[rows], sem))
        puts[-1].start()
    for put in puts:
        put.wait()


def slots_kernel(slot_ref, grad_ref, out_hbm, out_ref, sems):
    count = grad_ref.shape[0]
    slots = out_ref.shape[0]
    step = row_step(slots)
    stores = []
    for n, start in enumerate(range(0, slots, step)):
        put = hot((iota((step, count), 0) + start).astype(F32) == slot_ref[...])
        out_ref[start : start + step, :] = dot_nn(put, grad_ref[...]).astype(BF16)
        here = pl.ds(start, step)
        stores.append(pltpu.make_async_copy(out_ref.at[here], out_hbm.at[here], sems.at[n]))
        stores[-1].start()
    for store in stores:
        store.wait()


def plane_kernel(outer, terms, *refs):
    left, right, outs = refs[:terms], refs[terms : 2 * terms], refs[2 * terms :]
    cut = left[0].shape[2]
    high = lax.div(lax.axis_index("table"), lax.axis_size("table") // outer)
    for k in range(outer):
        at = lax.rem(high + k, outer)
        for parts, cols in ((left, slice(0, cut)), (right, slice(cut, None))):
            total = parts[0][at].astype(F32)
            for part in parts[1:]:
                total = total + part[at].astype(F32)
            outs[k][:, cols] = total.astype(outs[k].dtype)


def finish_kernel(kept_ref, *refs):
    got_refs, (in_ref, out_ref, gain_ref) = refs[:-3], refs[-3:]
    total = kept_ref[...]
    for got_ref in got_refs:
        total = total + got_ref[...].astype(F32)
    cols_in, cols_out = in_ref.shape[1], out_ref.shape[1]
    in_ref[...] = total[:, :cols_in]
    out_ref[...] = total[:, cols_in : cols_in + cols_out]
    gain_ref[...] = total[:, cols_in + cols_out :].T[0:1, :]


def shift(value, axis, size, amount):
    return lax.ppermute(value, axis, [(i, (i + amount) % size) for i in range(size)])


def on_device(item_owner, item_row, lengths, table, w_in, w_out, gain, cotangent):
    owners = lax.axis_size("table")
    groups = lax.axis_size("group")
    count = item_row.shape[0]
    width = table.shape[1]
    capacity = max(2, 3 * count // (2 * owners))
    slots = owners * capacity
    padded = -(-capacity // LANES) * LANES
    me = lax.axis_index("group")

    requested, slot = call(
        functools.partial(request_kernel, capacity),
        [
            jax.ShapeDtypeStruct((owners, padded), jnp.int32),
            jax.ShapeDtypeStruct((1, count), F32),
        ],
        4 * count * count * owners,
        8 * count,
        (item_owner.reshape(1, count), item_row.reshape(1, count)),
    )
    wanted = lax.all_to_all(requested, "table", split_axis=0, concat_axis=0, tiled=True)
    found, ids = call(
        functools.partial(lookup_kernel, capacity),
        [
            jax.ShapeDtypeStruct((slots, width), BF16),
            jax.ShapeDtypeStruct((1, slots), F32),
        ],
        2 * slots * table.shape[0] * width,
        2 * (slots + table.shape[0]) * width,
        (wanted, table),
    )
    returned = lax.all_to_all(found, "table", split_axis=0, concat_axis=0, tiled=True)
    all_ids = [ids] + [shift(ids, "group", groups, k) for k in range(1, groups)]
    returned, *all_ids = lax.optimization_barrier((returned, *all_ids))

    wparts = min(groups, width // LANES)
    heads_per = LANES // HEAD_DIM
    cols_in = 4 * width // groups
    cols_out = width // wparts
    cols_all = cols_in + cols_out + LANES
    cut = cols_all // LANES // 2 * LANES
    square = pltpu.VMEM((count, width), BF16)
    result, row_grad, *grads = call(
        functools.partial(layer_kernel, groups, wparts),
        [
            jax.ShapeDtypeStruct((count, width), BF16),
            jax.ShapeDtypeStruct((count, width), BF16),
            *[
                jax.ShapeDtypeStruct((width, cols), BF16)
                for _ in range(groups)
                for cols in (cut, cols_all - cut)
            ],
        ],
        32 * count * width * width + 14 * count * count * width,
        24 * count * width,
        (lengths, slot, returned, w_in, w_out, gain.reshape(1, width), cotangent),
        smem=(0,),
        far=(2, 3, 4, 6),
        far_out=range(2 + 2 * groups),
        scratch=[
            pltpu.VMEM((slots, width), BF16),
            pltpu.VMEM(w_in.shape, BF16),
            pltpu.VMEM(w_out.shape, BF16),
            square,
            square,
            square,
            pltpu.VMEM((groups, width, cols_all), BF16),
            pltpu.VMEM((count, slots), BF16),
            square,
            pltpu.VMEM((4, count, width), BF16),
            pltpu.VMEM((4, count, width), F32),
            pltpu.VMEM((count, count), F32),
            pltpu.VMEM((width // LANES, heads_per * count, count), BF16),
            pltpu.VMEM((width // LANES, heads_per * count, count), F32),
            pltpu.VMEM((count, width), F32),
            square,
            square,
            pltpu.VMEM((count, 4 * width), BF16),
            pltpu.VMEM((count, LANES), F32),
            pltpu.VMEM((count, LANES), F32),
            pltpu.VMEM((width, width), BF16),
            pltpu.SemaphoreType.DMA((10 + 2 * groups,)),
        ],
    )
    (outgoing,) = call(
        slots_kernel,
        [jax.ShapeDtypeStruct((slots, width), BF16)],
        2 * slots * count * width,
        4 * count * width,
        (slot, row_grad),
        far_out=(0,),
        scratch=[
            pltpu.VMEM((slots, width), BF16),
            pltpu.SemaphoreType.DMA((slots // row_step(slots),)),
        ],
    )
    rows = width // owners
    side = 2 if owners % 4 == 0 else 1
    plane = side * side
    outer = owners // plane
    here = lax.axis_index("table")
    high, middle, low = here // plane, here // side % side, here % side
    sides = []
    for i in range(2):
        terms = [grads[i]] + [shift(grads[2 * k + i], "group", groups, k) for k in range(1, groups)]
        sides.append([term.reshape(outer, side, side, rows, term.shape[1]) for term in terms])

    def entry(value, index, axis):
        return lax.dynamic_index_in_dim(value, index, axis, keepdims=False)

    def add(terms):
        return sum(term.astype(F32) for term in terms)

    def halve(terms, index, axis, bit):
        send = add([entry(term, 1 - index, axis) for term in terms]).astype(BF16)
        *terms, send = lax.optimization_barrier((*terms, send))
        got = lax.ppermute(send, "table", [(i, i ^ bit) for i in range(owners)])
        return [add([entry(term, index, axis) for term in terms]), got]

    if side == 2:
        left = halve(sides[0], low, 2, 1)
        right = halve(sides[1], middle, 1, 2)
        outgoing, left[0], right[0] = lax.optimization_barrier((outgoing, left[0], right[0]))
        left = halve(left, middle, 1, 2)
        right = halve(right, low, 1, 1)
    else:
        left, right = [[term[:, 0, 0] for term in terms] for terms in sides]
    cols = cols_all
    kept, *sends = call(
        functools.partial(plane_kernel, outer, len(left)),
        [
            jax.ShapeDtypeStruct((rows, cols), F32),
            *[jax.ShapeDtypeStruct((rows, cols), BF16) for _ in range(1, outer)],
        ],
        12 * outer * rows * cols,
        8 * outer * rows * cols,
        (*left, *right),
        limit=24,
    )
    got = [
        lax.ppermute(
            sends[k - 1],
            "table",
            [(i, ((i // plane + k) % outer) * plane + i % plane) for i in range(owners)],
        )
        for k in range(1, outer)
    ]

    incoming = lax.all_to_all(outgoing, "table", split_axis=0, concat_axis=0, tiled=True)
    all_incoming = [incoming] + [shift(incoming, "group", groups, k) for k in range(1, groups)]
    grad_rows = table.shape[0] // groups
    (table_grad,) = call(
        functools.partial(collect_kernel, groups),
        [jax.ShapeDtypeStruct((grad_rows, width), F32)],
        2 * slots * table.shape[0] * width,
        2 * groups * slots * width + 4 * grad_rows * width,
        (*all_ids, *all_incoming),
        far=range(groups, 2 * groups),
        far_out=(0,),
        limit=24,
        scratch=[
            *[pltpu.VMEM((slots, width), BF16) for _ in range(groups)],
            pltpu.VMEM((grad_rows, width), F32),
            pltpu.SemaphoreType.DMA((groups + grad_rows // row_step(grad_rows),)),
        ],
    )

    w_in_grad, mine, gain_grad = call(
        finish_kernel,
        [
            jax.ShapeDtypeStruct((rows, cols_in), F32),
            jax.ShapeDtypeStruct((rows, cols_out), F32),
            jax.ShapeDtypeStruct((1, rows), F32),
        ],
        4 * rows * cols_all,
        14 * rows * cols_all,
        (kept, *got),
        limit=24,
    )
    pieces = jnp.stack([mine] + [shift(mine, "group", groups, k) for k in range(1, groups)])
    w_out_grad = jnp.concatenate(
        [
            lax.dynamic_index_in_dim(pieces, (me - p) % groups, 0, keepdims=False)
            for p in range(wparts)
        ],
        1,
    )
    return (result, table_grad, w_in_grad, w_out_grad, gain_grad.reshape(rows))


def solution(mesh):
    return jax.shard_map(
        on_device,
        mesh=mesh,
        in_specs=(
            P(("table", "group"), None),
            P(("table", "group")),
            P(("table", "group"), None),
            P("table", None),
            P(),
            P(),
            P(),
            P(("table", "group"), None),
        ),
        out_specs=(
            P(("table", "group"), None),
            P(("table", "group"), None),
            P("table", "group"),
            P("table", None),
            P("table"),
        ),
        check_vma=False,
    )
```

```python
import functools
import math

import jax
import jax.numpy as jnp
from jax import lax
from jax.experimental import pallas as pl
from jax.experimental.pallas import tpu as pltpu
from jax.sharding import PartitionSpec as P

HEAD_DIM = 64
LANES = 128
QUERY_ROWS = 256

F32 = jnp.float32
BF16 = jnp.bfloat16


def iota(shape, dim):
    return lax.broadcasted_iota(jnp.int32, shape, dim)


def hot(cond):
    return jnp.where(cond, 1.0, 0.0).astype(BF16)


def dot_nn(a, b):
    return lax.dot_general(a, b, (((1,), (0,)), ((), ())), preferred_element_type=F32)


def dot_nt(a, b):
    return lax.dot_general(a, b, (((1,), (1,)), ((), ())), preferred_element_type=F32)


def dot_tn(a, b):
    return lax.dot_general(a, b, (((0,), (0,)), ((), ())), preferred_element_type=F32)


def row_step(rows):
    return 256 if rows % 256 == 0 else rows


def call(kernel, out_shape, flops, nbytes, operands, smem=(), far=(), far_out=(), limit=56, scratch=()):
    spaces = [
        pltpu.SMEM if i in smem else pl.ANY if i in far else pltpu.VMEM
        for i in range(len(operands))
    ]
    out_spaces = [pl.ANY if i in far_out else pltpu.VMEM for i in range(len(out_shape))]
    return pl.pallas_call(
        kernel,
        out_shape=out_shape,
        in_specs=[pl.BlockSpec(memory_space=space) for space in spaces],
        out_specs=[pl.BlockSpec(memory_space=space) for space in out_spaces],
        scratch_shapes=scratch,
        compiler_params=pltpu.CompilerParams(vmem_limit_bytes=limit * 1024 * 1024),
        cost_estimate=pl.CostEstimate(flops=flops, bytes_accessed=nbytes, transcendentals=0),
    )(*operands)


def request_kernel(cap, owner_ref, row_ref, req_ref, slot_ref):
    owners, width = req_ref.shape
    count = owner_ref.shape[1]
    owner = owner_ref[...]
    row = row_ref[...]
    mine = iota((owners, count), 0) == owner
    mine_b = hot(mine)
    before = hot(iota((count, count), 0) < iota((count, count), 1))
    earlier = dot_nn(mine_b, before)
    place = jnp.sum(jnp.where(mine, earlier, 0.0), axis=0, keepdims=True)
    slot_ref[...] = owner.astype(F32) * float(cap) + place
    at_place = hot(iota((width, count), 0).astype(F32) == place)
    high = jnp.where(mine, (row >> 8).astype(F32), 0.0).astype(BF16)
    low = jnp.where(mine, (row & 255).astype(F32), 0.0).astype(BF16)
    found = dot_nt(high, at_place) * 256.0 + dot_nt(low, at_place)
    req_ref[...] = found.astype(jnp.int32)


def lookup_kernel(cap, wanted_ref, table_ref, found_ref, ids_ref):
    owners, width = wanted_ref.shape
    slots = found_ref.shape[0]
    rows = table_ref.shape[0]
    wanted = wanted_ref[...]
    high = (wanted >> 8).astype(F32).astype(BF16)
    low = (wanted & 255).astype(F32).astype(BF16)
    slot = iota((slots, owners), 0).astype(F32)
    holder = jnp.floor((slot + 0.5) * (1.0 / cap))
    spread = hot(holder == iota((slots, owners), 1).astype(F32))
    ids = dot_nn(spread, high) * 256.0 + dot_nn(spread, low)
    slot = iota((slots, width), 0).astype(F32)
    place = slot - jnp.floor((slot + 0.5) * (1.0 / cap)) * float(cap)
    ids = jnp.sum(
        jnp.where(iota((slots, width), 1).astype(F32) == place, ids, 0.0), axis=1, keepdims=True
    )
    wide = jnp.broadcast_to(ids, (slots, LANES))
    ids_ref[...] = wide.T[0:1, :]
    step = 256 if slots % 256 == 0 else slots
    for start in range(0, slots, step):
        part = ids[start : start + step]
        pick = hot(iota((step, rows), 1).astype(F32) == part)
        found_ref[start : start + step, :] = dot_nn(pick, table_ref[...]).astype(BF16)


def collect_kernel(groups, *refs):
    ids_refs, in_hbms, out_hbm = refs[:groups], refs[groups : 2 * groups], refs[2 * groups]
    in_refs, out_ref, sems = refs[2 * groups + 1 : 3 * groups + 1], refs[-2], refs[-1]
    rows = out_ref.shape[0]
    slots = in_refs[0].shape[0]
    fetches = [
        pltpu.make_async_copy(hbm, ref, sems.at[n])
        for n, (hbm, ref) in enumerate(zip(in_hbms, in_refs))
    ]
    for fetch in fetches:
        fetch.start()
    base = lax.axis_index("group") * rows
    step = row_step(rows)
    for fetch in fetches:
        fetch.wait()
    stores = []
    for n, start in enumerate(range(0, rows, step)):
        own = (iota((step, slots), 0) + (base + start)).astype(F32)
        total = None
        for ids_ref, in_ref in zip(ids_refs, in_refs):
            part = dot_nn(hot(own == ids_ref[...]), in_ref[...])
            total = part if total is None else total + part
        out_ref[start : start + step, :] = total
        here = pl.ds(start, step)
        stores.append(
            pltpu.make_async_copy(out_ref.at[here], out_hbm.at[here], sems.at[groups + n])
        )
        stores[-1].start()
    for store in stores:
        store.wait()


def layer_kernel(
    groups,
    wparts,
    len_ref,
    slot_ref,
    ret_hbm,
    w_in_hbm,
    w_out_hbm,
    gain_ref,
    cot_hbm,
    *rest,
):
    result_hbm, row_hbm = rest[:2]
    grads_hbms = rest[2 : 2 + 2 * groups]
    (
    ret_ref,
    w_in_ref,
    w_out_ref,
    cot_ref,
    result_ref,
    row_ref,
    grads_ref,
    pick_ref,
    emb_ref,
    proj_ref,
    slope_ref,
    bias_ref,
    weight_ref,
    wslope_ref,
    att_ref,
    mixed_ref,
    gatt_ref,
    gpre_ref,
    gval_ref,
    gkey_ref,
    gwo_ref,
    sems,
    ) = rest[2 + 2 * groups :]
    count, width = cot_ref.shape
    slots = ret_hbm.shape[0]
    per = LANES // HEAD_DIM
    slabs = width // LANES
    qrows = QUERY_ROWS if count % QUERY_ROWS == 0 else count
    half_scale = 0.5 / math.sqrt(HEAD_DIM)

    get_ret = pltpu.make_async_copy(ret_hbm, ret_ref, sems.at[8 + 2 * groups])
    get_ret.start()
    parts = [pl.ds(i * width, width) for i in range(4)]
    get_ins = [
        pltpu.make_async_copy(w_in_hbm.at[:, part], w_in_ref.at[:, part], sems.at[i])
        for i, part in enumerate(parts)
    ]
    get_cot = pltpu.make_async_copy(cot_hbm, cot_ref, sems.at[4])
    get_out = pltpu.make_async_copy(w_out_hbm, w_out_ref, sems.at[5])
    for fetch in (*get_ins, get_cot, get_out):
        fetch.start()

    slot = jnp.broadcast_to(slot_ref[...], (LANES, count)).T
    for start in range(0, slots, LANES):
        pick_ref[:, start : start + LANES] = hot(
            slot == (iota((count, LANES), 1) + start).astype(F32)
        )
    get_ret.wait()
    emb_ref[...] = dot_nn(pick_ref[...], ret_ref[...]).astype(BF16)

    for i in range(4):
        get_ins[i].wait()
        pre = dot_nn(emb_ref[...], w_in_ref[:, parts[i]])
        half = 0.5 * pre
        th = jnp.tanh(half)
        act = half + half * th
        proj_ref[i] = act.astype(BF16)
        slope_ref[i] = 0.5 * ((1.0 + th) + act * (1.0 - th))

    pos = iota((count, 1), 0)
    begin = jnp.zeros((count, 1), jnp.int32)
    end = jnp.int32(0)
    for s in range(len_ref.shape[1]):
        end = end + len_ref[0, s]
        begin = jnp.where(pos >= end, end, begin)
    key = iota((count, count), 1)
    allowed = (key >= begin) & (key <= iota((count, count), 0))
    bias_ref[...] = jnp.where(allowed, 3.0e38, -30.0)

    lane = iota((qrows, LANES), 1)
    inside = [(lane >= a * HEAD_DIM) & (lane < (a + 1) * HEAD_DIM) for a in range(per)]
    lane = iota((count, LANES), 1)
    inside_all = [(lane >= a * HEAD_DIM) & (lane < (a + 1) * HEAD_DIM) for a in range(per)]

    def stacked(value, factor=1.0):
        value = value.astype(F32) * factor
        return jnp.concatenate([jnp.where(m, value, 0.0) for m in inside], 0).astype(BF16)

    row = iota((LANES, qrows), 0)
    inside_rows = [(row >= a * HEAD_DIM) & (row < (a + 1) * HEAD_DIM) for a in range(per)]

    def stacked_t(value, factor=1.0):
        value = (value.astype(F32) * factor).T
        return jnp.concatenate([jnp.where(m, value, 0.0) for m in inside_rows], 1).astype(BF16)

    def apart(value):
        value = value.astype(F32)
        return [jnp.where(m, value, 0.0).astype(BF16) for m in inside_all]

    def forward(p, _):
        cols = pl.ds(pl.multiple_of(p * LANES, LANES), LANES)
        key_all = proj_ref[3, :, cols]
        vals = apart(proj_ref[1, :, cols])
        for r0 in range(0, count, qrows):
            r1 = r0 + qrows
            half = dot_nt(stacked(proj_ref[2, r0:r1, cols], half_scale), key_all[:r1])
            half = jnp.minimum(half.reshape(per, qrows, r1), bias_ref[r0:r1, :r1][None])
            th = jnp.tanh(half)
            weight = half + half * th
            weight_b = weight.astype(BF16)
            base = per * r0
            weight_ref[p, base : base + per * qrows, :r1] = weight_b.reshape(per * qrows, r1)
            wslope_ref[p, base : base + per * qrows, :r1] = (
                (1.0 + th) + weight * (1.0 - th)
            ).reshape(per * qrows, r1)
            total = dot_nn(weight_b[0], vals[0][:r1])
            for a in range(1, per):
                total = total + dot_nn(weight_b[a], vals[a][:r1])
            att_ref[r0:r1, cols] = total
        return 0

    lax.fori_loop(0, slabs, forward, 0)

    get_cot.wait()
    get_out.wait()
    gain = gain_ref[...]
    gain_sum = jnp.zeros((1, width), F32)
    for r0 in range(0, count, qrows):
        rows = slice(r0, r0 + qrows)
        att = att_ref[rows, :]
        centered = att - jnp.mean(att, 1, keepdims=True)
        inv = lax.rsqrt(jnp.mean(centered * centered, 1, keepdims=True) + 1e-05)
        normed = centered * inv
        upd = proj_ref[0, rows, :].astype(F32)
        scaled = normed * gain
        mixed = (scaled * upd).astype(BF16)
        mixed_ref[rows, :] = mixed
        result_ref[rows, :] = (
            emb_ref[rows, :].astype(F32) + dot_nn(mixed, w_out_ref[...])
        ).astype(BF16)
        gmix = dot_nt(cot_ref[rows, :], w_out_ref[...]).astype(BF16).astype(F32)
        gpre_ref[rows, 0:width] = (gmix * scaled * slope_ref[0, rows, :]).astype(BF16)
        gnorm = gmix * gain * upd
        gain_sum = gain_sum + jnp.sum(gmix * normed * upd, 0, keepdims=True)
        mean1 = jnp.mean(gnorm, 1, keepdims=True)
        mean2 = jnp.mean(gnorm * normed, 1, keepdims=True)
        gatt_ref[rows, :] = ((gnorm - mean1 - normed * mean2) * inv).astype(BF16)
    put_result = pltpu.make_async_copy(result_ref, result_hbm, sems.at[6])
    put_result.start()
    gwo_ref[...] = dot_tn(mixed_ref[...], cot_ref[...]).astype(BF16)

    def backward(p, _):
        start = pl.multiple_of(p * LANES, LANES)
        cols = pl.ds(start, LANES)
        val = proj_ref[1, :, cols]
        keys = apart(proj_ref[3, :, cols])
        for r0 in reversed(range(0, count, qrows)):
            r1 = r0 + qrows
            base = per * r0
            rows = slice(base, base + per * qrows)
            gatt = stacked(gatt_ref[r0:r1, cols])
            gweight = dot_nt(gatt, val[:r1])
            gscore = (gweight * wslope_ref[p, rows, :r1]).astype(BF16)
            gqry = dot_nn(gscore[:qrows], keys[0][:r1])
            for a in range(1, per):
                gqry = gqry + dot_nn(gscore[a * qrows : (a + 1) * qrows], keys[a][:r1])
            gval = dot_nn(stacked_t(gatt_ref[r0:r1, cols]), weight_ref[p, rows, :r1])
            gkey = dot_nn(stacked_t(proj_ref[2, r0:r1, cols], half_scale), gscore)
            if r1 == count:
                gval_ref[...] = gval
                gkey_ref[...] = gkey
            else:
                gval_ref[:, :r1] += gval
                gkey_ref[:, :r1] += gkey
            gpre_ref[r0:r1, pl.ds(2 * width + start, LANES)] = (
                gqry * half_scale * slope_ref[2, r0:r1, cols]
            ).astype(BF16)
        gpre_ref[:, pl.ds(width + start, LANES)] = (gval_ref[...].T * slope_ref[1, :, cols]).astype(BF16)
        gpre_ref[:, pl.ds(3 * width + start, LANES)] = (gkey_ref[...].T * slope_ref[3, :, cols]).astype(BF16)
        return 0

    lax.fori_loop(0, slabs, backward, 0)

    puts = [put_result]
    me = lax.axis_index("group")
    emb_t = emb_ref[...].T
    cols_in = 4 * width // groups
    cols_out = width // wparts
    chunk = min(cols_in, 512)
    gain_col = jnp.broadcast_to(gain_sum, (LANES, width)).T.astype(BF16)
    for k in [*range(1, groups), 0]:
        part = lax.rem(me + k, groups)
        for c in range(0, cols_in, chunk):
            cols = pl.ds(pl.multiple_of(part * cols_in + c, LANES), chunk)
            grads_ref[k, :, c : c + chunk] = dot_nn(emb_t, gpre_ref[:, cols]).astype(BF16)
        cols = pl.ds(pl.multiple_of(lax.rem(part, wparts) * cols_out, LANES), cols_out)
        grads_ref[k, :, cols_in : cols_in + cols_out] = gwo_ref[:, cols]
        grads_ref[k, :, cols_in + cols_out :] = gain_col
        cut = grads_hbms[2 * k].shape[1]
        for i, cols in enumerate((pl.ds(0, cut), pl.ds(cut, grads_ref.shape[2] - cut))):
            put = pltpu.make_async_copy(
                grads_ref.at[k, :, cols], grads_hbms[2 * k + i], sems.at[8 + 2 * k + i]
            )
            put.start()
            puts.append(put)
    for i, r0 in enumerate((0, count // 2)):
        rows = pl.ds(r0, count // 2)
        row_ref[rows, :] = (
            cot_ref[rows, :].astype(F32) + dot_nt(gpre_ref[rows, :], w_in_ref[...])
        ).astype(BF16)
        sem = sems.at[7 + i * (2 + 2 * groups)]
        puts.append(pltpu.make_async_copy(row_ref.at[rows], row_hbm.at[rows], sem))
        puts[-1].start()
    for put in puts:
        put.wait()


def slots_kernel(slot_ref, grad_ref, out_hbm, out_ref, sems):
    count = grad_ref.shape[0]
    slots = out_ref.shape[0]
    step = row_step(slots)
    stores = []
    for n, start in enumerate(range(0, slots, step)):
        put = hot((iota((step, count), 0) + start).astype(F32) == slot_ref[...])
        out_ref[start : start + step, :] = dot_nn(put, grad_ref[...]).astype(BF16)
        here = pl.ds(start, step)
        stores.append(pltpu.make_async_copy(out_ref.at[here], out_hbm.at[here], sems.at[n]))
        stores[-1].start()
    for store in stores:
        store.wait()


def plane_kernel(outer, terms, *refs):
    left, right, outs = refs[:terms], refs[terms : 2 * terms], refs[2 * terms :]
    cut = left[0].shape[2]
    high = lax.div(lax.axis_index("table"), lax.axis_size("table") // outer)
    for k in range(outer):
        at = lax.rem(high + k, outer)
        for parts, cols in ((left, slice(0, cut)), (right, slice(cut, None))):
            total = parts[0][at].astype(F32)
            for part in parts[1:]:
                total = total + part[at].astype(F32)
            outs[k][:, cols] = total.astype(outs[k].dtype)


def finish_kernel(kept_ref, *refs):
    got_refs, (in_ref, out_ref, gain_ref) = refs[:-3], refs[-3:]
    total = kept_ref[...]
    for got_ref in got_refs:
        total = total + got_ref[...].astype(F32)
    cols_in, cols_out = in_ref.shape[1], out_ref.shape[1]
    in_ref[...] = total[:, :cols_in]
    out_ref[...] = total[:, cols_in : cols_in + cols_out]
    gain_ref[...] = total[:, cols_in + cols_out :].T[0:1, :]


def shift(value, axis, size, amount):
    return lax.ppermute(value, axis, [(i, (i + amount) % size) for i in range(size)])


def on_device(item_owner, item_row, lengths, table, w_in, w_out, gain, cotangent):
    owners = lax.axis_size("table")
    groups = lax.axis_size("group")
    count = item_row.shape[0]
    width = table.shape[1]
    capacity = max(2, 3 * count // (2 * owners))
    slots = owners * capacity
    padded = -(-capacity // LANES) * LANES
    me = lax.axis_index("group")

    requested, slot = call(
        functools.partial(request_kernel, capacity),
        [
            jax.ShapeDtypeStruct((owners, padded), jnp.int32),
            jax.ShapeDtypeStruct((1, count), F32),
        ],
        4 * count * count * owners,
        8 * count,
        (item_owner.reshape(1, count), item_row.reshape(1, count)),
    )
    wanted = lax.all_to_all(requested, "table", split_axis=0, concat_axis=0, tiled=True)
    found, ids = call(
        functools.partial(lookup_kernel, capacity),
        [
            jax.ShapeDtypeStruct((slots, width), BF16),
            jax.ShapeDtypeStruct((1, slots), F32),
        ],
        2 * slots * table.shape[0] * width,
        2 * (slots + table.shape[0]) * width,
        (wanted, table),
    )
    returned = lax.all_to_all(found, "table", split_axis=0, concat_axis=0, tiled=True)
    all_ids = [ids] + [shift(ids, "group", groups, k) for k in range(1, groups)]
    returned, *all_ids = lax.optimization_barrier((returned, *all_ids))

    wparts = min(groups, width // LANES)
    heads_per = LANES // HEAD_DIM
    cols_in = 4 * width // groups
    cols_out = width // wparts
    cols_all = cols_in + cols_out + LANES
    cut = cols_all // LANES // 2 * LANES
    square = pltpu.VMEM((count, width), BF16)
    result, row_grad, *grads = call(
        functools.partial(layer_kernel, groups, wparts),
        [
            jax.ShapeDtypeStruct((count, width), BF16),
            jax.ShapeDtypeStruct((count, width), BF16),
            *[
                jax.ShapeDtypeStruct((width, cols), BF16)
                for _ in range(groups)
                for cols in (cut, cols_all - cut)
            ],
        ],
        32 * count * width * width + 14 * count * count * width,
        24 * count * width,
        (lengths, slot, returned, w_in, w_out, gain.reshape(1, width), cotangent),
        smem=(0,),
        far=(2, 3, 4, 6),
        far_out=range(2 + 2 * groups),
        scratch=[
            pltpu.VMEM((slots, width), BF16),
            pltpu.VMEM(w_in.shape, BF16),
            pltpu.VMEM(w_out.shape, BF16),
            square,
            square,
            square,
            pltpu.VMEM((groups, width, cols_all), BF16),
            pltpu.VMEM((count, slots), BF16),
            square,
            pltpu.VMEM((4, count, width), BF16),
            pltpu.VMEM((4, count, width), F32),
            pltpu.VMEM((count, count), F32),
            pltpu.VMEM((width // LANES, heads_per * count, count), BF16),
            pltpu.VMEM((width // LANES, heads_per * count, count), F32),
            pltpu.VMEM((count, width), F32),
            square,
            square,
            pltpu.VMEM((count, 4 * width), BF16),
            pltpu.VMEM((LANES, count), F32),
            pltpu.VMEM((LANES, count), F32),
            pltpu.VMEM((width, width), BF16),
            pltpu.SemaphoreType.DMA((10 + 2 * groups,)),
        ],
    )
    rows = width // owners
    side = 2 if owners % 4 == 0 else 1
    plane = side * side
    outer = owners // plane
    here = lax.axis_index("table")
    high, middle, low = here // plane, here // side % side, here % side
    sides = []
    for i in range(2):
        terms = [grads[i]] + [shift(grads[2 * k + i], "group", groups, k) for k in range(1, groups)]
        sides.append([term.reshape(outer, side, side, rows, term.shape[1]) for term in terms])

    def entry(value, index, axis):
        return lax.dynamic_index_in_dim(value, index, axis, keepdims=False)

    def add(terms):
        return sum(term.astype(F32) for term in terms)

    def halve(terms, index, axis, bit, tie=None):
        send = add([entry(term, 1 - index, axis) for term in terms]).astype(BF16)
        if tie is not None:
            tie, send = lax.optimization_barrier((tie, send))
        got = lax.ppermute(send, "table", [(i, i ^ bit) for i in range(owners)])
        return [add([entry(term, index, axis) for term in terms]), got], tie

    if side == 2:
        left, row_grad = halve(sides[0], low, 2, 1, row_grad)
        right, row_grad = halve(sides[1], middle, 1, 2, row_grad)
        left, _ = halve(left, middle, 1, 2)
        right, _ = halve(right, low, 1, 1)
    else:
        left, right = [[term[:, 0, 0] for term in terms] for terms in sides]
    cols = cols_all
    kept, *sends = call(
        functools.partial(plane_kernel, outer, len(left)),
        [
            jax.ShapeDtypeStruct((rows, cols), F32),
            *[jax.ShapeDtypeStruct((rows, cols), BF16) for _ in range(1, outer)],
        ],
        12 * outer * rows * cols,
        8 * outer * rows * cols,
        (*left, *right),
        limit=24,
    )
    got = [
        lax.ppermute(
            sends[k - 1],
            "table",
            [(i, ((i // plane + k) % outer) * plane + i % plane) for i in range(owners)],
        )
        for k in range(1, outer)
    ]

    (outgoing,) = call(
        slots_kernel,
        [jax.ShapeDtypeStruct((slots, width), BF16)],
        2 * slots * count * width,
        4 * count * width,
        (slot, row_grad),
        far_out=(0,),
        scratch=[
            pltpu.VMEM((slots, width), BF16),
            pltpu.SemaphoreType.DMA((slots // row_step(slots),)),
        ],
    )
    incoming = lax.all_to_all(outgoing, "table", split_axis=0, concat_axis=0, tiled=True)
    incoming, *got = lax.optimization_barrier((incoming, *got))
    all_incoming = [incoming] + [shift(incoming, "group", groups, k) for k in range(1, groups)]
    grad_rows = table.shape[0] // groups
    (table_grad,) = call(
        functools.partial(collect_kernel, groups),
        [jax.ShapeDtypeStruct((grad_rows, width), F32)],
        2 * slots * table.shape[0] * width,
        2 * groups * slots * width + 4 * grad_rows * width,
        (*all_ids, *all_incoming),
        far=range(groups, 2 * groups),
        far_out=(0,),
        limit=24,
        scratch=[
            *[pltpu.VMEM((slots, width), BF16) for _ in range(groups)],
            pltpu.VMEM((grad_rows, width), F32),
            pltpu.SemaphoreType.DMA((groups + grad_rows // row_step(grad_rows),)),
        ],
    )

    w_in_grad, mine, gain_grad = call(
        finish_kernel,
        [
            jax.ShapeDtypeStruct((rows, cols_in), F32),
            jax.ShapeDtypeStruct((rows, cols_out), F32),
            jax.ShapeDtypeStruct((1, rows), F32),
        ],
        4 * rows * cols_all,
        14 * rows * cols_all,
        (kept, *got),
        limit=24,
    )
    pieces = jnp.stack([mine] + [shift(mine, "group", groups, k) for k in range(1, groups)])
    w_out_grad = jnp.concatenate(
        [
            lax.dynamic_index_in_dim(pieces, (me - p) % groups, 0, keepdims=False)
            for p in range(wparts)
        ],
        1,
    )
    return (result, table_grad, w_in_grad, w_out_grad, gain_grad.reshape(rows))


def solution(mesh):
    return jax.shard_map(
        on_device,
        mesh=mesh,
        in_specs=(
            P(("table", "group"), None),
            P(("table", "group")),
            P(("table", "group"), None),
            P("table", None),
            P(),
            P(),
            P(),
            P(("table", "group"), None),
        ),
        out_specs=(
            P(("table", "group"), None),
            P(("table", "group"), None),
            P("table", "group"),
            P("table", None),
            P("table"),
        ),
        check_vma=False,
    )
```

```python
import functools
import math

import jax
import jax.numpy as jnp
from jax import lax
from jax.experimental import pallas as pl
from jax.experimental.pallas import tpu as pltpu
from jax.sharding import PartitionSpec as P

HEAD_DIM = 64
LANES = 128
QUERY_ROWS = 128

F32 = jnp.float32
BF16 = jnp.bfloat16


def iota(shape, dim):
    return lax.broadcasted_iota(jnp.int32, shape, dim)


def hot(cond):
    return jnp.where(cond, 1.0, 0.0).astype(BF16)


def dot_nn(a, b):
    return lax.dot_general(a, b, (((1,), (0,)), ((), ())), preferred_element_type=F32)


def dot_nt(a, b):
    return lax.dot_general(a, b, (((1,), (1,)), ((), ())), preferred_element_type=F32)


def dot_tn(a, b):
    return lax.dot_general(a, b, (((0,), (0,)), ((), ())), preferred_element_type=F32)


def row_step(rows):
    return 256 if rows % 256 == 0 else rows


def call(kernel, out_shape, flops, nbytes, operands, smem=(), far=(), far_out=(), limit=56, scratch=()):
    spaces = [
        pltpu.SMEM if i in smem else pl.ANY if i in far else pltpu.VMEM
        for i in range(len(operands))
    ]
    out_spaces = [pl.ANY if i in far_out else pltpu.VMEM for i in range(len(out_shape))]
    return pl.pallas_call(
        kernel,
        out_shape=out_shape,
        in_specs=[pl.BlockSpec(memory_space=space) for space in spaces],
        out_specs=[pl.BlockSpec(memory_space=space) for space in out_spaces],
        scratch_shapes=scratch,
        compiler_params=pltpu.CompilerParams(vmem_limit_bytes=limit * 1024 * 1024),
        cost_estimate=pl.CostEstimate(flops=flops, bytes_accessed=nbytes, transcendentals=0),
    )(*operands)


def request_kernel(cap, owner_ref, row_ref, req_ref, slot_ref):
    owners, width = req_ref.shape
    count = owner_ref.shape[1]
    owner = owner_ref[...]
    row = row_ref[...]
    mine = iota((owners, count), 0) == owner
    mine_b = hot(mine)
    before = hot(iota((count, count), 0) < iota((count, count), 1))
    earlier = dot_nn(mine_b, before)
    place = jnp.sum(jnp.where(mine, earlier, 0.0), axis=0, keepdims=True)
    slot_ref[...] = owner.astype(F32) * float(cap) + place
    at_place = hot(iota((width, count), 0).astype(F32) == place)
    high = jnp.where(mine, (row >> 8).astype(F32), 0.0).astype(BF16)
    low = jnp.where(mine, (row & 255).astype(F32), 0.0).astype(BF16)
    found = dot_nt(high, at_place) * 256.0 + dot_nt(low, at_place)
    req_ref[...] = found.astype(jnp.int32)


def lookup_kernel(cap, wanted_ref, table_ref, found_ref, ids_ref):
    owners, width = wanted_ref.shape
    slots = found_ref.shape[0]
    rows = table_ref.shape[0]
    wanted = wanted_ref[...]
    high = (wanted >> 8).astype(F32).astype(BF16)
    low = (wanted & 255).astype(F32).astype(BF16)
    slot = iota((slots, owners), 0).astype(F32)
    holder = jnp.floor((slot + 0.5) * (1.0 / cap))
    spread = hot(holder == iota((slots, owners), 1).astype(F32))
    ids = dot_nn(spread, high) * 256.0 + dot_nn(spread, low)
    slot = iota((slots, width), 0).astype(F32)
    place = slot - jnp.floor((slot + 0.5) * (1.0 / cap)) * float(cap)
    ids = jnp.sum(
        jnp.where(iota((slots, width), 1).astype(F32) == place, ids, 0.0), axis=1, keepdims=True
    )
    wide = jnp.broadcast_to(ids, (slots, LANES))
    ids_ref[...] = wide.T[0:1, :]
    step = 256 if slots % 256 == 0 else slots
    for start in range(0, slots, step):
        part = ids[start : start + step]
        pick = hot(iota((step, rows), 1).astype(F32) == part)
        found_ref[start : start + step, :] = dot_nn(pick, table_ref[...]).astype(BF16)


def collect_kernel(groups, *refs):
    ids_refs, in_hbms, out_hbm = refs[:groups], refs[groups : 2 * groups], refs[2 * groups]
    in_refs, out_ref, sems = refs[2 * groups + 1 : 3 * groups + 1], refs[-2], refs[-1]
    rows = out_ref.shape[0]
    slots = in_refs[0].shape[0]
    fetches = [
        pltpu.make_async_copy(hbm, ref, sems.at[n])
        for n, (hbm, ref) in enumerate(zip(in_hbms, in_refs))
    ]
    for fetch in fetches:
        fetch.start()
    base = lax.axis_index("group") * rows
    step = row_step(rows)
    for fetch in fetches:
        fetch.wait()
    stores = []
    for n, start in enumerate(range(0, rows, step)):
        own = (iota((step, slots), 0) + (base + start)).astype(F32)
        total = None
        for ids_ref, in_ref in zip(ids_refs, in_refs):
            part = dot_nn(hot(own == ids_ref[...]), in_ref[...])
            total = part if total is None else total + part
        out_ref[start : start + step, :] = total
        here = pl.ds(start, step)
        stores.append(
            pltpu.make_async_copy(out_ref.at[here], out_hbm.at[here], sems.at[groups + n])
        )
        stores[-1].start()
    for store in stores:
        store.wait()


def layer_kernel(
    groups,
    wparts,
    len_ref,
    slot_ref,
    ret_hbm,
    w_in_hbm,
    w_out_hbm,
    gain_ref,
    cot_hbm,
    *rest,
):
    result_hbm, row_hbm = rest[:2]
    grads_hbms = rest[2 : 2 + 2 * groups]
    (
    ret_ref,
    w_in_ref,
    w_out_ref,
    cot_ref,
    result_ref,
    row_ref,
    grads_ref,
    pick_ref,
    emb_ref,
    proj_ref,
    slope_ref,
    bias_ref,
    weight_ref,
    wslope_ref,
    att_ref,
    mixed_ref,
    gatt_ref,
    gpre_ref,
    gval_ref,
    gkey_ref,
    gwo_ref,
    sems,
    ) = rest[2 + 2 * groups :]
    count, width = cot_ref.shape
    slots = ret_hbm.shape[0]
    per = LANES // HEAD_DIM
    slabs = width // LANES
    qrows = QUERY_ROWS if count % QUERY_ROWS == 0 else count
    half_scale = 0.5 / math.sqrt(HEAD_DIM)

    get_ret = pltpu.make_async_copy(ret_hbm, ret_ref, sems.at[8 + 2 * groups])
    get_ret.start()
    parts = [pl.ds(i * width, width) for i in range(4)]
    get_ins = [
        pltpu.make_async_copy(w_in_hbm.at[:, part], w_in_ref.at[:, part], sems.at[i])
        for i, part in enumerate(parts)
    ]
    get_cot = pltpu.make_async_copy(cot_hbm, cot_ref, sems.at[4])
    get_out = pltpu.make_async_copy(w_out_hbm, w_out_ref, sems.at[5])
    for fetch in (*get_ins, get_cot, get_out):
        fetch.start()

    slot = jnp.broadcast_to(slot_ref[...], (LANES, count)).T
    for start in range(0, slots, LANES):
        pick_ref[:, start : start + LANES] = hot(
            slot == (iota((count, LANES), 1) + start).astype(F32)
        )
    get_ret.wait()
    emb_ref[...] = dot_nn(pick_ref[...], ret_ref[...]).astype(BF16)

    for i in range(4):
        get_ins[i].wait()
        pre = dot_nn(emb_ref[...], w_in_ref[:, parts[i]])
        half = 0.5 * pre
        th = jnp.tanh(half)
        act = half + half * th
        proj_ref[i] = act.astype(BF16)
        slope_ref[i] = 0.5 * ((1.0 + th) + act * (1.0 - th))

    pos = iota((count, 1), 0)
    begin = jnp.zeros((count, 1), jnp.int32)
    end = jnp.int32(0)
    for s in range(len_ref.shape[1]):
        end = end + len_ref[0, s]
        begin = jnp.where(pos >= end, end, begin)
    key = iota((count, count), 1)
    allowed = (key >= begin) & (key <= iota((count, count), 0))
    bias_ref[...] = jnp.where(allowed, 3.0e38, -30.0)

    lane = iota((qrows, LANES), 1)
    inside = [(lane >= a * HEAD_DIM) & (lane < (a + 1) * HEAD_DIM) for a in range(per)]
    lane = iota((count, LANES), 1)
    inside_all = [(lane >= a * HEAD_DIM) & (lane < (a + 1) * HEAD_DIM) for a in range(per)]

    def stacked(value, factor=1.0):
        value = value.astype(F32) * factor
        return jnp.concatenate([jnp.where(m, value, 0.0) for m in inside], 0).astype(BF16)

    row = iota((LANES, qrows), 0)
    inside_rows = [(row >= a * HEAD_DIM) & (row < (a + 1) * HEAD_DIM) for a in range(per)]

    def stacked_t(value, factor=1.0):
        value = (value.astype(F32) * factor).T
        return jnp.concatenate([jnp.where(m, value, 0.0) for m in inside_rows], 1).astype(BF16)

    def apart(value):
        value = value.astype(F32)
        return [jnp.where(m, value, 0.0).astype(BF16) for m in inside_all]

    def forward(p, _):
        cols = pl.ds(pl.multiple_of(p * LANES, LANES), LANES)
        key_all = proj_ref[3, :, cols]
        vals = apart(proj_ref[1, :, cols])
        for r0 in range(0, count, qrows):
            r1 = r0 + qrows
            half = dot_nt(stacked(proj_ref[2, r0:r1, cols], half_scale), key_all[:r1])
            half = jnp.minimum(half.reshape(per, qrows, r1), bias_ref[r0:r1, :r1][None])
            th = jnp.tanh(half)
            weight = half + half * th
            weight_b = weight.astype(BF16)
            base = per * r0
            weight_ref[p, base : base + per * qrows, :r1] = weight_b.reshape(per * qrows, r1)
            wslope_ref[p, base : base + per * qrows, :r1] = (
                (1.0 + th) + weight * (1.0 - th)
            ).reshape(per * qrows, r1)
            total = dot_nn(weight_b[0], vals[0][:r1])
            for a in range(1, per):
                total = total + dot_nn(weight_b[a], vals[a][:r1])
            att_ref[r0:r1, cols] = total
        return 0

    lax.fori_loop(0, slabs, forward, 0)

    get_cot.wait()
    get_out.wait()
    gain = gain_ref[...]
    gain_sum = jnp.zeros((1, width), F32)
    for r0 in range(0, count, qrows):
        rows = slice(r0, r0 + qrows)
        att = att_ref[rows, :]
        centered = att - jnp.mean(att, 1, keepdims=True)
        inv = lax.rsqrt(jnp.mean(centered * centered, 1, keepdims=True) + 1e-05)
        normed = centered * inv
        upd = proj_ref[0, rows, :].astype(F32)
        scaled = normed * gain
        mixed = (scaled * upd).astype(BF16)
        mixed_ref[rows, :] = mixed
        result_ref[rows, :] = (
            emb_ref[rows, :].astype(F32) + dot_nn(mixed, w_out_ref[...])
        ).astype(BF16)
        gmix = dot_nt(cot_ref[rows, :], w_out_ref[...]).astype(BF16).astype(F32)
        gpre_ref[rows, 0:width] = (gmix * scaled * slope_ref[0, rows, :]).astype(BF16)
        gnorm = gmix * gain * upd
        gain_sum = gain_sum + jnp.sum(gmix * normed * upd, 0, keepdims=True)
        mean1 = jnp.mean(gnorm, 1, keepdims=True)
        mean2 = jnp.mean(gnorm * normed, 1, keepdims=True)
        gatt_ref[rows, :] = ((gnorm - mean1 - normed * mean2) * inv).astype(BF16)
    put_result = pltpu.make_async_copy(result_ref, result_hbm, sems.at[6])
    put_result.start()
    gwo_ref[...] = dot_tn(mixed_ref[...], cot_ref[...]).astype(BF16)

    def backward(p, _):
        start = pl.multiple_of(p * LANES, LANES)
        cols = pl.ds(start, LANES)
        val = proj_ref[1, :, cols]
        keys = apart(proj_ref[3, :, cols])
        for r0 in reversed(range(0, count, qrows)):
            r1 = r0 + qrows
            base = per * r0
            rows = slice(base, base + per * qrows)
            gatt = stacked(gatt_ref[r0:r1, cols])
            gweight = dot_nt(gatt, val[:r1])
            gscore = (gweight * wslope_ref[p, rows, :r1]).astype(BF16)
            gqry = dot_nn(gscore[:qrows], keys[0][:r1])
            for a in range(1, per):
                gqry = gqry + dot_nn(gscore[a * qrows : (a + 1) * qrows], keys[a][:r1])
            gval = dot_nn(stacked_t(gatt_ref[r0:r1, cols]), weight_ref[p, rows, :r1])
            gkey = dot_nn(stacked_t(proj_ref[2, r0:r1, cols], half_scale), gscore)
            if r1 == count:
                gval_ref[...] = gval
                gkey_ref[...] = gkey
            else:
                gval_ref[:, :r1] += gval
                gkey_ref[:, :r1] += gkey
            gpre_ref[r0:r1, pl.ds(2 * width + start, LANES)] = (
                gqry * half_scale * slope_ref[2, r0:r1, cols]
            ).astype(BF16)
        gpre_ref[:, pl.ds(width + start, LANES)] = (gval_ref[...].T * slope_ref[1, :, cols]).astype(BF16)
        gpre_ref[:, pl.ds(3 * width + start, LANES)] = (gkey_ref[...].T * slope_ref[3, :, cols]).astype(BF16)
        return 0

    lax.fori_loop(0, slabs, backward, 0)

    puts = [put_result]
    me = lax.axis_index("group")
    emb_t = emb_ref[...].T
    cols_in = 4 * width // groups
    cols_out = width // wparts
    chunk = min(cols_in, 512)
    gain_col = jnp.broadcast_to(gain_sum, (LANES, width)).T.astype(BF16)
    for k in [*range(1, groups), 0]:
        part = lax.rem(me + k, groups)
        for c in range(0, cols_in, chunk):
            cols = pl.ds(pl.multiple_of(part * cols_in + c, LANES), chunk)
            grads_ref[k, :, c : c + chunk] = dot_nn(emb_t, gpre_ref[:, cols]).astype(BF16)
        cols = pl.ds(pl.multiple_of(lax.rem(part, wparts) * cols_out, LANES), cols_out)
        grads_ref[k, :, cols_in : cols_in + cols_out] = gwo_ref[:, cols]
        grads_ref[k, :, cols_in + cols_out :] = gain_col
        cut = grads_hbms[2 * k].shape[1]
        for i, cols in enumerate((pl.ds(0, cut), pl.ds(cut, grads_ref.shape[2] - cut))):
            put = pltpu.make_async_copy(
                grads_ref.at[k, :, cols], grads_hbms[2 * k + i], sems.at[8 + 2 * k + i]
            )
            put.start()
            puts.append(put)
    for i, r0 in enumerate((0, count // 2)):
        rows = pl.ds(r0, count // 2)
        row_ref[rows, :] = (
            cot_ref[rows, :].astype(F32) + dot_nt(gpre_ref[rows, :], w_in_ref[...])
        ).astype(BF16)
        sem = sems.at[7 + i * (2 + 2 * groups)]
        puts.append(pltpu.make_async_copy(row_ref.at[rows], row_hbm.at[rows], sem))
        puts[-1].start()
    for put in puts:
        put.wait()


def slots_kernel(slot_ref, grad_ref, out_hbm, out_ref, sems):
    count = grad_ref.shape[0]
    slots = out_ref.shape[0]
    step = row_step(slots)
    stores = []
    for n, start in enumerate(range(0, slots, step)):
        put = hot((iota((step, count), 0) + start).astype(F32) == slot_ref[...])
        out_ref[start : start + step, :] = dot_nn(put, grad_ref[...]).astype(BF16)
        here = pl.ds(start, step)
        stores.append(pltpu.make_async_copy(out_ref.at[here], out_hbm.at[here], sems.at[n]))
        stores[-1].start()
    for store in stores:
        store.wait()


def plane_kernel(outer, terms, *refs):
    left, right, outs = refs[:terms], refs[terms : 2 * terms], refs[2 * terms :]
    cut = left[0].shape[2]
    high = lax.div(lax.axis_index("table"), lax.axis_size("table") // outer)
    for k in range(outer):
        at = lax.rem(high + k, outer)
        for parts, cols in ((left, slice(0, cut)), (right, slice(cut, None))):
            total = parts[0][at].astype(F32)
            for part in parts[1:]:
                total = total + part[at].astype(F32)
            outs[k][:, cols] = total.astype(outs[k].dtype)


def finish_kernel(kept_ref, *refs):
    got_refs, (in_ref, out_ref, gain_ref) = refs[:-3], refs[-3:]
    total = kept_ref[...]
    for got_ref in got_refs:
        total = total + got_ref[...].astype(F32)
    cols_in, cols_out = in_ref.shape[1], out_ref.shape[1]
    in_ref[...] = total[:, :cols_in]
    out_ref[...] = total[:, cols_in : cols_in + cols_out]
    gain_ref[...] = total[:, cols_in + cols_out :].T[0:1, :]


def shift(value, axis, size, amount):
    return lax.ppermute(value, axis, [(i, (i + amount) % size) for i in range(size)])


def on_device(item_owner, item_row, lengths, table, w_in, w_out, gain, cotangent):
    owners = lax.axis_size("table")
    groups = lax.axis_size("group")
    count = item_row.shape[0]
    width = table.shape[1]
    capacity = max(2, 3 * count // (2 * owners))
    slots = owners * capacity
    padded = -(-capacity // LANES) * LANES
    me = lax.axis_index("group")

    requested, slot = call(
        functools.partial(request_kernel, capacity),
        [
            jax.ShapeDtypeStruct((owners, padded), jnp.int32),
            jax.ShapeDtypeStruct((1, count), F32),
        ],
        4 * count * count * owners,
        8 * count,
        (item_owner.reshape(1, count), item_row.reshape(1, count)),
    )
    wanted = lax.all_to_all(requested, "table", split_axis=0, concat_axis=0, tiled=True)
    found, ids = call(
        functools.partial(lookup_kernel, capacity),
        [
            jax.ShapeDtypeStruct((slots, width), BF16),
            jax.ShapeDtypeStruct((1, slots), F32),
        ],
        2 * slots * table.shape[0] * width,
        2 * (slots + table.shape[0]) * width,
        (wanted, table),
    )
    returned = lax.all_to_all(found, "table", split_axis=0, concat_axis=0, tiled=True)
    all_ids = [ids] + [shift(ids, "group", groups, k) for k in range(1, groups)]
    returned, *all_ids = lax.optimization_barrier((returned, *all_ids))

    wparts = min(groups, width // LANES)
    heads_per = LANES // HEAD_DIM
    cols_in = 4 * width // groups
    cols_out = width // wparts
    cols_all = cols_in + cols_out + LANES
    cut = cols_all // LANES // 2 * LANES
    square = pltpu.VMEM((count, width), BF16)
    result, row_grad, *grads = call(
        functools.partial(layer_kernel, groups, wparts),
        [
            jax.ShapeDtypeStruct((count, width), BF16),
            jax.ShapeDtypeStruct((count, width), BF16),
            *[
                jax.ShapeDtypeStruct((width, cols), BF16)
                for _ in range(groups)
                for cols in (cut, cols_all - cut)
            ],
        ],
        32 * count * width * width + 14 * count * count * width,
        24 * count * width,
        (lengths, slot, returned, w_in, w_out, gain.reshape(1, width), cotangent),
        smem=(0,),
        far=(2, 3, 4, 6),
        far_out=range(2 + 2 * groups),
        scratch=[
            pltpu.VMEM((slots, width), BF16),
            pltpu.VMEM(w_in.shape, BF16),
            pltpu.VMEM(w_out.shape, BF16),
            square,
            square,
            square,
            pltpu.VMEM((groups, width, cols_all), BF16),
            pltpu.VMEM((count, slots), BF16),
            square,
            pltpu.VMEM((4, count, width), BF16),
            pltpu.VMEM((4, count, width), F32),
            pltpu.VMEM((count, count), F32),
            pltpu.VMEM((width // LANES, heads_per * count, count), BF16),
            pltpu.VMEM((width // LANES, heads_per * count, count), F32),
            pltpu.VMEM((count, width), F32),
            square,
            square,
            pltpu.VMEM((count, 4 * width), BF16),
            pltpu.VMEM((LANES, count), F32),
            pltpu.VMEM((LANES, count), F32),
            pltpu.VMEM((width, width), BF16),
            pltpu.SemaphoreType.DMA((10 + 2 * groups,)),
        ],
    )
    rows = width // owners
    side = 2 if owners % 4 == 0 else 1
    plane = side * side
    outer = owners // plane
    here = lax.axis_index("table")
    high, middle, low = here // plane, here // side % side, here % side
    sides = []
    for i in range(2):
        terms = [grads[i]] + [shift(grads[2 * k + i], "group", groups, k) for k in range(1, groups)]
        sides.append([term.reshape(outer, side, side, rows, term.shape[1]) for term in terms])

    def entry(value, index, axis):
        return lax.dynamic_index_in_dim(value, index, axis, keepdims=False)

    def add(terms):
        return sum(term.astype(F32) for term in terms)

    def halve(terms, index, axis, bit, tie=None):
        send = add([entry(term, 1 - index, axis) for term in terms]).astype(BF16)
        if tie is not None:
            tie, send = lax.optimization_barrier((tie, send))
        got = lax.ppermute(send, "table", [(i, i ^ bit) for i in range(owners)])
        kept = [entry(term, index, axis) for term in terms]
        return (kept if tie is not None else [add(kept)]) + [got], tie

    if side == 2:
        left, row_grad = halve(sides[0], low, 2, 1, row_grad)
        right, row_grad = halve(sides[1], middle, 1, 2, row_grad)
        left, _ = halve(left, middle, 1, 2)
        right, _ = halve(right, low, 1, 1)
    else:
        left, right = [[term[:, 0, 0] for term in terms] for terms in sides]
    cols = cols_all
    kept, *sends = call(
        functools.partial(plane_kernel, outer, len(left)),
        [
            jax.ShapeDtypeStruct((rows, cols), F32),
            *[jax.ShapeDtypeStruct((rows, cols), BF16) for _ in range(1, outer)],
        ],
        12 * outer * rows * cols,
        8 * outer * rows * cols,
        (*left, *right),
        limit=24,
    )
    got = [
        lax.ppermute(
            sends[k - 1],
            "table",
            [(i, ((i // plane + k) % outer) * plane + i % plane) for i in range(owners)],
        )
        for k in range(1, outer)
    ]

    (outgoing,) = call(
        slots_kernel,
        [jax.ShapeDtypeStruct((slots, width), BF16)],
        2 * slots * count * width,
        4 * count * width,
        (slot, row_grad),
        far_out=(0,),
        scratch=[
            pltpu.VMEM((slots, width), BF16),
            pltpu.SemaphoreType.DMA((slots // row_step(slots),)),
        ],
    )
    incoming = lax.all_to_all(outgoing, "table", split_axis=0, concat_axis=0, tiled=True)
    incoming, *got = lax.optimization_barrier((incoming, *got))
    all_incoming = [incoming] + [shift(incoming, "group", groups, k) for k in range(1, groups)]
    grad_rows = table.shape[0] // groups
    (table_grad,) = call(
        functools.partial(collect_kernel, groups),
        [jax.ShapeDtypeStruct((grad_rows, width), F32)],
        2 * slots * table.shape[0] * width,
        2 * groups * slots * width + 4 * grad_rows * width,
        (*all_ids, *all_incoming),
        far=range(groups, 2 * groups),
        far_out=(0,),
        limit=24,
        scratch=[
            *[pltpu.VMEM((slots, width), BF16) for _ in range(groups)],
            pltpu.VMEM((grad_rows, width), F32),
            pltpu.SemaphoreType.DMA((groups + grad_rows // row_step(grad_rows),)),
        ],
    )

    w_in_grad, mine, gain_grad = call(
        finish_kernel,
        [
            jax.ShapeDtypeStruct((rows, cols_in), F32),
            jax.ShapeDtypeStruct((rows, cols_out), F32),
            jax.ShapeDtypeStruct((1, rows), F32),
        ],
        4 * rows * cols_all,
        14 * rows * cols_all,
        (kept, *got),
        limit=24,
    )
    pieces = jnp.stack([mine] + [shift(mine, "group", groups, k) for k in range(1, groups)])
    w_out_grad = jnp.concatenate(
        [
            lax.dynamic_index_in_dim(pieces, (me - p) % groups, 0, keepdims=False)
            for p in range(wparts)
        ],
        1,
    )
    return (result, table_grad, w_in_grad, w_out_grad, gain_grad.reshape(rows))


def solution(mesh):
    return jax.shard_map(
        on_device,
        mesh=mesh,
        in_specs=(
            P(("table", "group"), None),
            P(("table", "group")),
            P(("table", "group"), None),
            P("table", None),
            P(),
            P(),
            P(),
            P(("table", "group"), None),
        ),
        out_specs=(
            P(("table", "group"), None),
            P(("table", "group"), None),
            P("table", "group"),
            P("table", None),
            P("table"),
        ),
        check_vma=False,
    )
```

```python
import functools
import math

import jax
import jax.numpy as jnp
from jax import lax
from jax.experimental import pallas as pl
from jax.experimental.pallas import tpu as pltpu
from jax.sharding import PartitionSpec as P

HEAD_DIM = 64
LANES = 128
QUERY_ROWS = 256

F32 = jnp.float32
BF16 = jnp.bfloat16


def iota(shape, dim):
    return lax.broadcasted_iota(jnp.int32, shape, dim)


def hot(cond):
    return jnp.where(cond, 1.0, 0.0).astype(BF16)


def dot_nn(a, b):
    return lax.dot_general(a, b, (((1,), (0,)), ((), ())), preferred_element_type=F32)


def dot_nt(a, b):
    return lax.dot_general(a, b, (((1,), (1,)), ((), ())), preferred_element_type=F32)


def dot_tn(a, b):
    return lax.dot_general(a, b, (((0,), (0,)), ((), ())), preferred_element_type=F32)


def row_step(rows):
    return 256 if rows % 256 == 0 else rows


def call(kernel, out_shape, flops, nbytes, operands, smem=(), far=(), far_out=(), limit=56, scratch=()):
    spaces = [
        pltpu.SMEM if i in smem else pl.ANY if i in far else pltpu.VMEM
        for i in range(len(operands))
    ]
    out_spaces = [pl.ANY if i in far_out else pltpu.VMEM for i in range(len(out_shape))]
    return pl.pallas_call(
        kernel,
        out_shape=out_shape,
        in_specs=[pl.BlockSpec(memory_space=space) for space in spaces],
        out_specs=[pl.BlockSpec(memory_space=space) for space in out_spaces],
        scratch_shapes=scratch,
        compiler_params=pltpu.CompilerParams(vmem_limit_bytes=limit * 1024 * 1024),
        cost_estimate=pl.CostEstimate(flops=flops, bytes_accessed=nbytes, transcendentals=0),
    )(*operands)


def request_kernel(cap, owner_ref, row_ref, req_ref, slot_ref):
    owners, width = req_ref.shape
    count = owner_ref.shape[1]
    owner = owner_ref[...]
    row = row_ref[...]
    mine = iota((owners, count), 0) == owner
    mine_b = hot(mine)
    before = hot(iota((count, count), 0) < iota((count, count), 1))
    earlier = dot_nn(mine_b, before)
    place = jnp.sum(jnp.where(mine, earlier, 0.0), axis=0, keepdims=True)
    slot_ref[...] = owner.astype(F32) * float(cap) + place
    at_place = hot(iota((width, count), 0).astype(F32) == place)
    high = jnp.where(mine, (row >> 8).astype(F32), 0.0).astype(BF16)
    low = jnp.where(mine, (row & 255).astype(F32), 0.0).astype(BF16)
    found = dot_nt(high, at_place) * 256.0 + dot_nt(low, at_place)
    req_ref[...] = found.astype(jnp.int32)


def lookup_kernel(cap, wanted_ref, table_ref, found_ref, ids_ref):
    owners, width = wanted_ref.shape
    slots = found_ref.shape[0]
    rows = table_ref.shape[0]
    wanted = wanted_ref[...]
    high = (wanted >> 8).astype(F32).astype(BF16)
    low = (wanted & 255).astype(F32).astype(BF16)
    slot = iota((slots, owners), 0).astype(F32)
    holder = jnp.floor((slot + 0.5) * (1.0 / cap))
    spread = hot(holder == iota((slots, owners), 1).astype(F32))
    ids = dot_nn(spread, high) * 256.0 + dot_nn(spread, low)
    slot = iota((slots, width), 0).astype(F32)
    place = slot - jnp.floor((slot + 0.5) * (1.0 / cap)) * float(cap)
    ids = jnp.sum(
        jnp.where(iota((slots, width), 1).astype(F32) == place, ids, 0.0), axis=1, keepdims=True
    )
    wide = jnp.broadcast_to(ids, (slots, LANES))
    ids_ref[...] = wide.T[0:1, :]
    step = 256 if slots % 256 == 0 else slots
    for start in range(0, slots, step):
        part = ids[start : start + step]
        pick = hot(iota((step, rows), 1).astype(F32) == part)
        found_ref[start : start + step, :] = dot_nn(pick, table_ref[...]).astype(BF16)


def collect_kernel(groups, *refs):
    ids_refs, in_hbms, out_hbm = refs[:groups], refs[groups : 2 * groups], refs[2 * groups]
    in_refs, out_ref, sems = refs[2 * groups + 1 : 3 * groups + 1], refs[-2], refs[-1]
    rows = out_ref.shape[0]
    slots = in_refs[0].shape[0]
    fetches = [
        pltpu.make_async_copy(hbm, ref, sems.at[n])
        for n, (hbm, ref) in enumerate(zip(in_hbms, in_refs))
    ]
    for fetch in fetches:
        fetch.start()
    base = lax.axis_index("group") * rows
    step = row_step(rows)
    for fetch in fetches:
        fetch.wait()
    stores = []
    for n, start in enumerate(range(0, rows, step)):
        own = (iota((step, slots), 0) + (base + start)).astype(F32)
        total = None
        for ids_ref, in_ref in zip(ids_refs, in_refs):
            part = dot_nn(hot(own == ids_ref[...]), in_ref[...])
            total = part if total is None else total + part
        out_ref[start : start + step, :] = total
        here = pl.ds(start, step)
        stores.append(
            pltpu.make_async_copy(out_ref.at[here], out_hbm.at[here], sems.at[groups + n])
        )
        stores[-1].start()
    for store in stores:
        store.wait()


def layer_kernel(
    groups,
    wparts,
    len_ref,
    slot_ref,
    ret_hbm,
    w_in_hbm,
    w_out_hbm,
    gain_ref,
    cot_hbm,
    *rest,
):
    result_hbm, row_hbm = rest[:2]
    grads_hbms = rest[2 : 2 + 2 * groups]
    (
    ret_ref,
    w_in_ref,
    w_out_ref,
    cot_ref,
    result_ref,
    row_ref,
    grads_ref,
    pick_ref,
    emb_ref,
    proj_ref,
    slope_ref,
    bias_ref,
    weight_ref,
    wslope_ref,
    att_ref,
    mixed_ref,
    gatt_ref,
    gpre_ref,
    gval_ref,
    gkey_ref,
    gwo_ref,
    sems,
    ) = rest[2 + 2 * groups :]
    count, width = cot_ref.shape
    slots = ret_hbm.shape[0]
    per = LANES // HEAD_DIM
    slabs = width // LANES
    qrows = QUERY_ROWS if count % QUERY_ROWS == 0 else count
    half_scale = 0.5 / math.sqrt(HEAD_DIM)

    get_ret = pltpu.make_async_copy(ret_hbm, ret_ref, sems.at[8 + 2 * groups])
    get_ret.start()
    parts = [pl.ds(i * width, width) for i in range(4)]
    get_ins = [
        pltpu.make_async_copy(w_in_hbm.at[:, part], w_in_ref.at[:, part], sems.at[i])
        for i, part in enumerate(parts)
    ]
    get_cot = pltpu.make_async_copy(cot_hbm, cot_ref, sems.at[4])
    get_out = pltpu.make_async_copy(w_out_hbm, w_out_ref, sems.at[5])
    for fetch in (*get_ins, get_cot, get_out):
        fetch.start()

    slot = jnp.broadcast_to(slot_ref[...], (LANES, count)).T
    for start in range(0, slots, LANES):
        pick_ref[:, start : start + LANES] = hot(
            slot == (iota((count, LANES), 1) + start).astype(F32)
        )
    get_ret.wait()
    emb_ref[...] = dot_nn(pick_ref[...], ret_ref[...]).astype(BF16)

    for i in range(4):
        get_ins[i].wait()
        pre = dot_nn(emb_ref[...], w_in_ref[:, parts[i]])
        half = 0.5 * pre
        th = jnp.tanh(half)
        act = half + half * th
        proj_ref[i] = act.astype(BF16)
        slope_ref[i] = 0.5 * ((1.0 + th) + act * (1.0 - th))

    pos = iota((count, 1), 0)
    begin = jnp.zeros((count, 1), jnp.int32)
    end = jnp.int32(0)
    for s in range(len_ref.shape[1]):
        end = end + len_ref[0, s]
        begin = jnp.where(pos >= end, end, begin)
    key = iota((count, count), 1)
    allowed = (key >= begin) & (key <= iota((count, count), 0))
    bias_ref[...] = jnp.where(allowed, 3.0e38, -30.0)

    lane = iota((qrows, LANES), 1)
    inside = [(lane >= a * HEAD_DIM) & (lane < (a + 1) * HEAD_DIM) for a in range(per)]
    lane = iota((count, LANES), 1)
    inside_all = [(lane >= a * HEAD_DIM) & (lane < (a + 1) * HEAD_DIM) for a in range(per)]

    def stacked(value, factor=1.0):
        value = value.astype(F32) * factor
        return jnp.concatenate([jnp.where(m, value, 0.0) for m in inside], 0).astype(BF16)

    row = iota((LANES, qrows), 0)
    inside_rows = [(row >= a * HEAD_DIM) & (row < (a + 1) * HEAD_DIM) for a in range(per)]

    def stacked_t(value, factor=1.0):
        value = (value.astype(F32) * factor).T
        return jnp.concatenate([jnp.where(m, value, 0.0) for m in inside_rows], 1).astype(BF16)

    def apart(value):
        value = value.astype(F32)
        return [jnp.where(m, value, 0.0).astype(BF16) for m in inside_all]

    def forward(p, _):
        cols = pl.ds(pl.multiple_of(p * LANES, LANES), LANES)
        key_all = proj_ref[3, :, cols]
        vals = apart(proj_ref[1, :, cols])
        for r0 in range(0, count, qrows):
            r1 = r0 + qrows
            half = dot_nt(stacked(proj_ref[2, r0:r1, cols], half_scale), key_all[:r1])
            half = jnp.minimum(half.reshape(per, qrows, r1), bias_ref[r0:r1, :r1][None])
            th = jnp.tanh(half)
            weight = half + half * th
            weight_b = weight.astype(BF16)
            base = per * r0
            weight_ref[p, base : base + per * qrows, :r1] = weight_b.reshape(per * qrows, r1)
            wslope_ref[p, base : base + per * qrows, :r1] = (
                (1.0 + th) + weight * (1.0 - th)
            ).reshape(per * qrows, r1)
            total = dot_nn(weight_b[0], vals[0][:r1])
            for a in range(1, per):
                total = total + dot_nn(weight_b[a], vals[a][:r1])
            att_ref[r0:r1, cols] = total
        return 0

    lax.fori_loop(0, slabs, forward, 0)

    get_cot.wait()
    get_out.wait()
    gain = gain_ref[...]
    gain_sum = jnp.zeros((1, width), F32)
    for r0 in range(0, count, qrows):
        rows = slice(r0, r0 + qrows)
        att = att_ref[rows, :]
        centered = att - jnp.mean(att, 1, keepdims=True)
        inv = lax.rsqrt(jnp.mean(centered * centered, 1, keepdims=True) + 1e-05)
        normed = centered * inv
        upd = proj_ref[0, rows, :].astype(F32)
        scaled = normed * gain
        mixed = (scaled * upd).astype(BF16)
        mixed_ref[rows, :] = mixed
        result_ref[rows, :] = (
            emb_ref[rows, :].astype(F32) + dot_nn(mixed, w_out_ref[...])
        ).astype(BF16)
        gmix = dot_nt(cot_ref[rows, :], w_out_ref[...]).astype(BF16).astype(F32)
        gpre_ref[rows, 0:width] = (gmix * scaled * slope_ref[0, rows, :]).astype(BF16)
        gnorm = gmix * gain * upd
        gain_sum = gain_sum + jnp.sum(gmix * normed * upd, 0, keepdims=True)
        mean1 = jnp.mean(gnorm, 1, keepdims=True)
        mean2 = jnp.mean(gnorm * normed, 1, keepdims=True)
        gatt_ref[rows, :] = ((gnorm - mean1 - normed * mean2) * inv).astype(BF16)
    put_result = pltpu.make_async_copy(result_ref, result_hbm, sems.at[6])
    put_result.start()
    gwo_ref[...] = dot_tn(mixed_ref[...], cot_ref[...]).astype(BF16)

    def backward(p, _):
        start = pl.multiple_of(p * LANES, LANES)
        cols = pl.ds(start, LANES)
        val = proj_ref[1, :, cols]
        keys = apart(proj_ref[3, :, cols])
        for r0 in reversed(range(0, count, qrows)):
            r1 = r0 + qrows
            base = per * r0
            rows = slice(base, base + per * qrows)
            gatt = stacked(gatt_ref[r0:r1, cols])
            gweight = dot_nt(gatt, val[:r1])
            gscore = (gweight * wslope_ref[p, rows, :r1]).astype(BF16)
            gqry = dot_nn(gscore[:qrows], keys[0][:r1])
            for a in range(1, per):
                gqry = gqry + dot_nn(gscore[a * qrows : (a + 1) * qrows], keys[a][:r1])
            gval = dot_nn(stacked_t(gatt_ref[r0:r1, cols]), weight_ref[p, rows, :r1])
            gkey = dot_nn(stacked_t(proj_ref[2, r0:r1, cols], half_scale), gscore)
            if r1 == count:
                gval_ref[...] = gval
                gkey_ref[...] = gkey
            else:
                gval_ref[:, :r1] += gval
                gkey_ref[:, :r1] += gkey
            gpre_ref[r0:r1, pl.ds(2 * width + start, LANES)] = (
                gqry * half_scale * slope_ref[2, r0:r1, cols]
            ).astype(BF16)
        gpre_ref[:, pl.ds(width + start, LANES)] = (gval_ref[...].T * slope_ref[1, :, cols]).astype(BF16)
        gpre_ref[:, pl.ds(3 * width + start, LANES)] = (gkey_ref[...].T * slope_ref[3, :, cols]).astype(BF16)
        return 0

    lax.fori_loop(0, slabs, backward, 0)

    puts = [put_result]
    me = lax.axis_index("group")
    emb_t = emb_ref[...].T
    cols_in = 4 * width // groups
    cols_out = width // wparts
    chunk = min(cols_in, 512)
    gain_col = jnp.broadcast_to(gain_sum, (LANES, width)).T.astype(BF16)
    for k in [*range(1, groups), 0]:
        part = lax.rem(me + k, groups)
        for c in range(0, cols_in, chunk):
            cols = pl.ds(pl.multiple_of(part * cols_in + c, LANES), chunk)
            grads_ref[k, :, c : c + chunk] = dot_nn(emb_t, gpre_ref[:, cols]).astype(BF16)
        cols = pl.ds(pl.multiple_of(lax.rem(part, wparts) * cols_out, LANES), cols_out)
        grads_ref[k, :, cols_in : cols_in + cols_out] = gwo_ref[:, cols]
        grads_ref[k, :, cols_in + cols_out :] = gain_col
        cut = grads_hbms[2 * k].shape[1]
        for i, cols in enumerate((pl.ds(0, cut), pl.ds(cut, grads_ref.shape[2] - cut))):
            put = pltpu.make_async_copy(
                grads_ref.at[k, :, cols], grads_hbms[2 * k + i], sems.at[8 + 2 * k + i]
            )
            put.start()
            puts.append(put)
    for i, r0 in enumerate((0, count // 2)):
        rows = pl.ds(r0, count // 2)
        row_ref[rows, :] = (
            cot_ref[rows, :].astype(F32) + dot_nt(gpre_ref[rows, :], w_in_ref[...])
        ).astype(BF16)
        sem = sems.at[7 + i * (2 + 2 * groups)]
        puts.append(pltpu.make_async_copy(row_ref.at[rows], row_hbm.at[rows], sem))
        puts[-1].start()
    for put in puts:
        put.wait()


def slots_kernel(slot_ref, grad_ref, out_hbm, out_ref, sems):
    count = grad_ref.shape[0]
    slots = out_ref.shape[0]
    step = row_step(slots)
    stores = []
    for n, start in enumerate(range(0, slots, step)):
        put = hot((iota((step, count), 0) + start).astype(F32) == slot_ref[...])
        out_ref[start : start + step, :] = dot_nn(put, grad_ref[...]).astype(BF16)
        here = pl.ds(start, step)
        stores.append(pltpu.make_async_copy(out_ref.at[here], out_hbm.at[here], sems.at[n]))
        stores[-1].start()
    for store in stores:
        store.wait()


def plane_kernel(outer, terms, *refs):
    left, right, outs = refs[:terms], refs[terms : 2 * terms], refs[2 * terms :]
    cut = left[0].shape[2]
    high = lax.div(lax.axis_index("table"), lax.axis_size("table") // outer)
    for k in range(outer):
        at = lax.rem(high + k, outer)
        for parts, cols in ((left, slice(0, cut)), (right, slice(cut, None))):
            total = parts[0][at].astype(F32)
            for part in parts[1:]:
                total = total + part[at].astype(F32)
            outs[k][:, cols] = total.astype(outs[k].dtype)


def finish_kernel(kept_ref, *refs):
    got_refs, (in_ref, out_ref, gain_ref) = refs[:-3], refs[-3:]
    total = kept_ref[...]
    for got_ref in got_refs:
        total = total + got_ref[...].astype(F32)
    cols_in, cols_out = in_ref.shape[1], out_ref.shape[1]
    in_ref[...] = total[:, :cols_in]
    out_ref[...] = total[:, cols_in : cols_in + cols_out]
    gain_ref[...] = total[:, cols_in + cols_out :].T[0:1, :]


def shift(value, axis, size, amount):
    return lax.ppermute(value, axis, [(i, (i + amount) % size) for i in range(size)])


def on_device(item_owner, item_row, lengths, table, w_in, w_out, gain, cotangent):
    owners = lax.axis_size("table")
    groups = lax.axis_size("group")
    count = item_row.shape[0]
    width = table.shape[1]
    capacity = max(2, 3 * count // (2 * owners))
    slots = owners * capacity
    padded = -(-capacity // LANES) * LANES
    me = lax.axis_index("group")

    requested, slot = call(
        functools.partial(request_kernel, capacity),
        [
            jax.ShapeDtypeStruct((owners, padded), jnp.int32),
            jax.ShapeDtypeStruct((1, count), F32),
        ],
        4 * count * count * owners,
        8 * count,
        (item_owner.reshape(1, count), item_row.reshape(1, count)),
    )
    wanted = lax.all_to_all(requested, "table", split_axis=0, concat_axis=0, tiled=True)
    found, ids = call(
        functools.partial(lookup_kernel, capacity),
        [
            jax.ShapeDtypeStruct((slots, width), BF16),
            jax.ShapeDtypeStruct((1, slots), F32),
        ],
        2 * slots * table.shape[0] * width,
        2 * (slots + table.shape[0]) * width,
        (wanted, table),
    )
    returned = lax.all_to_all(found, "table", split_axis=0, concat_axis=0, tiled=True)
    all_ids = [ids] + [shift(ids, "group", groups, k) for k in range(1, groups)]
    returned, *all_ids = lax.optimization_barrier((returned, *all_ids))

    wparts = min(groups, width // LANES)
    heads_per = LANES // HEAD_DIM
    cols_in = 4 * width // groups
    cols_out = width // wparts
    cols_all = cols_in + cols_out + LANES
    cut = cols_all // LANES // 2 * LANES
    square = pltpu.VMEM((count, width), BF16)
    result, row_grad, *grads = call(
        functools.partial(layer_kernel, groups, wparts),
        [
            jax.ShapeDtypeStruct((count, width), BF16),
            jax.ShapeDtypeStruct((count, width), BF16),
            *[
                jax.ShapeDtypeStruct((width, cols), BF16)
                for _ in range(groups)
                for cols in (cut, cols_all - cut)
            ],
        ],
        32 * count * width * width + 14 * count * count * width,
        24 * count * width,
        (lengths, slot, returned, w_in, w_out, gain.reshape(1, width), cotangent),
        smem=(0,),
        far=(2, 3, 4, 6),
        far_out=range(2 + 2 * groups),
        scratch=[
            pltpu.VMEM((slots, width), BF16),
            pltpu.VMEM(w_in.shape, BF16),
            pltpu.VMEM(w_out.shape, BF16),
            square,
            square,
            square,
            pltpu.VMEM((groups, width, cols_all), BF16),
            pltpu.VMEM((count, slots), BF16),
            square,
            pltpu.VMEM((4, count, width), BF16),
            pltpu.VMEM((4, count, width), F32),
            pltpu.VMEM((count, count), F32),
            pltpu.VMEM((width // LANES, heads_per * count, count), BF16),
            pltpu.VMEM((width // LANES, heads_per * count, count), F32),
            pltpu.VMEM((count, width), F32),
            square,
            square,
            pltpu.VMEM((count, 4 * width), BF16),
            pltpu.VMEM((LANES, count), F32),
            pltpu.VMEM((LANES, count), F32),
            pltpu.VMEM((width, width), BF16),
            pltpu.SemaphoreType.DMA((10 + 2 * groups,)),
        ],
    )
    def fill_slots(row_grad):
        return call(
            slots_kernel,
            [jax.ShapeDtypeStruct((slots, width), BF16)],
            2 * slots * count * width,
            4 * count * width,
            (slot, row_grad),
            far_out=(0,),
            scratch=[
                pltpu.VMEM((slots, width), BF16),
                pltpu.SemaphoreType.DMA((slots // row_step(slots),)),
            ],
        )[0]

    rows = width // owners
    side = 2 if owners % 4 == 0 else 1
    plane = side * side
    outer = owners // plane
    here = lax.axis_index("table")
    high, middle, low = here // plane, here // side % side, here % side
    sides = []
    for i in range(2):
        terms = [grads[i]] + [shift(grads[2 * k + i], "group", groups, k) for k in range(1, groups)]
        sides.append([term.reshape(outer, side, side, rows, term.shape[1]) for term in terms])

    def entry(value, index, axis):
        return lax.dynamic_index_in_dim(value, index, axis, keepdims=False)

    def add(terms):
        return sum(term.astype(F32) for term in terms)

    def halve(terms, index, axis, bit, tie=None):
        send = add([entry(term, 1 - index, axis) for term in terms]).astype(BF16)
        if tie is not None:
            tie, send = lax.optimization_barrier((tie, send))
        got = lax.ppermute(send, "table", [(i, i ^ bit) for i in range(owners)])
        kept = [entry(term, index, axis) for term in terms]
        return (kept if tie is not None else [add(kept)]) + [got], tie

    if side == 2:
        left, row_grad = halve(sides[0], low, 2, 1, row_grad)
        right, row_grad = halve(sides[1], middle, 1, 2, row_grad)
        outgoing = fill_slots(row_grad)
        outgoing, left[-1], right[-1] = lax.optimization_barrier((outgoing, left[-1], right[-1]))
        left, _ = halve(left, middle, 1, 2)
        right, _ = halve(right, low, 1, 1)
    else:
        outgoing = fill_slots(row_grad)
        left, right = [[term[:, 0, 0] for term in terms] for terms in sides]
    cols = cols_all
    kept, *sends = call(
        functools.partial(plane_kernel, outer, len(left)),
        [
            jax.ShapeDtypeStruct((rows, cols), F32),
            *[jax.ShapeDtypeStruct((rows, cols), BF16) for _ in range(1, outer)],
        ],
        12 * outer * rows * cols,
        8 * outer * rows * cols,
        (*left, *right),
        limit=24,
    )
    got = [
        lax.ppermute(
            sends[k - 1],
            "table",
            [(i, ((i // plane + k) % outer) * plane + i % plane) for i in range(owners)],
        )
        for k in range(1, outer)
    ]

    incoming = lax.all_to_all(outgoing, "table", split_axis=0, concat_axis=0, tiled=True)
    incoming, *got = lax.optimization_barrier((incoming, *got))
    all_incoming = [incoming] + [shift(incoming, "group", groups, k) for k in range(1, groups)]
    grad_rows = table.shape[0] // groups
    (table_grad,) = call(
        functools.partial(collect_kernel, groups),
        [jax.ShapeDtypeStruct((grad_rows, width), F32)],
        2 * slots * table.shape[0] * width,
        2 * groups * slots * width + 4 * grad_rows * width,
        (*all_ids, *all_incoming),
        far=range(groups, 2 * groups),
        far_out=(0,),
        limit=24,
        scratch=[
            *[pltpu.VMEM((slots, width), BF16) for _ in range(groups)],
            pltpu.VMEM((grad_rows, width), F32),
            pltpu.SemaphoreType.DMA((groups + grad_rows // row_step(grad_rows),)),
        ],
    )

    w_in_grad, mine, gain_grad = call(
        finish_kernel,
        [
            jax.ShapeDtypeStruct((rows, cols_in), F32),
            jax.ShapeDtypeStruct((rows, cols_out), F32),
            jax.ShapeDtypeStruct((1, rows), F32),
        ],
        4 * rows * cols_all,
        14 * rows * cols_all,
        (kept, *got),
        limit=24,
    )
    pieces = jnp.stack([mine] + [shift(mine, "group", groups, k) for k in range(1, groups)])
    w_out_grad = jnp.concatenate(
        [
            lax.dynamic_index_in_dim(pieces, (me - p) % groups, 0, keepdims=False)
            for p in range(wparts)
        ],
        1,
    )
    return (result, table_grad, w_in_grad, w_out_grad, gain_grad.reshape(rows))


def solution(mesh):
    return jax.shard_map(
        on_device,
        mesh=mesh,
        in_specs=(
            P(("table", "group"), None),
            P(("table", "group")),
            P(("table", "group"), None),
            P("table", None),
            P(),
            P(),
            P(),
            P(("table", "group"), None),
        ),
        out_specs=(
            P(("table", "group"), None),
            P(("table", "group"), None),
            P("table", "group"),
            P("table", None),
            P("table"),
        ),
        check_vma=False,
    )
```

```python
import functools
import math

import jax
import jax.numpy as jnp
from jax import lax
from jax.experimental import pallas as pl
from jax.experimental.pallas import tpu as pltpu
from jax.sharding import PartitionSpec as P

HEAD_DIM = 64
LANES = 128
QUERY_ROWS = 256

F32 = jnp.float32
BF16 = jnp.bfloat16


def iota(shape, dim):
    return lax.broadcasted_iota(jnp.int32, shape, dim)


def hot(cond):
    return jnp.where(cond, 1.0, 0.0).astype(BF16)


def dot_nn(a, b):
    return lax.dot_general(a, b, (((1,), (0,)), ((), ())), preferred_element_type=F32)


def dot_nt(a, b):
    return lax.dot_general(a, b, (((1,), (1,)), ((), ())), preferred_element_type=F32)


def dot_tn(a, b):
    return lax.dot_general(a, b, (((0,), (0,)), ((), ())), preferred_element_type=F32)


def row_step(rows):
    return 256 if rows % 256 == 0 else rows


def call(kernel, out_shape, flops, nbytes, operands, smem=(), far=(), far_out=(), limit=56, scratch=()):
    spaces = [
        pltpu.SMEM if i in smem else pl.ANY if i in far else pltpu.VMEM
        for i in range(len(operands))
    ]
    out_spaces = [pl.ANY if i in far_out else pltpu.VMEM for i in range(len(out_shape))]
    return pl.pallas_call(
        kernel,
        out_shape=out_shape,
        in_specs=[pl.BlockSpec(memory_space=space) for space in spaces],
        out_specs=[pl.BlockSpec(memory_space=space) for space in out_spaces],
        scratch_shapes=scratch,
        compiler_params=pltpu.CompilerParams(vmem_limit_bytes=limit * 1024 * 1024),
        cost_estimate=pl.CostEstimate(flops=flops, bytes_accessed=nbytes, transcendentals=0),
    )(*operands)


def request_kernel(cap, owner_ref, row_ref, req_ref, slot_ref):
    owners, width = req_ref.shape
    count = owner_ref.shape[1]
    owner = owner_ref[...]
    row = row_ref[...]
    mine = iota((owners, count), 0) == owner
    mine_b = hot(mine)
    before = hot(iota((count, count), 0) < iota((count, count), 1))
    earlier = dot_nn(mine_b, before)
    place = jnp.sum(jnp.where(mine, earlier, 0.0), axis=0, keepdims=True)
    slot_ref[...] = owner.astype(F32) * float(cap) + place
    at_place = hot(iota((width, count), 0).astype(F32) == place)
    high = jnp.where(mine, (row >> 8).astype(F32), 0.0).astype(BF16)
    low = jnp.where(mine, (row & 255).astype(F32), 0.0).astype(BF16)
    found = dot_nt(high, at_place) * 256.0 + dot_nt(low, at_place)
    req_ref[...] = found.astype(jnp.int32)


def lookup_kernel(cap, wanted_ref, table_ref, found_ref, ids_ref):
    owners, width = wanted_ref.shape
    slots = found_ref.shape[0]
    rows = table_ref.shape[0]
    wanted = wanted_ref[...]
    high = (wanted >> 8).astype(F32).astype(BF16)
    low = (wanted & 255).astype(F32).astype(BF16)
    slot = iota((slots, owners), 0).astype(F32)
    holder = jnp.floor((slot + 0.5) * (1.0 / cap))
    spread = hot(holder == iota((slots, owners), 1).astype(F32))
    ids = dot_nn(spread, high) * 256.0 + dot_nn(spread, low)
    slot = iota((slots, width), 0).astype(F32)
    place = slot - jnp.floor((slot + 0.5) * (1.0 / cap)) * float(cap)
    ids = jnp.sum(
        jnp.where(iota((slots, width), 1).astype(F32) == place, ids, 0.0), axis=1, keepdims=True
    )
    wide = jnp.broadcast_to(ids, (slots, LANES))
    ids_ref[...] = wide.T[0:1, :]
    step = 256 if slots % 256 == 0 else slots
    for start in range(0, slots, step):
        part = ids[start : start + step]
        pick = hot(iota((step, rows), 1).astype(F32) == part)
        found_ref[start : start + step, :] = dot_nn(pick, table_ref[...]).astype(BF16)


def collect_kernel(groups, *refs):
    ids_refs, in_hbms, out_hbm = refs[:groups], refs[groups : 2 * groups], refs[2 * groups]
    in_refs, out_ref, sems = refs[2 * groups + 1 : 3 * groups + 1], refs[-2], refs[-1]
    rows = out_ref.shape[0]
    slots = in_refs[0].shape[0]
    fetches = [
        pltpu.make_async_copy(hbm, ref, sems.at[n])
        for n, (hbm, ref) in enumerate(zip(in_hbms, in_refs))
    ]
    for fetch in fetches:
        fetch.start()
    base = lax.axis_index("group") * rows
    step = row_step(rows)
    for fetch in fetches:
        fetch.wait()
    stores = []
    for n, start in enumerate(range(0, rows, step)):
        own = (iota((step, slots), 0) + (base + start)).astype(F32)
        total = None
        for ids_ref, in_ref in zip(ids_refs, in_refs):
            part = dot_nn(hot(own == ids_ref[...]), in_ref[...])
            total = part if total is None else total + part
        out_ref[start : start + step, :] = total
        here = pl.ds(start, step)
        stores.append(
            pltpu.make_async_copy(out_ref.at[here], out_hbm.at[here], sems.at[groups + n])
        )
        stores[-1].start()
    for store in stores:
        store.wait()


def layer_kernel(
    groups,
    wparts,
    len_ref,
    slot_ref,
    ret_hbm,
    w_in_hbm,
    w_out_hbm,
    gain_ref,
    cot_hbm,
    *rest,
):
    result_hbm, row_hbm = rest[:2]
    grads_hbms = rest[2 : 2 + 2 * groups]
    (
    ret_ref,
    w_in_ref,
    w_out_ref,
    cot_ref,
    result_ref,
    row_ref,
    grads_ref,
    pick_ref,
    emb_ref,
    proj_ref,
    slope_ref,
    bias_ref,
    weight_ref,
    wslope_ref,
    att_ref,
    mixed_ref,
    gatt_ref,
    gpre_ref,
    gval_ref,
    gkey_ref,
    gwo_ref,
    sems,
    ) = rest[2 + 2 * groups :]
    count, width = cot_ref.shape
    slots = ret_hbm.shape[0]
    per = LANES // HEAD_DIM
    slabs = width // LANES
    qrows = QUERY_ROWS if count % QUERY_ROWS == 0 else count
    half_scale = 0.5 / math.sqrt(HEAD_DIM)

    get_ret = pltpu.make_async_copy(ret_hbm, ret_ref, sems.at[8 + 2 * groups])
    get_ret.start()
    parts = [pl.ds(i * width, width) for i in range(4)]
    get_ins = [
        pltpu.make_async_copy(w_in_hbm.at[:, part], w_in_ref.at[:, part], sems.at[i])
        for i, part in enumerate(parts)
    ]
    get_cot = pltpu.make_async_copy(cot_hbm, cot_ref, sems.at[4])
    get_out = pltpu.make_async_copy(w_out_hbm, w_out_ref, sems.at[5])
    for fetch in (*get_ins, get_cot, get_out):
        fetch.start()

    slot = jnp.broadcast_to(slot_ref[...], (LANES, count)).T
    for start in range(0, slots, LANES):
        pick_ref[:, start : start + LANES] = hot(
            slot == (iota((count, LANES), 1) + start).astype(F32)
        )
    get_ret.wait()
    emb_ref[...] = dot_nn(pick_ref[...], ret_ref[...]).astype(BF16)

    for fetch in get_ins:
        fetch.wait()
    for i in range(4):
        pre = dot_nn(emb_ref[...], w_in_ref[:, parts[i]])
        half = 0.5 * pre
        th = jnp.tanh(half)
        act = half + half * th
        proj_ref[i] = act.astype(BF16)
        slope_ref[i] = 0.5 * ((1.0 + th) + act * (1.0 - th))

    pos = iota((count, 1), 0)
    begin = jnp.zeros((count, 1), jnp.int32)
    end = jnp.int32(0)
    for s in range(len_ref.shape[1]):
        end = end + len_ref[0, s]
        begin = jnp.where(pos >= end, end, begin)
    key = iota((count, count), 1)
    allowed = (key >= begin) & (key <= iota((count, count), 0))
    bias_ref[...] = jnp.where(allowed, 3.0e38, -30.0)

    lane = iota((qrows, LANES), 1)
    inside = [(lane >= a * HEAD_DIM) & (lane < (a + 1) * HEAD_DIM) for a in range(per)]
    lane = iota((count, LANES), 1)
    inside_all = [(lane >= a * HEAD_DIM) & (lane < (a + 1) * HEAD_DIM) for a in range(per)]

    def stacked(value, factor=1.0):
        value = value.astype(F32) * factor
        return jnp.concatenate([jnp.where(m, value, 0.0) for m in inside], 0).astype(BF16)

    row = iota((LANES, qrows), 0)
    inside_rows = [(row >= a * HEAD_DIM) & (row < (a + 1) * HEAD_DIM) for a in range(per)]

    def stacked_t(value, factor=1.0):
        value = (value.astype(F32) * factor).T
        return jnp.concatenate([jnp.where(m, value, 0.0) for m in inside_rows], 1).astype(BF16)

    def apart(value):
        value = value.astype(F32)
        return [jnp.where(m, value, 0.0).astype(BF16) for m in inside_all]

    def forward(p, _):
        cols = pl.ds(pl.multiple_of(p * LANES, LANES), LANES)
        key_all = proj_ref[3, :, cols]
        vals = apart(proj_ref[1, :, cols])
        for r0 in range(0, count, qrows):
            r1 = r0 + qrows
            half = dot_nt(stacked(proj_ref[2, r0:r1, cols], half_scale), key_all[:r1])
            half = jnp.minimum(half.reshape(per, qrows, r1), bias_ref[r0:r1, :r1][None])
            th = jnp.tanh(half)
            weight = half + half * th
            weight_b = weight.astype(BF16)
            base = per * r0
            weight_ref[p, base : base + per * qrows, :r1] = weight_b.reshape(per * qrows, r1)
            wslope_ref[p, base : base + per * qrows, :r1] = (
                (1.0 + th) + weight * (1.0 - th)
            ).reshape(per * qrows, r1)
            total = dot_nn(weight_b[0], vals[0][:r1])
            for a in range(1, per):
                total = total + dot_nn(weight_b[a], vals[a][:r1])
            att_ref[r0:r1, cols] = total
        return 0

    lax.fori_loop(0, slabs, forward, 0, unroll=2)

    get_cot.wait()
    get_out.wait()
    gain = gain_ref[...]
    gain_sum = jnp.zeros((1, width), F32)
    for r0 in range(0, count, qrows):
        rows = slice(r0, r0 + qrows)
        att = att_ref[rows, :]
        centered = att - jnp.mean(att, 1, keepdims=True)
        inv = lax.rsqrt(jnp.mean(centered * centered, 1, keepdims=True) + 1e-05)
        normed = centered * inv
        upd = proj_ref[0, rows, :].astype(F32)
        scaled = normed * gain
        mixed = (scaled * upd).astype(BF16)
        mixed_ref[rows, :] = mixed
        result_ref[rows, :] = (
            emb_ref[rows, :].astype(F32) + dot_nn(mixed, w_out_ref[...])
        ).astype(BF16)
        gmix = dot_nt(cot_ref[rows, :], w_out_ref[...]).astype(BF16).astype(F32)
        gpre_ref[rows, 0:width] = (gmix * scaled * slope_ref[0, rows, :]).astype(BF16)
        gnorm = gmix * gain * upd
        gain_sum = gain_sum + jnp.sum(gmix * normed * upd, 0, keepdims=True)
        mean1 = jnp.mean(gnorm, 1, keepdims=True)
        mean2 = jnp.mean(gnorm * normed, 1, keepdims=True)
        gatt_ref[rows, :] = ((gnorm - mean1 - normed * mean2) * inv).astype(BF16)
    put_result = pltpu.make_async_copy(result_ref, result_hbm, sems.at[6])
    put_result.start()
    gwo_ref[...] = dot_tn(mixed_ref[...], cot_ref[...]).astype(BF16)

    def backward(p, _):
        start = pl.multiple_of(p * LANES, LANES)
        cols = pl.ds(start, LANES)
        val = proj_ref[1, :, cols]
        keys = apart(proj_ref[3, :, cols])
        for r0 in reversed(range(0, count, qrows)):
            r1 = r0 + qrows
            base = per * r0
            rows = slice(base, base + per * qrows)
            gatt = stacked(gatt_ref[r0:r1, cols])
            gweight = dot_nt(gatt, val[:r1])
            gscore = (gweight * wslope_ref[p, rows, :r1]).astype(BF16)
            gqry = dot_nn(gscore[:qrows], keys[0][:r1])
            for a in range(1, per):
                gqry = gqry + dot_nn(gscore[a * qrows : (a + 1) * qrows], keys[a][:r1])
            gval = dot_nn(stacked_t(gatt_ref[r0:r1, cols]), weight_ref[p, rows, :r1])
            gkey = dot_nn(stacked_t(proj_ref[2, r0:r1, cols], half_scale), gscore)
            if r1 == count:
                gval_ref[...] = gval
                gkey_ref[...] = gkey
            else:
                gval_ref[:, :r1] += gval
                gkey_ref[:, :r1] += gkey
            gpre_ref[r0:r1, pl.ds(2 * width + start, LANES)] = (
                gqry * half_scale * slope_ref[2, r0:r1, cols]
            ).astype(BF16)
        gpre_ref[:, pl.ds(width + start, LANES)] = (gval_ref[...].T * slope_ref[1, :, cols]).astype(BF16)
        gpre_ref[:, pl.ds(3 * width + start, LANES)] = (gkey_ref[...].T * slope_ref[3, :, cols]).astype(BF16)
        return 0

    lax.fori_loop(0, slabs, backward, 0, unroll=2)

    puts = [put_result]
    me = lax.axis_index("group")
    emb_t = emb_ref[...].T
    cols_in = 4 * width // groups
    cols_out = width // wparts
    chunk = min(cols_in, 512)
    gain_col = jnp.broadcast_to(gain_sum, (LANES, width)).T.astype(BF16)
    for k in [*range(1, groups), 0]:
        part = lax.rem(me + k, groups)
        for c in range(0, cols_in, chunk):
            cols = pl.ds(pl.multiple_of(part * cols_in + c, LANES), chunk)
            grads_ref[k, :, c : c + chunk] = dot_nn(emb_t, gpre_ref[:, cols]).astype(BF16)
        cols = pl.ds(pl.multiple_of(lax.rem(part, wparts) * cols_out, LANES), cols_out)
        grads_ref[k, :, cols_in : cols_in + cols_out] = gwo_ref[:, cols]
        grads_ref[k, :, cols_in + cols_out :] = gain_col
        cut = grads_hbms[2 * k].shape[1]
        for i, cols in enumerate((pl.ds(0, cut), pl.ds(cut, grads_ref.shape[2] - cut))):
            put = pltpu.make_async_copy(
                grads_ref.at[k, :, cols], grads_hbms[2 * k + i], sems.at[8 + 2 * k + i]
            )
            put.start()
            puts.append(put)
    for i, r0 in enumerate((0, count // 2)):
        rows = pl.ds(r0, count // 2)
        row_ref[rows, :] = (
            cot_ref[rows, :].astype(F32) + dot_nt(gpre_ref[rows, :], w_in_ref[...])
        ).astype(BF16)
        sem = sems.at[7 + i * (2 + 2 * groups)]
        puts.append(pltpu.make_async_copy(row_ref.at[rows], row_hbm.at[rows], sem))
        puts[-1].start()
    for put in puts:
        put.wait()


def slots_kernel(slot_ref, grad_ref, out_hbm, out_ref, sems):
    count = grad_ref.shape[0]
    slots = out_ref.shape[0]
    step = row_step(slots)
    stores = []
    for n, start in enumerate(range(0, slots, step)):
        put = hot((iota((step, count), 0) + start).astype(F32) == slot_ref[...])
        out_ref[start : start + step, :] = dot_nn(put, grad_ref[...]).astype(BF16)
        here = pl.ds(start, step)
        stores.append(pltpu.make_async_copy(out_ref.at[here], out_hbm.at[here], sems.at[n]))
        stores[-1].start()
    for store in stores:
        store.wait()


def plane_kernel(outer, terms, *refs):
    left, right, outs = refs[:terms], refs[terms : 2 * terms], refs[2 * terms :]
    cut = left[0].shape[2]
    high = lax.div(lax.axis_index("table"), lax.axis_size("table") // outer)
    for k in range(outer):
        at = lax.rem(high + k, outer)
        for parts, cols in ((left, slice(0, cut)), (right, slice(cut, None))):
            total = parts[0][at].astype(F32)
            for part in parts[1:]:
                total = total + part[at].astype(F32)
            outs[k][:, cols] = total.astype(outs[k].dtype)


def finish_kernel(kept_ref, *refs):
    got_refs, (in_ref, out_ref, gain_ref) = refs[:-3], refs[-3:]
    total = kept_ref[...]
    for got_ref in got_refs:
        total = total + got_ref[...].astype(F32)
    cols_in, cols_out = in_ref.shape[1], out_ref.shape[1]
    in_ref[...] = total[:, :cols_in]
    out_ref[...] = total[:, cols_in : cols_in + cols_out]
    gain_ref[...] = total[:, cols_in + cols_out :].T[0:1, :]


def shift(value, axis, size, amount):
    return lax.ppermute(value, axis, [(i, (i + amount) % size) for i in range(size)])


def on_device(item_owner, item_row, lengths, table, w_in, w_out, gain, cotangent):
    owners = lax.axis_size("table")
    groups = lax.axis_size("group")
    count = item_row.shape[0]
    width = table.shape[1]
    capacity = max(2, 3 * count // (2 * owners))
    slots = owners * capacity
    padded = -(-capacity // LANES) * LANES
    me = lax.axis_index("group")

    requested, slot = call(
        functools.partial(request_kernel, capacity),
        [
            jax.ShapeDtypeStruct((owners, padded), jnp.int32),
            jax.ShapeDtypeStruct((1, count), F32),
        ],
        4 * count * count * owners,
        8 * count,
        (item_owner.reshape(1, count), item_row.reshape(1, count)),
    )
    wanted = lax.all_to_all(requested, "table", split_axis=0, concat_axis=0, tiled=True)
    found, ids = call(
        functools.partial(lookup_kernel, capacity),
        [
            jax.ShapeDtypeStruct((slots, width), BF16),
            jax.ShapeDtypeStruct((1, slots), F32),
        ],
        2 * slots * table.shape[0] * width,
        2 * (slots + table.shape[0]) * width,
        (wanted, table),
    )
    returned = lax.all_to_all(found, "table", split_axis=0, concat_axis=0, tiled=True)
    all_ids = [ids] + [shift(ids, "group", groups, k) for k in range(1, groups)]
    returned, *all_ids = lax.optimization_barrier((returned, *all_ids))

    wparts = min(groups, width // LANES)
    heads_per = LANES // HEAD_DIM
    cols_in = 4 * width // groups
    cols_out = width // wparts
    cols_all = cols_in + cols_out + LANES
    cut = cols_all // LANES // 2 * LANES
    square = pltpu.VMEM((count, width), BF16)
    result, row_grad, *grads = call(
        functools.partial(layer_kernel, groups, wparts),
        [
            jax.ShapeDtypeStruct((count, width), BF16),
            jax.ShapeDtypeStruct((count, width), BF16),
            *[
                jax.ShapeDtypeStruct((width, cols), BF16)
                for _ in range(groups)
                for cols in (cut, cols_all - cut)
            ],
        ],
        32 * count * width * width + 14 * count * count * width,
        24 * count * width,
        (lengths, slot, returned, w_in, w_out, gain.reshape(1, width), cotangent),
        smem=(0,),
        far=(2, 3, 4, 6),
        far_out=range(2 + 2 * groups),
        scratch=[
            pltpu.VMEM((slots, width), BF16),
            pltpu.VMEM(w_in.shape, BF16),
            pltpu.VMEM(w_out.shape, BF16),
            square,
            square,
            square,
            pltpu.VMEM((groups, width, cols_all), BF16),
            pltpu.VMEM((count, slots), BF16),
            square,
            pltpu.VMEM((4, count, width), BF16),
            pltpu.VMEM((4, count, width), F32),
            pltpu.VMEM((count, count), F32),
            pltpu.VMEM((width // LANES, heads_per * count, count), BF16),
            pltpu.VMEM((width // LANES, heads_per * count, count), F32),
            pltpu.VMEM((count, width), F32),
            square,
            square,
            pltpu.VMEM((count, 4 * width), BF16),
            pltpu.VMEM((LANES, count), F32),
            pltpu.VMEM((LANES, count), F32),
            pltpu.VMEM((width, width), BF16),
            pltpu.SemaphoreType.DMA((10 + 2 * groups,)),
        ],
    )
    def fill_slots(row_grad):
        return call(
            slots_kernel,
            [jax.ShapeDtypeStruct((slots, width), BF16)],
            2 * slots * count * width,
            4 * count * width,
            (slot, row_grad),
            far_out=(0,),
            scratch=[
                pltpu.VMEM((slots, width), BF16),
                pltpu.SemaphoreType.DMA((slots // row_step(slots),)),
            ],
        )[0]

    rows = width // owners
    side = 2 if owners % 4 == 0 else 1
    plane = side * side
    outer = owners // plane
    here = lax.axis_index("table")
    high, middle, low = here // plane, here // side % side, here % side
    sides = []
    for i in range(2):
        terms = [grads[i]] + [shift(grads[2 * k + i], "group", groups, k) for k in range(1, groups)]
        sides.append([term.reshape(outer, side, side, rows, term.shape[1]) for term in terms])

    def entry(value, index, axis):
        return lax.dynamic_index_in_dim(value, index, axis, keepdims=False)

    def add(terms):
        return sum(term.astype(F32) for term in terms)

    def halve(terms, index, axis, bit, tie=None):
        send = add([entry(term, 1 - index, axis) for term in terms]).astype(BF16)
        if tie is not None:
            tie, send = lax.optimization_barrier((tie, send))
        got = lax.ppermute(send, "table", [(i, i ^ bit) for i in range(owners)])
        kept = [entry(term, index, axis) for term in terms]
        return (kept if tie is not None else [add(kept)]) + [got], tie

    if side == 2:
        left, row_grad = halve(sides[0], low, 2, 1, row_grad)
        right, row_grad = halve(sides[1], middle, 1, 2, row_grad)
        outgoing = fill_slots(row_grad)
        left, _ = halve(left, middle, 1, 2)
        right, _ = halve(right, low, 1, 1)
    else:
        outgoing = fill_slots(row_grad)
        left, right = [[term[:, 0, 0] for term in terms] for terms in sides]
    cols = cols_all
    kept, *sends = call(
        functools.partial(plane_kernel, outer, len(left)),
        [
            jax.ShapeDtypeStruct((rows, cols), F32),
            *[jax.ShapeDtypeStruct((rows, cols), BF16) for _ in range(1, outer)],
        ],
        12 * outer * rows * cols,
        160 * outer * rows * cols,
        (*left, *right),
        limit=24,
    )
    got = [
        lax.ppermute(
            sends[k - 1],
            "table",
            [(i, ((i // plane + k) % outer) * plane + i % plane) for i in range(owners)],
        )
        for k in range(1, outer)
    ]

    incoming = lax.all_to_all(outgoing, "table", split_axis=0, concat_axis=0, tiled=True)
    incoming, kept = lax.optimization_barrier((incoming, kept))
    all_incoming = [incoming] + [shift(incoming, "group", groups, k) for k in range(1, groups)]
    grad_rows = table.shape[0] // groups
    (table_grad,) = call(
        functools.partial(collect_kernel, groups),
        [jax.ShapeDtypeStruct((grad_rows, width), F32)],
        2 * slots * table.shape[0] * width,
        2 * groups * slots * width + 4 * grad_rows * width,
        (*all_ids, *all_incoming),
        far=range(groups, 2 * groups),
        far_out=(0,),
        limit=24,
        scratch=[
            *[pltpu.VMEM((slots, width), BF16) for _ in range(groups)],
            pltpu.VMEM((grad_rows, width), F32),
            pltpu.SemaphoreType.DMA((groups + grad_rows // row_step(grad_rows),)),
        ],
    )

    w_in_grad, mine, gain_grad = call(
        finish_kernel,
        [
            jax.ShapeDtypeStruct((rows, cols_in), F32),
            jax.ShapeDtypeStruct((rows, cols_out), F32),
            jax.ShapeDtypeStruct((1, rows), F32),
        ],
        4 * rows * cols_all,
        14 * rows * cols_all,
        (kept, *got),
        limit=24,
    )
    pieces = jnp.stack([mine] + [shift(mine, "group", groups, k) for k in range(1, groups)])
    w_out_grad = jnp.concatenate(
        [
            lax.dynamic_index_in_dim(pieces, (me - p) % groups, 0, keepdims=False)
            for p in range(wparts)
        ],
        1,
    )
    return (result, table_grad, w_in_grad, w_out_grad, gain_grad.reshape(rows))


def solution(mesh):
    return jax.shard_map(
        on_device,
        mesh=mesh,
        in_specs=(
            P(("table", "group"), None),
            P(("table", "group")),
            P(("table", "group"), None),
            P("table", None),
            P(),
            P(),
            P(),
            P(("table", "group"), None),
        ),
        out_specs=(
            P(("table", "group"), None),
            P(("table", "group"), None),
            P("table", "group"),
            P("table", None),
            P("table"),
        ),
        check_vma=False,
    )
```

```python
import functools
import math

import jax
import jax.numpy as jnp
from jax import lax
from jax.experimental import pallas as pl
from jax.experimental.pallas import tpu as pltpu
from jax.sharding import PartitionSpec as P

HEAD_DIM = 64
LANES = 128
QUERY_ROWS = 256

F32 = jnp.float32
BF16 = jnp.bfloat16


def iota(shape, dim):
    return lax.broadcasted_iota(jnp.int32, shape, dim)


def hot(cond):
    return jnp.where(cond, 1.0, 0.0).astype(BF16)


def dot_nn(a, b):
    return lax.dot_general(a, b, (((1,), (0,)), ((), ())), preferred_element_type=F32)


def dot_nt(a, b):
    return lax.dot_general(a, b, (((1,), (1,)), ((), ())), preferred_element_type=F32)


def dot_tn(a, b):
    return lax.dot_general(a, b, (((0,), (0,)), ((), ())), preferred_element_type=F32)


def row_step(rows):
    return 256 if rows % 256 == 0 else rows


def call(kernel, out_shape, flops, nbytes, operands, smem=(), far=(), far_out=(), limit=56, scratch=()):
    spaces = [
        pltpu.SMEM if i in smem else pl.ANY if i in far else pltpu.VMEM
        for i in range(len(operands))
    ]
    out_spaces = [pl.ANY if i in far_out else pltpu.VMEM for i in range(len(out_shape))]
    return pl.pallas_call(
        kernel,
        out_shape=out_shape,
        in_specs=[pl.BlockSpec(memory_space=space) for space in spaces],
        out_specs=[pl.BlockSpec(memory_space=space) for space in out_spaces],
        scratch_shapes=scratch,
        compiler_params=pltpu.CompilerParams(vmem_limit_bytes=limit * 1024 * 1024),
        cost_estimate=pl.CostEstimate(flops=flops, bytes_accessed=nbytes, transcendentals=0),
    )(*operands)


def request_kernel(cap, owner_ref, row_ref, req_ref, slot_ref):
    owners, width = req_ref.shape
    count = owner_ref.shape[1]
    owner = owner_ref[...]
    row = row_ref[...]
    mine = iota((owners, count), 0) == owner
    mine_b = hot(mine)
    before = hot(iota((count, count), 0) < iota((count, count), 1))
    earlier = dot_nn(mine_b, before)
    place = jnp.sum(jnp.where(mine, earlier, 0.0), axis=0, keepdims=True)
    slot_ref[...] = owner.astype(F32) * float(cap) + place
    at_place = hot(iota((width, count), 0).astype(F32) == place)
    high = jnp.where(mine, (row >> 8).astype(F32), 0.0).astype(BF16)
    low = jnp.where(mine, (row & 255).astype(F32), 0.0).astype(BF16)
    found = dot_nt(high, at_place) * 256.0 + dot_nt(low, at_place)
    req_ref[...] = found.astype(jnp.int32)


def lookup_kernel(cap, wanted_ref, table_ref, found_ref, ids_ref):
    owners, width = wanted_ref.shape
    slots = found_ref.shape[0]
    rows = table_ref.shape[0]
    wanted = wanted_ref[...]
    high = (wanted >> 8).astype(F32).astype(BF16)
    low = (wanted & 255).astype(F32).astype(BF16)
    slot = iota((slots, owners), 0).astype(F32)
    holder = jnp.floor((slot + 0.5) * (1.0 / cap))
    spread = hot(holder == iota((slots, owners), 1).astype(F32))
    ids = dot_nn(spread, high) * 256.0 + dot_nn(spread, low)
    slot = iota((slots, width), 0).astype(F32)
    place = slot - jnp.floor((slot + 0.5) * (1.0 / cap)) * float(cap)
    ids = jnp.sum(
        jnp.where(iota((slots, width), 1).astype(F32) == place, ids, 0.0), axis=1, keepdims=True
    )
    wide = jnp.broadcast_to(ids, (slots, LANES))
    ids_ref[...] = wide.T[0:1, :]
    step = 256 if slots % 256 == 0 else slots
    for start in range(0, slots, step):
        part = ids[start : start + step]
        pick = hot(iota((step, rows), 1).astype(F32) == part)
        found_ref[start : start + step, :] = dot_nn(pick, table_ref[...]).astype(BF16)


def collect_kernel(groups, *refs):
    ids_refs, in_hbms, out_hbm = refs[:groups], refs[groups : 2 * groups], refs[2 * groups]
    in_refs, out_ref, sems = refs[2 * groups + 1 : 3 * groups + 1], refs[-2], refs[-1]
    rows = out_ref.shape[0]
    slots = in_refs[0].shape[0]
    fetches = [
        pltpu.make_async_copy(hbm, ref, sems.at[n])
        for n, (hbm, ref) in enumerate(zip(in_hbms, in_refs))
    ]
    for fetch in fetches:
        fetch.start()
    base = lax.axis_index("group") * rows
    step = row_step(rows)
    for fetch in fetches:
        fetch.wait()
    stores = []
    for n, start in enumerate(range(0, rows, step)):
        own = (iota((step, slots), 0) + (base + start)).astype(F32)
        total = None
        for ids_ref, in_ref in zip(ids_refs, in_refs):
            part = dot_nn(hot(own == ids_ref[...]), in_ref[...])
            total = part if total is None else total + part
        out_ref[start : start + step, :] = total
        here = pl.ds(start, step)
        stores.append(
            pltpu.make_async_copy(out_ref.at[here], out_hbm.at[here], sems.at[groups + n])
        )
        stores[-1].start()
    for store in stores:
        store.wait()


def layer_kernel(
    groups,
    wparts,
    len_ref,
    slot_ref,
    ret_hbm,
    w_in_hbm,
    w_out_hbm,
    gain_ref,
    cot_hbm,
    *rest,
):
    result_hbm, row_hbm = rest[:2]
    grads_hbms = rest[2 : 2 + 2 * groups]
    (
    ret_ref,
    w_in_ref,
    w_out_ref,
    cot_ref,
    result_ref,
    row_ref,
    grads_ref,
    pick_ref,
    emb_ref,
    proj_ref,
    slope_ref,
    bias_ref,
    weight_ref,
    wslope_ref,
    att_ref,
    mixed_ref,
    gatt_ref,
    gpre_ref,
    gval_ref,
    gkey_ref,
    gwo_ref,
    sems,
    ) = rest[2 + 2 * groups :]
    count, width = cot_ref.shape
    slots = ret_hbm.shape[0]
    per = LANES // HEAD_DIM
    slabs = width // LANES
    qrows = QUERY_ROWS if count % QUERY_ROWS == 0 else count
    half_scale = 0.5 / math.sqrt(HEAD_DIM)

    get_ret = pltpu.make_async_copy(ret_hbm, ret_ref, sems.at[8 + 2 * groups])
    get_ret.start()
    parts = [pl.ds(i * width, width) for i in range(4)]
    get_ins = [
        pltpu.make_async_copy(w_in_hbm.at[:, part], w_in_ref.at[:, part], sems.at[i])
        for i, part in enumerate(parts)
    ]
    get_cot = pltpu.make_async_copy(cot_hbm, cot_ref, sems.at[4])
    get_out = pltpu.make_async_copy(w_out_hbm, w_out_ref, sems.at[5])
    for fetch in (*get_ins, get_cot, get_out):
        fetch.start()

    slot = jnp.broadcast_to(slot_ref[...], (LANES, count)).T
    for start in range(0, slots, LANES):
        pick_ref[:, start : start + LANES] = hot(
            slot == (iota((count, LANES), 1) + start).astype(F32)
        )
    get_ret.wait()
    emb_ref[...] = dot_nn(pick_ref[...], ret_ref[...]).astype(BF16)

    for fetch in get_ins:
        fetch.wait()
    for i in range(4):
        pre = dot_nn(emb_ref[...], w_in_ref[:, parts[i]])
        half = 0.5 * pre
        th = jnp.tanh(half)
        act = half + half * th
        proj_ref[i] = act.astype(BF16)
        slope_ref[i] = 0.5 * ((1.0 + th) + act * (1.0 - th))

    pos = iota((count, 1), 0)
    begin = jnp.zeros((count, 1), jnp.int32)
    end = jnp.int32(0)
    for s in range(len_ref.shape[1]):
        end = end + len_ref[0, s]
        begin = jnp.where(pos >= end, end, begin)
    key = iota((count, count), 1)
    allowed = (key >= begin) & (key <= iota((count, count), 0))
    bias_ref[...] = jnp.where(allowed, 3.0e38, -30.0)

    lane = iota((qrows, LANES), 1)
    inside = [(lane >= a * HEAD_DIM) & (lane < (a + 1) * HEAD_DIM) for a in range(per)]
    lane = iota((count, LANES), 1)
    inside_all = [(lane >= a * HEAD_DIM) & (lane < (a + 1) * HEAD_DIM) for a in range(per)]

    def stacked(value, factor=1.0):
        value = value.astype(F32) * factor
        return jnp.concatenate([jnp.where(m, value, 0.0) for m in inside], 0).astype(BF16)

    row = iota((LANES, qrows), 0)
    inside_rows = [(row >= a * HEAD_DIM) & (row < (a + 1) * HEAD_DIM) for a in range(per)]

    def stacked_t(value, factor=1.0):
        value = (value.astype(F32) * factor).T
        return jnp.concatenate([jnp.where(m, value, 0.0) for m in inside_rows], 1).astype(BF16)

    def apart(value):
        value = value.astype(F32)
        return [jnp.where(m, value, 0.0).astype(BF16) for m in inside_all]

    def forward(p, _):
        cols = pl.ds(pl.multiple_of(p * LANES, LANES), LANES)
        key_all = proj_ref[3, :, cols]
        vals = apart(proj_ref[1, :, cols])
        for r0 in range(0, count, qrows):
            r1 = r0 + qrows
            half = dot_nt(stacked(proj_ref[2, r0:r1, cols], half_scale), key_all[:r1])
            half = jnp.minimum(half.reshape(per, qrows, r1), bias_ref[r0:r1, :r1][None])
            th = jnp.tanh(half)
            weight = half + half * th
            weight_b = weight.astype(BF16)
            base = per * r0
            weight_ref[p, base : base + per * qrows, :r1] = weight_b.reshape(per * qrows, r1)
            wslope_ref[p, base : base + per * qrows, :r1] = (
                (1.0 + th) + weight * (1.0 - th)
            ).reshape(per * qrows, r1)
            total = dot_nn(weight_b[0], vals[0][:r1])
            for a in range(1, per):
                total = total + dot_nn(weight_b[a], vals[a][:r1])
            att_ref[r0:r1, cols] = total
        return 0

    lax.fori_loop(0, slabs, forward, 0, unroll=4)

    get_cot.wait()
    get_out.wait()
    gain = gain_ref[...]
    gain_sum = jnp.zeros((1, width), F32)
    for r0 in range(0, count, qrows):
        rows = slice(r0, r0 + qrows)
        att = att_ref[rows, :]
        centered = att - jnp.mean(att, 1, keepdims=True)
        inv = lax.rsqrt(jnp.mean(centered * centered, 1, keepdims=True) + 1e-05)
        normed = centered * inv
        upd = proj_ref[0, rows, :].astype(F32)
        scaled = normed * gain
        mixed = (scaled * upd).astype(BF16)
        mixed_ref[rows, :] = mixed
        result_ref[rows, :] = (
            emb_ref[rows, :].astype(F32) + dot_nn(mixed, w_out_ref[...])
        ).astype(BF16)
        gmix = dot_nt(cot_ref[rows, :], w_out_ref[...]).astype(BF16).astype(F32)
        gpre_ref[rows, 0:width] = (gmix * scaled * slope_ref[0, rows, :]).astype(BF16)
        gnorm = gmix * gain * upd
        gain_sum = gain_sum + jnp.sum(gmix * normed * upd, 0, keepdims=True)
        mean1 = jnp.mean(gnorm, 1, keepdims=True)
        mean2 = jnp.mean(gnorm * normed, 1, keepdims=True)
        gatt_ref[rows, :] = ((gnorm - mean1 - normed * mean2) * inv).astype(BF16)
    put_result = pltpu.make_async_copy(result_ref, result_hbm, sems.at[6])
    put_result.start()
    gwo_ref[...] = dot_tn(mixed_ref[...], cot_ref[...]).astype(BF16)

    def backward(p, _):
        start = pl.multiple_of(p * LANES, LANES)
        cols = pl.ds(start, LANES)
        val = proj_ref[1, :, cols]
        keys = apart(proj_ref[3, :, cols])
        for r0 in reversed(range(0, count, qrows)):
            r1 = r0 + qrows
            base = per * r0
            rows = slice(base, base + per * qrows)
            gatt = stacked(gatt_ref[r0:r1, cols])
            gweight = dot_nt(gatt, val[:r1])
            gscore = (gweight * wslope_ref[p, rows, :r1]).astype(BF16)
            gqry = dot_nn(gscore[:qrows], keys[0][:r1])
            for a in range(1, per):
                gqry = gqry + dot_nn(gscore[a * qrows : (a + 1) * qrows], keys[a][:r1])
            gval = dot_nn(stacked_t(gatt_ref[r0:r1, cols]), weight_ref[p, rows, :r1])
            gkey = dot_nn(stacked_t(proj_ref[2, r0:r1, cols], half_scale), gscore)
            if r1 == count:
                gval_ref[...] = gval
                gkey_ref[...] = gkey
            else:
                gval_ref[:, :r1] += gval
                gkey_ref[:, :r1] += gkey
            gpre_ref[r0:r1, pl.ds(2 * width + start, LANES)] = (
                gqry * half_scale * slope_ref[2, r0:r1, cols]
            ).astype(BF16)
        gpre_ref[:, pl.ds(width + start, LANES)] = (gval_ref[...].T * slope_ref[1, :, cols]).astype(BF16)
        gpre_ref[:, pl.ds(3 * width + start, LANES)] = (gkey_ref[...].T * slope_ref[3, :, cols]).astype(BF16)
        return 0

    lax.fori_loop(0, slabs, backward, 0, unroll=4)

    puts = [put_result]
    me = lax.axis_index("group")
    emb_t = emb_ref[...].T
    cols_in = 4 * width // groups
    cols_out = width // wparts
    chunk = min(cols_in, 512)
    gain_col = jnp.broadcast_to(gain_sum, (LANES, width)).T.astype(BF16)
    for k in [*range(1, groups), 0]:
        part = lax.rem(me + k, groups)
        for c in range(0, cols_in, chunk):
            cols = pl.ds(pl.multiple_of(part * cols_in + c, LANES), chunk)
            grads_ref[k, :, c : c + chunk] = dot_nn(emb_t, gpre_ref[:, cols]).astype(BF16)
        cols = pl.ds(pl.multiple_of(lax.rem(part, wparts) * cols_out, LANES), cols_out)
        grads_ref[k, :, cols_in : cols_in + cols_out] = gwo_ref[:, cols]
        grads_ref[k, :, cols_in + cols_out :] = gain_col
        cut = grads_hbms[2 * k].shape[1]
        for i, cols in enumerate((pl.ds(0, cut), pl.ds(cut, grads_ref.shape[2] - cut))):
            put = pltpu.make_async_copy(
                grads_ref.at[k, :, cols], grads_hbms[2 * k + i], sems.at[8 + 2 * k + i]
            )
            put.start()
            puts.append(put)
    for i, r0 in enumerate((0, count // 2)):
        rows = pl.ds(r0, count // 2)
        row_ref[rows, :] = (
            cot_ref[rows, :].astype(F32) + dot_nt(gpre_ref[rows, :], w_in_ref[...])
        ).astype(BF16)
        sem = sems.at[7 + i * (2 + 2 * groups)]
        puts.append(pltpu.make_async_copy(row_ref.at[rows], row_hbm.at[rows], sem))
        puts[-1].start()
    for put in puts:
        put.wait()


def slots_kernel(slot_ref, grad_ref, out_hbm, out_ref, sems):
    count = grad_ref.shape[0]
    slots = out_ref.shape[0]
    step = row_step(slots)
    stores = []
    for n, start in enumerate(range(0, slots, step)):
        put = hot((iota((step, count), 0) + start).astype(F32) == slot_ref[...])
        out_ref[start : start + step, :] = dot_nn(put, grad_ref[...]).astype(BF16)
        here = pl.ds(start, step)
        stores.append(pltpu.make_async_copy(out_ref.at[here], out_hbm.at[here], sems.at[n]))
        stores[-1].start()
    for store in stores:
        store.wait()


def plane_kernel(outer, terms, *refs):
    left, right, outs = refs[:terms], refs[terms : 2 * terms], refs[2 * terms :]
    cut = left[0].shape[2]
    high = lax.div(lax.axis_index("table"), lax.axis_size("table") // outer)
    for k in range(outer):
        at = lax.rem(high + k, outer)
        for parts, cols in ((left, slice(0, cut)), (right, slice(cut, None))):
            total = parts[0][at].astype(F32)
            for part in parts[1:]:
                total = total + part[at].astype(F32)
            outs[k][:, cols] = total.astype(outs[k].dtype)


def finish_kernel(kept_ref, *refs):
    got_refs, (in_ref, out_ref, gain_ref) = refs[:-3], refs[-3:]
    total = kept_ref[...]
    for got_ref in got_refs:
        total = total + got_ref[...].astype(F32)
    cols_in, cols_out = in_ref.shape[1], out_ref.shape[1]
    in_ref[...] = total[:, :cols_in]
    out_ref[...] = total[:, cols_in : cols_in + cols_out]
    gain_ref[...] = total[:, cols_in + cols_out :].T[0:1, :]


def shift(value, axis, size, amount):
    return lax.ppermute(value, axis, [(i, (i + amount) % size) for i in range(size)])


def on_device(item_owner, item_row, lengths, table, w_in, w_out, gain, cotangent):
    owners = lax.axis_size("table")
    groups = lax.axis_size("group")
    count = item_row.shape[0]
    width = table.shape[1]
    capacity = max(2, 3 * count // (2 * owners))
    slots = owners * capacity
    padded = -(-capacity // LANES) * LANES
    me = lax.axis_index("group")

    requested, slot = call(
        functools.partial(request_kernel, capacity),
        [
            jax.ShapeDtypeStruct((owners, padded), jnp.int32),
            jax.ShapeDtypeStruct((1, count), F32),
        ],
        4 * count * count * owners,
        8 * count,
        (item_owner.reshape(1, count), item_row.reshape(1, count)),
    )
    wanted = lax.all_to_all(requested, "table", split_axis=0, concat_axis=0, tiled=True)
    found, ids = call(
        functools.partial(lookup_kernel, capacity),
        [
            jax.ShapeDtypeStruct((slots, width), BF16),
            jax.ShapeDtypeStruct((1, slots), F32),
        ],
        2 * slots * table.shape[0] * width,
        2 * (slots + table.shape[0]) * width,
        (wanted, table),
    )
    returned = lax.all_to_all(found, "table", split_axis=0, concat_axis=0, tiled=True)
    all_ids = [ids] + [shift(ids, "group", groups, k) for k in range(1, groups)]
    returned, *all_ids = lax.optimization_barrier((returned, *all_ids))

    wparts = min(groups, width // LANES)
    heads_per = LANES // HEAD_DIM
    cols_in = 4 * width // groups
    cols_out = width // wparts
    cols_all = cols_in + cols_out + LANES
    cut = cols_all // LANES // 2 * LANES
    square = pltpu.VMEM((count, width), BF16)
    result, row_grad, *grads = call(
        functools.partial(layer_kernel, groups, wparts),
        [
            jax.ShapeDtypeStruct((count, width), BF16),
            jax.ShapeDtypeStruct((count, width), BF16),
            *[
                jax.ShapeDtypeStruct((width, cols), BF16)
                for _ in range(groups)
                for cols in (cut, cols_all - cut)
            ],
        ],
        32 * count * width * width + 14 * count * count * width,
        24 * count * width,
        (lengths, slot, returned, w_in, w_out, gain.reshape(1, width), cotangent),
        smem=(0,),
        far=(2, 3, 4, 6),
        far_out=range(2 + 2 * groups),
        scratch=[
            pltpu.VMEM((slots, width), BF16),
            pltpu.VMEM(w_in.shape, BF16),
            pltpu.VMEM(w_out.shape, BF16),
            square,
            square,
            square,
            pltpu.VMEM((groups, width, cols_all), BF16),
            pltpu.VMEM((count, slots), BF16),
            square,
            pltpu.VMEM((4, count, width), BF16),
            pltpu.VMEM((4, count, width), F32),
            pltpu.VMEM((count, count), F32),
            pltpu.VMEM((width // LANES, heads_per * count, count), BF16),
            pltpu.VMEM((width // LANES, heads_per * count, count), F32),
            pltpu.VMEM((count, width), F32),
            square,
            square,
            pltpu.VMEM((count, 4 * width), BF16),
            pltpu.VMEM((LANES, count), F32),
            pltpu.VMEM((LANES, count), F32),
            pltpu.VMEM((width, width), BF16),
            pltpu.SemaphoreType.DMA((10 + 2 * groups,)),
        ],
    )
    def fill_slots(row_grad):
        return call(
            slots_kernel,
            [jax.ShapeDtypeStruct((slots, width), BF16)],
            2 * slots * count * width,
            4 * count * width,
            (slot, row_grad),
            far_out=(0,),
            scratch=[
                pltpu.VMEM((slots, width), BF16),
                pltpu.SemaphoreType.DMA((slots // row_step(slots),)),
            ],
        )[0]

    rows = width // owners
    side = 2 if owners % 4 == 0 else 1
    plane = side * side
    outer = owners // plane
    here = lax.axis_index("table")
    high, middle, low = here // plane, here // side % side, here % side
    sides = []
    for i in range(2):
        terms = [grads[i]] + [shift(grads[2 * k + i], "group", groups, k) for k in range(1, groups)]
        sides.append([term.reshape(outer, side, side, rows, term.shape[1]) for term in terms])

    def entry(value, index, axis):
        return lax.dynamic_index_in_dim(value, index, axis, keepdims=False)

    def add(terms):
        return sum(term.astype(F32) for term in terms)

    def halve(terms, index, axis, bit, tie=None):
        send = add([entry(term, 1 - index, axis) for term in terms]).astype(BF16)
        if tie is not None:
            tie, send = lax.optimization_barrier((tie, send))
        got = lax.ppermute(send, "table", [(i, i ^ bit) for i in range(owners)])
        kept = [entry(term, index, axis) for term in terms]
        return (kept if tie is not None else [add(kept)]) + [got], tie

    if side == 2:
        left, row_grad = halve(sides[0], low, 2, 1, row_grad)
        right, row_grad = halve(sides[1], middle, 1, 2, row_grad)
        outgoing = fill_slots(row_grad)
        left, _ = halve(left, middle, 1, 2)
        right, _ = halve(right, low, 1, 1)
    else:
        outgoing = fill_slots(row_grad)
        left, right = [[term[:, 0, 0] for term in terms] for terms in sides]
    cols = cols_all
    kept, *sends = call(
        functools.partial(plane_kernel, outer, len(left)),
        [
            jax.ShapeDtypeStruct((rows, cols), F32),
            *[jax.ShapeDtypeStruct((rows, cols), BF16) for _ in range(1, outer)],
        ],
        12 * outer * rows * cols,
        160 * outer * rows * cols,
        (*left, *right),
        limit=24,
    )
    got = [
        lax.ppermute(
            sends[k - 1],
            "table",
            [(i, ((i // plane + k) % outer) * plane + i % plane) for i in range(owners)],
        )
        for k in range(1, outer)
    ]

    incoming = lax.all_to_all(outgoing, "table", split_axis=0, concat_axis=0, tiled=True)
    incoming, *got = lax.optimization_barrier((incoming, *got))
    all_incoming = [incoming] + [shift(incoming, "group", groups, k) for k in range(1, groups)]
    grad_rows = table.shape[0] // groups
    (table_grad,) = call(
        functools.partial(collect_kernel, groups),
        [jax.ShapeDtypeStruct((grad_rows, width), F32)],
        2 * slots * table.shape[0] * width,
        2 * groups * slots * width + 4 * grad_rows * width,
        (*all_ids, *all_incoming),
        far=range(groups, 2 * groups),
        far_out=(0,),
        limit=24,
        scratch=[
            *[pltpu.VMEM((slots, width), BF16) for _ in range(groups)],
            pltpu.VMEM((grad_rows, width), F32),
            pltpu.SemaphoreType.DMA((groups + grad_rows // row_step(grad_rows),)),
        ],
    )

    w_in_grad, mine, gain_grad = call(
        finish_kernel,
        [
            jax.ShapeDtypeStruct((rows, cols_in), F32),
            jax.ShapeDtypeStruct((rows, cols_out), F32),
            jax.ShapeDtypeStruct((1, rows), F32),
        ],
        4 * rows * cols_all,
        14 * rows * cols_all,
        (kept, *got),
        limit=24,
    )
    others = [shift(mine, "group", groups, k) for k in range(1, groups)]
    table_grad, *others = lax.optimization_barrier((table_grad, *others))
    pieces = jnp.stack([mine, *others])
    w_out_grad = jnp.concatenate(
        [
            lax.dynamic_index_in_dim(pieces, (me - p) % groups, 0, keepdims=False)
            for p in range(wparts)
        ],
        1,
    )
    return (result, table_grad, w_in_grad, w_out_grad, gain_grad.reshape(rows))


def solution(mesh):
    return jax.shard_map(
        on_device,
        mesh=mesh,
        in_specs=(
            P(("table", "group"), None),
            P(("table", "group")),
            P(("table", "group"), None),
            P("table", None),
            P(),
            P(),
            P(),
            P(("table", "group"), None),
        ),
        out_specs=(
            P(("table", "group"), None),
            P(("table", "group"), None),
            P("table", "group"),
            P("table", None),
            P("table"),
        ),
        check_vma=False,
    )
```

```python
import functools
import math

import jax
import jax.numpy as jnp
from jax import lax
from jax.experimental import pallas as pl
from jax.experimental.pallas import tpu as pltpu
from jax.sharding import PartitionSpec as P

HEAD_DIM = 64
LANES = 128
QUERY_ROWS = 256

F32 = jnp.float32
BF16 = jnp.bfloat16


def iota(shape, dim):
    return lax.broadcasted_iota(jnp.int32, shape, dim)


def hot(cond):
    return jnp.where(cond, 1.0, 0.0).astype(BF16)


def dot_nn(a, b):
    return lax.dot_general(a, b, (((1,), (0,)), ((), ())), preferred_element_type=F32)


def dot_nt(a, b):
    return lax.dot_general(a, b, (((1,), (1,)), ((), ())), preferred_element_type=F32)


def dot_tn(a, b):
    return lax.dot_general(a, b, (((0,), (0,)), ((), ())), preferred_element_type=F32)


def row_step(rows):
    return 256 if rows % 256 == 0 else rows


def call(kernel, out_shape, flops, nbytes, operands, smem=(), far=(), far_out=(), limit=56, scratch=()):
    spaces = [
        pltpu.SMEM if i in smem else pl.ANY if i in far else pltpu.VMEM
        for i in range(len(operands))
    ]
    out_spaces = [pl.ANY if i in far_out else pltpu.VMEM for i in range(len(out_shape))]
    return pl.pallas_call(
        kernel,
        out_shape=out_shape,
        in_specs=[pl.BlockSpec(memory_space=space) for space in spaces],
        out_specs=[pl.BlockSpec(memory_space=space) for space in out_spaces],
        scratch_shapes=scratch,
        compiler_params=pltpu.CompilerParams(vmem_limit_bytes=limit * 1024 * 1024),
        cost_estimate=pl.CostEstimate(flops=flops, bytes_accessed=nbytes, transcendentals=0),
    )(*operands)


def request_kernel(cap, owner_ref, row_ref, req_ref, slot_ref):
    owners, width = req_ref.shape
    count = owner_ref.shape[1]
    owner = owner_ref[...]
    row = row_ref[...]
    mine = iota((owners, count), 0) == owner
    mine_b = hot(mine)
    before = hot(iota((count, count), 0) < iota((count, count), 1))
    earlier = dot_nn(mine_b, before)
    place = jnp.sum(jnp.where(mine, earlier, 0.0), axis=0, keepdims=True)
    slot_ref[...] = owner.astype(F32) * float(cap) + place
    at_place = hot(iota((width, count), 0).astype(F32) == place)
    high = jnp.where(mine, (row >> 8).astype(F32), 0.0).astype(BF16)
    low = jnp.where(mine, (row & 255).astype(F32), 0.0).astype(BF16)
    found = dot_nt(high, at_place) * 256.0 + dot_nt(low, at_place)
    req_ref[...] = found.astype(jnp.int32)


def lookup_kernel(cap, wanted_ref, table_ref, found_ref, ids_ref):
    owners, width = wanted_ref.shape
    slots = found_ref.shape[0]
    rows = table_ref.shape[0]
    wanted = wanted_ref[...]
    high = (wanted >> 8).astype(F32).astype(BF16)
    low = (wanted & 255).astype(F32).astype(BF16)
    slot = iota((slots, owners), 0).astype(F32)
    holder = jnp.floor((slot + 0.5) * (1.0 / cap))
    spread = hot(holder == iota((slots, owners), 1).astype(F32))
    ids = dot_nn(spread, high) * 256.0 + dot_nn(spread, low)
    slot = iota((slots, width), 0).astype(F32)
    place = slot - jnp.floor((slot + 0.5) * (1.0 / cap)) * float(cap)
    ids = jnp.sum(
        jnp.where(iota((slots, width), 1).astype(F32) == place, ids, 0.0), axis=1, keepdims=True
    )
    wide = jnp.broadcast_to(ids, (slots, LANES))
    ids_ref[...] = wide.T[0:1, :]
    step = 256 if slots % 256 == 0 else slots
    for start in range(0, slots, step):
        part = ids[start : start + step]
        pick = hot(iota((step, rows), 1).astype(F32) == part)
        found_ref[start : start + step, :] = dot_nn(pick, table_ref[...]).astype(BF16)


def collect_kernel(groups, *refs):
    ids_refs, in_hbms, out_hbm = refs[:groups], refs[groups : 2 * groups], refs[2 * groups]
    in_refs, out_ref, sems = refs[2 * groups + 1 : 3 * groups + 1], refs[-2], refs[-1]
    rows = out_ref.shape[0]
    slots = in_refs[0].shape[0]
    fetches = [
        pltpu.make_async_copy(hbm, ref, sems.at[n])
        for n, (hbm, ref) in enumerate(zip(in_hbms, in_refs))
    ]
    for fetch in fetches:
        fetch.start()
    base = lax.axis_index("group") * rows
    step = row_step(rows)
    for fetch in fetches:
        fetch.wait()
    stores = []
    for n, start in enumerate(range(0, rows, step)):
        own = (iota((step, slots), 0) + (base + start)).astype(F32)
        total = None
        for ids_ref, in_ref in zip(ids_refs, in_refs):
            part = dot_nn(hot(own == ids_ref[...]), in_ref[...])
            total = part if total is None else total + part
        out_ref[start : start + step, :] = total
        here = pl.ds(start, step)
        stores.append(
            pltpu.make_async_copy(out_ref.at[here], out_hbm.at[here], sems.at[groups + n])
        )
        stores[-1].start()
    for store in stores:
        store.wait()


def layer_kernel(
    groups,
    wparts,
    len_ref,
    slot_ref,
    ret_hbm,
    w_in_hbm,
    w_out_hbm,
    gain_ref,
    cot_hbm,
    *rest,
):
    result_hbm, row_hbm = rest[:2]
    grads_hbms = rest[2 : 2 + 2 * groups]
    (
    ret_ref,
    w_in_ref,
    w_out_ref,
    cot_ref,
    result_ref,
    row_ref,
    grads_ref,
    pick_ref,
    emb_ref,
    proj_ref,
    slope_ref,
    bias_ref,
    weight_ref,
    wslope_ref,
    att_ref,
    mixed_ref,
    gatt_ref,
    gpre_ref,
    gval_ref,
    gkey_ref,
    gwo_ref,
    sems,
    ) = rest[2 + 2 * groups :]
    count, width = cot_ref.shape
    slots = ret_hbm.shape[0]
    per = LANES // HEAD_DIM
    slabs = width // LANES
    qrows = QUERY_ROWS if count % QUERY_ROWS == 0 else count
    half_scale = 0.5 / math.sqrt(HEAD_DIM)

    get_ret = pltpu.make_async_copy(ret_hbm, ret_ref, sems.at[8 + 2 * groups])
    get_ret.start()
    parts = [pl.ds(i * width, width) for i in range(4)]
    get_ins = [
        pltpu.make_async_copy(w_in_hbm.at[:, part], w_in_ref.at[:, part], sems.at[i])
        for i, part in enumerate(parts)
    ]
    get_cot = pltpu.make_async_copy(cot_hbm, cot_ref, sems.at[4])
    get_out = pltpu.make_async_copy(w_out_hbm, w_out_ref, sems.at[5])
    for fetch in (*get_ins, get_cot, get_out):
        fetch.start()

    slot = jnp.broadcast_to(slot_ref[...], (LANES, count)).T
    for start in range(0, slots, LANES):
        pick_ref[:, start : start + LANES] = hot(
            slot == (iota((count, LANES), 1) + start).astype(F32)
        )
    get_ret.wait()
    emb_ref[...] = dot_nn(pick_ref[...], ret_ref[...]).astype(BF16)

    for fetch in (*get_ins, get_cot, get_out):
        fetch.wait()
    for i in range(4):
        pre = dot_nn(emb_ref[...], w_in_ref[:, parts[i]])
        half = 0.5 * pre
        th = jnp.tanh(half)
        act = half + half * th
        proj_ref[i] = act.astype(BF16)
        slope_ref[i] = 0.5 * ((1.0 + th) + act * (1.0 - th))

    pos = iota((count, 1), 0)
    begin = jnp.zeros((count, 1), jnp.int32)
    end = jnp.int32(0)
    for s in range(len_ref.shape[1]):
        end = end + len_ref[0, s]
        begin = jnp.where(pos >= end, end, begin)
    key = iota((count, count), 1)
    allowed = (key >= begin) & (key <= iota((count, count), 0))
    bias_ref[...] = jnp.where(allowed, 3.0e38, -30.0)

    lane = iota((qrows, LANES), 1)
    inside = [(lane >= a * HEAD_DIM) & (lane < (a + 1) * HEAD_DIM) for a in range(per)]
    lane = iota((count, LANES), 1)
    inside_all = [(lane >= a * HEAD_DIM) & (lane < (a + 1) * HEAD_DIM) for a in range(per)]

    def stacked(value, factor=1.0):
        value = value.astype(F32) * factor
        return jnp.concatenate([jnp.where(m, value, 0.0) for m in inside], 0).astype(BF16)

    row = iota((LANES, qrows), 0)
    inside_rows = [(row >= a * HEAD_DIM) & (row < (a + 1) * HEAD_DIM) for a in range(per)]

    def stacked_t(value, factor=1.0):
        value = (value.astype(F32) * factor).T
        return jnp.concatenate([jnp.where(m, value, 0.0) for m in inside_rows], 1).astype(BF16)

    def apart(value):
        value = value.astype(F32)
        return [jnp.where(m, value, 0.0).astype(BF16) for m in inside_all]

    def forward(p, _):
        cols = pl.ds(pl.multiple_of(p * LANES, LANES), LANES)
        key_all = proj_ref[3, :, cols]
        vals = apart(proj_ref[1, :, cols])
        for r0 in range(0, count, qrows):
            r1 = r0 + qrows
            half = dot_nt(stacked(proj_ref[2, r0:r1, cols], half_scale), key_all[:r1])
            half = jnp.minimum(half.reshape(per, qrows, r1), bias_ref[r0:r1, :r1][None])
            th = jnp.tanh(half)
            weight = half + half * th
            weight_b = weight.astype(BF16)
            base = per * r0
            weight_ref[p, base : base + per * qrows, :r1] = weight_b.reshape(per * qrows, r1)
            wslope_ref[p, base : base + per * qrows, :r1] = (
                (1.0 + th) + weight * (1.0 - th)
            ).reshape(per * qrows, r1)
            total = dot_nn(weight_b[0], vals[0][:r1])
            for a in range(1, per):
                total = total + dot_nn(weight_b[a], vals[a][:r1])
            att_ref[r0:r1, cols] = total
        return 0

    lax.fori_loop(0, slabs, forward, 0, unroll=4)

    gain = gain_ref[...]
    gain_sum = jnp.zeros((1, width), F32)
    for r0 in range(0, count, qrows):
        rows = slice(r0, r0 + qrows)
        att = att_ref[rows, :]
        centered = att - jnp.mean(att, 1, keepdims=True)
        inv = lax.rsqrt(jnp.mean(centered * centered, 1, keepdims=True) + 1e-05)
        normed = centered * inv
        upd = proj_ref[0, rows, :].astype(F32)
        scaled = normed * gain
        mixed = (scaled * upd).astype(BF16)
        mixed_ref[rows, :] = mixed
        result_ref[rows, :] = (
            emb_ref[rows, :].astype(F32) + dot_nn(mixed, w_out_ref[...])
        ).astype(BF16)
        gmix = dot_nt(cot_ref[rows, :], w_out_ref[...]).astype(BF16).astype(F32)
        gpre_ref[rows, 0:width] = (gmix * scaled * slope_ref[0, rows, :]).astype(BF16)
        gnorm = gmix * gain * upd
        gain_sum = gain_sum + jnp.sum(gmix * normed * upd, 0, keepdims=True)
        mean1 = jnp.mean(gnorm, 1, keepdims=True)
        mean2 = jnp.mean(gnorm * normed, 1, keepdims=True)
        gatt_ref[rows, :] = ((gnorm - mean1 - normed * mean2) * inv).astype(BF16)
    gwo_ref[...] = dot_tn(mixed_ref[...], cot_ref[...]).astype(BF16)

    def backward(p, _):
        start = pl.multiple_of(p * LANES, LANES)
        cols = pl.ds(start, LANES)
        val = proj_ref[1, :, cols]
        keys = apart(proj_ref[3, :, cols])
        for r0 in reversed(range(0, count, qrows)):
            r1 = r0 + qrows
            base = per * r0
            rows = slice(base, base + per * qrows)
            gatt = stacked(gatt_ref[r0:r1, cols])
            gweight = dot_nt(gatt, val[:r1])
            gscore = (gweight * wslope_ref[p, rows, :r1]).astype(BF16)
            gqry = dot_nn(gscore[:qrows], keys[0][:r1])
            for a in range(1, per):
                gqry = gqry + dot_nn(gscore[a * qrows : (a + 1) * qrows], keys[a][:r1])
            gval = dot_nn(stacked_t(gatt_ref[r0:r1, cols]), weight_ref[p, rows, :r1])
            gkey = dot_nn(stacked_t(proj_ref[2, r0:r1, cols], half_scale), gscore)
            if r1 == count:
                gval_ref[...] = gval
                gkey_ref[...] = gkey
            else:
                gval_ref[:, :r1] += gval
                gkey_ref[:, :r1] += gkey
            gpre_ref[r0:r1, pl.ds(2 * width + start, LANES)] = (
                gqry * half_scale * slope_ref[2, r0:r1, cols]
            ).astype(BF16)
        gpre_ref[:, pl.ds(width + start, LANES)] = (gval_ref[...].T * slope_ref[1, :, cols]).astype(BF16)
        gpre_ref[:, pl.ds(3 * width + start, LANES)] = (gkey_ref[...].T * slope_ref[3, :, cols]).astype(BF16)
        return 0

    lax.fori_loop(0, slabs, backward, 0, unroll=4)

    put_result = pltpu.make_async_copy(result_ref, result_hbm, sems.at[6])
    put_result.start()
    puts = [put_result]
    me = lax.axis_index("group")
    emb_t = emb_ref[...].T
    cols_in = 4 * width // groups
    cols_out = width // wparts
    chunk = min(cols_in, 512)
    gain_col = jnp.broadcast_to(gain_sum, (LANES, width)).T.astype(BF16)
    for k in [*range(1, groups), 0]:
        part = lax.rem(me + k, groups)
        for c in range(0, cols_in, chunk):
            cols = pl.ds(pl.multiple_of(part * cols_in + c, LANES), chunk)
            grads_ref[k, :, c : c + chunk] = dot_nn(emb_t, gpre_ref[:, cols]).astype(BF16)
        cols = pl.ds(pl.multiple_of(lax.rem(part, wparts) * cols_out, LANES), cols_out)
        grads_ref[k, :, cols_in : cols_in + cols_out] = gwo_ref[:, cols]
        grads_ref[k, :, cols_in + cols_out :] = gain_col
        cut = grads_hbms[2 * k].shape[1]
        for i, cols in enumerate((pl.ds(0, cut), pl.ds(cut, grads_ref.shape[2] - cut))):
            put = pltpu.make_async_copy(
                grads_ref.at[k, :, cols], grads_hbms[2 * k + i], sems.at[8 + 2 * k + i]
            )
            put.start()
            puts.append(put)
    for i, r0 in enumerate((0, count // 2)):
        rows = pl.ds(r0, count // 2)
        row_ref[rows, :] = (
            cot_ref[rows, :].astype(F32) + dot_nt(gpre_ref[rows, :], w_in_ref[...])
        ).astype(BF16)
        sem = sems.at[7 + i * (2 + 2 * groups)]
        puts.append(pltpu.make_async_copy(row_ref.at[rows], row_hbm.at[rows], sem))
        puts[-1].start()
    for put in puts:
        put.wait()


def slots_kernel(slot_ref, grad_ref, out_hbm, out_ref, sems):
    count = grad_ref.shape[0]
    slots = out_ref.shape[0]
    step = row_step(slots)
    stores = []
    for n, start in enumerate(range(0, slots, step)):
        put = hot((iota((step, count), 0) + start).astype(F32) == slot_ref[...])
        out_ref[start : start + step, :] = dot_nn(put, grad_ref[...]).astype(BF16)
        here = pl.ds(start, step)
        stores.append(pltpu.make_async_copy(out_ref.at[here], out_hbm.at[here], sems.at[n]))
        stores[-1].start()
    for store in stores:
        store.wait()


def plane_kernel(outer, terms, *refs):
    left, right, outs = refs[:terms], refs[terms : 2 * terms], refs[2 * terms :]
    cut = left[0].shape[2]
    high = lax.div(lax.axis_index("table"), lax.axis_size("table") // outer)
    for k in range(outer):
        at = lax.rem(high + k, outer)
        for parts, cols in ((left, slice(0, cut)), (right, slice(cut, None))):
            total = parts[0][at].astype(F32)
            for part in parts[1:]:
                total = total + part[at].astype(F32)
            outs[k][:, cols] = total.astype(outs[k].dtype)


def finish_kernel(kept_ref, *refs):
    got_refs, (in_ref, out_ref, gain_ref) = refs[:-3], refs[-3:]
    total = kept_ref[...]
    for got_ref in got_refs:
        total = total + got_ref[...].astype(F32)
    cols_in, cols_out = in_ref.shape[1], out_ref.shape[1]
    in_ref[...] = total[:, :cols_in]
    out_ref[...] = total[:, cols_in : cols_in + cols_out]
    gain_ref[...] = total[:, cols_in + cols_out :].T[0:1, :]


def shift(value, axis, size, amount):
    return lax.ppermute(value, axis, [(i, (i + amount) % size) for i in range(size)])


def on_device(item_owner, item_row, lengths, table, w_in, w_out, gain, cotangent):
    owners = lax.axis_size("table")
    groups = lax.axis_size("group")
    count = item_row.shape[0]
    width = table.shape[1]
    capacity = max(2, 3 * count // (2 * owners))
    slots = owners * capacity
    padded = -(-capacity // LANES) * LANES
    me = lax.axis_index("group")

    requested, slot = call(
        functools.partial(request_kernel, capacity),
        [
            jax.ShapeDtypeStruct((owners, padded), jnp.int32),
            jax.ShapeDtypeStruct((1, count), F32),
        ],
        4 * count * count * owners,
        8 * count,
        (item_owner.reshape(1, count), item_row.reshape(1, count)),
    )
    wanted = lax.all_to_all(requested, "table", split_axis=0, concat_axis=0, tiled=True)
    found, ids = call(
        functools.partial(lookup_kernel, capacity),
        [
            jax.ShapeDtypeStruct((slots, width), BF16),
            jax.ShapeDtypeStruct((1, slots), F32),
        ],
        2 * slots * table.shape[0] * width,
        2 * (slots + table.shape[0]) * width,
        (wanted, table),
    )
    returned = lax.all_to_all(found, "table", split_axis=0, concat_axis=0, tiled=True)
    all_ids = [ids] + [shift(ids, "group", groups, k) for k in range(1, groups)]
    returned, *all_ids = lax.optimization_barrier((returned, *all_ids))

    wparts = min(groups, width // LANES)
    heads_per = LANES // HEAD_DIM
    cols_in = 4 * width // groups
    cols_out = width // wparts
    cols_all = cols_in + cols_out + LANES
    cut = cols_all // LANES // 2 * LANES
    square = pltpu.VMEM((count, width), BF16)
    result, row_grad, *grads = call(
        functools.partial(layer_kernel, groups, wparts),
        [
            jax.ShapeDtypeStruct((count, width), BF16),
            jax.ShapeDtypeStruct((count, width), BF16),
            *[
                jax.ShapeDtypeStruct((width, cols), BF16)
                for _ in range(groups)
                for cols in (cut, cols_all - cut)
            ],
        ],
        32 * count * width * width + 14 * count * count * width,
        24 * count * width,
        (lengths, slot, returned, w_in, w_out, gain.reshape(1, width), cotangent),
        smem=(0,),
        far=(2, 3, 4, 6),
        far_out=range(2 + 2 * groups),
        scratch=[
            pltpu.VMEM((slots, width), BF16),
            pltpu.VMEM(w_in.shape, BF16),
            pltpu.VMEM(w_out.shape, BF16),
            square,
            square,
            square,
            pltpu.VMEM((groups, width, cols_all), BF16),
            pltpu.VMEM((count, slots), BF16),
            square,
            pltpu.VMEM((4, count, width), BF16),
            pltpu.VMEM((4, count, width), F32),
            pltpu.VMEM((count, count), F32),
            pltpu.VMEM((width // LANES, heads_per * count, count), BF16),
            pltpu.VMEM((width // LANES, heads_per * count, count), F32),
            pltpu.VMEM((count, width), F32),
            square,
            square,
            pltpu.VMEM((count, 4 * width), BF16),
            pltpu.VMEM((LANES, count), F32),
            pltpu.VMEM((LANES, count), F32),
            pltpu.VMEM((width, width), BF16),
            pltpu.SemaphoreType.DMA((10 + 2 * groups,)),
        ],
    )
    def fill_slots(row_grad):
        return call(
            slots_kernel,
            [jax.ShapeDtypeStruct((slots, width), BF16)],
            2 * slots * count * width,
            4 * count * width,
            (slot, row_grad),
            far_out=(0,),
            scratch=[
                pltpu.VMEM((slots, width), BF16),
                pltpu.SemaphoreType.DMA((slots // row_step(slots),)),
            ],
        )[0]

    rows = width // owners
    side = 2 if owners % 4 == 0 else 1
    plane = side * side
    outer = owners // plane
    here = lax.axis_index("table")
    high, middle, low = here // plane, here // side % side, here % side
    sides = []
    for i in range(2):
        terms = [grads[i]] + [shift(grads[2 * k + i], "group", groups, k) for k in range(1, groups)]
        sides.append([term.reshape(outer, side, side, rows, term.shape[1]) for term in terms])

    def entry(value, index, axis):
        return lax.dynamic_index_in_dim(value, index, axis, keepdims=False)

    def add(terms):
        return sum(term.astype(F32) for term in terms)

    def halve(terms, index, axis, bit, tie=None):
        send = add([entry(term, 1 - index, axis) for term in terms]).astype(BF16)
        if tie is not None:
            tie, send = lax.optimization_barrier((tie, send))
        got = lax.ppermute(send, "table", [(i, i ^ bit) for i in range(owners)])
        kept = [entry(term, index, axis) for term in terms]
        return (kept if tie is not None else [add(kept)]) + [got], tie

    if side == 2:
        left, row_grad = halve(sides[0], low, 2, 1, row_grad)
        right, row_grad = halve(sides[1], middle, 1, 2, row_grad)
        outgoing = fill_slots(row_grad)
        outgoing, left[-1], right[-1] = lax.optimization_barrier((outgoing, left[-1], right[-1]))
        left, _ = halve(left, middle, 1, 2)
        right, _ = halve(right, low, 1, 1)
    else:
        outgoing = fill_slots(row_grad)
        left, right = [[term[:, 0, 0] for term in terms] for terms in sides]
    cols = cols_all
    kept, *sends = call(
        functools.partial(plane_kernel, outer, len(left)),
        [
            jax.ShapeDtypeStruct((rows, cols), F32),
            *[jax.ShapeDtypeStruct((rows, cols), BF16) for _ in range(1, outer)],
        ],
        12 * outer * rows * cols,
        160 * outer * rows * cols,
        (*left, *right),
        limit=24,
    )
    got = [
        lax.ppermute(
            sends[k - 1],
            "table",
            [(i, ((i // plane + k) % outer) * plane + i % plane) for i in range(owners)],
        )
        for k in range(1, outer)
    ]

    incoming = lax.all_to_all(outgoing, "table", split_axis=0, concat_axis=0, tiled=True)
    incoming, *got = lax.optimization_barrier((incoming, *got))
    all_incoming = [incoming] + [shift(incoming, "group", groups, k) for k in range(1, groups)]
    grad_rows = table.shape[0] // groups
    (table_grad,) = call(
        functools.partial(collect_kernel, groups),
        [jax.ShapeDtypeStruct((grad_rows, width), F32)],
        2 * slots * table.shape[0] * width,
        2 * groups * slots * width + 4 * grad_rows * width,
        (*all_ids, *all_incoming),
        far=range(groups, 2 * groups),
        far_out=(0,),
        limit=24,
        scratch=[
            *[pltpu.VMEM((slots, width), BF16) for _ in range(groups)],
            pltpu.VMEM((grad_rows, width), F32),
            pltpu.SemaphoreType.DMA((groups + grad_rows // row_step(grad_rows),)),
        ],
    )

    w_in_grad, mine, gain_grad = call(
        finish_kernel,
        [
            jax.ShapeDtypeStruct((rows, cols_in), F32),
            jax.ShapeDtypeStruct((rows, cols_out), F32),
            jax.ShapeDtypeStruct((1, rows), F32),
        ],
        4 * rows * cols_all,
        14 * rows * cols_all,
        (kept, *got),
        limit=24,
    )
    others = [shift(mine, "group", groups, k) for k in range(1, groups)]
    table_grad, *others = lax.optimization_barrier((table_grad, *others))
    pieces = jnp.stack([mine, *others])
    w_out_grad = jnp.concatenate(
        [
            lax.dynamic_index_in_dim(pieces, (me - p) % groups, 0, keepdims=False)
            for p in range(wparts)
        ],
        1,
    )
    return (result, table_grad, w_in_grad, w_out_grad, gain_grad.reshape(rows))


def solution(mesh):
    return jax.shard_map(
        on_device,
        mesh=mesh,
        in_specs=(
            P(("table", "group"), None),
            P(("table", "group")),
            P(("table", "group"), None),
            P("table", None),
            P(),
            P(),
            P(),
            P(("table", "group"), None),
        ),
        out_specs=(
            P(("table", "group"), None),
            P(("table", "group"), None),
            P("table", "group"),
            P("table", None),
            P("table"),
        ),
        check_vma=False,
    )
```

```python
import functools
import math

import jax
import jax.numpy as jnp
from jax import lax
from jax.experimental import pallas as pl
from jax.experimental.pallas import tpu as pltpu
from jax.sharding import PartitionSpec as P

HEAD_DIM = 64
LANES = 128
QUERY_ROWS = 256

F32 = jnp.float32
BF16 = jnp.bfloat16


def iota(shape, dim):
    return lax.broadcasted_iota(jnp.int32, shape, dim)


def hot(cond):
    return jnp.where(cond, 1.0, 0.0).astype(BF16)


def dot_nn(a, b):
    return lax.dot_general(a, b, (((1,), (0,)), ((), ())), preferred_element_type=F32)


def dot_nt(a, b):
    return lax.dot_general(a, b, (((1,), (1,)), ((), ())), preferred_element_type=F32)


def dot_tn(a, b):
    return lax.dot_general(a, b, (((0,), (0,)), ((), ())), preferred_element_type=F32)


def row_step(rows):
    return 256 if rows % 256 == 0 else rows


def call(kernel, out_shape, flops, nbytes, operands, smem=(), far=(), far_out=(), limit=56, scratch=()):
    spaces = [
        pltpu.SMEM if i in smem else pl.ANY if i in far else pltpu.VMEM
        for i in range(len(operands))
    ]
    out_spaces = [pl.ANY if i in far_out else pltpu.VMEM for i in range(len(out_shape))]
    return pl.pallas_call(
        kernel,
        out_shape=out_shape,
        in_specs=[pl.BlockSpec(memory_space=space) for space in spaces],
        out_specs=[pl.BlockSpec(memory_space=space) for space in out_spaces],
        scratch_shapes=scratch,
        compiler_params=pltpu.CompilerParams(vmem_limit_bytes=limit * 1024 * 1024),
        cost_estimate=pl.CostEstimate(flops=flops, bytes_accessed=nbytes, transcendentals=0),
    )(*operands)


def request_kernel(cap, owner_ref, row_ref, req_ref, slot_ref):
    owners, width = req_ref.shape
    count = owner_ref.shape[1]
    owner = owner_ref[...]
    row = row_ref[...]
    mine = iota((owners, count), 0) == owner
    mine_b = hot(mine)
    before = hot(iota((count, count), 0) < iota((count, count), 1))
    earlier = dot_nn(mine_b, before)
    place = jnp.sum(jnp.where(mine, earlier, 0.0), axis=0, keepdims=True)
    slot_ref[...] = owner.astype(F32) * float(cap) + place
    at_place = hot(iota((width, count), 0).astype(F32) == place)
    high = jnp.where(mine, (row >> 8).astype(F32), 0.0).astype(BF16)
    low = jnp.where(mine, (row & 255).astype(F32), 0.0).astype(BF16)
    found = dot_nt(high, at_place) * 256.0 + dot_nt(low, at_place)
    req_ref[...] = found.astype(jnp.int32)


def lookup_kernel(cap, wanted_ref, table_hbm, found_ref, ids_ref, table_ref, pick_ref, sem):
    owners, width = wanted_ref.shape
    slots = found_ref.shape[0]
    rows = table_ref.shape[0]
    fetch = pltpu.make_async_copy(table_hbm, table_ref, sem)
    fetch.start()
    wanted = wanted_ref[...]
    high = (wanted >> 8).astype(F32).astype(BF16)
    low = (wanted & 255).astype(F32).astype(BF16)
    slot = iota((slots, owners), 0).astype(F32)
    holder = jnp.floor((slot + 0.5) * (1.0 / cap))
    spread = hot(holder == iota((slots, owners), 1).astype(F32))
    ids = dot_nn(spread, high) * 256.0 + dot_nn(spread, low)
    slot = iota((slots, width), 0).astype(F32)
    place = slot - jnp.floor((slot + 0.5) * (1.0 / cap)) * float(cap)
    ids = jnp.sum(
        jnp.where(iota((slots, width), 1).astype(F32) == place, ids, 0.0), axis=1, keepdims=True
    )
    wide = jnp.broadcast_to(ids, (slots, LANES))
    ids_ref[...] = wide.T[0:1, :]
    step = row_step(slots)
    for start in range(0, slots, step):
        part = ids[start : start + step]
        pick_ref[start : start + step, :] = hot(iota((step, rows), 1).astype(F32) == part)
    fetch.wait()
    for start in range(0, slots, step):
        found_ref[start : start + step, :] = dot_nn(
            pick_ref[start : start + step, :], table_ref[...]
        ).astype(BF16)


def collect_kernel(groups, *refs):
    ids_refs, in_hbms, out_hbm = refs[:groups], refs[groups : 2 * groups], refs[2 * groups]
    in_refs, out_ref, sems = refs[2 * groups + 1 : 3 * groups + 1], refs[-2], refs[-1]
    rows = out_ref.shape[0]
    slots = in_refs[0].shape[0]
    fetches = [
        pltpu.make_async_copy(hbm, ref, sems.at[n])
        for n, (hbm, ref) in enumerate(zip(in_hbms, in_refs))
    ]
    for fetch in fetches:
        fetch.start()
    base = lax.axis_index("group") * rows
    step = row_step(rows)
    for fetch in fetches:
        fetch.wait()
    stores = []
    for n, start in enumerate(range(0, rows, step)):
        own = (iota((step, slots), 0) + (base + start)).astype(F32)
        total = None
        for ids_ref, in_ref in zip(ids_refs, in_refs):
            part = dot_nn(hot(own == ids_ref[...]), in_ref[...])
            total = part if total is None else total + part
        out_ref[start : start + step, :] = total
        here = pl.ds(start, step)
        stores.append(
            pltpu.make_async_copy(out_ref.at[here], out_hbm.at[here], sems.at[groups + n])
        )
        stores[-1].start()
    for store in stores:
        store.wait()


def layer_kernel(
    groups,
    wparts,
    len_ref,
    slot_ref,
    ret_hbm,
    w_in_hbm,
    w_out_hbm,
    gain_ref,
    cot_hbm,
    *rest,
):
    result_hbm, row_hbm = rest[:2]
    grads_hbms = rest[2 : 2 + 2 * groups]
    (
    ret_ref,
    w_in_ref,
    w_out_ref,
    cot_ref,
    result_ref,
    row_ref,
    grads_ref,
    pick_ref,
    emb_ref,
    proj_ref,
    slope_ref,
    bias_ref,
    weight_ref,
    wslope_ref,
    att_ref,
    mixed_ref,
    gatt_ref,
    gpre_ref,
    gval_ref,
    gkey_ref,
    gwo_ref,
    sems,
    ) = rest[2 + 2 * groups :]
    count, width = cot_ref.shape
    slots = ret_hbm.shape[0]
    per = LANES // HEAD_DIM
    slabs = width // LANES
    qrows = QUERY_ROWS if count % QUERY_ROWS == 0 else count
    half_scale = 0.5 / math.sqrt(HEAD_DIM)

    get_ret = pltpu.make_async_copy(ret_hbm, ret_ref, sems.at[8 + 2 * groups])
    get_ret.start()
    parts = [pl.ds(i * width, width) for i in range(4)]
    get_ins = [
        pltpu.make_async_copy(w_in_hbm.at[:, part], w_in_ref.at[:, part], sems.at[i])
        for i, part in enumerate(parts)
    ]
    get_cot = pltpu.make_async_copy(cot_hbm, cot_ref, sems.at[4])
    get_out = pltpu.make_async_copy(w_out_hbm, w_out_ref, sems.at[5])
    for fetch in (*get_ins, get_cot, get_out):
        fetch.start()

    slot = jnp.broadcast_to(slot_ref[...], (LANES, count)).T
    for start in range(0, slots, LANES):
        pick_ref[:, start : start + LANES] = hot(
            slot == (iota((count, LANES), 1) + start).astype(F32)
        )
    get_ret.wait()
    emb_ref[...] = dot_nn(pick_ref[...], ret_ref[...]).astype(BF16)

    for fetch in (*get_ins, get_cot, get_out):
        fetch.wait()
    for i in range(4):
        pre = dot_nn(emb_ref[...], w_in_ref[:, parts[i]])
        half = 0.5 * pre
        th = jnp.tanh(half)
        act = half + half * th
        proj_ref[i] = act.astype(BF16)
        slope_ref[i] = 0.5 * ((1.0 + th) + act * (1.0 - th))

    pos = iota((count, 1), 0)
    begin = jnp.zeros((count, 1), jnp.int32)
    end = jnp.int32(0)
    for s in range(len_ref.shape[1]):
        end = end + len_ref[0, s]
        begin = jnp.where(pos >= end, end, begin)
    key = iota((count, count), 1)
    allowed = (key >= begin) & (key <= iota((count, count), 0))
    bias_ref[...] = jnp.where(allowed, 3.0e38, -30.0)

    lane = iota((qrows, LANES), 1)
    inside = [(lane >= a * HEAD_DIM) & (lane < (a + 1) * HEAD_DIM) for a in range(per)]
    lane = iota((count, LANES), 1)
    inside_all = [(lane >= a * HEAD_DIM) & (lane < (a + 1) * HEAD_DIM) for a in range(per)]

    def stacked(value, factor=1.0):
        value = value.astype(F32) * factor
        return jnp.concatenate([jnp.where(m, value, 0.0) for m in inside], 0).astype(BF16)

    row = iota((LANES, qrows), 0)
    inside_rows = [(row >= a * HEAD_DIM) & (row < (a + 1) * HEAD_DIM) for a in range(per)]

    def stacked_t(value, factor=1.0):
        value = (value.astype(F32) * factor).T
        return jnp.concatenate([jnp.where(m, value, 0.0) for m in inside_rows], 1).astype(BF16)

    def apart(value):
        value = value.astype(F32)
        return [jnp.where(m, value, 0.0).astype(BF16) for m in inside_all]

    def forward(p, _):
        cols = pl.ds(pl.multiple_of(p * LANES, LANES), LANES)
        key_all = proj_ref[3, :, cols]
        vals = apart(proj_ref[1, :, cols])
        for r0 in range(0, count, qrows):
            r1 = r0 + qrows
            half = dot_nt(stacked(proj_ref[2, r0:r1, cols], half_scale), key_all[:r1])
            half = jnp.minimum(half.reshape(per, qrows, r1), bias_ref[r0:r1, :r1][None])
            th = jnp.tanh(half)
            weight = half + half * th
            weight_b = weight.astype(BF16)
            base = per * r0
            weight_ref[p, base : base + per * qrows, :r1] = weight_b.reshape(per * qrows, r1)
            wslope_ref[p, base : base + per * qrows, :r1] = (
                (1.0 + th) + weight * (1.0 - th)
            ).reshape(per * qrows, r1)
            total = dot_nn(weight_b[0], vals[0][:r1])
            for a in range(1, per):
                total = total + dot_nn(weight_b[a], vals[a][:r1])
            att_ref[r0:r1, cols] = total
        return 0

    lax.fori_loop(0, slabs, forward, 0, unroll=4)

    gain = gain_ref[...]
    gain_sum = jnp.zeros((1, width), F32)
    for r0 in range(0, count, qrows):
        rows = slice(r0, r0 + qrows)
        att = att_ref[rows, :]
        centered = att - jnp.mean(att, 1, keepdims=True)
        inv = lax.rsqrt(jnp.mean(centered * centered, 1, keepdims=True) + 1e-05)
        normed = centered * inv
        upd = proj_ref[0, rows, :].astype(F32)
        scaled = normed * gain
        mixed = (scaled * upd).astype(BF16)
        mixed_ref[rows, :] = mixed
        result_ref[rows, :] = (
            emb_ref[rows, :].astype(F32) + dot_nn(mixed, w_out_ref[...])
        ).astype(BF16)
        gmix = dot_nt(cot_ref[rows, :], w_out_ref[...]).astype(BF16).astype(F32)
        gpre_ref[rows, 0:width] = (gmix * scaled * slope_ref[0, rows, :]).astype(BF16)
        gnorm = gmix * gain * upd
        gain_sum = gain_sum + jnp.sum(gmix * normed * upd, 0, keepdims=True)
        mean1 = jnp.mean(gnorm, 1, keepdims=True)
        mean2 = jnp.mean(gnorm * normed, 1, keepdims=True)
        gatt_ref[rows, :] = ((gnorm - mean1 - normed * mean2) * inv).astype(BF16)
    gwo_ref[...] = dot_tn(mixed_ref[...], cot_ref[...]).astype(BF16)

    def backward(p, _):
        start = pl.multiple_of(p * LANES, LANES)
        cols = pl.ds(start, LANES)
        val = proj_ref[1, :, cols]
        keys = apart(proj_ref[3, :, cols])
        for r0 in reversed(range(0, count, qrows)):
            r1 = r0 + qrows
            base = per * r0
            rows = slice(base, base + per * qrows)
            gatt = stacked(gatt_ref[r0:r1, cols])
            gweight = dot_nt(gatt, val[:r1])
            gscore = (gweight * wslope_ref[p, rows, :r1]).astype(BF16)
            gqry = dot_nn(gscore[:qrows], keys[0][:r1])
            for a in range(1, per):
                gqry = gqry + dot_nn(gscore[a * qrows : (a + 1) * qrows], keys[a][:r1])
            gval = dot_nn(stacked_t(gatt_ref[r0:r1, cols]), weight_ref[p, rows, :r1])
            gkey = dot_nn(stacked_t(proj_ref[2, r0:r1, cols], half_scale), gscore)
            if r1 == count:
                gval_ref[...] = gval
                gkey_ref[...] = gkey
            else:
                gval_ref[:, :r1] += gval
                gkey_ref[:, :r1] += gkey
            gpre_ref[r0:r1, pl.ds(2 * width + start, LANES)] = (
                gqry * half_scale * slope_ref[2, r0:r1, cols]
            ).astype(BF16)
        gpre_ref[:, pl.ds(width + start, LANES)] = (gval_ref[...].T * slope_ref[1, :, cols]).astype(BF16)
        gpre_ref[:, pl.ds(3 * width + start, LANES)] = (gkey_ref[...].T * slope_ref[3, :, cols]).astype(BF16)
        return 0

    lax.fori_loop(0, slabs, backward, 0, unroll=4)

    put_result = pltpu.make_async_copy(result_ref, result_hbm, sems.at[6])
    put_result.start()
    puts = [put_result]
    me = lax.axis_index("group")
    emb_t = emb_ref[...].T
    cols_in = 4 * width // groups
    cols_out = width // wparts
    chunk = min(cols_in, 512)
    gain_col = jnp.broadcast_to(gain_sum, (LANES, width)).T.astype(BF16)
    for k in [*range(1, groups), 0]:
        part = lax.rem(me + k, groups)
        for c in range(0, cols_in, chunk):
            cols = pl.ds(pl.multiple_of(part * cols_in + c, LANES), chunk)
            grads_ref[k, :, c : c + chunk] = dot_nn(emb_t, gpre_ref[:, cols]).astype(BF16)
        cols = pl.ds(pl.multiple_of(lax.rem(part, wparts) * cols_out, LANES), cols_out)
        grads_ref[k, :, cols_in : cols_in + cols_out] = gwo_ref[:, cols]
        grads_ref[k, :, cols_in + cols_out :] = gain_col
    cut = grads_hbms[0].shape[1]
    for k in range(groups):
        for i, cols in enumerate((pl.ds(0, cut), pl.ds(cut, grads_ref.shape[2] - cut))):
            put = pltpu.make_async_copy(
                grads_ref.at[k, :, cols], grads_hbms[2 * k + i], sems.at[8 + 2 * k + i]
            )
            put.start()
            puts.append(put)
    for i, r0 in enumerate((0, count // 2)):
        rows = pl.ds(r0, count // 2)
        row_ref[rows, :] = (
            cot_ref[rows, :].astype(F32) + dot_nt(gpre_ref[rows, :], w_in_ref[...])
        ).astype(BF16)
        sem = sems.at[7 + i * (2 + 2 * groups)]
        puts.append(pltpu.make_async_copy(row_ref.at[rows], row_hbm.at[rows], sem))
        puts[-1].start()
    for put in puts:
        put.wait()


def slots_kernel(slot_ref, grad_ref, out_hbm, out_ref, sems):
    count = grad_ref.shape[0]
    slots = out_ref.shape[0]
    step = row_step(slots)
    stores = []
    for n, start in enumerate(range(0, slots, step)):
        put = hot((iota((step, count), 0) + start).astype(F32) == slot_ref[...])
        out_ref[start : start + step, :] = dot_nn(put, grad_ref[...]).astype(BF16)
        here = pl.ds(start, step)
        stores.append(pltpu.make_async_copy(out_ref.at[here], out_hbm.at[here], sems.at[n]))
        stores[-1].start()
    for store in stores:
        store.wait()


def plane_kernel(outer, terms, *refs):
    left, right, outs = refs[:terms], refs[terms : 2 * terms], refs[2 * terms :]
    cut = left[0].shape[2]
    high = lax.div(lax.axis_index("table"), lax.axis_size("table") // outer)
    for k in range(outer):
        at = lax.rem(high + k, outer)
        for parts, cols in ((left, slice(0, cut)), (right, slice(cut, None))):
            total = parts[0][at].astype(F32)
            for part in parts[1:]:
                total = total + part[at].astype(F32)
            outs[k][:, cols] = total.astype(outs[k].dtype)


def finish_kernel(kept_ref, *refs):
    got_refs, (in_ref, out_ref, gain_ref) = refs[:-3], refs[-3:]
    total = kept_ref[...]
    for got_ref in got_refs:
        total = total + got_ref[...].astype(F32)
    cols_in, cols_out = in_ref.shape[1], out_ref.shape[1]
    in_ref[...] = total[:, :cols_in]
    out_ref[...] = total[:, cols_in : cols_in + cols_out]
    gain_ref[...] = total[:, cols_in + cols_out :].T[0:1, :]


def shift(value, axis, size, amount):
    return lax.ppermute(value, axis, [(i, (i + amount) % size) for i in range(size)])


def on_device(item_owner, item_row, lengths, table, w_in, w_out, gain, cotangent):
    owners = lax.axis_size("table")
    groups = lax.axis_size("group")
    count = item_row.shape[0]
    width = table.shape[1]
    capacity = max(2, 3 * count // (2 * owners))
    slots = owners * capacity
    padded = -(-capacity // LANES) * LANES
    me = lax.axis_index("group")

    requested, slot = call(
        functools.partial(request_kernel, capacity),
        [
            jax.ShapeDtypeStruct((owners, padded), jnp.int32),
            jax.ShapeDtypeStruct((1, count), F32),
        ],
        4 * count * count * owners,
        8 * count,
        (item_owner.reshape(1, count), item_row.reshape(1, count)),
    )
    wanted = lax.all_to_all(requested, "table", split_axis=0, concat_axis=0, tiled=True)
    found, ids = call(
        functools.partial(lookup_kernel, capacity),
        [
            jax.ShapeDtypeStruct((slots, width), BF16),
            jax.ShapeDtypeStruct((1, slots), F32),
        ],
        2 * slots * table.shape[0] * width,
        2 * (slots + table.shape[0]) * width,
        (wanted, table),
        far=(1,),
        scratch=[
            pltpu.VMEM(table.shape, BF16),
            pltpu.VMEM((slots, table.shape[0]), BF16),
            pltpu.SemaphoreType.DMA,
        ],
    )
    returned = lax.all_to_all(found, "table", split_axis=0, concat_axis=0, tiled=True)
    all_ids = [ids] + [shift(ids, "group", groups, k) for k in range(1, groups)]
    returned, *all_ids = lax.optimization_barrier((returned, *all_ids))

    wparts = min(groups, width // LANES)
    heads_per = LANES // HEAD_DIM
    cols_in = 4 * width // groups
    cols_out = width // wparts
    cols_all = cols_in + cols_out + LANES
    cut = cols_all // LANES // 2 * LANES
    square = pltpu.VMEM((count, width), BF16)
    result, row_grad, *grads = call(
        functools.partial(layer_kernel, groups, wparts),
        [
            jax.ShapeDtypeStruct((count, width), BF16),
            jax.ShapeDtypeStruct((count, width), BF16),
            *[
                jax.ShapeDtypeStruct((width, cols), BF16)
                for _ in range(groups)
                for cols in (cut, cols_all - cut)
            ],
        ],
        32 * count * width * width + 14 * count * count * width,
        24 * count * width,
        (lengths, slot, returned, w_in, w_out, gain.reshape(1, width), cotangent),
        smem=(0,),
        far=(2, 3, 4, 6),
        far_out=range(2 + 2 * groups),
        scratch=[
            pltpu.VMEM((slots, width), BF16),
            pltpu.VMEM(w_in.shape, BF16),
            pltpu.VMEM(w_out.shape, BF16),
            square,
            square,
            square,
            pltpu.VMEM((groups, width, cols_all), BF16),
            pltpu.VMEM((count, slots), BF16),
            square,
            pltpu.VMEM((4, count, width), BF16),
            pltpu.VMEM((4, count, width), F32),
            pltpu.VMEM((count, count), F32),
            pltpu.VMEM((width // LANES, heads_per * count, count), BF16),
            pltpu.VMEM((width // LANES, heads_per * count, count), F32),
            pltpu.VMEM((count, width), F32),
            square,
            square,
            pltpu.VMEM((count, 4 * width), BF16),
            pltpu.VMEM((LANES, count), F32),
            pltpu.VMEM((LANES, count), F32),
            pltpu.VMEM((width, width), BF16),
            pltpu.SemaphoreType.DMA((10 + 2 * groups,)),
        ],
    )
    (outgoing,) = call(
        slots_kernel,
        [jax.ShapeDtypeStruct((slots, width), BF16)],
        2 * slots * count * width,
        4 * count * width,
        (slot, row_grad),
        far_out=(0,),
        scratch=[
            pltpu.VMEM((slots, width), BF16),
            pltpu.SemaphoreType.DMA((slots // row_step(slots),)),
        ],
    )

    rows = width // owners
    side = 2 if owners % 4 == 0 else 1
    plane = side * side
    outer = owners // plane
    here = lax.axis_index("table")
    high, middle, low = here // plane, here // side % side, here % side
    sides = []
    for i in range(2):
        terms = [grads[i]] + [shift(grads[2 * k + i], "group", groups, k) for k in range(1, groups)]
        sides.append([term.reshape(outer, side, side, rows, term.shape[1]) for term in terms])

    def entry(value, index, axis):
        return lax.dynamic_index_in_dim(value, index, axis, keepdims=False)

    def add(terms):
        return sum(term.astype(F32) for term in terms)

    def halve(terms, index, axis, bit, last):
        send = add([entry(term, 1 - index, axis) for term in terms]).astype(BF16)
        got = lax.ppermute(send, "table", [(i, i ^ bit) for i in range(owners)])
        kept = [entry(term, index, axis) for term in terms]
        return ([add(kept)] if last else kept) + [got]

    if side == 2:
        left = halve(sides[0], low, 2, 1, False)
        right = halve(sides[1], middle, 1, 2, False)
        left = halve(left, middle, 1, 2, True)
        right = halve(right, low, 1, 1, True)
    else:
        left, right = [[term[:, 0, 0] for term in terms] for terms in sides]
    cols = cols_all
    kept, *sends = call(
        functools.partial(plane_kernel, outer, len(left)),
        [
            jax.ShapeDtypeStruct((rows, cols), F32),
            *[jax.ShapeDtypeStruct((rows, cols), BF16) for _ in range(1, outer)],
        ],
        12 * outer * rows * cols,
        8 * outer * rows * cols,
        (*left, *right),
        limit=24,
    )
    got = [
        lax.ppermute(
            sends[k - 1],
            "table",
            [(i, ((i // plane + k) % outer) * plane + i % plane) for i in range(owners)],
        )
        for k in range(1, outer)
    ]

    incoming = lax.all_to_all(outgoing, "table", split_axis=0, concat_axis=0, tiled=True)
    incoming, kept = lax.optimization_barrier((incoming, kept))
    all_incoming = [incoming] + [shift(incoming, "group", groups, k) for k in range(1, groups)]
    grad_rows = table.shape[0] // groups
    (table_grad,) = call(
        functools.partial(collect_kernel, groups),
        [jax.ShapeDtypeStruct((grad_rows, width), F32)],
        2 * slots * table.shape[0] * width,
        2 * groups * slots * width + 4 * grad_rows * width,
        (*all_ids, *all_incoming),
        far=range(groups, 2 * groups),
        far_out=(0,),
        limit=24,
        scratch=[
            *[pltpu.VMEM((slots, width), BF16) for _ in range(groups)],
            pltpu.VMEM((grad_rows, width), F32),
            pltpu.SemaphoreType.DMA((groups + grad_rows // row_step(grad_rows),)),
        ],
    )

    kept, table_grad = lax.optimization_barrier((kept, table_grad))
    w_in_grad, mine, gain_grad = call(
        finish_kernel,
        [
            jax.ShapeDtypeStruct((rows, cols_in), F32),
            jax.ShapeDtypeStruct((rows, cols_out), F32),
            jax.ShapeDtypeStruct((1, rows), F32),
        ],
        4 * rows * cols_all,
        14 * rows * cols_all,
        (kept, *got),
        limit=24,
    )
    others = [shift(mine, "group", groups, k) for k in range(1, groups)]
    pieces = jnp.stack([mine, *others])
    w_out_grad = jnp.concatenate(
        [
            lax.dynamic_index_in_dim(pieces, (me - p) % groups, 0, keepdims=False)
            for p in range(wparts)
        ],
        1,
    )
    return (result, table_grad, w_in_grad, w_out_grad, gain_grad.reshape(rows))


def solution(mesh):
    return jax.shard_map(
        on_device,
        mesh=mesh,
        in_specs=(
            P(("table", "group"), None),
            P(("table", "group")),
            P(("table", "group"), None),
            P("table", None),
            P(),
            P(),
            P(),
            P(("table", "group"), None),
        ),
        out_specs=(
            P(("table", "group"), None),
            P(("table", "group"), None),
            P("table", "group"),
            P("table", None),
            P("table"),
        ),
        check_vma=False,
    )
```

```python
import functools
import math

import jax
import jax.numpy as jnp
from jax import lax
from jax.experimental import pallas as pl
from jax.experimental.pallas import tpu as pltpu
from jax.sharding import PartitionSpec as P

HEAD_DIM = 64
LANES = 128
QUERY_ROWS = 128

F32 = jnp.float32
BF16 = jnp.bfloat16


def iota(shape, dim):
    return lax.broadcasted_iota(jnp.int32, shape, dim)


def hot(cond):
    return jnp.where(cond, 1.0, 0.0).astype(BF16)


def dot_nn(a, b):
    return lax.dot_general(a, b, (((1,), (0,)), ((), ())), preferred_element_type=F32)


def dot_nt(a, b):
    return lax.dot_general(a, b, (((1,), (1,)), ((), ())), preferred_element_type=F32)


def dot_tn(a, b):
    return lax.dot_general(a, b, (((0,), (0,)), ((), ())), preferred_element_type=F32)


def row_step(rows):
    return 256 if rows % 256 == 0 else rows


def call(kernel, out_shape, flops, nbytes, operands, smem=(), far=(), far_out=(), limit=56, scratch=()):
    spaces = [
        pltpu.SMEM if i in smem else pl.ANY if i in far else pltpu.VMEM
        for i in range(len(operands))
    ]
    out_spaces = [pl.ANY if i in far_out else pltpu.VMEM for i in range(len(out_shape))]
    return pl.pallas_call(
        kernel,
        out_shape=out_shape,
        in_specs=[pl.BlockSpec(memory_space=space) for space in spaces],
        out_specs=[pl.BlockSpec(memory_space=space) for space in out_spaces],
        scratch_shapes=scratch,
        compiler_params=pltpu.CompilerParams(vmem_limit_bytes=limit * 1024 * 1024),
        cost_estimate=pl.CostEstimate(flops=flops, bytes_accessed=nbytes, transcendentals=0),
    )(*operands)


def request_kernel(cap, owner_ref, row_ref, req_ref, slot_ref):
    owners, width = req_ref.shape
    count = owner_ref.shape[1]
    owner = owner_ref[...]
    row = row_ref[...]
    mine = iota((owners, count), 0) == owner
    mine_b = hot(mine)
    before = hot(iota((count, count), 0) < iota((count, count), 1))
    earlier = dot_nn(mine_b, before)
    place = jnp.sum(jnp.where(mine, earlier, 0.0), axis=0, keepdims=True)
    slot_ref[...] = owner.astype(F32) * float(cap) + place
    at_place = hot(iota((width, count), 0).astype(F32) == place)
    high = jnp.where(mine, (row >> 8).astype(F32), 0.0).astype(BF16)
    low = jnp.where(mine, (row & 255).astype(F32), 0.0).astype(BF16)
    found = dot_nt(high, at_place) * 256.0 + dot_nt(low, at_place)
    req_ref[...] = found.astype(jnp.int32)


def lookup_kernel(cap, wanted_ref, table_ref, found_ref, ids_ref):
    owners, width = wanted_ref.shape
    slots = found_ref.shape[0]
    rows = table_ref.shape[0]
    wanted = wanted_ref[...]
    high = (wanted >> 8).astype(F32).astype(BF16)
    low = (wanted & 255).astype(F32).astype(BF16)
    slot = iota((slots, owners), 0).astype(F32)
    holder = jnp.floor((slot + 0.5) * (1.0 / cap))
    spread = hot(holder == iota((slots, owners), 1).astype(F32))
    ids = dot_nn(spread, high) * 256.0 + dot_nn(spread, low)
    slot = iota((slots, width), 0).astype(F32)
    place = slot - jnp.floor((slot + 0.5) * (1.0 / cap)) * float(cap)
    ids = jnp.sum(
        jnp.where(iota((slots, width), 1).astype(F32) == place, ids, 0.0), axis=1, keepdims=True
    )
    wide = jnp.broadcast_to(ids, (slots, LANES))
    ids_ref[...] = wide.T[0:1, :]
    step = 256 if slots % 256 == 0 else slots
    for start in range(0, slots, step):
        part = ids[start : start + step]
        pick = hot(iota((step, rows), 1).astype(F32) == part)
        found_ref[start : start + step, :] = dot_nn(pick, table_ref[...]).astype(BF16)


def collect_kernel(groups, *refs):
    ids_refs, in_hbms, out_hbm = refs[:groups], refs[groups : 2 * groups], refs[2 * groups]
    in_refs, out_ref, sems = refs[2 * groups + 1 : 3 * groups + 1], refs[-2], refs[-1]
    rows = out_ref.shape[0]
    slots = in_refs[0].shape[0]
    fetches = [
        pltpu.make_async_copy(hbm, ref, sems.at[n])
        for n, (hbm, ref) in enumerate(zip(in_hbms, in_refs))
    ]
    for fetch in fetches:
        fetch.start()
    base = lax.axis_index("group") * rows
    step = row_step(rows)
    for fetch in fetches:
        fetch.wait()
    stores = []
    for n, start in enumerate(range(0, rows, step)):
        own = (iota((step, slots), 0) + (base + start)).astype(F32)
        total = None
        for ids_ref, in_ref in zip(ids_refs, in_refs):
            part = dot_nn(hot(own == ids_ref[...]), in_ref[...])
            total = part if total is None else total + part
        out_ref[start : start + step, :] = total
        here = pl.ds(start, step)
        stores.append(
            pltpu.make_async_copy(out_ref.at[here], out_hbm.at[here], sems.at[groups + n])
        )
        stores[-1].start()
    for store in stores:
        store.wait()


def layer_kernel(
    groups,
    wparts,
    len_ref,
    slot_ref,
    ret_hbm,
    w_in_hbm,
    w_out_hbm,
    gain_ref,
    cot_hbm,
    *rest,
):
    result_hbm, row_hbm = rest[:2]
    grads_hbms = rest[2 : 2 + 2 * groups]
    (
    ret_ref,
    w_in_ref,
    w_out_ref,
    cot_ref,
    result_ref,
    row_ref,
    grads_ref,
    pick_ref,
    emb_ref,
    proj_ref,
    slope_ref,
    bias_ref,
    weight_ref,
    wslope_ref,
    att_ref,
    mixed_ref,
    gatt_ref,
    gpre_ref,
    gval_ref,
    gkey_ref,
    gwo_ref,
    sems,
    ) = rest[2 + 2 * groups :]
    count, width = cot_ref.shape
    slots = ret_hbm.shape[0]
    per = LANES // HEAD_DIM
    slabs = width // LANES
    qrows = QUERY_ROWS if count % QUERY_ROWS == 0 else count
    half_scale = 0.5 / math.sqrt(HEAD_DIM)

    get_ret = pltpu.make_async_copy(ret_hbm, ret_ref, sems.at[8 + 2 * groups])
    get_ret.start()
    parts = [pl.ds(i * width, width) for i in range(4)]
    get_ins = [
        pltpu.make_async_copy(w_in_hbm.at[:, part], w_in_ref.at[:, part], sems.at[i])
        for i, part in enumerate(parts)
    ]
    get_cot = pltpu.make_async_copy(cot_hbm, cot_ref, sems.at[4])
    get_out = pltpu.make_async_copy(w_out_hbm, w_out_ref, sems.at[5])
    for fetch in (*get_ins, get_cot, get_out):
        fetch.start()

    slot = jnp.broadcast_to(slot_ref[...], (LANES, count)).T
    for start in range(0, slots, LANES):
        pick_ref[:, start : start + LANES] = hot(
            slot == (iota((count, LANES), 1) + start).astype(F32)
        )
    get_ret.wait()
    emb_ref[...] = dot_nn(pick_ref[...], ret_ref[...]).astype(BF16)

    for fetch in (*get_ins, get_cot, get_out):
        fetch.wait()
    for i in range(4):
        pre = dot_nn(emb_ref[...], w_in_ref[:, parts[i]])
        half = 0.5 * pre
        th = jnp.tanh(half)
        act = half + half * th
        proj_ref[i] = act.astype(BF16)
        slope_ref[i] = 0.5 * ((1.0 + th) + act * (1.0 - th))

    pos = iota((count, 1), 0)
    begin = jnp.zeros((count, 1), jnp.int32)
    end = jnp.int32(0)
    for s in range(len_ref.shape[1]):
        end = end + len_ref[0, s]
        begin = jnp.where(pos >= end, end, begin)
    key = iota((count, count), 1)
    allowed = (key >= begin) & (key <= iota((count, count), 0))
    bias_ref[...] = jnp.where(allowed, 3.0e38, -30.0)

    lane = iota((qrows, LANES), 1)
    inside = [(lane >= a * HEAD_DIM) & (lane < (a + 1) * HEAD_DIM) for a in range(per)]
    lane = iota((count, LANES), 1)
    inside_all = [(lane >= a * HEAD_DIM) & (lane < (a + 1) * HEAD_DIM) for a in range(per)]

    def stacked(value, factor=1.0):
        value = value.astype(F32) * factor
        return jnp.concatenate([jnp.where(m, value, 0.0) for m in inside], 0).astype(BF16)

    row = iota((LANES, qrows), 0)
    inside_rows = [(row >= a * HEAD_DIM) & (row < (a + 1) * HEAD_DIM) for a in range(per)]

    def stacked_t(value, factor=1.0):
        value = (value.astype(F32) * factor).T
        return jnp.concatenate([jnp.where(m, value, 0.0) for m in inside_rows], 1).astype(BF16)

    def apart(value):
        value = value.astype(F32)
        return [jnp.where(m, value, 0.0).astype(BF16) for m in inside_all]

    def forward(p, _):
        cols = pl.ds(pl.multiple_of(p * LANES, LANES), LANES)
        key_all = proj_ref[3, :, cols]
        vals = apart(proj_ref[1, :, cols])
        for r0 in range(0, count, qrows):
            r1 = r0 + qrows
            half = dot_nt(stacked(proj_ref[2, r0:r1, cols], half_scale), key_all[:r1])
            half = jnp.minimum(half.reshape(per, qrows, r1), bias_ref[r0:r1, :r1][None])
            th = jnp.tanh(half)
            weight = half + half * th
            weight_b = weight.astype(BF16)
            base = per * r0
            weight_ref[p, base : base + per * qrows, :r1] = weight_b.reshape(per * qrows, r1)
            wslope_ref[p, base : base + per * qrows, :r1] = (
                (1.0 + th) + weight * (1.0 - th)
            ).reshape(per * qrows, r1)
            total = dot_nn(weight_b[0], vals[0][:r1])
            for a in range(1, per):
                total = total + dot_nn(weight_b[a], vals[a][:r1])
            att_ref[r0:r1, cols] = total
        return 0

    lax.fori_loop(0, slabs, forward, 0, unroll=4)

    gain = gain_ref[...]
    gain_sum = jnp.zeros((1, width), F32)
    for r0 in range(0, count, qrows):
        rows = slice(r0, r0 + qrows)
        att = att_ref[rows, :]
        centered = att - jnp.mean(att, 1, keepdims=True)
        inv = lax.rsqrt(jnp.mean(centered * centered, 1, keepdims=True) + 1e-05)
        normed = centered * inv
        upd = proj_ref[0, rows, :].astype(F32)
        scaled = normed * gain
        mixed = (scaled * upd).astype(BF16)
        mixed_ref[rows, :] = mixed
        result_ref[rows, :] = (
            emb_ref[rows, :].astype(F32) + dot_nn(mixed, w_out_ref[...])
        ).astype(BF16)
        gmix = dot_nt(cot_ref[rows, :], w_out_ref[...]).astype(BF16).astype(F32)
        gpre_ref[rows, 0:width] = (gmix * scaled * slope_ref[0, rows, :]).astype(BF16)
        gnorm = gmix * gain * upd
        gain_sum = gain_sum + jnp.sum(gmix * normed * upd, 0, keepdims=True)
        mean1 = jnp.mean(gnorm, 1, keepdims=True)
        mean2 = jnp.mean(gnorm * normed, 1, keepdims=True)
        gatt_ref[rows, :] = ((gnorm - mean1 - normed * mean2) * inv).astype(BF16)
    gwo_ref[...] = dot_tn(mixed_ref[...], cot_ref[...]).astype(BF16)

    def backward(p, _):
        start = pl.multiple_of(p * LANES, LANES)
        cols = pl.ds(start, LANES)
        val = proj_ref[1, :, cols]
        keys = apart(proj_ref[3, :, cols])
        for r0 in reversed(range(0, count, qrows)):
            r1 = r0 + qrows
            base = per * r0
            rows = slice(base, base + per * qrows)
            gatt = stacked(gatt_ref[r0:r1, cols])
            gweight = dot_nt(gatt, val[:r1])
            gscore = (gweight * wslope_ref[p, rows, :r1]).astype(BF16)
            gqry = dot_nn(gscore[:qrows], keys[0][:r1])
            for a in range(1, per):
                gqry = gqry + dot_nn(gscore[a * qrows : (a + 1) * qrows], keys[a][:r1])
            gval = dot_nn(stacked_t(gatt_ref[r0:r1, cols]), weight_ref[p, rows, :r1])
            gkey = dot_nn(stacked_t(proj_ref[2, r0:r1, cols], half_scale), gscore)
            if r1 == count:
                gval_ref[...] = gval
                gkey_ref[...] = gkey
            else:
                gval_ref[:, :r1] += gval
                gkey_ref[:, :r1] += gkey
            gpre_ref[r0:r1, pl.ds(2 * width + start, LANES)] = (
                gqry * half_scale * slope_ref[2, r0:r1, cols]
            ).astype(BF16)
        gpre_ref[:, pl.ds(width + start, LANES)] = (gval_ref[...].T * slope_ref[1, :, cols]).astype(BF16)
        gpre_ref[:, pl.ds(3 * width + start, LANES)] = (gkey_ref[...].T * slope_ref[3, :, cols]).astype(BF16)
        return 0

    lax.fori_loop(0, slabs, backward, 0, unroll=4)

    put_result = pltpu.make_async_copy(result_ref, result_hbm, sems.at[6])
    put_result.start()
    puts = [put_result]
    me = lax.axis_index("group")
    emb_t = emb_ref[...].T
    cols_in = 4 * width // groups
    cols_out = width // wparts
    chunk = min(cols_in, 512)
    gain_col = jnp.broadcast_to(gain_sum, (LANES, width)).T.astype(BF16)
    for k in [*range(1, groups), 0]:
        part = lax.rem(me + k, groups)
        for c in range(0, cols_in, chunk):
            cols = pl.ds(pl.multiple_of(part * cols_in + c, LANES), chunk)
            grads_ref[k, :, c : c + chunk] = dot_nn(emb_t, gpre_ref[:, cols]).astype(BF16)
        cols = pl.ds(pl.multiple_of(lax.rem(part, wparts) * cols_out, LANES), cols_out)
        grads_ref[k, :, cols_in : cols_in + cols_out] = gwo_ref[:, cols]
        grads_ref[k, :, cols_in + cols_out :] = gain_col
        cut = grads_hbms[2 * k].shape[1]
        for i, cols in enumerate((pl.ds(0, cut), pl.ds(cut, grads_ref.shape[2] - cut))):
            put = pltpu.make_async_copy(
                grads_ref.at[k, :, cols], grads_hbms[2 * k + i], sems.at[8 + 2 * k + i]
            )
            put.start()
            puts.append(put)
    for i, r0 in enumerate((0, count // 2)):
        rows = pl.ds(r0, count // 2)
        row_ref[rows, :] = (
            cot_ref[rows, :].astype(F32) + dot_nt(gpre_ref[rows, :], w_in_ref[...])
        ).astype(BF16)
        sem = sems.at[7 + i * (2 + 2 * groups)]
        puts.append(pltpu.make_async_copy(row_ref.at[rows], row_hbm.at[rows], sem))
        puts[-1].start()
    for put in puts:
        put.wait()


def slots_kernel(slot_ref, grad_ref, out_hbm, out_ref, sems):
    count = grad_ref.shape[0]
    slots = out_ref.shape[0]
    step = row_step(slots)
    stores = []
    for n, start in enumerate(range(0, slots, step)):
        put = hot((iota((step, count), 0) + start).astype(F32) == slot_ref[...])
        out_ref[start : start + step, :] = dot_nn(put, grad_ref[...]).astype(BF16)
        here = pl.ds(start, step)
        stores.append(pltpu.make_async_copy(out_ref.at[here], out_hbm.at[here], sems.at[n]))
        stores[-1].start()
    for store in stores:
        store.wait()


def plane_kernel(outer, terms, *refs):
    left, right, outs = refs[:terms], refs[terms : 2 * terms], refs[2 * terms :]
    cut = left[0].shape[2]
    high = lax.div(lax.axis_index("table"), lax.axis_size("table") // outer)
    for k in range(outer):
        at = lax.rem(high + k, outer)
        for parts, cols in ((left, slice(0, cut)), (right, slice(cut, None))):
            total = parts[0][at].astype(F32)
            for part in parts[1:]:
                total = total + part[at].astype(F32)
            outs[k][:, cols] = total.astype(outs[k].dtype)


def finish_kernel(kept_ref, *refs):
    got_refs, (in_ref, out_ref, gain_ref) = refs[:-3], refs[-3:]
    total = kept_ref[...]
    for got_ref in got_refs:
        total = total + got_ref[...].astype(F32)
    cols_in, cols_out = in_ref.shape[1], out_ref.shape[1]
    in_ref[...] = total[:, :cols_in]
    out_ref[...] = total[:, cols_in : cols_in + cols_out]
    gain_ref[...] = total[:, cols_in + cols_out :].T[0:1, :]


def shift(value, axis, size, amount):
    return lax.ppermute(value, axis, [(i, (i + amount) % size) for i in range(size)])


def on_device(item_owner, item_row, lengths, table, w_in, w_out, gain, cotangent):
    owners = lax.axis_size("table")
    groups = lax.axis_size("group")
    count = item_row.shape[0]
    width = table.shape[1]
    capacity = max(2, 3 * count // (2 * owners))
    slots = owners * capacity
    padded = -(-capacity // LANES) * LANES
    me = lax.axis_index("group")

    requested, slot = call(
        functools.partial(request_kernel, capacity),
        [
            jax.ShapeDtypeStruct((owners, padded), jnp.int32),
            jax.ShapeDtypeStruct((1, count), F32),
        ],
        4 * count * count * owners,
        8 * count,
        (item_owner.reshape(1, count), item_row.reshape(1, count)),
    )
    wanted = lax.all_to_all(requested, "table", split_axis=0, concat_axis=0, tiled=True)
    found, ids = call(
        functools.partial(lookup_kernel, capacity),
        [
            jax.ShapeDtypeStruct((slots, width), BF16),
            jax.ShapeDtypeStruct((1, slots), F32),
        ],
        2 * slots * table.shape[0] * width,
        2 * (slots + table.shape[0]) * width,
        (wanted, table),
    )
    returned = lax.all_to_all(found, "table", split_axis=0, concat_axis=0, tiled=True)
    all_ids = [ids] + [shift(ids, "group", groups, k) for k in range(1, groups)]
    returned, *all_ids = lax.optimization_barrier((returned, *all_ids))

    wparts = min(groups, width // LANES)
    heads_per = LANES // HEAD_DIM
    cols_in = 4 * width // groups
    cols_out = width // wparts
    cols_all = cols_in + cols_out + LANES
    cut = cols_all // LANES // 2 * LANES
    square = pltpu.VMEM((count, width), BF16)
    result, row_grad, *grads = call(
        functools.partial(layer_kernel, groups, wparts),
        [
            jax.ShapeDtypeStruct((count, width), BF16),
            jax.ShapeDtypeStruct((count, width), BF16),
            *[
                jax.ShapeDtypeStruct((width, cols), BF16)
                for _ in range(groups)
                for cols in (cut, cols_all - cut)
            ],
        ],
        32 * count * width * width + 14 * count * count * width,
        24 * count * width,
        (lengths, slot, returned, w_in, w_out, gain.reshape(1, width), cotangent),
        smem=(0,),
        far=(2, 3, 4, 6),
        far_out=range(2 + 2 * groups),
        scratch=[
            pltpu.VMEM((slots, width), BF16),
            pltpu.VMEM(w_in.shape, BF16),
            pltpu.VMEM(w_out.shape, BF16),
            square,
            square,
            square,
            pltpu.VMEM((groups, width, cols_all), BF16),
            pltpu.VMEM((count, slots), BF16),
            square,
            pltpu.VMEM((4, count, width), BF16),
            pltpu.VMEM((4, count, width), F32),
            pltpu.VMEM((count, count), F32),
            pltpu.VMEM((width // LANES, heads_per * count, count), BF16),
            pltpu.VMEM((width // LANES, heads_per * count, count), F32),
            pltpu.VMEM((count, width), F32),
            square,
            square,
            pltpu.VMEM((count, 4 * width), BF16),
            pltpu.VMEM((LANES, count), F32),
            pltpu.VMEM((LANES, count), F32),
            pltpu.VMEM((width, width), BF16),
            pltpu.SemaphoreType.DMA((10 + 2 * groups,)),
        ],
    )
    (outgoing,) = call(
        slots_kernel,
        [jax.ShapeDtypeStruct((slots, width), BF16)],
        2 * slots * count * width,
        4 * count * width,
        (slot, row_grad),
        far_out=(0,),
        scratch=[
            pltpu.VMEM((slots, width), BF16),
            pltpu.SemaphoreType.DMA((slots // row_step(slots),)),
        ],
    )

    rows = width // owners
    side = 2 if owners % 4 == 0 else 1
    plane = side * side
    outer = owners // plane
    here = lax.axis_index("table")
    high, middle, low = here // plane, here // side % side, here % side
    sides = []
    for i in range(2):
        terms = [grads[i]] + [shift(grads[2 * k + i], "group", groups, k) for k in range(1, groups)]
        sides.append([term.reshape(outer, side, side, rows, term.shape[1]) for term in terms])

    def entry(value, index, axis):
        return lax.dynamic_index_in_dim(value, index, axis, keepdims=False)

    def add(terms):
        return sum(term.astype(F32) for term in terms)

    def halve(terms, index, axis, bit, last):
        send = add([entry(term, 1 - index, axis) for term in terms]).astype(BF16)
        got = lax.ppermute(send, "table", [(i, i ^ bit) for i in range(owners)])
        kept = [entry(term, index, axis) for term in terms]
        return ([add(kept)] if last else kept) + [got]

    if side == 2:
        left = halve(sides[0], low, 2, 1, False)
        right = halve(sides[1], middle, 1, 2, False)
        left = halve(left, middle, 1, 2, True)
        right = halve(right, low, 1, 1, True)
    else:
        left, right = [[term[:, 0, 0] for term in terms] for terms in sides]
    cols = cols_all
    kept, *sends = call(
        functools.partial(plane_kernel, outer, len(left)),
        [
            jax.ShapeDtypeStruct((rows, cols), F32),
            *[jax.ShapeDtypeStruct((rows, cols), BF16) for _ in range(1, outer)],
        ],
        12 * outer * rows * cols,
        8 * outer * rows * cols,
        (*left, *right),
        limit=24,
    )
    got = [
        lax.ppermute(
            sends[k - 1],
            "table",
            [(i, ((i // plane + k) % outer) * plane + i % plane) for i in range(owners)],
        )
        for k in range(1, outer)
    ]

    incoming = lax.all_to_all(outgoing, "table", split_axis=0, concat_axis=0, tiled=True)
    incoming, kept = lax.optimization_barrier((incoming, kept))
    all_incoming = [incoming] + [shift(incoming, "group", groups, k) for k in range(1, groups)]
    grad_rows = table.shape[0] // groups
    (table_grad,) = call(
        functools.partial(collect_kernel, groups),
        [jax.ShapeDtypeStruct((grad_rows, width), F32)],
        2 * slots * table.shape[0] * width,
        2 * groups * slots * width + 4 * grad_rows * width,
        (*all_ids, *all_incoming),
        far=range(groups, 2 * groups),
        far_out=(0,),
        limit=24,
        scratch=[
            *[pltpu.VMEM((slots, width), BF16) for _ in range(groups)],
            pltpu.VMEM((grad_rows, width), F32),
            pltpu.SemaphoreType.DMA((groups + grad_rows // row_step(grad_rows),)),
        ],
    )

    kept, table_grad = lax.optimization_barrier((kept, table_grad))
    w_in_grad, mine, gain_grad = call(
        finish_kernel,
        [
            jax.ShapeDtypeStruct((rows, cols_in), F32),
            jax.ShapeDtypeStruct((rows, cols_out), F32),
            jax.ShapeDtypeStruct((1, rows), F32),
        ],
        4 * rows * cols_all,
        14 * rows * cols_all,
        (kept, *got),
        limit=24,
    )
    others = [shift(mine, "group", groups, k) for k in range(1, groups)]
    pieces = jnp.stack([mine, *others])
    w_out_grad = jnp.concatenate(
        [
            lax.dynamic_index_in_dim(pieces, (me - p) % groups, 0, keepdims=False)
            for p in range(wparts)
        ],
        1,
    )
    return (result, table_grad, w_in_grad, w_out_grad, gain_grad.reshape(rows))


def solution(mesh):
    return jax.shard_map(
        on_device,
        mesh=mesh,
        in_specs=(
            P(("table", "group"), None),
            P(("table", "group")),
            P(("table", "group"), None),
            P("table", None),
            P(),
            P(),
            P(),
            P(("table", "group"), None),
        ),
        out_specs=(
            P(("table", "group"), None),
            P(("table", "group"), None),
            P("table", "group"),
            P("table", None),
            P("table"),
        ),
        check_vma=False,
    )
```

```python
import functools
import math

import jax
import jax.numpy as jnp
from jax import lax
from jax.experimental import pallas as pl
from jax.experimental.pallas import tpu as pltpu
from jax.sharding import PartitionSpec as P

HEAD_DIM = 64
LANES = 128
QUERY_ROWS = 256

F32 = jnp.float32
BF16 = jnp.bfloat16


def iota(shape, dim):
    return lax.broadcasted_iota(jnp.int32, shape, dim)


def hot(cond):
    return jnp.where(cond, 1.0, 0.0).astype(BF16)


def dot_nn(a, b):
    return lax.dot_general(a, b, (((1,), (0,)), ((), ())), preferred_element_type=F32)


def dot_nt(a, b):
    return lax.dot_general(a, b, (((1,), (1,)), ((), ())), preferred_element_type=F32)


def dot_tn(a, b):
    return lax.dot_general(a, b, (((0,), (0,)), ((), ())), preferred_element_type=F32)


def row_step(rows):
    return 256 if rows % 256 == 0 else rows


def call(kernel, out_shape, flops, nbytes, operands, smem=(), far=(), far_out=(), limit=56, scratch=()):
    spaces = [
        pltpu.SMEM if i in smem else pl.ANY if i in far else pltpu.VMEM
        for i in range(len(operands))
    ]
    out_spaces = [pl.ANY if i in far_out else pltpu.VMEM for i in range(len(out_shape))]
    return pl.pallas_call(
        kernel,
        out_shape=out_shape,
        in_specs=[pl.BlockSpec(memory_space=space) for space in spaces],
        out_specs=[pl.BlockSpec(memory_space=space) for space in out_spaces],
        scratch_shapes=scratch,
        compiler_params=pltpu.CompilerParams(vmem_limit_bytes=limit * 1024 * 1024),
        cost_estimate=pl.CostEstimate(flops=flops, bytes_accessed=nbytes, transcendentals=0),
    )(*operands)


def request_kernel(cap, owner_ref, row_ref, req_ref, slot_ref):
    owners, width = req_ref.shape
    count = owner_ref.shape[1]
    owner = owner_ref[...]
    row = row_ref[...]
    mine = iota((owners, count), 0) == owner
    mine_b = hot(mine)
    before = hot(iota((count, count), 0) < iota((count, count), 1))
    earlier = dot_nn(mine_b, before)
    place = jnp.sum(jnp.where(mine, earlier, 0.0), axis=0, keepdims=True)
    slot_ref[...] = owner.astype(F32) * float(cap) + place
    at_place = hot(iota((width, count), 0).astype(F32) == place)
    high = jnp.where(mine, (row >> 8).astype(F32), 0.0).astype(BF16)
    low = jnp.where(mine, (row & 255).astype(F32), 0.0).astype(BF16)
    found = dot_nt(high, at_place) * 256.0 + dot_nt(low, at_place)
    req_ref[...] = found.astype(jnp.int32)


def lookup_kernel(cap, wanted_ref, table_ref, found_ref, ids_ref):
    owners, width = wanted_ref.shape
    slots = found_ref.shape[0]
    rows = table_ref.shape[0]
    wanted = wanted_ref[...]
    high = (wanted >> 8).astype(F32).astype(BF16)
    low = (wanted & 255).astype(F32).astype(BF16)
    slot = iota((slots, owners), 0).astype(F32)
    holder = jnp.floor((slot + 0.5) * (1.0 / cap))
    spread = hot(holder == iota((slots, owners), 1).astype(F32))
    ids = dot_nn(spread, high) * 256.0 + dot_nn(spread, low)
    slot = iota((slots, width), 0).astype(F32)
    place = slot - jnp.floor((slot + 0.5) * (1.0 / cap)) * float(cap)
    ids = jnp.sum(
        jnp.where(iota((slots, width), 1).astype(F32) == place, ids, 0.0), axis=1, keepdims=True
    )
    wide = jnp.broadcast_to(ids, (slots, LANES))
    ids_ref[...] = wide.T[0:1, :]
    step = 256 if slots % 256 == 0 else slots
    for start in range(0, slots, step):
        part = ids[start : start + step]
        pick = hot(iota((step, rows), 1).astype(F32) == part)
        found_ref[start : start + step, :] = dot_nn(pick, table_ref[...]).astype(BF16)


def collect_kernel(groups, *refs):
    ids_refs, in_hbms, out_hbm = refs[:groups], refs[groups : 2 * groups], refs[2 * groups]
    in_refs, out_ref, sems = refs[2 * groups + 1 : 3 * groups + 1], refs[-2], refs[-1]
    rows = out_ref.shape[0]
    slots = in_refs[0].shape[0]
    fetches = [
        pltpu.make_async_copy(hbm, ref, sems.at[n])
        for n, (hbm, ref) in enumerate(zip(in_hbms, in_refs))
    ]
    for fetch in fetches:
        fetch.start()
    base = lax.axis_index("group") * rows
    step = row_step(rows)
    for fetch in fetches:
        fetch.wait()
    stores = []
    for n, start in enumerate(range(0, rows, step)):
        own = (iota((step, slots), 0) + (base + start)).astype(F32)
        total = None
        for ids_ref, in_ref in zip(ids_refs, in_refs):
            part = dot_nn(hot(own == ids_ref[...]), in_ref[...])
            total = part if total is None else total + part
        out_ref[start : start + step, :] = total
        here = pl.ds(start, step)
        stores.append(
            pltpu.make_async_copy(out_ref.at[here], out_hbm.at[here], sems.at[groups + n])
        )
        stores[-1].start()
    for store in stores:
        store.wait()


def layer_kernel(
    groups,
    wparts,
    len_ref,
    slot_ref,
    ret_hbm,
    w_in_hbm,
    w_out_hbm,
    gain_ref,
    cot_hbm,
    *rest,
):
    result_hbm, row_hbm = rest[:2]
    grads_hbms = rest[2 : 2 + 2 * groups]
    (
    ret_ref,
    w_in_ref,
    w_out_ref,
    cot_ref,
    result_ref,
    row_ref,
    grads_ref,
    pick_ref,
    put_ref,
    emb_ref,
    proj_ref,
    slope_ref,
    bias_ref,
    weight_ref,
    wslope_ref,
    att_ref,
    mixed_ref,
    gatt_ref,
    gpre_ref,
    gval_ref,
    gkey_ref,
    gwo_ref,
    sems,
    ) = rest[2 + 2 * groups :]
    count, width = cot_ref.shape
    slots = ret_hbm.shape[0]
    per = LANES // HEAD_DIM
    slabs = width // LANES
    qrows = QUERY_ROWS if count % QUERY_ROWS == 0 else count
    half_scale = 0.5 / math.sqrt(HEAD_DIM)

    get_ret = pltpu.make_async_copy(ret_hbm, ret_ref, sems.at[8 + 2 * groups])
    get_ret.start()
    parts = [pl.ds(i * width, width) for i in range(4)]
    get_ins = [
        pltpu.make_async_copy(w_in_hbm.at[:, part], w_in_ref.at[:, part], sems.at[i])
        for i, part in enumerate(parts)
    ]
    get_cot = pltpu.make_async_copy(cot_hbm, cot_ref, sems.at[4])
    get_out = pltpu.make_async_copy(w_out_hbm, w_out_ref, sems.at[5])
    for fetch in (*get_ins, get_cot, get_out):
        fetch.start()

    slot = jnp.broadcast_to(slot_ref[...], (LANES, count)).T
    for start in range(0, slots, LANES):
        pick_ref[:, start : start + LANES] = hot(
            slot == (iota((count, LANES), 1) + start).astype(F32)
        )
    get_ret.wait()
    emb_ref[...] = dot_nn(pick_ref[...], ret_ref[...]).astype(BF16)

    for fetch in (*get_ins, get_cot, get_out):
        fetch.wait()
    for i in range(4):
        pre = dot_nn(emb_ref[...], w_in_ref[:, parts[i]])
        half = 0.5 * pre
        th = jnp.tanh(half)
        act = half + half * th
        proj_ref[i] = act.astype(BF16)
        slope_ref[i] = 0.5 * ((1.0 + th) + act * (1.0 - th))

    pos = iota((count, 1), 0)
    begin = jnp.zeros((count, 1), jnp.int32)
    end = jnp.int32(0)
    for s in range(len_ref.shape[1]):
        end = end + len_ref[0, s]
        begin = jnp.where(pos >= end, end, begin)
    key = iota((count, count), 1)
    allowed = (key >= begin) & (key <= iota((count, count), 0))
    bias_ref[...] = jnp.where(allowed, 3.0e38, -30.0)

    lane = iota((qrows, LANES), 1)
    inside = [(lane >= a * HEAD_DIM) & (lane < (a + 1) * HEAD_DIM) for a in range(per)]
    lane = iota((count, LANES), 1)
    inside_all = [(lane >= a * HEAD_DIM) & (lane < (a + 1) * HEAD_DIM) for a in range(per)]

    def stacked(value, factor=1.0):
        value = value.astype(F32) * factor
        return jnp.concatenate([jnp.where(m, value, 0.0) for m in inside], 0).astype(BF16)

    row = iota((LANES, qrows), 0)
    inside_rows = [(row >= a * HEAD_DIM) & (row < (a + 1) * HEAD_DIM) for a in range(per)]

    def stacked_t(value, factor=1.0):
        value = (value.astype(F32) * factor).T
        return jnp.concatenate([jnp.where(m, value, 0.0) for m in inside_rows], 1).astype(BF16)

    def apart(value):
        value = value.astype(F32)
        return [jnp.where(m, value, 0.0).astype(BF16) for m in inside_all]

    def forward(p, _):
        cols = pl.ds(pl.multiple_of(p * LANES, LANES), LANES)
        key_all = proj_ref[3, :, cols]
        vals = apart(proj_ref[1, :, cols])
        for r0 in range(0, count, qrows):
            r1 = r0 + qrows
            half = dot_nt(stacked(proj_ref[2, r0:r1, cols], half_scale), key_all[:r1])
            half = jnp.minimum(half.reshape(per, qrows, r1), bias_ref[r0:r1, :r1][None])
            th = jnp.tanh(half)
            weight = half + half * th
            weight_b = weight.astype(BF16)
            base = per * r0
            weight_ref[p, base : base + per * qrows, :r1] = weight_b.reshape(per * qrows, r1)
            wslope_ref[p, base : base + per * qrows, :r1] = (
                (1.0 + th) + weight * (1.0 - th)
            ).reshape(per * qrows, r1)
            total = dot_nn(weight_b[0], vals[0][:r1])
            for a in range(1, per):
                total = total + dot_nn(weight_b[a], vals[a][:r1])
            att_ref[r0:r1, cols] = total
        return 0

    lax.fori_loop(0, slabs, forward, 0, unroll=4)

    gain = gain_ref[...]
    gain_sum = jnp.zeros((1, width), F32)
    for r0 in range(0, count, qrows):
        rows = slice(r0, r0 + qrows)
        att = att_ref[rows, :]
        centered = att - jnp.mean(att, 1, keepdims=True)
        inv = lax.rsqrt(jnp.mean(centered * centered, 1, keepdims=True) + 1e-05)
        normed = centered * inv
        upd = proj_ref[0, rows, :].astype(F32)
        scaled = normed * gain
        mixed = (scaled * upd).astype(BF16)
        mixed_ref[rows, :] = mixed
        result_ref[rows, :] = (
            emb_ref[rows, :].astype(F32) + dot_nn(mixed, w_out_ref[...])
        ).astype(BF16)
        gmix = dot_nt(cot_ref[rows, :], w_out_ref[...]).astype(BF16).astype(F32)
        gpre_ref[rows, 0:width] = (gmix * scaled * slope_ref[0, rows, :]).astype(BF16)
        gnorm = gmix * gain * upd
        gain_sum = gain_sum + jnp.sum(gmix * normed * upd, 0, keepdims=True)
        mean1 = jnp.mean(gnorm, 1, keepdims=True)
        mean2 = jnp.mean(gnorm * normed, 1, keepdims=True)
        gatt_ref[rows, :] = ((gnorm - mean1 - normed * mean2) * inv).astype(BF16)
    gwo_ref[...] = dot_tn(mixed_ref[...], cot_ref[...]).astype(BF16)

    def backward(p, _):
        start = pl.multiple_of(p * LANES, LANES)
        cols = pl.ds(start, LANES)
        val = proj_ref[1, :, cols]
        keys = apart(proj_ref[3, :, cols])
        for r0 in reversed(range(0, count, qrows)):
            r1 = r0 + qrows
            base = per * r0
            rows = slice(base, base + per * qrows)
            gatt = stacked(gatt_ref[r0:r1, cols])
            gweight = dot_nt(gatt, val[:r1])
            gscore = (gweight * wslope_ref[p, rows, :r1]).astype(BF16)
            gqry = dot_nn(gscore[:qrows], keys[0][:r1])
            for a in range(1, per):
                gqry = gqry + dot_nn(gscore[a * qrows : (a + 1) * qrows], keys[a][:r1])
            gval = dot_nn(stacked_t(gatt_ref[r0:r1, cols]), weight_ref[p, rows, :r1])
            gkey = dot_nn(stacked_t(proj_ref[2, r0:r1, cols], half_scale), gscore)
            if r1 == count:
                gval_ref[...] = gval
                gkey_ref[...] = gkey
            else:
                gval_ref[:, :r1] += gval
                gkey_ref[:, :r1] += gkey
            gpre_ref[r0:r1, pl.ds(2 * width + start, LANES)] = (
                gqry * half_scale * slope_ref[2, r0:r1, cols]
            ).astype(BF16)
        gpre_ref[:, pl.ds(width + start, LANES)] = (gval_ref[...].T * slope_ref[1, :, cols]).astype(BF16)
        gpre_ref[:, pl.ds(3 * width + start, LANES)] = (gkey_ref[...].T * slope_ref[3, :, cols]).astype(BF16)
        return 0

    lax.fori_loop(0, slabs, backward, 0, unroll=4)

    put_result = pltpu.make_async_copy(result_ref, result_hbm, sems.at[6])
    put_result.start()
    puts = [put_result]
    put_ref[...] = hot(iota((slots, count), 0).astype(F32) == slot_ref[...])

    me = lax.axis_index("group")
    emb_t = emb_ref[...].T
    cols_in = 4 * width // groups
    cols_out = width // wparts
    chunk = min(cols_in, 512)
    gain_col = jnp.broadcast_to(gain_sum, (LANES, width)).T.astype(BF16)
    for k in [*range(1, groups), 0]:
        part = lax.rem(me + k, groups)
        for c in range(0, cols_in, chunk):
            cols = pl.ds(pl.multiple_of(part * cols_in + c, LANES), chunk)
            grads_ref[k, :, c : c + chunk] = dot_nn(emb_t, gpre_ref[:, cols]).astype(BF16)
        cols = pl.ds(pl.multiple_of(lax.rem(part, wparts) * cols_out, LANES), cols_out)
        grads_ref[k, :, cols_in : cols_in + cols_out] = gwo_ref[:, cols]
        grads_ref[k, :, cols_in + cols_out :] = gain_col
        cut = grads_hbms[2 * k].shape[1]
        for i, cols in enumerate((pl.ds(0, cut), pl.ds(cut, grads_ref.shape[2] - cut))):
            put = pltpu.make_async_copy(
                grads_ref.at[k, :, cols], grads_hbms[2 * k + i], sems.at[8 + 2 * k + i]
            )
            put.start()
            puts.append(put)
    gemb = (cot_ref[...].astype(F32) + dot_nt(gpre_ref[...], w_in_ref[...])).astype(BF16)
    step = slots // 2
    for i, start in enumerate((0, step)):
        rows = pl.ds(start, step)
        row_ref[rows, :] = dot_nn(put_ref[rows, :], gemb).astype(BF16)
        sem = sems.at[7 + i * (2 + 2 * groups)]
        puts.append(pltpu.make_async_copy(row_ref.at[rows], row_hbm.at[rows], sem))
        puts[-1].start()
    for put in puts:
        put.wait()


def plane_kernel(outer, terms, *refs):
    left, right, outs = refs[:terms], refs[terms : 2 * terms], refs[2 * terms :]
    cut = left[0].shape[2]
    high = lax.div(lax.axis_index("table"), lax.axis_size("table") // outer)
    for k in range(outer):
        at = lax.rem(high + k, outer)
        for parts, cols in ((left, slice(0, cut)), (right, slice(cut, None))):
            total = parts[0][at].astype(F32)
            for part in parts[1:]:
                total = total + part[at].astype(F32)
            outs[k][:, cols] = total.astype(outs[k].dtype)


def finish_kernel(kept_ref, *refs):
    got_refs, (in_ref, out_ref, gain_ref) = refs[:-3], refs[-3:]
    total = kept_ref[...]
    for got_ref in got_refs:
        total = total + got_ref[...].astype(F32)
    cols_in, cols_out = in_ref.shape[1], out_ref.shape[1]
    in_ref[...] = total[:, :cols_in]
    out_ref[...] = total[:, cols_in : cols_in + cols_out]
    gain_ref[...] = total[:, cols_in + cols_out :].T[0:1, :]


def shift(value, axis, size, amount):
    return lax.ppermute(value, axis, [(i, (i + amount) % size) for i in range(size)])


def on_device(item_owner, item_row, lengths, table, w_in, w_out, gain, cotangent):
    owners = lax.axis_size("table")
    groups = lax.axis_size("group")
    count = item_row.shape[0]
    width = table.shape[1]
    capacity = max(2, 3 * count // (2 * owners))
    slots = owners * capacity
    padded = -(-capacity // LANES) * LANES
    me = lax.axis_index("group")

    requested, slot = call(
        functools.partial(request_kernel, capacity),
        [
            jax.ShapeDtypeStruct((owners, padded), jnp.int32),
            jax.ShapeDtypeStruct((1, count), F32),
        ],
        4 * count * count * owners,
        8 * count,
        (item_owner.reshape(1, count), item_row.reshape(1, count)),
    )
    wanted = lax.all_to_all(requested, "table", split_axis=0, concat_axis=0, tiled=True)
    found, ids = call(
        functools.partial(lookup_kernel, capacity),
        [
            jax.ShapeDtypeStruct((slots, width), BF16),
            jax.ShapeDtypeStruct((1, slots), F32),
        ],
        2 * slots * table.shape[0] * width,
        2 * (slots + table.shape[0]) * width,
        (wanted, table),
    )
    returned = lax.all_to_all(found, "table", split_axis=0, concat_axis=0, tiled=True)
    all_ids = [ids] + [shift(ids, "group", groups, k) for k in range(1, groups)]
    returned, *all_ids = lax.optimization_barrier((returned, *all_ids))

    wparts = min(groups, width // LANES)
    heads_per = LANES // HEAD_DIM
    cols_in = 4 * width // groups
    cols_out = width // wparts
    cols_all = cols_in + cols_out + LANES
    cut = cols_all // LANES // 2 * LANES
    square = pltpu.VMEM((count, width), BF16)
    result, outgoing, *grads = call(
        functools.partial(layer_kernel, groups, wparts),
        [
            jax.ShapeDtypeStruct((count, width), BF16),
            jax.ShapeDtypeStruct((slots, width), BF16),
            *[
                jax.ShapeDtypeStruct((width, cols), BF16)
                for _ in range(groups)
                for cols in (cut, cols_all - cut)
            ],
        ],
        32 * count * width * width + 14 * count * count * width,
        24 * count * width,
        (lengths, slot, returned, w_in, w_out, gain.reshape(1, width), cotangent),
        smem=(0,),
        far=(2, 3, 4, 6),
        far_out=range(2 + 2 * groups),
        scratch=[
            pltpu.VMEM((slots, width), BF16),
            pltpu.VMEM(w_in.shape, BF16),
            pltpu.VMEM(w_out.shape, BF16),
            square,
            square,
            pltpu.VMEM((slots, width), BF16),
            pltpu.VMEM((groups, width, cols_all), BF16),
            pltpu.VMEM((count, slots), BF16),
            pltpu.VMEM((slots, count), BF16),
            square,
            pltpu.VMEM((4, count, width), BF16),
            pltpu.VMEM((4, count, width), F32),
            pltpu.VMEM((count, count), F32),
            pltpu.VMEM((width // LANES, heads_per * count, count), BF16),
            pltpu.VMEM((width // LANES, heads_per * count, count), F32),
            pltpu.VMEM((count, width), F32),
            square,
            square,
            pltpu.VMEM((count, 4 * width), BF16),
            pltpu.VMEM((LANES, count), F32),
            pltpu.VMEM((LANES, count), F32),
            pltpu.VMEM((width, width), BF16),
            pltpu.SemaphoreType.DMA((10 + 2 * groups,)),
        ],
    )
    rows = width // owners
    side = 2 if owners % 4 == 0 else 1
    plane = side * side
    outer = owners // plane
    here = lax.axis_index("table")
    high, middle, low = here // plane, here // side % side, here % side
    sides = []
    for i in range(2):
        terms = [grads[i]] + [shift(grads[2 * k + i], "group", groups, k) for k in range(1, groups)]
        sides.append([term.reshape(outer, side, side, rows, term.shape[1]) for term in terms])

    def entry(value, index, axis):
        return lax.dynamic_index_in_dim(value, index, axis, keepdims=False)

    def add(terms):
        return sum(term.astype(F32) for term in terms)

    def halve(terms, index, axis, bit, last):
        send = add([entry(term, 1 - index, axis) for term in terms]).astype(BF16)
        got = lax.ppermute(send, "table", [(i, i ^ bit) for i in range(owners)])
        kept = [entry(term, index, axis) for term in terms]
        return ([add(kept)] if last else kept) + [got]

    if side == 2:
        left = halve(sides[0], low, 2, 1, False)
        right = halve(sides[1], middle, 1, 2, False)
        left = halve(left, middle, 1, 2, True)
        right = halve(right, low, 1, 1, True)
    else:
        left, right = [[term[:, 0, 0] for term in terms] for terms in sides]
    cols = cols_all
    kept, *sends = call(
        functools.partial(plane_kernel, outer, len(left)),
        [
            jax.ShapeDtypeStruct((rows, cols), F32),
            *[jax.ShapeDtypeStruct((rows, cols), BF16) for _ in range(1, outer)],
        ],
        12 * outer * rows * cols,
        8 * outer * rows * cols,
        (*left, *right),
        limit=24,
    )
    got = [
        lax.ppermute(
            sends[k - 1],
            "table",
            [(i, ((i // plane + k) % outer) * plane + i % plane) for i in range(owners)],
        )
        for k in range(1, outer)
    ]

    incoming = lax.all_to_all(outgoing, "table", split_axis=0, concat_axis=0, tiled=True)
    incoming, kept = lax.optimization_barrier((incoming, kept))
    all_incoming = [incoming] + [shift(incoming, "group", groups, k) for k in range(1, groups)]
    grad_rows = table.shape[0] // groups
    (table_grad,) = call(
        functools.partial(collect_kernel, groups),
        [jax.ShapeDtypeStruct((grad_rows, width), F32)],
        2 * slots * table.shape[0] * width,
        2 * groups * slots * width + 4 * grad_rows * width,
        (*all_ids, *all_incoming),
        far=range(groups, 2 * groups),
        far_out=(0,),
        limit=24,
        scratch=[
            *[pltpu.VMEM((slots, width), BF16) for _ in range(groups)],
            pltpu.VMEM((grad_rows, width), F32),
            pltpu.SemaphoreType.DMA((groups + grad_rows // row_step(grad_rows),)),
        ],
    )

    kept, table_grad = lax.optimization_barrier((kept, table_grad))
    w_in_grad, mine, gain_grad = call(
        finish_kernel,
        [
            jax.ShapeDtypeStruct((rows, cols_in), F32),
            jax.ShapeDtypeStruct((rows, cols_out), F32),
            jax.ShapeDtypeStruct((1, rows), F32),
        ],
        4 * rows * cols_all,
        14 * rows * cols_all,
        (kept, *got),
        limit=24,
    )
    others = [shift(mine, "group", groups, k) for k in range(1, groups)]
    pieces = jnp.stack([mine, *others])
    w_out_grad = jnp.concatenate(
        [
            lax.dynamic_index_in_dim(pieces, (me - p) % groups, 0, keepdims=False)
            for p in range(wparts)
        ],
        1,
    )
    return (result, table_grad, w_in_grad, w_out_grad, gain_grad.reshape(rows))


def solution(mesh):
    return jax.shard_map(
        on_device,
        mesh=mesh,
        in_specs=(
            P(("table", "group"), None),
            P(("table", "group")),
            P(("table", "group"), None),
            P("table", None),
            P(),
            P(),
            P(),
            P(("table", "group"), None),
        ),
        out_specs=(
            P(("table", "group"), None),
            P(("table", "group"), None),
            P("table", "group"),
            P("table", None),
            P("table"),
        ),
        check_vma=False,
    )
```

```python
import functools
import math

import jax
import jax.numpy as jnp
from jax import lax
from jax.experimental import pallas as pl
from jax.experimental.pallas import tpu as pltpu
from jax.sharding import PartitionSpec as P

HEAD_DIM = 64
LANES = 128
QUERY_ROWS = 256

F32 = jnp.float32
BF16 = jnp.bfloat16


def iota(shape, dim):
    return lax.broadcasted_iota(jnp.int32, shape, dim)


def hot(cond):
    return jnp.where(cond, 1.0, 0.0).astype(BF16)


def dot_nn(a, b):
    return lax.dot_general(a, b, (((1,), (0,)), ((), ())), preferred_element_type=F32)


def dot_nt(a, b):
    return lax.dot_general(a, b, (((1,), (1,)), ((), ())), preferred_element_type=F32)


def dot_tn(a, b):
    return lax.dot_general(a, b, (((0,), (0,)), ((), ())), preferred_element_type=F32)


def row_step(rows):
    return 256 if rows % 256 == 0 else rows


def call(kernel, out_shape, flops, nbytes, operands, smem=(), far=(), far_out=(), limit=56, scratch=()):
    spaces = [
        pltpu.SMEM if i in smem else pl.ANY if i in far else pltpu.VMEM
        for i in range(len(operands))
    ]
    out_spaces = [pl.ANY if i in far_out else pltpu.VMEM for i in range(len(out_shape))]
    return pl.pallas_call(
        kernel,
        out_shape=out_shape,
        in_specs=[pl.BlockSpec(memory_space=space) for space in spaces],
        out_specs=[pl.BlockSpec(memory_space=space) for space in out_spaces],
        scratch_shapes=scratch,
        compiler_params=pltpu.CompilerParams(vmem_limit_bytes=limit * 1024 * 1024),
        cost_estimate=pl.CostEstimate(flops=flops, bytes_accessed=nbytes, transcendentals=0),
    )(*operands)


def request_kernel(cap, owner_ref, row_ref, req_ref, slot_ref):
    owners, width = req_ref.shape
    count = owner_ref.shape[1]
    owner = owner_ref[...]
    row = row_ref[...]
    mine = iota((owners, count), 0) == owner
    mine_b = hot(mine)
    before = hot(iota((count, count), 0) < iota((count, count), 1))
    earlier = dot_nn(mine_b, before)
    place = jnp.sum(jnp.where(mine, earlier, 0.0), axis=0, keepdims=True)
    slot_ref[...] = owner.astype(F32) * float(cap) + place
    at_place = hot(iota((width, count), 0).astype(F32) == place)
    high = jnp.where(mine, (row >> 8).astype(F32), 0.0).astype(BF16)
    low = jnp.where(mine, (row & 255).astype(F32), 0.0).astype(BF16)
    found = dot_nt(high, at_place) * 256.0 + dot_nt(low, at_place)
    req_ref[...] = found.astype(jnp.int32)


def lookup_kernel(cap, wanted_ref, table_ref, found_ref, ids_ref):
    owners, width = wanted_ref.shape
    slots = found_ref.shape[0]
    rows = table_ref.shape[0]
    wanted = wanted_ref[...]
    high = (wanted >> 8).astype(F32).astype(BF16)
    low = (wanted & 255).astype(F32).astype(BF16)
    slot = iota((slots, owners), 0).astype(F32)
    holder = jnp.floor((slot + 0.5) * (1.0 / cap))
    spread = hot(holder == iota((slots, owners), 1).astype(F32))
    ids = dot_nn(spread, high) * 256.0 + dot_nn(spread, low)
    slot = iota((slots, width), 0).astype(F32)
    place = slot - jnp.floor((slot + 0.5) * (1.0 / cap)) * float(cap)
    ids = jnp.sum(
        jnp.where(iota((slots, width), 1).astype(F32) == place, ids, 0.0), axis=1, keepdims=True
    )
    wide = jnp.broadcast_to(ids, (slots, LANES))
    ids_ref[...] = wide.T[0:1, :]
    step = 256 if slots % 256 == 0 else slots
    for start in range(0, slots, step):
        part = ids[start : start + step]
        pick = hot(iota((step, rows), 1).astype(F32) == part)
        found_ref[start : start + step, :] = dot_nn(pick, table_ref[...]).astype(BF16)


def collect_kernel(groups, *refs):
    ids_refs, in_hbms, out_hbm = refs[:groups], refs[groups : 2 * groups], refs[2 * groups]
    in_refs, out_ref, sems = refs[2 * groups + 1 : 3 * groups + 1], refs[-2], refs[-1]
    rows = out_ref.shape[0]
    slots = in_refs[0].shape[0]
    fetches = [
        pltpu.make_async_copy(hbm, ref, sems.at[n])
        for n, (hbm, ref) in enumerate(zip(in_hbms, in_refs))
    ]
    for fetch in fetches:
        fetch.start()
    base = lax.axis_index("group") * rows
    step = row_step(rows)
    for fetch in fetches:
        fetch.wait()
    stores = []
    for n, start in enumerate(range(0, rows, step)):
        own = (iota((step, slots), 0) + (base + start)).astype(F32)
        total = None
        for ids_ref, in_ref in zip(ids_refs, in_refs):
            part = dot_nn(hot(own == ids_ref[...]), in_ref[...])
            total = part if total is None else total + part
        out_ref[start : start + step, :] = total
        here = pl.ds(start, step)
        stores.append(
            pltpu.make_async_copy(out_ref.at[here], out_hbm.at[here], sems.at[groups + n])
        )
        stores[-1].start()
    for store in stores:
        store.wait()


def layer_kernel(
    groups,
    wparts,
    len_ref,
    slot_ref,
    ret_hbm,
    w_in_hbm,
    w_out_hbm,
    gain_ref,
    cot_hbm,
    *rest,
):
    result_hbm, row_hbm = rest[:2]
    grads_hbms = rest[2 : 2 + 2 * groups]
    (
    ret_ref,
    w_in_ref,
    w_out_ref,
    cot_ref,
    result_ref,
    row_ref,
    grads_ref,
    pick_ref,
    put_ref,
    emb_ref,
    proj_ref,
    slope_ref,
    bias_ref,
    weight_ref,
    wslope_ref,
    att_ref,
    mixed_ref,
    gatt_ref,
    gpre_ref,
    gval_ref,
    gkey_ref,
    gwo_ref,
    sems,
    ) = rest[2 + 2 * groups :]
    count, width = cot_ref.shape
    slots = ret_hbm.shape[0]
    per = LANES // HEAD_DIM
    slabs = width // LANES
    qrows = QUERY_ROWS if count % QUERY_ROWS == 0 else count
    half_scale = 0.5 / math.sqrt(HEAD_DIM)

    get_ret = pltpu.make_async_copy(ret_hbm, ret_ref, sems.at[8 + 2 * groups])
    get_ret.start()
    parts = [pl.ds(i * width, width) for i in range(4)]
    get_ins = [
        pltpu.make_async_copy(w_in_hbm.at[:, part], w_in_ref.at[:, part], sems.at[i])
        for i, part in enumerate(parts)
    ]
    get_cot = pltpu.make_async_copy(cot_hbm, cot_ref, sems.at[4])
    get_out = pltpu.make_async_copy(w_out_hbm, w_out_ref, sems.at[5])
    for fetch in (*get_ins, get_cot, get_out):
        fetch.start()

    slot = jnp.broadcast_to(slot_ref[...], (LANES, count)).T
    for start in range(0, slots, LANES):
        pick_ref[:, start : start + LANES] = hot(
            slot == (iota((count, LANES), 1) + start).astype(F32)
        )
    get_ret.wait()
    emb_ref[...] = dot_nn(pick_ref[...], ret_ref[...]).astype(BF16)

    for fetch in (*get_ins, get_cot, get_out):
        fetch.wait()
    for i in range(4):
        pre = dot_nn(emb_ref[...], w_in_ref[:, parts[i]])
        half = 0.5 * pre
        th = jnp.tanh(half)
        act = half + half * th
        proj_ref[i] = act.astype(BF16)
        slope_ref[i] = 0.5 * ((1.0 + th) + act * (1.0 - th))

    pos = iota((count, 1), 0)
    begin = jnp.zeros((count, 1), jnp.int32)
    end = jnp.int32(0)
    for s in range(len_ref.shape[1]):
        end = end + len_ref[0, s]
        begin = jnp.where(pos >= end, end, begin)
    key = iota((count, count), 1)
    allowed = (key >= begin) & (key <= iota((count, count), 0))
    bias_ref[...] = jnp.where(allowed, 3.0e38, -30.0)

    lane = iota((qrows, LANES), 1)
    inside = [(lane >= a * HEAD_DIM) & (lane < (a + 1) * HEAD_DIM) for a in range(per)]
    lane = iota((count, LANES), 1)
    inside_all = [(lane >= a * HEAD_DIM) & (lane < (a + 1) * HEAD_DIM) for a in range(per)]

    def stacked(value, factor=1.0):
        value = value.astype(F32) * factor
        return jnp.concatenate([jnp.where(m, value, 0.0) for m in inside], 0).astype(BF16)

    row = iota((LANES, qrows), 0)
    inside_rows = [(row >= a * HEAD_DIM) & (row < (a + 1) * HEAD_DIM) for a in range(per)]

    def stacked_t(value, factor=1.0):
        value = (value.astype(F32) * factor).T
        return jnp.concatenate([jnp.where(m, value, 0.0) for m in inside_rows], 1).astype(BF16)

    def apart(value):
        value = value.astype(F32)
        return [jnp.where(m, value, 0.0).astype(BF16) for m in inside_all]

    def forward(p, _):
        cols = pl.ds(pl.multiple_of(p * LANES, LANES), LANES)
        key_all = proj_ref[3, :, cols]
        vals = apart(proj_ref[1, :, cols])
        for r0 in range(0, count, qrows):
            r1 = r0 + qrows
            half = dot_nt(stacked(proj_ref[2, r0:r1, cols], half_scale), key_all[:r1])
            half = jnp.minimum(half.reshape(per, qrows, r1), bias_ref[r0:r1, :r1][None])
            th = jnp.tanh(half)
            weight = half + half * th
            weight_b = weight.astype(BF16)
            base = per * r0
            weight_ref[p, base : base + per * qrows, :r1] = weight_b.reshape(per * qrows, r1)
            wslope_ref[p, base : base + per * qrows, :r1] = (
                (1.0 + th) + weight * (1.0 - th)
            ).reshape(per * qrows, r1)
            total = dot_nn(weight_b[0], vals[0][:r1])
            for a in range(1, per):
                total = total + dot_nn(weight_b[a], vals[a][:r1])
            att_ref[r0:r1, cols] = total
        return 0

    lax.fori_loop(0, slabs, forward, 0, unroll=4)

    gain = gain_ref[...]
    gain_sum = jnp.zeros((1, width), F32)
    for r0 in range(0, count, qrows):
        rows = slice(r0, r0 + qrows)
        att = att_ref[rows, :]
        centered = att - jnp.mean(att, 1, keepdims=True)
        inv = lax.rsqrt(jnp.mean(centered * centered, 1, keepdims=True) + 1e-05)
        normed = centered * inv
        upd = proj_ref[0, rows, :].astype(F32)
        scaled = normed * gain
        mixed = (scaled * upd).astype(BF16)
        mixed_ref[rows, :] = mixed
        result_ref[rows, :] = (
            emb_ref[rows, :].astype(F32) + dot_nn(mixed, w_out_ref[...])
        ).astype(BF16)
        gmix = dot_nt(cot_ref[rows, :], w_out_ref[...]).astype(BF16).astype(F32)
        gpre_ref[rows, 0:width] = (gmix * scaled * slope_ref[0, rows, :]).astype(BF16)
        gnorm = gmix * gain * upd
        gain_sum = gain_sum + jnp.sum(gmix * normed * upd, 0, keepdims=True)
        mean1 = jnp.mean(gnorm, 1, keepdims=True)
        mean2 = jnp.mean(gnorm * normed, 1, keepdims=True)
        gatt_ref[rows, :] = ((gnorm - mean1 - normed * mean2) * inv).astype(BF16)
    gwo_ref[...] = dot_tn(mixed_ref[...], cot_ref[...]).astype(BF16)

    def backward(p, _):
        start = pl.multiple_of(p * LANES, LANES)
        cols = pl.ds(start, LANES)
        val = proj_ref[1, :, cols]
        keys = apart(proj_ref[3, :, cols])
        for r0 in reversed(range(0, count, qrows)):
            r1 = r0 + qrows
            base = per * r0
            rows = slice(base, base + per * qrows)
            gatt = stacked(gatt_ref[r0:r1, cols])
            gweight = dot_nt(gatt, val[:r1])
            gscore = (gweight * wslope_ref[p, rows, :r1]).astype(BF16)
            gqry = dot_nn(gscore[:qrows], keys[0][:r1])
            for a in range(1, per):
                gqry = gqry + dot_nn(gscore[a * qrows : (a + 1) * qrows], keys[a][:r1])
            gval = dot_nn(stacked_t(gatt_ref[r0:r1, cols]), weight_ref[p, rows, :r1])
            gkey = dot_nn(stacked_t(proj_ref[2, r0:r1, cols], half_scale), gscore)
            if r1 == count:
                gval_ref[...] = gval
                gkey_ref[...] = gkey
            else:
                gval_ref[:, :r1] += gval
                gkey_ref[:, :r1] += gkey
            gpre_ref[r0:r1, pl.ds(2 * width + start, LANES)] = (
                gqry * half_scale * slope_ref[2, r0:r1, cols]
            ).astype(BF16)
        gpre_ref[:, pl.ds(width + start, LANES)] = (gval_ref[...].T * slope_ref[1, :, cols]).astype(BF16)
        gpre_ref[:, pl.ds(3 * width + start, LANES)] = (gkey_ref[...].T * slope_ref[3, :, cols]).astype(BF16)
        return 0

    lax.fori_loop(0, slabs, backward, 0, unroll=4)

    put_result = pltpu.make_async_copy(result_ref, result_hbm, sems.at[6])
    put_result.start()
    puts = [put_result]
    put_ref[...] = hot(iota((slots, count), 0).astype(F32) == slot_ref[...])

    me = lax.axis_index("group")
    emb_t = emb_ref[...].T
    cols_in = 4 * width // groups
    cols_out = width // wparts
    chunk = min(cols_in, 512)
    gain_col = jnp.broadcast_to(gain_sum, (LANES, width)).T.astype(BF16)
    for k in [*range(1, groups), 0]:
        part = lax.rem(me + k, groups)
        for c in range(0, cols_in, chunk):
            cols = pl.ds(pl.multiple_of(part * cols_in + c, LANES), chunk)
            grads_ref[k, :, c : c + chunk] = dot_nn(emb_t, gpre_ref[:, cols]).astype(BF16)
        cols = pl.ds(pl.multiple_of(lax.rem(part, wparts) * cols_out, LANES), cols_out)
        grads_ref[k, :, cols_in : cols_in + cols_out] = gwo_ref[:, cols]
        grads_ref[k, :, cols_in + cols_out :] = gain_col
        cut = grads_hbms[2 * k].shape[1]
        for i, cols in enumerate((pl.ds(0, cut), pl.ds(cut, grads_ref.shape[2] - cut))):
            put = pltpu.make_async_copy(
                grads_ref.at[k, :, cols], grads_hbms[2 * k + i], sems.at[8 + 2 * k + i]
            )
            put.start()
            puts.append(put)
    gemb = (cot_ref[...].astype(F32) + dot_nt(gpre_ref[...], w_in_ref[...])).astype(BF16)
    step = slots // 2
    for i, start in enumerate((0, step)):
        rows = pl.ds(start, step)
        row_ref[rows, :] = dot_nn(put_ref[rows, :], gemb).astype(BF16)
        sem = sems.at[7 + i * (2 + 2 * groups)]
        puts.append(pltpu.make_async_copy(row_ref.at[rows], row_hbm.at[rows], sem))
        puts[-1].start()
    for put in puts:
        put.wait()


def plane_kernel(outer, terms, *refs):
    left, right, outs = refs[:terms], refs[terms : 2 * terms], refs[2 * terms :]
    cut = left[0].shape[2]
    high = lax.div(lax.axis_index("table"), lax.axis_size("table") // outer)
    for k in range(outer):
        at = lax.rem(high + k, outer)
        for parts, cols in ((left, slice(0, cut)), (right, slice(cut, None))):
            total = parts[0][at].astype(F32)
            for part in parts[1:]:
                total = total + part[at].astype(F32)
            outs[k][:, cols] = total.astype(outs[k].dtype)


def finish_kernel(kept_ref, *refs):
    got_refs, (in_ref, out_ref, gain_ref) = refs[:-3], refs[-3:]
    total = kept_ref[...]
    for got_ref in got_refs:
        total = total + got_ref[...].astype(F32)
    cols_in, cols_out = in_ref.shape[1], out_ref.shape[1]
    in_ref[...] = total[:, :cols_in]
    out_ref[...] = total[:, cols_in : cols_in + cols_out]
    gain_ref[...] = total[:, cols_in + cols_out :].T[0:1, :]


def shift(value, axis, size, amount):
    return lax.ppermute(value, axis, [(i, (i + amount) % size) for i in range(size)])


def on_device(item_owner, item_row, lengths, table, w_in, w_out, gain, cotangent):
    owners = lax.axis_size("table")
    groups = lax.axis_size("group")
    count = item_row.shape[0]
    width = table.shape[1]
    capacity = max(2, 3 * count // (2 * owners))
    slots = owners * capacity
    padded = -(-capacity // LANES) * LANES
    me = lax.axis_index("group")

    requested, slot = call(
        functools.partial(request_kernel, capacity),
        [
            jax.ShapeDtypeStruct((owners, padded), jnp.int32),
            jax.ShapeDtypeStruct((1, count), F32),
        ],
        4 * count * count * owners,
        8 * count,
        (item_owner.reshape(1, count), item_row.reshape(1, count)),
    )
    wanted = lax.all_to_all(requested, "table", split_axis=0, concat_axis=0, tiled=True)
    found, ids = call(
        functools.partial(lookup_kernel, capacity),
        [
            jax.ShapeDtypeStruct((slots, width), BF16),
            jax.ShapeDtypeStruct((1, slots), F32),
        ],
        2 * slots * table.shape[0] * width,
        2 * (slots + table.shape[0]) * width,
        (wanted, table),
    )
    returned = lax.all_to_all(found, "table", split_axis=0, concat_axis=0, tiled=True)
    all_ids = [ids] + [shift(ids, "group", groups, k) for k in range(1, groups)]
    returned, *all_ids = lax.optimization_barrier((returned, *all_ids))

    wparts = min(groups, width // LANES)
    heads_per = LANES // HEAD_DIM
    cols_in = 4 * width // groups
    cols_out = width // wparts
    cols_all = cols_in + cols_out + LANES
    cut = cols_all // LANES // 2 * LANES
    square = pltpu.VMEM((count, width), BF16)
    result, outgoing, *grads = call(
        functools.partial(layer_kernel, groups, wparts),
        [
            jax.ShapeDtypeStruct((count, width), BF16),
            jax.ShapeDtypeStruct((slots, width), BF16),
            *[
                jax.ShapeDtypeStruct((width, cols), BF16)
                for _ in range(groups)
                for cols in (cut, cols_all - cut)
            ],
        ],
        32 * count * width * width + 14 * count * count * width,
        24 * count * width,
        (lengths, slot, returned, w_in, w_out, gain.reshape(1, width), cotangent),
        smem=(0,),
        far=(2, 3, 4, 6),
        far_out=range(2 + 2 * groups),
        scratch=[
            pltpu.VMEM((slots, width), BF16),
            pltpu.VMEM(w_in.shape, BF16),
            pltpu.VMEM(w_out.shape, BF16),
            square,
            square,
            pltpu.VMEM((slots, width), BF16),
            pltpu.VMEM((groups, width, cols_all), BF16),
            pltpu.VMEM((count, slots), BF16),
            pltpu.VMEM((slots, count), BF16),
            square,
            pltpu.VMEM((4, count, width), BF16),
            pltpu.VMEM((4, count, width), F32),
            pltpu.VMEM((count, count), F32),
            pltpu.VMEM((width // LANES, heads_per * count, count), BF16),
            pltpu.VMEM((width // LANES, heads_per * count, count), F32),
            pltpu.VMEM((count, width), F32),
            square,
            square,
            pltpu.VMEM((count, 4 * width), BF16),
            pltpu.VMEM((LANES, count), F32),
            pltpu.VMEM((LANES, count), F32),
            pltpu.VMEM((width, width), BF16),
            pltpu.SemaphoreType.DMA((10 + 2 * groups,)),
        ],
    )
    rows = width // owners
    side = 2 if owners % 4 == 0 else 1
    plane = side * side
    outer = owners // plane
    here = lax.axis_index("table")
    high, middle, low = here // plane, here // side % side, here % side
    sides = []
    for i in range(2):
        terms = [grads[i]] + [shift(grads[2 * k + i], "group", groups, k) for k in range(1, groups)]
        sides.append([term.reshape(outer, side, side, rows, term.shape[1]) for term in terms])

    def entry(value, index, axis):
        return lax.dynamic_index_in_dim(value, index, axis, keepdims=False)

    def add(terms):
        return sum(term.astype(F32) for term in terms)

    def halve(terms, index, axis, bit, last):
        send = add([entry(term, 1 - index, axis) for term in terms]).astype(BF16)
        got = lax.ppermute(send, "table", [(i, i ^ bit) for i in range(owners)])
        if not last:
            *terms, got = lax.optimization_barrier((*terms, got))
        kept = [entry(term, index, axis) for term in terms]
        return ([add(kept)] if last else kept) + [got]

    if side == 2:
        left = halve(sides[0], low, 2, 1, False)
        right = halve(sides[1], middle, 1, 2, False)
        left = halve(left, middle, 1, 2, True)
        right = halve(right, low, 1, 1, True)
    else:
        left, right = [[term[:, 0, 0] for term in terms] for terms in sides]
    cols = cols_all
    kept, *sends = call(
        functools.partial(plane_kernel, outer, len(left)),
        [
            jax.ShapeDtypeStruct((rows, cols), F32),
            *[jax.ShapeDtypeStruct((rows, cols), BF16) for _ in range(1, outer)],
        ],
        12 * outer * rows * cols,
        8 * outer * rows * cols,
        (*left, *right),
        limit=24,
    )
    got = [
        lax.ppermute(
            sends[k - 1],
            "table",
            [(i, ((i // plane + k) % outer) * plane + i % plane) for i in range(owners)],
        )
        for k in range(1, outer)
    ]

    incoming = lax.all_to_all(outgoing, "table", split_axis=0, concat_axis=0, tiled=True)
    incoming, kept = lax.optimization_barrier((incoming, kept))
    all_incoming = [incoming] + [shift(incoming, "group", groups, k) for k in range(1, groups)]
    grad_rows = table.shape[0] // groups
    (table_grad,) = call(
        functools.partial(collect_kernel, groups),
        [jax.ShapeDtypeStruct((grad_rows, width), F32)],
        2 * slots * table.shape[0] * width,
        2 * groups * slots * width + 4 * grad_rows * width,
        (*all_ids, *all_incoming),
        far=range(groups, 2 * groups),
        far_out=(0,),
        limit=24,
        scratch=[
            *[pltpu.VMEM((slots, width), BF16) for _ in range(groups)],
            pltpu.VMEM((grad_rows, width), F32),
            pltpu.SemaphoreType.DMA((groups + grad_rows // row_step(grad_rows),)),
        ],
    )

    kept, table_grad = lax.optimization_barrier((kept, table_grad))
    w_in_grad, mine, gain_grad = call(
        finish_kernel,
        [
            jax.ShapeDtypeStruct((rows, cols_in), F32),
            jax.ShapeDtypeStruct((rows, cols_out), F32),
            jax.ShapeDtypeStruct((1, rows), F32),
        ],
        4 * rows * cols_all,
        14 * rows * cols_all,
        (kept, *got),
        limit=24,
    )
    others = [shift(mine, "group", groups, k) for k in range(1, groups)]
    pieces = jnp.stack([mine, *others])
    w_out_grad = jnp.concatenate(
        [
            lax.dynamic_index_in_dim(pieces, (me - p) % groups, 0, keepdims=False)
            for p in range(wparts)
        ],
        1,
    )
    return (result, table_grad, w_in_grad, w_out_grad, gain_grad.reshape(rows))


def solution(mesh):
    return jax.shard_map(
        on_device,
        mesh=mesh,
        in_specs=(
            P(("table", "group"), None),
            P(("table", "group")),
            P(("table", "group"), None),
            P("table", None),
            P(),
            P(),
            P(),
            P(("table", "group"), None),
        ),
        out_specs=(
            P(("table", "group"), None),
            P(("table", "group"), None),
            P("table", "group"),
            P("table", None),
            P("table"),
        ),
        check_vma=False,
    )
```

```python
import functools
import math

import jax
import jax.numpy as jnp
from jax import lax
from jax.experimental import pallas as pl
from jax.experimental.pallas import tpu as pltpu
from jax.sharding import PartitionSpec as P

HEAD_DIM = 64
LANES = 128
QUERY_ROWS = 256

F32 = jnp.float32
BF16 = jnp.bfloat16


def iota(shape, dim):
    return lax.broadcasted_iota(jnp.int32, shape, dim)


def hot(cond):
    return jnp.where(cond, 1.0, 0.0).astype(BF16)


def dot_nn(a, b):
    return lax.dot_general(a, b, (((1,), (0,)), ((), ())), preferred_element_type=F32)


def dot_nt(a, b):
    return lax.dot_general(a, b, (((1,), (1,)), ((), ())), preferred_element_type=F32)


def dot_tn(a, b):
    return lax.dot_general(a, b, (((0,), (0,)), ((), ())), preferred_element_type=F32)


def row_step(rows):
    return 256 if rows % 256 == 0 else rows


def call(kernel, out_shape, flops, nbytes, operands, smem=(), far=(), far_out=(), limit=56, scratch=()):
    spaces = [
        pltpu.SMEM if i in smem else pl.ANY if i in far else pltpu.VMEM
        for i in range(len(operands))
    ]
    out_spaces = [pl.ANY if i in far_out else pltpu.VMEM for i in range(len(out_shape))]
    return pl.pallas_call(
        kernel,
        out_shape=out_shape,
        in_specs=[pl.BlockSpec(memory_space=space) for space in spaces],
        out_specs=[pl.BlockSpec(memory_space=space) for space in out_spaces],
        scratch_shapes=scratch,
        compiler_params=pltpu.CompilerParams(vmem_limit_bytes=limit * 1024 * 1024),
        cost_estimate=pl.CostEstimate(flops=flops, bytes_accessed=nbytes, transcendentals=0),
    )(*operands)


def request_kernel(cap, owner_ref, row_ref, req_ref, slot_ref):
    owners, width = req_ref.shape
    count = owner_ref.shape[1]
    owner = owner_ref[...]
    row = row_ref[...]
    mine = iota((owners, count), 0) == owner
    mine_b = hot(mine)
    before = hot(iota((count, count), 0) < iota((count, count), 1))
    earlier = dot_nn(mine_b, before)
    place = jnp.sum(jnp.where(mine, earlier, 0.0), axis=0, keepdims=True)
    slot_ref[...] = owner.astype(F32) * float(cap) + place
    at_place = hot(iota((width, count), 0).astype(F32) == place)
    high = jnp.where(mine, (row >> 8).astype(F32), 0.0).astype(BF16)
    low = jnp.where(mine, (row & 255).astype(F32), 0.0).astype(BF16)
    found = dot_nt(high, at_place) * 256.0 + dot_nt(low, at_place)
    req_ref[...] = found.astype(jnp.int32)


def lookup_kernel(cap, wanted_ref, table_ref, found_ref, ids_ref):
    owners, width = wanted_ref.shape
    slots = found_ref.shape[0]
    rows = table_ref.shape[0]
    wanted = wanted_ref[...]
    high = (wanted >> 8).astype(F32).astype(BF16)
    low = (wanted & 255).astype(F32).astype(BF16)
    slot = iota((slots, owners), 0).astype(F32)
    holder = jnp.floor((slot + 0.5) * (1.0 / cap))
    spread = hot(holder == iota((slots, owners), 1).astype(F32))
    ids = dot_nn(spread, high) * 256.0 + dot_nn(spread, low)
    slot = iota((slots, width), 0).astype(F32)
    place = slot - jnp.floor((slot + 0.5) * (1.0 / cap)) * float(cap)
    ids = jnp.sum(
        jnp.where(iota((slots, width), 1).astype(F32) == place, ids, 0.0), axis=1, keepdims=True
    )
    wide = jnp.broadcast_to(ids, (slots, LANES))
    ids_ref[...] = wide.T[0:1, :]
    step = 256 if slots % 256 == 0 else slots
    for start in range(0, slots, step):
        part = ids[start : start + step]
        pick = hot(iota((step, rows), 1).astype(F32) == part)
        found_ref[start : start + step, :] = dot_nn(pick, table_ref[...]).astype(BF16)


def collect_kernel(groups, *refs):
    ids_refs, in_hbms, out_hbm = refs[:groups], refs[groups : 2 * groups], refs[2 * groups]
    in_refs, out_ref, sems = refs[2 * groups + 1 : 3 * groups + 1], refs[-2], refs[-1]
    rows = out_ref.shape[0]
    slots = in_refs[0].shape[0]
    fetches = [
        pltpu.make_async_copy(hbm, ref, sems.at[n])
        for n, (hbm, ref) in enumerate(zip(in_hbms, in_refs))
    ]
    for fetch in fetches:
        fetch.start()
    base = lax.axis_index("group") * rows
    step = row_step(rows)
    for fetch in fetches:
        fetch.wait()
    stores = []
    for n, start in enumerate(range(0, rows, step)):
        own = (iota((step, slots), 0) + (base + start)).astype(F32)
        total = None
        for ids_ref, in_ref in zip(ids_refs, in_refs):
            part = dot_nn(hot(own == ids_ref[...]), in_ref[...])
            total = part if total is None else total + part
        out_ref[start : start + step, :] = total
        here = pl.ds(start, step)
        stores.append(
            pltpu.make_async_copy(out_ref.at[here], out_hbm.at[here], sems.at[groups + n])
        )
        stores[-1].start()
    for store in stores:
        store.wait()


def layer_kernel(
    groups,
    wparts,
    len_ref,
    slot_ref,
    ret_hbm,
    w_in_hbm,
    w_out_hbm,
    gain_ref,
    cot_hbm,
    *rest,
):
    result_hbm, row_hbm = rest[:2]
    grads_hbms = rest[2 : 2 + 2 * groups]
    (
    ret_ref,
    w_in_ref,
    w_out_ref,
    cot_ref,
    result_ref,
    row_ref,
    grads_ref,
    pick_ref,
    put_ref,
    emb_ref,
    proj_ref,
    slope_ref,
    bias_ref,
    weight_ref,
    wslope_ref,
    att_ref,
    mixed_ref,
    gatt_ref,
    gpre_ref,
    gval_ref,
    gkey_ref,
    gwo_ref,
    sems,
    ) = rest[2 + 2 * groups :]
    count, width = cot_ref.shape
    slots = ret_hbm.shape[0]
    per = LANES // HEAD_DIM
    slabs = width // LANES
    qrows = QUERY_ROWS if count % QUERY_ROWS == 0 else count
    half_scale = 0.5 / math.sqrt(HEAD_DIM)

    get_ret = pltpu.make_async_copy(ret_hbm, ret_ref, sems.at[8 + 2 * groups])
    get_ret.start()
    parts = [pl.ds(i * width, width) for i in range(4)]
    get_ins = [
        pltpu.make_async_copy(w_in_hbm.at[:, part], w_in_ref.at[:, part], sems.at[i])
        for i, part in enumerate(parts)
    ]
    get_cot = pltpu.make_async_copy(cot_hbm, cot_ref, sems.at[4])
    get_out = pltpu.make_async_copy(w_out_hbm, w_out_ref, sems.at[5])
    for fetch in (*get_ins, get_cot, get_out):
        fetch.start()

    slot = jnp.broadcast_to(slot_ref[...], (LANES, count)).T
    for start in range(0, slots, LANES):
        pick_ref[:, start : start + LANES] = hot(
            slot == (iota((count, LANES), 1) + start).astype(F32)
        )
    get_ret.wait()
    emb_ref[...] = dot_nn(pick_ref[...], ret_ref[...]).astype(BF16)

    for fetch in (*get_ins, get_cot, get_out):
        fetch.wait()
    for i in range(4):
        pre = dot_nn(emb_ref[...], w_in_ref[:, parts[i]])
        half = 0.5 * pre
        th = jnp.tanh(half)
        act = half + half * th
        proj_ref[i] = act.astype(BF16)
        slope_ref[i] = 0.5 * ((1.0 + th) + act * (1.0 - th))

    pos = iota((count, 1), 0)
    begin = jnp.zeros((count, 1), jnp.int32)
    end = jnp.int32(0)
    for s in range(len_ref.shape[1]):
        end = end + len_ref[0, s]
        begin = jnp.where(pos >= end, end, begin)
    key = iota((count, count), 1)
    allowed = (key >= begin) & (key <= iota((count, count), 0))
    bias_ref[...] = jnp.where(allowed, 3.0e38, -30.0)

    lane = iota((qrows, LANES), 1)
    inside = [(lane >= a * HEAD_DIM) & (lane < (a + 1) * HEAD_DIM) for a in range(per)]
    lane = iota((count, LANES), 1)
    inside_all = [(lane >= a * HEAD_DIM) & (lane < (a + 1) * HEAD_DIM) for a in range(per)]

    def stacked(value, factor=1.0):
        value = value.astype(F32) * factor
        return jnp.concatenate([jnp.where(m, value, 0.0) for m in inside], 0).astype(BF16)

    row = iota((LANES, qrows), 0)
    inside_rows = [(row >= a * HEAD_DIM) & (row < (a + 1) * HEAD_DIM) for a in range(per)]

    def stacked_t(value, factor=1.0):
        value = (value.astype(F32) * factor).T
        return jnp.concatenate([jnp.where(m, value, 0.0) for m in inside_rows], 1).astype(BF16)

    def apart(value):
        value = value.astype(F32)
        return [jnp.where(m, value, 0.0).astype(BF16) for m in inside_all]

    def forward(p, _):
        cols = pl.ds(pl.multiple_of(p * LANES, LANES), LANES)
        key_all = proj_ref[3, :, cols]
        vals = apart(proj_ref[1, :, cols])
        for r0 in range(0, count, qrows):
            r1 = r0 + qrows
            half = dot_nt(stacked(proj_ref[2, r0:r1, cols], half_scale), key_all[:r1])
            half = jnp.minimum(half.reshape(per, qrows, r1), bias_ref[r0:r1, :r1][None])
            th = jnp.tanh(half)
            weight = half + half * th
            weight_b = weight.astype(BF16)
            base = per * r0
            weight_ref[p, base : base + per * qrows, :r1] = weight_b.reshape(per * qrows, r1)
            wslope_ref[p, base : base + per * qrows, :r1] = (
                (1.0 + th) + weight * (1.0 - th)
            ).reshape(per * qrows, r1)
            total = dot_nn(weight_b[0], vals[0][:r1])
            for a in range(1, per):
                total = total + dot_nn(weight_b[a], vals[a][:r1])
            att_ref[r0:r1, cols] = total
        return 0

    lax.fori_loop(0, slabs, forward, 0, unroll=4)

    gain = gain_ref[...]
    gain_sum = jnp.zeros((1, width), F32)
    for r0 in range(0, count, qrows):
        rows = slice(r0, r0 + qrows)
        att = att_ref[rows, :]
        centered = att - jnp.mean(att, 1, keepdims=True)
        inv = lax.rsqrt(jnp.mean(centered * centered, 1, keepdims=True) + 1e-05)
        normed = centered * inv
        upd = proj_ref[0, rows, :].astype(F32)
        scaled = normed * gain
        mixed = (scaled * upd).astype(BF16)
        mixed_ref[rows, :] = mixed
        result_ref[rows, :] = (
            emb_ref[rows, :].astype(F32) + dot_nn(mixed, w_out_ref[...])
        ).astype(BF16)
        gmix = dot_nt(cot_ref[rows, :], w_out_ref[...]).astype(BF16).astype(F32)
        gpre_ref[rows, 0:width] = (gmix * scaled * slope_ref[0, rows, :]).astype(BF16)
        gnorm = gmix * gain * upd
        gain_sum = gain_sum + jnp.sum(gmix * normed * upd, 0, keepdims=True)
        mean1 = jnp.mean(gnorm, 1, keepdims=True)
        mean2 = jnp.mean(gnorm * normed, 1, keepdims=True)
        gatt_ref[rows, :] = ((gnorm - mean1 - normed * mean2) * inv).astype(BF16)
    gwo_ref[...] = dot_tn(mixed_ref[...], cot_ref[...]).astype(BF16)

    def backward(p, _):
        start = pl.multiple_of(p * LANES, LANES)
        cols = pl.ds(start, LANES)
        val = proj_ref[1, :, cols]
        keys = apart(proj_ref[3, :, cols])
        for r0 in reversed(range(0, count, qrows)):
            r1 = r0 + qrows
            base = per * r0
            rows = slice(base, base + per * qrows)
            gatt = stacked(gatt_ref[r0:r1, cols])
            gweight = dot_nt(gatt, val[:r1])
            gscore = (gweight * wslope_ref[p, rows, :r1]).astype(BF16)
            gqry = dot_nn(gscore[:qrows], keys[0][:r1])
            for a in range(1, per):
                gqry = gqry + dot_nn(gscore[a * qrows : (a + 1) * qrows], keys[a][:r1])
            gval = dot_nn(stacked_t(gatt_ref[r0:r1, cols]), weight_ref[p, rows, :r1])
            gkey = dot_nn(stacked_t(proj_ref[2, r0:r1, cols], half_scale), gscore)
            if r1 == count:
                gval_ref[...] = gval
                gkey_ref[...] = gkey
            else:
                gval_ref[:, :r1] += gval
                gkey_ref[:, :r1] += gkey
            gpre_ref[r0:r1, pl.ds(2 * width + start, LANES)] = (
                gqry * half_scale * slope_ref[2, r0:r1, cols]
            ).astype(BF16)
        gpre_ref[:, pl.ds(width + start, LANES)] = (gval_ref[...].T * slope_ref[1, :, cols]).astype(BF16)
        gpre_ref[:, pl.ds(3 * width + start, LANES)] = (gkey_ref[...].T * slope_ref[3, :, cols]).astype(BF16)
        return 0

    lax.fori_loop(0, slabs, backward, 0, unroll=4)

    put_result = pltpu.make_async_copy(result_ref, result_hbm, sems.at[6])
    put_result.start()
    puts = [put_result]
    put_ref[...] = hot(iota((slots, count), 0).astype(F32) == slot_ref[...])

    me = lax.axis_index("group")
    emb_t = emb_ref[...].T
    cols_in = 4 * width // groups
    cols_out = width // wparts
    chunk = min(cols_in, 512)
    gain_col = jnp.broadcast_to(gain_sum, (LANES, width)).T.astype(BF16)
    for k in [*range(1, groups), 0]:
        part = lax.rem(me + k, groups)
        for c in range(0, cols_in, chunk):
            cols = pl.ds(pl.multiple_of(part * cols_in + c, LANES), chunk)
            grads_ref[k, :, c : c + chunk] = dot_nn(emb_t, gpre_ref[:, cols]).astype(BF16)
        cols = pl.ds(pl.multiple_of(lax.rem(part, wparts) * cols_out, LANES), cols_out)
        grads_ref[k, :, cols_in : cols_in + cols_out] = gwo_ref[:, cols]
        grads_ref[k, :, cols_in + cols_out :] = gain_col
        cut = grads_hbms[2 * k].shape[1]
        for i, cols in enumerate((pl.ds(0, cut), pl.ds(cut, grads_ref.shape[2] - cut))):
            put = pltpu.make_async_copy(
                grads_ref.at[k, :, cols], grads_hbms[2 * k + i], sems.at[8 + 2 * k + i]
            )
            put.start()
            puts.append(put)
    gemb = (cot_ref[...].astype(F32) + dot_nt(gpre_ref[...], w_in_ref[...])).astype(BF16)
    step = slots // 2
    for i, start in enumerate((0, step)):
        rows = pl.ds(start, step)
        row_ref[rows, :] = dot_nn(put_ref[rows, :], gemb).astype(BF16)
        sem = sems.at[7 + i * (2 + 2 * groups)]
        puts.append(pltpu.make_async_copy(row_ref.at[rows], row_hbm.at[rows], sem))
        puts[-1].start()
    for put in puts:
        put.wait()


def plane_kernel(outer, terms, *refs):
    left, right, outs = refs[:terms], refs[terms : 2 * terms], refs[2 * terms :]
    cut = left[0].shape[2]
    high = lax.div(lax.axis_index("table"), lax.axis_size("table") // outer)
    for k in range(outer):
        at = lax.rem(high + k, outer)
        for parts, cols in ((left, slice(0, cut)), (right, slice(cut, None))):
            total = parts[0][at].astype(F32)
            for part in parts[1:]:
                total = total + part[at].astype(F32)
            outs[k][:, cols] = total.astype(outs[k].dtype)


def finish_kernel(kept_ref, *refs):
    got_refs, (in_ref, out_ref, gain_ref) = refs[:-3], refs[-3:]
    total = kept_ref[...]
    for got_ref in got_refs:
        total = total + got_ref[...].astype(F32)
    cols_in, cols_out = in_ref.shape[1], out_ref.shape[1]
    in_ref[...] = total[:, :cols_in]
    out_ref[...] = total[:, cols_in : cols_in + cols_out]
    gain_ref[...] = total[:, cols_in + cols_out :].T[0:1, :]


def shift(value, axis, size, amount):
    return lax.ppermute(value, axis, [(i, (i + amount) % size) for i in range(size)])


def on_device(item_owner, item_row, lengths, table, w_in, w_out, gain, cotangent):
    owners = lax.axis_size("table")
    groups = lax.axis_size("group")
    count = item_row.shape[0]
    width = table.shape[1]
    capacity = max(2, 3 * count // (2 * owners))
    slots = owners * capacity
    padded = -(-capacity // LANES) * LANES
    me = lax.axis_index("group")

    requested, slot = call(
        functools.partial(request_kernel, capacity),
        [
            jax.ShapeDtypeStruct((owners, padded), jnp.int32),
            jax.ShapeDtypeStruct((1, count), F32),
        ],
        4 * count * count * owners,
        8 * count,
        (item_owner.reshape(1, count), item_row.reshape(1, count)),
    )
    wanted = lax.all_to_all(requested, "table", split_axis=0, concat_axis=0, tiled=True)
    found, ids = call(
        functools.partial(lookup_kernel, capacity),
        [
            jax.ShapeDtypeStruct((slots, width), BF16),
            jax.ShapeDtypeStruct((1, slots), F32),
        ],
        2 * slots * table.shape[0] * width,
        2 * (slots + table.shape[0]) * width,
        (wanted, table),
    )
    returned = lax.all_to_all(found, "table", split_axis=0, concat_axis=0, tiled=True)
    all_ids = [ids] + [shift(ids, "group", groups, k) for k in range(1, groups)]
    returned, *all_ids = lax.optimization_barrier((returned, *all_ids))

    wparts = min(groups, width // LANES)
    heads_per = LANES // HEAD_DIM
    cols_in = 4 * width // groups
    cols_out = width // wparts
    cols_all = cols_in + cols_out + LANES
    cut = cols_all // LANES // 2 * LANES
    square = pltpu.VMEM((count, width), BF16)
    result, outgoing, *grads = call(
        functools.partial(layer_kernel, groups, wparts),
        [
            jax.ShapeDtypeStruct((count, width), BF16),
            jax.ShapeDtypeStruct((slots, width), BF16),
            *[
                jax.ShapeDtypeStruct((width, cols), BF16)
                for _ in range(groups)
                for cols in (cut, cols_all - cut)
            ],
        ],
        32 * count * width * width + 14 * count * count * width,
        24 * count * width,
        (lengths, slot, returned, w_in, w_out, gain.reshape(1, width), cotangent),
        smem=(0,),
        far=(2, 3, 4, 6),
        far_out=range(2 + 2 * groups),
        scratch=[
            pltpu.VMEM((slots, width), BF16),
            pltpu.VMEM(w_in.shape, BF16),
            pltpu.VMEM(w_out.shape, BF16),
            square,
            square,
            pltpu.VMEM((slots, width), BF16),
            pltpu.VMEM((groups, width, cols_all), BF16),
            pltpu.VMEM((count, slots), BF16),
            pltpu.VMEM((slots, count), BF16),
            square,
            pltpu.VMEM((4, count, width), BF16),
            pltpu.VMEM((4, count, width), F32),
            pltpu.VMEM((count, count), F32),
            pltpu.VMEM((width // LANES, heads_per * count, count), BF16),
            pltpu.VMEM((width // LANES, heads_per * count, count), F32),
            pltpu.VMEM((count, width), F32),
            square,
            square,
            pltpu.VMEM((count, 4 * width), BF16),
            pltpu.VMEM((LANES, count), F32),
            pltpu.VMEM((LANES, count), F32),
            pltpu.VMEM((width, width), BF16),
            pltpu.SemaphoreType.DMA((10 + 2 * groups,)),
        ],
    )
    rows = width // owners
    side = 2 if owners % 4 == 0 else 1
    plane = side * side
    outer = owners // plane
    here = lax.axis_index("table")
    high, middle, low = here // plane, here // side % side, here % side
    sides = []
    for i in range(2):
        terms = [grads[i]] + [shift(grads[2 * k + i], "group", groups, k) for k in range(1, groups)]
        sides.append([term.reshape(outer, side, side, rows, term.shape[1]) for term in terms])

    def entry(value, index, axis):
        return lax.dynamic_index_in_dim(value, index, axis, keepdims=False)

    def add(terms):
        return sum(term.astype(F32) for term in terms)

    def halve(terms, index, axis, bit, last):
        send = add([entry(term, 1 - index, axis) for term in terms]).astype(BF16)
        got = lax.ppermute(send, "table", [(i, i ^ bit) for i in range(owners)])
        kept = [entry(term, index, axis) for term in terms]
        return ([add(kept)] if last else kept) + [got]

    if side == 2:
        left = halve(sides[0], middle, 1, 2, False)
        right = halve(sides[1], low, 2, 1, False)
        left = halve(left, low, 1, 1, True)
        right = halve(right, middle, 1, 2, True)
    else:
        left, right = [[term[:, 0, 0] for term in terms] for terms in sides]
    cols = cols_all
    kept, *sends = call(
        functools.partial(plane_kernel, outer, len(left)),
        [
            jax.ShapeDtypeStruct((rows, cols), F32),
            *[jax.ShapeDtypeStruct((rows, cols), BF16) for _ in range(1, outer)],
        ],
        12 * outer * rows * cols,
        8 * outer * rows * cols,
        (*left, *right),
        limit=24,
    )
    got = [
        lax.ppermute(
            sends[k - 1],
            "table",
            [(i, ((i // plane + k) % outer) * plane + i % plane) for i in range(owners)],
        )
        for k in range(1, outer)
    ]

    incoming = lax.all_to_all(outgoing, "table", split_axis=0, concat_axis=0, tiled=True)
    incoming, kept = lax.optimization_barrier((incoming, kept))
    all_incoming = [incoming] + [shift(incoming, "group", groups, k) for k in range(1, groups)]
    grad_rows = table.shape[0] // groups
    (table_grad,) = call(
        functools.partial(collect_kernel, groups),
        [jax.ShapeDtypeStruct((grad_rows, width), F32)],
        2 * slots * table.shape[0] * width,
        2 * groups * slots * width + 4 * grad_rows * width,
        (*all_ids, *all_incoming),
        far=range(groups, 2 * groups),
        far_out=(0,),
        limit=24,
        scratch=[
            *[pltpu.VMEM((slots, width), BF16) for _ in range(groups)],
            pltpu.VMEM((grad_rows, width), F32),
            pltpu.SemaphoreType.DMA((groups + grad_rows // row_step(grad_rows),)),
        ],
    )

    kept, table_grad = lax.optimization_barrier((kept, table_grad))
    w_in_grad, mine, gain_grad = call(
        finish_kernel,
        [
            jax.ShapeDtypeStruct((rows, cols_in), F32),
            jax.ShapeDtypeStruct((rows, cols_out), F32),
            jax.ShapeDtypeStruct((1, rows), F32),
        ],
        4 * rows * cols_all,
        14 * rows * cols_all,
        (kept, *got),
        limit=24,
    )
    others = [shift(mine, "group", groups, k) for k in range(1, groups)]
    pieces = jnp.stack([mine, *others])
    w_out_grad = jnp.concatenate(
        [
            lax.dynamic_index_in_dim(pieces, (me - p) % groups, 0, keepdims=False)
            for p in range(wparts)
        ],
        1,
    )
    return (result, table_grad, w_in_grad, w_out_grad, gain_grad.reshape(rows))


def solution(mesh):
    return jax.shard_map(
        on_device,
        mesh=mesh,
        in_specs=(
            P(("table", "group"), None),
            P(("table", "group")),
            P(("table", "group"), None),
            P("table", None),
            P(),
            P(),
            P(),
            P(("table", "group"), None),
        ),
        out_specs=(
            P(("table", "group"), None),
            P(("table", "group"), None),
            P("table", "group"),
            P("table", None),
            P("table"),
        ),
        check_vma=False,
    )
```

```python
import functools
import math

import jax
import jax.numpy as jnp
from jax import lax
from jax.experimental import pallas as pl
from jax.experimental.pallas import tpu as pltpu
from jax.sharding import PartitionSpec as P

HEAD_DIM = 64
LANES = 128
QUERY_ROWS = 256

F32 = jnp.float32
BF16 = jnp.bfloat16


def iota(shape, dim):
    return lax.broadcasted_iota(jnp.int32, shape, dim)


def hot(cond):
    return jnp.where(cond, 1.0, 0.0).astype(BF16)


def dot_nn(a, b):
    return lax.dot_general(a, b, (((1,), (0,)), ((), ())), preferred_element_type=F32)


def dot_nt(a, b):
    return lax.dot_general(a, b, (((1,), (1,)), ((), ())), preferred_element_type=F32)


def dot_tn(a, b):
    return lax.dot_general(a, b, (((0,), (0,)), ((), ())), preferred_element_type=F32)


def row_step(rows):
    return 256 if rows % 256 == 0 else rows


def call(kernel, out_shape, flops, nbytes, operands, smem=(), far=(), far_out=(), limit=56, scratch=()):
    spaces = [
        pltpu.SMEM if i in smem else pl.ANY if i in far else pltpu.VMEM
        for i in range(len(operands))
    ]
    out_spaces = [pl.ANY if i in far_out else pltpu.VMEM for i in range(len(out_shape))]
    return pl.pallas_call(
        kernel,
        out_shape=out_shape,
        in_specs=[pl.BlockSpec(memory_space=space) for space in spaces],
        out_specs=[pl.BlockSpec(memory_space=space) for space in out_spaces],
        scratch_shapes=scratch,
        compiler_params=pltpu.CompilerParams(vmem_limit_bytes=limit * 1024 * 1024),
        cost_estimate=pl.CostEstimate(flops=flops, bytes_accessed=nbytes, transcendentals=0),
    )(*operands)


def request_kernel(cap, owner_ref, row_ref, req_ref, slot_ref):
    owners, width = req_ref.shape
    count = owner_ref.shape[1]
    owner = owner_ref[...]
    row = row_ref[...]
    mine = iota((owners, count), 0) == owner
    mine_b = hot(mine)
    before = hot(iota((count, count), 0) < iota((count, count), 1))
    earlier = dot_nn(mine_b, before)
    place = jnp.sum(jnp.where(mine, earlier, 0.0), axis=0, keepdims=True)
    slot_ref[...] = owner.astype(F32) * float(cap) + place
    at_place = hot(iota((width, count), 0).astype(F32) == place)
    high = jnp.where(mine, (row >> 8).astype(F32), 0.0).astype(BF16)
    low = jnp.where(mine, (row & 255).astype(F32), 0.0).astype(BF16)
    found = dot_nt(high, at_place) * 256.0 + dot_nt(low, at_place)
    req_ref[...] = found.astype(jnp.int32)


def lookup_kernel(cap, wanted_ref, table_ref, found_ref, ids_ref):
    owners, width = wanted_ref.shape
    slots = found_ref.shape[0]
    rows = table_ref.shape[0]
    wanted = wanted_ref[...]
    high = (wanted >> 8).astype(F32).astype(BF16)
    low = (wanted & 255).astype(F32).astype(BF16)
    slot = iota((slots, owners), 0).astype(F32)
    holder = jnp.floor((slot + 0.5) * (1.0 / cap))
    spread = hot(holder == iota((slots, owners), 1).astype(F32))
    ids = dot_nn(spread, high) * 256.0 + dot_nn(spread, low)
    slot = iota((slots, width), 0).astype(F32)
    place = slot - jnp.floor((slot + 0.5) * (1.0 / cap)) * float(cap)
    ids = jnp.sum(
        jnp.where(iota((slots, width), 1).astype(F32) == place, ids, 0.0), axis=1, keepdims=True
    )
    wide = jnp.broadcast_to(ids, (slots, LANES))
    ids_ref[...] = wide.T[0:1, :]
    step = 256 if slots % 256 == 0 else slots
    for start in range(0, slots, step):
        part = ids[start : start + step]
        pick = hot(iota((step, rows), 1).astype(F32) == part)
        found_ref[start : start + step, :] = dot_nn(pick, table_ref[...]).astype(BF16)


def collect_kernel(groups, *refs):
    ids_refs, in_hbms, out_hbm = refs[:groups], refs[groups : 2 * groups], refs[2 * groups]
    in_refs, out_ref, sems = refs[2 * groups + 1 : 3 * groups + 1], refs[-2], refs[-1]
    rows = out_ref.shape[0]
    slots = in_refs[0].shape[0]
    fetches = [
        pltpu.make_async_copy(hbm, ref, sems.at[n])
        for n, (hbm, ref) in enumerate(zip(in_hbms, in_refs))
    ]
    for fetch in fetches:
        fetch.start()
    base = lax.axis_index("group") * rows
    step = row_step(rows)
    for fetch in fetches:
        fetch.wait()
    stores = []
    for n, start in enumerate(range(0, rows, step)):
        own = (iota((step, slots), 0) + (base + start)).astype(F32)
        total = None
        for ids_ref, in_ref in zip(ids_refs, in_refs):
            part = dot_nn(hot(own == ids_ref[...]), in_ref[...])
            total = part if total is None else total + part
        out_ref[start : start + step, :] = total
        here = pl.ds(start, step)
        stores.append(
            pltpu.make_async_copy(out_ref.at[here], out_hbm.at[here], sems.at[groups + n])
        )
        stores[-1].start()
    for store in stores:
        store.wait()


def layer_kernel(
    groups,
    wparts,
    len_ref,
    slot_ref,
    ret_hbm,
    w_in_hbm,
    w_out_hbm,
    gain_ref,
    cot_hbm,
    *rest,
):
    result_hbm, row_hbm = rest[:2]
    grads_hbms = rest[2 : 2 + 2 * groups]
    (
    ret_ref,
    w_in_ref,
    w_out_ref,
    cot_ref,
    result_ref,
    row_ref,
    grads_ref,
    pick_ref,
    put_ref,
    emb_ref,
    proj_ref,
    slope_ref,
    bias_ref,
    weight_ref,
    wslope_ref,
    att_ref,
    mixed_ref,
    gatt_ref,
    gpre_ref,
    gval_ref,
    gkey_ref,
    gwo_ref,
    sems,
    ) = rest[2 + 2 * groups :]
    count, width = cot_ref.shape
    slots = ret_hbm.shape[0]
    per = LANES // HEAD_DIM
    slabs = width // LANES
    qrows = QUERY_ROWS if count % QUERY_ROWS == 0 else count
    half_scale = 0.5 / math.sqrt(HEAD_DIM)

    get_ret = pltpu.make_async_copy(ret_hbm, ret_ref, sems.at[8 + 2 * groups])
    get_ret.start()
    parts = [pl.ds(i * width, width) for i in range(4)]
    get_ins = [
        pltpu.make_async_copy(w_in_hbm.at[:, part], w_in_ref.at[:, part], sems.at[i])
        for i, part in enumerate(parts)
    ]
    get_cot = pltpu.make_async_copy(cot_hbm, cot_ref, sems.at[4])
    get_out = pltpu.make_async_copy(w_out_hbm, w_out_ref, sems.at[5])
    for fetch in (*get_ins, get_cot, get_out):
        fetch.start()

    slot = jnp.broadcast_to(slot_ref[...], (LANES, count)).T
    for start in range(0, slots, LANES):
        pick_ref[:, start : start + LANES] = hot(
            slot == (iota((count, LANES), 1) + start).astype(F32)
        )
    get_ret.wait()
    emb_ref[...] = dot_nn(pick_ref[...], ret_ref[...]).astype(BF16)

    for fetch in (*get_ins, get_cot, get_out):
        fetch.wait()
    for i in range(4):
        pre = dot_nn(emb_ref[...], w_in_ref[:, parts[i]])
        half = 0.5 * pre
        th = jnp.tanh(half)
        act = half + half * th
        proj_ref[i] = act.astype(BF16)
        slope_ref[i] = 0.5 * ((1.0 + th) + act * (1.0 - th))

    pos = iota((count, 1), 0)
    begin = jnp.zeros((count, 1), jnp.int32)
    end = jnp.int32(0)
    for s in range(len_ref.shape[1]):
        end = end + len_ref[0, s]
        begin = jnp.where(pos >= end, end, begin)
    key = iota((count, count), 1)
    allowed = (key >= begin) & (key <= iota((count, count), 0))
    bias_ref[...] = jnp.where(allowed, 3.0e38, -30.0)

    lane = iota((qrows, LANES), 1)
    inside = [(lane >= a * HEAD_DIM) & (lane < (a + 1) * HEAD_DIM) for a in range(per)]
    lane = iota((count, LANES), 1)
    inside_all = [(lane >= a * HEAD_DIM) & (lane < (a + 1) * HEAD_DIM) for a in range(per)]

    def stacked(value, factor=1.0):
        value = value.astype(F32) * factor
        return jnp.concatenate([jnp.where(m, value, 0.0) for m in inside], 0).astype(BF16)

    row = iota((LANES, qrows), 0)
    inside_rows = [(row >= a * HEAD_DIM) & (row < (a + 1) * HEAD_DIM) for a in range(per)]

    def stacked_t(value, factor=1.0):
        value = (value.astype(F32) * factor).T
        return jnp.concatenate([jnp.where(m, value, 0.0) for m in inside_rows], 1).astype(BF16)

    def apart(value):
        value = value.astype(F32)
        return [jnp.where(m, value, 0.0).astype(BF16) for m in inside_all]

    def forward(p, _):
        cols = pl.ds(pl.multiple_of(p * LANES, LANES), LANES)
        key_all = proj_ref[3, :, cols]
        vals = apart(proj_ref[1, :, cols])
        for r0 in range(0, count, qrows):
            r1 = r0 + qrows
            half = dot_nt(stacked(proj_ref[2, r0:r1, cols], half_scale), key_all[:r1])
            half = jnp.minimum(half.reshape(per, qrows, r1), bias_ref[r0:r1, :r1][None])
            th = jnp.tanh(half)
            weight = half + half * th
            weight_b = weight.astype(BF16)
            base = per * r0
            weight_ref[p, base : base + per * qrows, :r1] = weight_b.reshape(per * qrows, r1)
            wslope_ref[p, base : base + per * qrows, :r1] = (
                (1.0 + th) + weight * (1.0 - th)
            ).astype(BF16).reshape(per * qrows, r1)
            total = dot_nn(weight_b[0], vals[0][:r1])
            for a in range(1, per):
                total = total + dot_nn(weight_b[a], vals[a][:r1])
            att_ref[r0:r1, cols] = total
        return 0

    lax.fori_loop(0, slabs, forward, 0, unroll=4)

    gain = gain_ref[...]
    gain_sum = jnp.zeros((1, width), F32)
    for r0 in range(0, count, qrows):
        rows = slice(r0, r0 + qrows)
        att = att_ref[rows, :]
        centered = att - jnp.mean(att, 1, keepdims=True)
        inv = lax.rsqrt(jnp.mean(centered * centered, 1, keepdims=True) + 1e-05)
        normed = centered * inv
        upd = proj_ref[0, rows, :].astype(F32)
        scaled = normed * gain
        mixed = (scaled * upd).astype(BF16)
        mixed_ref[rows, :] = mixed
        result_ref[rows, :] = (
            emb_ref[rows, :].astype(F32) + dot_nn(mixed, w_out_ref[...])
        ).astype(BF16)
        gmix = dot_nt(cot_ref[rows, :], w_out_ref[...]).astype(BF16).astype(F32)
        gpre_ref[rows, 0:width] = (gmix * scaled * slope_ref[0, rows, :]).astype(BF16)
        gnorm = gmix * gain * upd
        gain_sum = gain_sum + jnp.sum(gmix * normed * upd, 0, keepdims=True)
        mean1 = jnp.mean(gnorm, 1, keepdims=True)
        mean2 = jnp.mean(gnorm * normed, 1, keepdims=True)
        gatt_ref[rows, :] = ((gnorm - mean1 - normed * mean2) * inv).astype(BF16)
    gwo_ref[...] = dot_tn(mixed_ref[...], cot_ref[...]).astype(BF16)

    def backward(p, _):
        start = pl.multiple_of(p * LANES, LANES)
        cols = pl.ds(start, LANES)
        val = proj_ref[1, :, cols]
        keys = apart(proj_ref[3, :, cols])
        for r0 in reversed(range(0, count, qrows)):
            r1 = r0 + qrows
            base = per * r0
            rows = slice(base, base + per * qrows)
            gatt = stacked(gatt_ref[r0:r1, cols])
            gweight = dot_nt(gatt, val[:r1])
            gscore = (gweight * wslope_ref[p, rows, :r1].astype(F32)).astype(BF16)
            gqry = dot_nn(gscore[:qrows], keys[0][:r1])
            for a in range(1, per):
                gqry = gqry + dot_nn(gscore[a * qrows : (a + 1) * qrows], keys[a][:r1])
            gval = dot_nn(stacked_t(gatt_ref[r0:r1, cols]), weight_ref[p, rows, :r1])
            gkey = dot_nn(stacked_t(proj_ref[2, r0:r1, cols], half_scale), gscore)
            if r1 == count:
                gval_ref[...] = gval
                gkey_ref[...] = gkey
            else:
                gval_ref[:, :r1] += gval
                gkey_ref[:, :r1] += gkey
            gpre_ref[r0:r1, pl.ds(2 * width + start, LANES)] = (
                gqry * half_scale * slope_ref[2, r0:r1, cols]
            ).astype(BF16)
        gpre_ref[:, pl.ds(width + start, LANES)] = (gval_ref[...].T * slope_ref[1, :, cols]).astype(BF16)
        gpre_ref[:, pl.ds(3 * width + start, LANES)] = (gkey_ref[...].T * slope_ref[3, :, cols]).astype(BF16)
        return 0

    lax.fori_loop(0, slabs, backward, 0, unroll=4)

    put_result = pltpu.make_async_copy(result_ref, result_hbm, sems.at[6])
    put_result.start()
    puts = [put_result]
    put_ref[...] = hot(iota((slots, count), 0).astype(F32) == slot_ref[...])

    me = lax.axis_index("group")
    emb_t = emb_ref[...].T
    cols_in = 4 * width // groups
    cols_out = width // wparts
    chunk = min(cols_in, 512)
    gain_col = jnp.broadcast_to(gain_sum, (LANES, width)).T.astype(BF16)
    for k in [*range(1, groups), 0]:
        part = lax.rem(me + k, groups)
        for c in range(0, cols_in, chunk):
            cols = pl.ds(pl.multiple_of(part * cols_in + c, LANES), chunk)
            grads_ref[k, :, c : c + chunk] = dot_nn(emb_t, gpre_ref[:, cols]).astype(BF16)
        cols = pl.ds(pl.multiple_of(lax.rem(part, wparts) * cols_out, LANES), cols_out)
        grads_ref[k, :, cols_in : cols_in + cols_out] = gwo_ref[:, cols]
        grads_ref[k, :, cols_in + cols_out :] = gain_col
        cut = grads_hbms[2 * k].shape[1]
        for i, cols in enumerate((pl.ds(0, cut), pl.ds(cut, grads_ref.shape[2] - cut))):
            put = pltpu.make_async_copy(
                grads_ref.at[k, :, cols], grads_hbms[2 * k + i], sems.at[8 + 2 * k + i]
            )
            put.start()
            puts.append(put)
    gemb = (cot_ref[...].astype(F32) + dot_nt(gpre_ref[...], w_in_ref[...])).astype(BF16)
    step = slots // 2
    for i, start in enumerate((0, step)):
        rows = pl.ds(start, step)
        row_ref[rows, :] = dot_nn(put_ref[rows, :], gemb).astype(BF16)
        sem = sems.at[7 + i * (2 + 2 * groups)]
        puts.append(pltpu.make_async_copy(row_ref.at[rows], row_hbm.at[rows], sem))
        puts[-1].start()
    for put in puts:
        put.wait()


def plane_kernel(outer, terms, *refs):
    left, right, outs = refs[:terms], refs[terms : 2 * terms], refs[2 * terms :]
    cut = left[0].shape[2]
    high = lax.div(lax.axis_index("table"), lax.axis_size("table") // outer)
    for k in range(outer):
        at = lax.rem(high + k, outer)
        for parts, cols in ((left, slice(0, cut)), (right, slice(cut, None))):
            total = parts[0][at].astype(F32)
            for part in parts[1:]:
                total = total + part[at].astype(F32)
            outs[k][:, cols] = total.astype(outs[k].dtype)


def finish_kernel(kept_ref, *refs):
    got_refs, (in_ref, out_ref, gain_ref) = refs[:-3], refs[-3:]
    total = kept_ref[...]
    for got_ref in got_refs:
        total = total + got_ref[...].astype(F32)
    cols_in, cols_out = in_ref.shape[1], out_ref.shape[1]
    in_ref[...] = total[:, :cols_in]
    out_ref[...] = total[:, cols_in : cols_in + cols_out]
    gain_ref[...] = total[:, cols_in + cols_out :].T[0:1, :]


def shift(value, axis, size, amount):
    return lax.ppermute(value, axis, [(i, (i + amount) % size) for i in range(size)])


def on_device(item_owner, item_row, lengths, table, w_in, w_out, gain, cotangent):
    owners = lax.axis_size("table")
    groups = lax.axis_size("group")
    count = item_row.shape[0]
    width = table.shape[1]
    capacity = max(2, 3 * count // (2 * owners))
    slots = owners * capacity
    padded = -(-capacity // LANES) * LANES
    me = lax.axis_index("group")

    requested, slot = call(
        functools.partial(request_kernel, capacity),
        [
            jax.ShapeDtypeStruct((owners, padded), jnp.int32),
            jax.ShapeDtypeStruct((1, count), F32),
        ],
        4 * count * count * owners,
        8 * count,
        (item_owner.reshape(1, count), item_row.reshape(1, count)),
    )
    wanted = lax.all_to_all(requested, "table", split_axis=0, concat_axis=0, tiled=True)
    found, ids = call(
        functools.partial(lookup_kernel, capacity),
        [
            jax.ShapeDtypeStruct((slots, width), BF16),
            jax.ShapeDtypeStruct((1, slots), F32),
        ],
        2 * slots * table.shape[0] * width,
        2 * (slots + table.shape[0]) * width,
        (wanted, table),
    )
    returned = lax.all_to_all(found, "table", split_axis=0, concat_axis=0, tiled=True)
    all_ids = [ids] + [shift(ids, "group", groups, k) for k in range(1, groups)]
    returned, *all_ids = lax.optimization_barrier((returned, *all_ids))

    wparts = min(groups, width // LANES)
    heads_per = LANES // HEAD_DIM
    cols_in = 4 * width // groups
    cols_out = width // wparts
    cols_all = cols_in + cols_out + LANES
    cut = cols_all // LANES // 2 * LANES
    square = pltpu.VMEM((count, width), BF16)
    result, outgoing, *grads = call(
        functools.partial(layer_kernel, groups, wparts),
        [
            jax.ShapeDtypeStruct((count, width), BF16),
            jax.ShapeDtypeStruct((slots, width), BF16),
            *[
                jax.ShapeDtypeStruct((width, cols), BF16)
                for _ in range(groups)
                for cols in (cut, cols_all - cut)
            ],
        ],
        32 * count * width * width + 14 * count * count * width,
        24 * count * width,
        (lengths, slot, returned, w_in, w_out, gain.reshape(1, width), cotangent),
        smem=(0,),
        far=(2, 3, 4, 6),
        far_out=range(2 + 2 * groups),
        scratch=[
            pltpu.VMEM((slots, width), BF16),
            pltpu.VMEM(w_in.shape, BF16),
            pltpu.VMEM(w_out.shape, BF16),
            square,
            square,
            pltpu.VMEM((slots, width), BF16),
            pltpu.VMEM((groups, width, cols_all), BF16),
            pltpu.VMEM((count, slots), BF16),
            pltpu.VMEM((slots, count), BF16),
            square,
            pltpu.VMEM((4, count, width), BF16),
            pltpu.VMEM((4, count, width), F32),
            pltpu.VMEM((count, count), F32),
            pltpu.VMEM((width // LANES, heads_per * count, count), BF16),
            pltpu.VMEM((width // LANES, heads_per * count, count), BF16),
            pltpu.VMEM((count, width), F32),
            square,
            square,
            pltpu.VMEM((count, 4 * width), BF16),
            pltpu.VMEM((LANES, count), F32),
            pltpu.VMEM((LANES, count), F32),
            pltpu.VMEM((width, width), BF16),
            pltpu.SemaphoreType.DMA((10 + 2 * groups,)),
        ],
    )
    rows = width // owners
    side = 2 if owners % 4 == 0 else 1
    plane = side * side
    outer = owners // plane
    here = lax.axis_index("table")
    high, middle, low = here // plane, here // side % side, here % side
    sides = []
    for i in range(2):
        terms = [grads[i]] + [shift(grads[2 * k + i], "group", groups, k) for k in range(1, groups)]
        sides.append([term.reshape(outer, side, side, rows, term.shape[1]) for term in terms])

    def entry(value, index, axis):
        return lax.dynamic_index_in_dim(value, index, axis, keepdims=False)

    def add(terms):
        return sum(term.astype(F32) for term in terms)

    def halve(terms, index, axis, bit, last):
        send = add([entry(term, 1 - index, axis) for term in terms]).astype(BF16)
        got = lax.ppermute(send, "table", [(i, i ^ bit) for i in range(owners)])
        kept = [entry(term, index, axis) for term in terms]
        return ([add(kept)] if last else kept) + [got]

    if side == 2:
        left = halve(sides[0], low, 2, 1, False)
        right = halve(sides[1], middle, 1, 2, False)
        left = halve(left, middle, 1, 2, True)
        right = halve(right, low, 1, 1, True)
    else:
        left, right = [[term[:, 0, 0] for term in terms] for terms in sides]
    cols = cols_all
    kept, *sends = call(
        functools.partial(plane_kernel, outer, len(left)),
        [
            jax.ShapeDtypeStruct((rows, cols), F32),
            *[jax.ShapeDtypeStruct((rows, cols), BF16) for _ in range(1, outer)],
        ],
        12 * outer * rows * cols,
        8 * outer * rows * cols,
        (*left, *right),
        limit=24,
    )
    got = [
        lax.ppermute(
            sends[k - 1],
            "table",
            [(i, ((i // plane + k) % outer) * plane + i % plane) for i in range(owners)],
        )
        for k in range(1, outer)
    ]

    incoming = lax.all_to_all(outgoing, "table", split_axis=0, concat_axis=0, tiled=True)
    incoming, kept = lax.optimization_barrier((incoming, kept))
    all_incoming = [incoming] + [shift(incoming, "group", groups, k) for k in range(1, groups)]
    grad_rows = table.shape[0] // groups
    (table_grad,) = call(
        functools.partial(collect_kernel, groups),
        [jax.ShapeDtypeStruct((grad_rows, width), F32)],
        2 * slots * table.shape[0] * width,
        2 * groups * slots * width + 4 * grad_rows * width,
        (*all_ids, *all_incoming),
        far=range(groups, 2 * groups),
        far_out=(0,),
        limit=24,
        scratch=[
            *[pltpu.VMEM((slots, width), BF16) for _ in range(groups)],
            pltpu.VMEM((grad_rows, width), F32),
            pltpu.SemaphoreType.DMA((groups + grad_rows // row_step(grad_rows),)),
        ],
    )

    kept, table_grad = lax.optimization_barrier((kept, table_grad))
    w_in_grad, mine, gain_grad = call(
        finish_kernel,
        [
            jax.ShapeDtypeStruct((rows, cols_in), F32),
            jax.ShapeDtypeStruct((rows, cols_out), F32),
            jax.ShapeDtypeStruct((1, rows), F32),
        ],
        4 * rows * cols_all,
        14 * rows * cols_all,
        (kept, *got),
        limit=24,
    )
    others = [shift(mine, "group", groups, k) for k in range(1, groups)]
    pieces = jnp.stack([mine, *others])
    w_out_grad = jnp.concatenate(
        [
            lax.dynamic_index_in_dim(pieces, (me - p) % groups, 0, keepdims=False)
            for p in range(wparts)
        ],
        1,
    )
    return (result, table_grad, w_in_grad, w_out_grad, gain_grad.reshape(rows))


def solution(mesh):
    return jax.shard_map(
        on_device,
        mesh=mesh,
        in_specs=(
            P(("table", "group"), None),
            P(("table", "group")),
            P(("table", "group"), None),
            P("table", None),
            P(),
            P(),
            P(),
            P(("table", "group"), None),
        ),
        out_specs=(
            P(("table", "group"), None),
            P(("table", "group"), None),
            P("table", "group"),
            P("table", None),
            P("table"),
        ),
        check_vma=False,
    )
```
